128 devices in a mesh: dp: 32 (over x, z, core), row: 2 (over y_lo), col: 2 (over y_hi).
Axes of the slice: x: 4, y: 4 (y_hi: 2, y_lo: 2; y = y_hi * 2 + y_lo), z: 4, core: 2. Of those that a mesh axis runs over, the one named last changes fastest.
Arguments:
- tokens: bfloat16 [32768, 1536], P(('dp', 'row'), 'col'), may hold values from -6 to 6
- cotangent: bfloat16 [32768, 1536], P(('dp', 'row'), 'col'), may hold values from -6 to 6
- attn_gain: float32 [1536], P('col'), may hold values from 0.25 to 1.75
- ffn_gain: float32 [1536], P('col'), may hold values from 0.25 to 1.75
- qkv_weight: bfloat16 [1536, 2048], P('col', 'row'), may hold values from -0.15625 to 0.15625
- out_weight: bfloat16 [1536, 1536], P('row', 'col'), may hold values from -1.25 to 1.25
- router_weight: bfloat16 [1536, 6], P('col'), may hold values from -0.078125 to 0.078125
- gate_weight: bfloat16 [6, 1536, 768], P(None, 'col', 'row'), may hold values from -0.15625 to 0.15625
- up_weight: bfloat16 [6, 1536, 768], P(None, 'col', 'row'), may hold values from -0.15625 to 0.15625
- down_weight: bfloat16 [6, 768, 1536], P(None, 'row', 'col'), may hold values from -0.625 to 0.625
- routes: int32 [32768, 4], P('dp'), may hold values from 0 to 5, all different within a row
- segments: int32 [32768], P('dp'), may hold values from 0 to 4, as said below
Outputs:
- layer_out: bfloat16 [32768, 1536], P(('dp', 'row'), 'col')
- input_grad: float32 [32768, 1536], P(('dp', 'row'), 'col')
- attn_gain_grad: float32 [1536], P('col')
- ffn_gain_grad: float32 [1536], P('col')
- qkv_grad: float32 [1536, 2048], P('col', 'row')
- out_grad: float32 [1536, 1536], P('row', 'col')
- router_grad: float32 [1536, 6], P('col')
- gate_grad: float32 [6, 1536, 768], P(None, 'col', 'row')
- up_grad: float32 [6, 1536, 768], P(None, 'col', 'row')
- down_grad: float32 [6, 768, 1536], P(None, 'row', 'col')
The draws below stay inside these ranges and needn't reach their ends.
Inputs may be any that keep to these rules, and one draw needn't show every extreme that they name: `routes`: each token names 4 different experts; every expert is named by some token. Within each packed sequence of 1024 tokens the segment numbers run from 0 to 4 without falling; segment 2 holds exactly 512 tokens and contains the sequence's middle, the other segments are shorter.
All inputs are finite; a program needn't handle non-finite values.
Results may differ from the reference program's by a relative error of at most 0.022.
Values may be sent and summed in bfloat16 or wider, within the bound.
A program may use at most 256 MiB of HBM per device.

```python
import math
from functools import partial
import jax
import jax.numpy as jnp
from jax import lax

D = 1536
QUERY_HEADS = 12
KEY_VALUE_HEADS = 2
HEAD_SIZE = 128
H = 768
TOPK = 4
E = 6
TOK_GRP = 1024
TOKENS = 32768
QKV = 2048


def draw_segments(key, part):
    key = jax.random.fold_in(key, 7)
    group_count = TOKENS // TOK_GRP
    middle = TOK_GRP // 2
    group_keys = jax.random.split(key, group_count)

    def one_group(group_key):
        key_a, key_b, key_c = jax.random.split(group_key, 3)
        opening = jax.random.randint(key_a, (), 2, middle - 1)
        leading = jax.random.randint(key_b, (), 1, opening)
        trailing = jax.random.randint(key_c, (), opening + middle + 1, TOK_GRP)
        places = jnp.arange(TOK_GRP, dtype=jnp.int32)
        return (places >= leading).astype(jnp.int32) + (places >= opening).astype(jnp.int32) + (places >= opening + middle).astype(jnp.int32) + (places >= trailing).astype(jnp.int32)
    return jax.vmap(one_group)(group_keys).reshape(-1).astype(jnp.int32)


def shard_levels(key, shape, cuts, low, top_value):
    def one(position, parts):
        steps = jax.random.uniform(jax.random.fold_in(jax.random.fold_in(key, 6), position), (parts,), jnp.float32, low / len(cuts), top_value / len(cuts))
        return jnp.repeat(jnp.exp(steps), shape[position] // parts).reshape((-1,) + (1,) * (len(shape) - position - 1))

    level = one(*cuts[0])
    for cut in cuts[1:]:
        level = level * one(*cut)
    return level


def choose_distinct(own_key, rows, amount, top, lift):
    sequence = jax.random.permutation(jax.random.fold_in(own_key, 1), amount)
    pull = sequence
    for power in range(3):
        pull = pull * pull // amount
    pull = pull * lift // amount
    tickets = jax.random.randint(jax.random.fold_in(own_key, 2), (rows, amount), 0, 4096) + pull
    fixed_rows = jax.random.permutation(jax.random.fold_in(own_key, 3), rows)[jnp.arange(amount) % rows]
    tickets = jnp.where(jnp.arange(rows)[:, None] == fixed_rows[None, :], 1 << 14, tickets)
    priority = tickets * amount + jnp.arange(amount)
    return lax.top_k(priority.astype(jnp.int32), top)[1].astype(jnp.int32)


def noise(key, dims, spread, most, cuts=(), kind=jnp.bfloat16):
    values = spread * jax.random.normal(key, dims, jnp.float32)
    if cuts:
        values = values * shard_levels(key, dims, cuts, -0.22, 0.18)
    return jnp.clip(values, -most, most).astype(kind)


def setup_inputs(seed: int = 0) -> dict:
    key_list = jax.random.split(jax.random.key(seed), 13)
    return {
        "tokens": noise(key_list[0], (TOKENS, D), 1.0, 6.0, ((0, 64), (1, 2))),
        "cotangent": noise(key_list[1], (TOKENS, D), 1.0, 6.0, ((0, 64), (1, 2))),
        "attn_gain": jnp.clip(1.0 + 0.15 * jax.random.normal(key_list[2], (D,), jnp.float32), 0.25, 1.75),
        "ffn_gain": jnp.clip(1.0 + 0.15 * jax.random.normal(key_list[3], (D,), jnp.float32), 0.25, 1.75),
        "qkv_weight": noise(key_list[4], (D, QKV), D ** -0.5, 0.15625, ((0, 2), (1, 2))),
        "out_weight": noise(key_list[5], (QUERY_HEADS * HEAD_SIZE, D), (D // 64) ** -0.5, 1.25, ((0, 2), (1, 2))),
        "router_weight": noise(key_list[6], (D, E), (4 * D) ** -0.5, 0.078125, ((0, 2),)),
        "gate_weight": noise(key_list[7], (E, D, H), D ** -0.5, 0.15625, ((1, 2), (2, 2))),
        "up_weight": noise(key_list[8], (E, D, H), D ** -0.5, 0.15625, ((1, 2), (2, 2))),
        "down_weight": noise(key_list[9], (E, H, D), (H // 8) ** -0.5, 0.625, ((1, 2), (2, 2))),
        "routes": choose_distinct(key_list[10], TOKENS, E, TOPK, 0),
        "segments": draw_segments(jax.random.fold_in(key_list[12], 71), 0),
    }


epsilon = 1e-06
rope_base = 10000.0
masked_value = -1e+30
highest = lax.Precision.HIGHEST

@jax.custom_vjp
def low(v):
    return lax.optimization_barrier(v.astype(jnp.bfloat16)).astype(jnp.float32)

@jax.custom_vjp
def low_back(v):
    return v

def low_keep(v):
    return (low(v), None)

def low_pass(kept, grad):
    return (grad,)

def back_keep(v):
    return (v, None)

def back_low(kept, grad):
    return (low(grad),)
low.defvjp(low_keep, low_pass)
low_back.defvjp(back_keep, back_low)

def tables(positions):
    steps_up = jnp.arange(HEAD_SIZE // 2, dtype=jnp.float32) * (2.0 / HEAD_SIZE)
    inverse = jnp.exp(-math.log(rope_base) * steps_up)
    angles = positions[:, None] * inverse[None, :]
    return (jnp.cos(angles), jnp.sin(angles))

def rotate(values, cosine_table, sine_table):
    half_width = values.shape[-1] // 2
    first_half = values[..., :half_width]
    second_half = values[..., half_width:]
    return jnp.concatenate([first_half * cosine_table - second_half * sine_table, second_half * cosine_table + first_half * sine_table], axis=-1)

def attend(allowed, pieces):
    query_group, key_group, value_group = pieces
    scores = low_back(jnp.einsum('qnd,kd->nqk', query_group, key_group, precision=highest) * HEAD_SIZE ** (-0.5))
    scores = jnp.where(allowed[None], scores, masked_value)
    top_score = lax.optimization_barrier(jnp.max(scores, axis=-1, keepdims=True))
    exp_scores = jnp.exp(scores - top_score)
    probabilities = low(exp_scores / lax.optimization_barrier(jnp.sum(exp_scores, axis=-1, keepdims=True)))
    return jnp.einsum('nqk,kd->qnd', probabilities, value_group, precision=highest)

def block_forward(residual, attn_gain, ffn_gain, qkv_weight, out_weight, router_weight, gate_weight, up_weight, down_weight, routes, segments):
    row_sum_total = residual.shape[0]
    scale_one = lax.rsqrt(lax.optimization_barrier(jnp.mean(residual * residual, axis=1)) + epsilon)
    normed_one = low(residual * scale_one[:, None] * attn_gain)
    router_logits = low_back(jnp.dot(normed_one, router_weight, precision=highest))
    chosen = jnp.any(routes[:, :, None] == jnp.arange(E, dtype=jnp.int32)[None, None, :], axis=1)
    masked = jnp.where(chosen, router_logits, masked_value)
    top_logit = lax.optimization_barrier(jnp.max(masked, axis=1, keepdims=True))
    raised_values = jnp.exp(masked - top_logit)
    gate_values = raised_values / lax.optimization_barrier(jnp.sum(raised_values, axis=1, keepdims=True))
    tokens_per_group = QUERY_HEADS // KEY_VALUE_HEADS
    projected_rows = low_back(jnp.dot(normed_one, qkv_weight, precision=highest))
    projected_rows = projected_rows.reshape(row_sum_total, KEY_VALUE_HEADS, tokens_per_group + 2, HEAD_SIZE)
    cosine_table, sine_table = tables(jnp.arange(row_sum_total).astype(jnp.float32))
    queries = low(rotate(projected_rows[:, :, :tokens_per_group], cosine_table[:, None, None], sine_table[:, None, None]))
    keys_all = low(rotate(projected_rows[:, :, tokens_per_group], cosine_table[:, None], sine_table[:, None]))
    values_all = low(projected_rows[:, :, tokens_per_group + 1])
    places = jnp.arange(row_sum_total)
    allowed = (places[None, :] <= places[:, None]) & (segments[None, :] == segments[:, None])
    attended = lax.map(jax.checkpoint(partial(attend, allowed)), (jnp.moveaxis(queries, 1, 0), jnp.moveaxis(keys_all, 1, 0), jnp.moveaxis(values_all, 1, 0)))
    context = low_back(low(jnp.moveaxis(attended, 0, 1).reshape(row_sum_total, QUERY_HEADS * HEAD_SIZE)))
    mixed_attn = low_back(jnp.dot(context, out_weight, precision=highest))
    hidden_in = residual + mixed_attn
    scale_two = lax.rsqrt(lax.optimization_barrier(jnp.mean(hidden_in * hidden_in, axis=1)) + epsilon)
    normed_two = low(hidden_in * scale_two[:, None] * ffn_gain)
    gate_pre = low_back(jnp.einsum('td,edh->teh', normed_two, gate_weight, precision=highest))
    up_pre = low_back(jnp.einsum('td,edh->teh', normed_two, up_weight, precision=highest))
    weighted = low(gate_values[:, :, None] * jax.nn.silu(gate_pre) * up_pre)
    expert_out = low_back(jnp.einsum('teh,ehd->td', weighted, down_weight, precision=highest))
    return hidden_in + expert_out

def reference(tokens, cotangent, attn_gain, ffn_gain, qkv_weight, out_weight, router_weight, gate_weight, up_weight, down_weight, routes, segments):
    params = tuple((item.astype(jnp.float32) for item in (attn_gain, ffn_gain, qkv_weight, out_weight, router_weight, gate_weight, up_weight, down_weight)))
    group_count = tokens.shape[0] // TOK_GRP
    inputs = tokens.astype(jnp.float32).reshape(group_count, TOK_GRP, D)
    grads_in = cotangent.astype(jnp.float32).reshape(group_count, TOK_GRP, D)
    route_groups = routes.reshape(group_count, TOK_GRP, TOPK)
    segment_groups = segments.reshape(group_count, TOK_GRP)

    def group_step(running, pieces):
        block_in, block_grad, block_routes, block_segments = pieces

        def apply_block(values, *weights):
            return block_forward(values, *weights, block_routes, block_segments)
        result, pullback = jax.vjp(apply_block, block_in, *params)
        gradients = pullback(block_grad)
        running = tuple((total_now + gradient for total_now, gradient in zip(running, gradients[1:])))
        return (running, (result.astype(jnp.bfloat16), gradients[0]))
    zero_totals = tuple((jnp.zeros(item.shape, jnp.float32) for item in params))
    running, (results, input_grads) = lax.scan(group_step, zero_totals, (inputs, grads_in, route_groups, segment_groups))
    return (results.reshape(-1, D), input_grads.reshape(-1, D), running[0], running[1], running[2], running[3], running[4], running[5], running[6], running[7])
```

```python
import functools
import math

import jax
import jax.numpy as jnp
from jax import lax
from jax.experimental import pallas as pl
from jax.experimental.pallas import tpu as pltpu
from jax.sharding import PartitionSpec as P

f32 = jnp.float32
bf16 = jnp.bfloat16

HEAD = 128
GROUP_HEADS = 6
EPS = 1e-06
ROPE_BASE = 10000.0
MASKED = -1e30
BLOCK = 256


def flip(v, k):
    return lax.ppermute(v, ("row", "col"), [(i, i ^ k) for i in range(4)])


def gather4(x):
    half = x.shape[0] // 2
    a = flip(x, 2)
    b = flip(x, 3)
    c = jnp.concatenate([flip(b[:half], 2), flip(a[half:], 3)], axis=0)
    return x, c, a, b


def scatter4(p0, p1, p2, p3):
    half = p1.shape[0] // 2
    r2 = flip(p1[:half], 2)
    r3 = flip(p1[half:], 3)
    p3_top = (p3[:half].astype(f32) + r2.astype(f32)).astype(bf16)
    p2_end = (p2[half:].astype(f32) + r3.astype(f32)).astype(bf16)
    o3 = jnp.concatenate([flip(p3_top, 3), flip(p3[half:], 3)], axis=0)
    o2 = jnp.concatenate([flip(p2[:half], 2), flip(p2_end, 2)], axis=0)
    return p0.astype(f32) + o2.astype(f32) + o3.astype(f32)


def scatter_tokens(partial):
    rows, width = partial.shape[0] // 2, partial.shape[1] // 2
    low = partial.astype(bf16)
    return scatter4(
        partial[:rows, :width], low[:rows, width:], low[rows:, :width], low[rows:, width:]
    )


def dp_sizes():
    total = lax.axis_size("dp")
    cores = 2 if total % 2 == 0 else 1
    side = math.isqrt(total // cores)
    return side, side, cores


def dp_place():
    xs, zs, cs = dp_sizes()
    d = lax.axis_index("dp")
    return d // (zs * cs), (d // cs) % zs, d % cs


def shift(v, axis, k):
    xs, zs, cs = dp_sizes()
    pairs = []
    for x in range(xs):
        for z in range(zs):
            for c in range(cs):
                to = [x, z, c]
                to[axis] = (to[axis] + k) % (xs, zs, cs)[axis]
                pairs.append(((x * zs + z) * cs + c, (to[0] * zs + to[1]) * cs + to[2]))
    return lax.ppermute(v, "dp", pairs)


def pick(v, index):
    return lax.dynamic_index_in_dim(v, index, 0, keepdims=False)


def core_sum(part0, part1):
    xs, zs, cs = dp_sizes()
    if cs == 1:
        return jnp.concatenate([part0, part1], axis=0)
    core = dp_place()[2]
    send = jnp.where(core == 0, part1, part0)
    keep = jnp.where(core == 0, part0, part1)
    return (keep.astype(f32) + shift(send, 2, 1).astype(f32)).astype(bf16)


def axis_sum(v, axis):
    n = dp_sizes()[axis]
    place = dp_place()[axis]
    total = pick(v, place).astype(f32)
    for k in range(1, n):
        total = total + shift(pick(v, (place + k) % n), axis, k).astype(f32)
    return total.astype(bf16)


def plane_sums(a, b):
    xs, zs, _ = dp_sizes()
    width = a.shape[-1]
    a = axis_sum(a.reshape(xs, -1, width), 0)
    b = axis_sum(b.reshape(zs, -1, width), 1)
    a = axis_sum(a.reshape(zs, -1, width), 1)
    b = axis_sum(b.reshape(xs, -1, width), 0)
    return a, b


def small_sum(v):
    for axis, n in enumerate(dp_sizes()):
        total = v
        for k in range(1, n):
            total = total + shift(v, axis, k)
        v = total
    return v


def dp_gather(v):
    return lax.all_gather(v, "dp", axis=0, tiled=False).reshape(dp_sizes() + v.shape)


def by_col(col, mine, other, axis):
    return jnp.where(
        col == 0,
        jnp.concatenate([mine, other], axis=axis),
        jnp.concatenate([other, mine], axis=axis),
    )


def window(i, block):
    first = max(0, (i + 1) * block - 512 - block)
    return first, (i + 1) * block


def nt(a, b):
    return lax.dot_general(a, b, (((1,), (1,)), ((), ())), preferred_element_type=f32)


def nn(a, b):
    return lax.dot_general(a, b, (((1,), (0,)), ((), ())), preferred_element_type=f32)


def own_places(ref, out, row, half):
    for h in range(2):
        start = pl.multiple_of(half * jnp.bitwise_xor(row, h), half)
        out[h * half : (h + 1) * half] = ref[pl.ds(start, half)]


def allowed_keys(segk_ref, segq_ref, i, first, last):
    block = BLOCK
    width = last - first
    keys = lax.broadcasted_iota(jnp.int32, (width, block), 0) + first
    queries = lax.broadcasted_iota(jnp.int32, (width, block), 1) + i * block
    same = segk_ref[first:last] == segq_ref[:, i * block : (i + 1) * block]
    return (keys <= queries) & same


def attend_kernel(heads, q_ref, k_ref, v_ref, segk_ref, segq_ref, o_ref, lse_ref, q, k, vt):
    row = lax.axis_index("row")
    total = q_ref.shape[0]
    half = total // 2
    own_places(q_ref, q, row, half)
    own_places(k_ref, k, row, half)
    for h in range(2):
        start = pl.multiple_of(half * jnp.bitwise_xor(row, h), half)
        vt[:, h * half : (h + 1) * half] = v_ref[pl.ds(start, half)].astype(f32).T.astype(bf16)
    for i in range(total // BLOCK):
        first, last = window(i, BLOCK)
        at = slice(i * BLOCK, (i + 1) * BLOCK)
        allowed = allowed_keys(segk_ref, segq_ref, i, first, last)
        place = i * BLOCK // half
        start = pl.multiple_of(
            half * jnp.bitwise_xor(row, place) + (i * BLOCK - place * half), BLOCK
        )
        for h in range(heads):
            s = nt(k[first:last], q[at, h * HEAD : (h + 1) * HEAD]) * (HEAD**-0.5)
            s = jnp.where(allowed, s, MASKED)
            top = jnp.max(s, axis=0, keepdims=True)
            p = jnp.exp(s - top)
            total_p = jnp.sum(p, axis=0, keepdims=True)
            p = (p * (1.0 / total_p)).astype(bf16)
            ot = nn(vt[:, first:last], p)
            o_ref[pl.ds(start, BLOCK), h * HEAD : (h + 1) * HEAD] = ot.T.astype(bf16)
            lse_ref[h : h + 1, at] = top + jnp.log(total_p)


def attend(q, k, v, seg):
    total, width = q.shape
    heads = width // HEAD
    vm = pl.BlockSpec(memory_space=pltpu.VMEM)
    return pl.pallas_call(
        functools.partial(attend_kernel, heads),
        out_shape=(
            jax.ShapeDtypeStruct((total, width), bf16),
            jax.ShapeDtypeStruct((8, total), f32),
        ),
        in_specs=[vm] * 5,
        out_specs=(vm, vm),
        scratch_shapes=[
            pltpu.VMEM((total, width), bf16),
            pltpu.VMEM((total, HEAD), bf16),
            pltpu.VMEM((HEAD, total), bf16),
        ],
        compiler_params=pltpu.CompilerParams(vmem_limit_bytes=32 * 2**20),
        cost_estimate=pl.CostEstimate(
            flops=2 * heads * total * total * HEAD * 2,
            bytes_accessed=6 * total * width,
            transcendentals=heads * total * total,
        ),
        name="attend",
    )(q, k, v, seg.reshape(total, 1), seg.reshape(1, total))


def attend_back_kernel(
    heads,
    q_ref,
    k_ref,
    v_ref,
    do_ref,
    segk_ref,
    segq_ref,
    lse_ref,
    dq_ref,
    dk_ref,
    dv_ref,
    q,
    k,
    v,
    kt,
    do,
    dk,
    dv,
):
    row = lax.axis_index("row")
    total = q_ref.shape[0]
    half = total // 2
    scale = HEAD**-0.5
    own_places(q_ref, q, row, half)
    own_places(k_ref, k, row, half)
    own_places(v_ref, v, row, half)
    own_places(do_ref, do, row, half)
    kt[...] = k[...].astype(f32).T.astype(bf16)
    dk[...] = jnp.zeros_like(dk)
    dv[...] = jnp.zeros_like(dv)
    for i in range(total // BLOCK):
        first, last = window(i, BLOCK)
        at = slice(i * BLOCK, (i + 1) * BLOCK)
        allowed = allowed_keys(segk_ref, segq_ref, i, first, last)
        place = i * BLOCK // half
        start = pl.multiple_of(
            half * jnp.bitwise_xor(row, place) + (i * BLOCK - place * half), BLOCK
        )
        for h in range(heads):
            cols = slice(h * HEAD, (h + 1) * HEAD)
            s = nt(k[first:last], q[at, cols]) * scale
            s = jnp.where(allowed, s, MASKED)
            p = jnp.exp(s - lse_ref[h : h + 1, at])
            dp = nt(v[first:last], do[at, cols])
            inner = jnp.sum(dp * p, axis=0, keepdims=True)
            ds = (p * (dp - inner)).astype(bf16)
            dqt = nn(kt[:, first:last], ds) * scale
            dq_ref[pl.ds(start, BLOCK), cols] = dqt.T
            dk[first:last] += nn(ds, q[at, cols]) * scale
            dv[first:last] += nn(p.astype(bf16), do[at, cols])
    for h in range(2):
        start = pl.multiple_of(half * jnp.bitwise_xor(row, h), half)
        dk_ref[pl.ds(start, half)] = dk[h * half : (h + 1) * half]
        dv_ref[pl.ds(start, half)] = dv[h * half : (h + 1) * half]


def attend_back(q, k, v, do, seg, lse):
    total, width = q.shape
    heads = width // HEAD
    vm = pl.BlockSpec(memory_space=pltpu.VMEM)
    return pl.pallas_call(
        functools.partial(attend_back_kernel, heads),
        out_shape=(
            jax.ShapeDtypeStruct((total, width), f32),
            jax.ShapeDtypeStruct((total, HEAD), f32),
            jax.ShapeDtypeStruct((total, HEAD), f32),
        ),
        in_specs=[vm] * 7,
        out_specs=(vm, vm, vm),
        scratch_shapes=[
            pltpu.VMEM((total, width), bf16),
            pltpu.VMEM((total, HEAD), bf16),
            pltpu.VMEM((total, HEAD), bf16),
            pltpu.VMEM((HEAD, total), bf16),
            pltpu.VMEM((total, width), bf16),
            pltpu.VMEM((total, HEAD), f32),
            pltpu.VMEM((total, HEAD), f32),
        ],
        compiler_params=pltpu.CompilerParams(vmem_limit_bytes=40 * 2**20),
        cost_estimate=pl.CostEstimate(
            flops=5 * heads * total * total * HEAD * 2,
            bytes_accessed=10 * total * width,
            transcendentals=heads * total * total,
        ),
        name="attend_back",
    )(q, k, v, do, seg.reshape(total, 1), seg.reshape(1, total), lse)


def turn_tables(places):
    steps_up = jnp.arange(HEAD // 2, dtype=f32) * (2.0 / HEAD)
    inverse = jnp.exp(-math.log(ROPE_BASE) * steps_up)
    angles = places[:, None] * inverse[None, :]
    cosine, sine = jnp.cos(angles), jnp.sin(angles)
    return (
        jnp.concatenate([cosine, cosine], axis=1)[:, None],
        jnp.concatenate([-sine, sine], axis=1)[:, None],
    )


def swap_halves(v):
    half = v.shape[-1] // 2
    return jnp.concatenate([v[..., half:], v[..., :half]], axis=-1)


def turn(v, cosine, sine):
    return v * cosine + swap_halves(v) * sine


def turn_back(v, cosine, sine):
    return v * cosine - swap_halves(v) * sine


def dot(a, b):
    return jnp.dot(a, b, preferred_element_type=f32)


def local(
    tokens,
    cotangent,
    attn_gain,
    ffn_gain,
    qkv_weight,
    out_weight,
    router_weight,
    gate_weight,
    up_weight,
    down_weight,
    routes,
    segments,
):
    row = lax.axis_index("row")
    col = lax.axis_index("col")
    dp = lax.axis_index("dp")
    dp_count = lax.axis_size("dp")
    xs, zs, cs = dp_sizes()
    own_rows, own_width = tokens.shape
    total = 2 * own_rows
    width = 2 * own_width
    experts, _, hidden = gate_weight.shape
    own_experts = experts // 2
    own_heads = GROUP_HEADS // 2
    head_cols = own_heads * HEAD
    hid = own_experts * hidden
    other_col = 1 - col

    token_blocks = gather4(tokens)
    kv_first = 2 * head_cols

    def qkv_columns(weight, which):
        heads_part = lax.dynamic_slice_in_dim(weight, which * head_cols, head_cols, 1)
        return jnp.concatenate([heads_part, weight[:, kv_first:]], axis=1)

    core = dp_place()[2]
    piece = own_width // cs
    sent = flip(
        qkv_columns(lax.dynamic_slice_in_dim(qkv_weight, core * piece, piece, 0), other_col), 1
    )
    if cs == 2:
        swapped = shift(sent, 2, 1)
        qkv_other = by_col(core, sent, swapped, 0)
    else:
        qkv_other = sent
    qkv_local = jnp.concatenate([qkv_columns(qkv_weight, col), qkv_other], axis=0)
    small = jnp.concatenate(
        [router_weight.T.astype(f32), attn_gain[None], ffn_gain[None]], axis=0
    )
    small = jnp.concatenate([small, flip(small, 1)], axis=1)
    router_local = small[:experts].T.astype(bf16)
    gain_one = small[experts]
    gain_two = small[experts + 1]

    rolled = jnp.where(col == 0, out_weight, jnp.roll(out_weight, head_cols, axis=0))
    share = own_width // dp_count

    def dp_rows(v, count):
        return lax.dynamic_slice_in_dim(v, dp * count, count, v.ndim - 2)

    out_piece = dp_rows(rolled, share)
    out_pieces = jnp.concatenate([flip(out_piece, 1), flip(out_piece, 2), flip(out_piece, 3)], 0)

    def expert_half(v, which):
        return lax.dynamic_slice_in_dim(v, which * own_experts, own_experts, 0)

    gate_up_piece = jnp.concatenate(
        [
            dp_rows(expert_half(gate_weight, other_col), share),
            dp_rows(expert_half(up_weight, other_col), share),
        ],
        axis=2,
    ).reshape(own_experts * share, own_width)
    down_share = hid // dp_count
    down_piece = dp_rows(expert_half(down_weight, other_col).reshape(hid, own_width), down_share)
    expert_pieces = flip(jnp.concatenate([gate_up_piece, down_piece], axis=0), 1)
    gathered = lax.all_gather(
        jnp.concatenate([out_pieces, expert_pieces], axis=0), "dp", axis=0, tiled=False
    )
    out_other = (
        gathered[:, : 3 * share]
        .reshape(dp_count, 3, share, own_width)
        .transpose(1, 0, 2, 3)
        .reshape(3, own_width, own_width)
    )
    gate_up_other = (
        gathered[:, 3 * share : 3 * share + own_experts * share]
        .reshape(dp_count, own_experts, share, own_width)
        .transpose(1, 0, 2, 3)
        .reshape(own_experts, own_width, own_width)
    )
    down_other = gathered[:, (3 + own_experts) * share :].reshape(hid, own_width)

    o1, o2, o3 = out_other[0], out_other[1], out_other[2]
    out_local = jnp.concatenate(
        [
            jnp.concatenate([rolled, o2], axis=0),
            jnp.concatenate(
                [o1[head_cols:], o1[:head_cols], o3[head_cols:], o3[:head_cols]], axis=0
            ),
        ],
        axis=1,
    )
    gate_up_own = jnp.concatenate(
        [expert_half(gate_weight, col), expert_half(up_weight, col)], axis=2
    )
    gate_up_local = jnp.concatenate([gate_up_own, gate_up_other], axis=1)
    down_local = jnp.concatenate(
        [expert_half(down_weight, col).reshape(hid, own_width), down_other], axis=1
    )

    def own_order(v):
        return jnp.where(row == 0, v, jnp.roll(v, own_rows, axis=0))

    seg = segments
    routes_local = own_order(routes)
    places = own_order(jnp.arange(total, dtype=f32))
    cosine, sine = turn_tables(places)

    def two_by_two(blocks):
        return jnp.concatenate(
            [
                jnp.concatenate([blocks[0], blocks[1]], axis=1),
                jnp.concatenate([blocks[2], blocks[3]], axis=1),
            ],
            axis=0,
        )

    tokens_all = two_by_two(token_blocks)
    residual = tokens_all.astype(f32)
    scale_one = lax.rsqrt(jnp.mean(residual * residual, axis=1) + EPS)
    normed_one = (residual * scale_one[:, None] * gain_one).astype(bf16)
    logits = dot(normed_one, router_local)
    chosen = jnp.any(
        routes_local[:, :, None] == jnp.arange(experts, dtype=jnp.int32)[None, None, :], axis=1
    )
    masked = jnp.where(chosen, logits, MASKED)
    raised = jnp.exp(masked - jnp.max(masked, axis=1, keepdims=True))
    gate_values = raised / jnp.sum(raised, axis=1, keepdims=True)
    local_gates = lax.dynamic_slice_in_dim(gate_values, col * own_experts, own_experts, 1)

    projected = dot(normed_one, qkv_local).reshape(total, own_heads + 2, HEAD)
    turned = turn(projected[:, : own_heads + 1], cosine, sine).astype(bf16)
    queries = turned[:, :own_heads].reshape(total, head_cols)
    keys = turned[:, own_heads]
    values = projected[:, own_heads + 1].astype(bf16)
    context, lse = attend(queries, keys, values, seg)

    context_blocks = gather4(context)
    cot_blocks = gather4(cotangent)
    cot_all = two_by_two(cot_blocks)
    context_all = jnp.concatenate(
        [context, context_blocks[1]]
        + [jnp.roll(block, own_rows, axis=0) for block in context_blocks[2:]],
        axis=1,
    )
    mixed = dot(context_all, out_local)
    hidden_in = residual + mixed
    scale_two = lax.rsqrt(jnp.mean(hidden_in * hidden_in, axis=1) + EPS)
    normed_two = (hidden_in * scale_two[:, None] * gain_two).astype(bf16)

    weighted_list, gate_up_grads, gates_parts = [], [], []
    down_experts = down_local.reshape(own_experts, hidden, width)
    for e in range(own_experts):
        gate_up = dot(normed_two, gate_up_local[e])
        gate_pre, up_pre = gate_up[:, :hidden], gate_up[:, hidden:]
        sigmoid_gate = jax.nn.sigmoid(gate_pre)
        silu_gate = gate_pre * sigmoid_gate
        activated = silu_gate * up_pre
        gates = local_gates[:, e : e + 1]
        weighted_list.append((gates * activated).astype(bf16))
        weighted_grad = nt(cot_all, down_experts[e])
        gates_parts.append(jnp.sum(activated * weighted_grad, axis=1))
        activated_grad = gates * weighted_grad
        silu_grad = sigmoid_gate * (1.0 + gate_pre * (1.0 - sigmoid_gate))
        gate_up_grads.append(
            jnp.concatenate(
                [activated_grad * up_pre * silu_grad, activated_grad * silu_gate], axis=1
            ).astype(bf16)
        )
    weighted = jnp.concatenate(weighted_list, axis=1)

    normed_two_part = nt(gate_up_grads[0], gate_up_local[0])
    for e in range(1, own_experts):
        normed_two_part = normed_two_part + nt(gate_up_grads[e], gate_up_local[e])
    normed_two_grad = scatter_tokens(normed_two_part)

    gates_rows = jnp.stack(gates_parts, axis=0)
    gates_rows = gates_rows + jnp.roll(flip(gates_rows, 2), own_rows, axis=1)
    gates_other = flip(gates_rows, 1)
    gates_grad = by_col(col, gates_rows, gates_other, 0).T

    def tn(a, b):
        return lax.dot_general(a, b, (((0,), (0,)), ((), ())), preferred_element_type=f32)

    gate_up_weight_grads = [tn(normed_two, g).astype(bf16) for g in gate_up_grads]
    down_weight_grad = tn(weighted, cot_all).astype(bf16)

    def expert_part(feature_half, which):
        rows = slice(feature_half * own_width, (feature_half + 1) * own_width)
        cols = slice(which * hidden, (which + 1) * hidden)
        first = feature_half * own_width + which * hidden
        gate_or_up = jnp.concatenate([g[rows, cols] for g in gate_up_weight_grads], axis=0)
        down = down_weight_grad[:, first : first + hidden]
        pieces = xs * zs
        return jnp.concatenate(
            [gate_or_up.reshape(pieces, -1, hidden), down.reshape(pieces, -1, hidden)], axis=1
        ).reshape(-1, hidden)

    own_sum = core_sum(expert_part(0, 0), expert_part(0, 1))
    other_sum = core_sum(expert_part(1, 0), expert_part(1, 1))
    own_shard, other_shard = plane_sums(own_sum, other_sum)
    shard_rows = own_shard.shape[0]
    expert_sums = dp_gather(jnp.concatenate([own_shard, flip(other_shard, 1)], axis=0))

    layer_out_part = dot(weighted, down_local)
    layer_out = (hidden_in[:own_rows, :own_width] + scatter_tokens(layer_out_part)).astype(bf16)

    hidden_own = hidden_in[:own_rows, :own_width]
    scale_two_own = scale_two[:own_rows, None]

    def norm_back(grad_normed, values_own, scale, gain):
        scaled = grad_normed * gain
        inner = jnp.sum(scaled * values_own, axis=1)
        inner = (inner + flip(inner, 1))[:, None]
        values_grad = scale * scaled - values_own * (scale * scale * scale * inner / width)
        return values_grad, jnp.sum(grad_normed * values_own * scale, axis=0)

    hidden_norm_grad, ffn_gain_part = norm_back(
        normed_two_grad, hidden_own, scale_two_own, ffn_gain
    )
    hidden_grad = cotangent.astype(f32) + hidden_norm_grad
    hidden_grad_all = two_by_two(gather4(hidden_grad.astype(bf16)))
    out_weight_grad = tn(context, hidden_grad_all).astype(bf16)
    context_grad = nt(hidden_grad_all, out_local[:head_cols]).astype(bf16)

    query_grad, key_grad, value_grad = attend_back(queries, keys, values, context_grad, seg, lse)
    turned_grad = jnp.concatenate(
        [query_grad.reshape(total, own_heads, HEAD), key_grad[:, None]], axis=1
    )
    projected_grad = (
        jnp.concatenate([turn_back(turned_grad, cosine, sine), value_grad[:, None]], axis=1)
        .reshape(total, head_cols + 2 * HEAD)
        .astype(bf16)
    )
    normed_one_grad = scatter_tokens(nt(projected_grad, qkv_local))
    qkv_weight_grad = tn(normed_one, projected_grad).astype(bf16)

    half = own_width // 2

    def attn_part(feature_half, which):
        first = feature_half * own_width + which * half
        return jnp.concatenate(
            [qkv_weight_grad[first : first + half], out_weight_grad[:, first : first + half]],
            axis=1,
        )

    own_attn = core_sum(attn_part(0, 0), attn_part(0, 1))
    other_attn = core_sum(attn_part(1, 0), attn_part(1, 1))
    own_attn, other_attn = plane_sums(own_attn, other_attn)
    attn_sums = dp_gather(jnp.concatenate([own_attn, flip(other_attn, 1)], axis=0))

    logits_grad = (
        gate_values * (gates_grad - jnp.sum(gate_values * gates_grad, axis=1, keepdims=True))
    ).astype(bf16)
    router_grad_rows = tn(logits_grad, normed_one[:, :own_width])
    normed_one_grad = normed_one_grad + dot(logits_grad[:own_rows], router_weight.T)
    input_norm_grad, attn_gain_part = norm_back(
        normed_one_grad, residual[:own_rows, :own_width], scale_one[:own_rows, None], attn_gain
    )
    input_grad = hidden_grad + input_norm_grad
    gain_parts = jnp.stack([attn_gain_part, ffn_gain_part], axis=0)
    gain_parts = gain_parts + flip(gain_parts, 2)
    small_sums = small_sum(jnp.concatenate([router_grad_rows, gain_parts], axis=0))
    router_grad = small_sums[:experts].T
    attn_gain_grad = small_sums[experts]
    ffn_gain_grad = small_sums[experts + 1]

    gate_rows = 2 * shard_rows // 3
    down_rows = shard_rows - gate_rows

    def spread(v, swap):
        v = v.transpose(1, 0, 2, 3) if swap else v
        return v.reshape(-1, v.shape[-1])

    def expert_out(first, count, which):
        which = which % cs
        mine = spread(expert_sums[:, :, which, first : first + count], False)
        other = spread(
            expert_sums[:, :, which, shard_rows + first : shard_rows + first + count], True
        )
        return mine, other

    def gate_or_up(which):
        mine, other = expert_out(0, gate_rows, which)
        shape = (own_experts, own_width, hidden)
        return by_col(col, mine.reshape(shape), other.reshape(shape), 0).astype(f32)

    gate_grad = gate_or_up(0)
    up_grad = gate_or_up(1)
    down_mine, down_other_sum = [
        jnp.concatenate(list(parts), axis=1)
        for parts in zip(expert_out(gate_rows, down_rows, 0), expert_out(gate_rows, down_rows, 1))
    ]
    shape = (own_experts, hidden, own_width)
    down_grad = by_col(col, down_mine.reshape(shape), down_other_sum.reshape(shape), 0).astype(f32)

    attn_rows = own_attn.shape[0]
    qkv_cols = head_cols + 2 * HEAD

    def attn_out(first, swap):
        block = attn_sums[:, :, :, first : first + attn_rows]
        if swap:
            block = block.transpose(1, 0, 2, 3, 4)
        qkv = block[..., :qkv_cols].transpose(2, 0, 1, 3, 4).reshape(own_width, qkv_cols)
        out = block[..., qkv_cols:].transpose(0, 1, 3, 2, 4).reshape(head_cols, own_width)
        return qkv.astype(f32), out.astype(f32)

    qkv_mine, out_mine = attn_out(0, False)
    qkv_peer, out_peer = attn_out(attn_rows, True)
    qkv_grad = jnp.concatenate(
        [
            by_col(col, qkv_mine[:, :head_cols], qkv_peer[:, :head_cols], 1),
            qkv_mine[:, head_cols:] + qkv_peer[:, head_cols:],
        ],
        axis=1,
    )
    out_grad = by_col(col, out_mine, out_peer, 0)
    return (
        layer_out,
        input_grad,
        attn_gain_grad,
        ffn_gain_grad,
        qkv_grad,
        out_grad,
        router_grad,
        gate_grad,
        up_grad,
        down_grad,
    )


def solution(mesh):
    in_specs = (
        P(("dp", "row"), "col"),
        P(("dp", "row"), "col"),
        P("col"),
        P("col"),
        P("col", "row"),
        P("row", "col"),
        P("col", None),
        P(None, "col", "row"),
        P(None, "col", "row"),
        P(None, "row", "col"),
        P("dp", None),
        P("dp"),
    )
    out_specs = (
        P(("dp", "row"), "col"),
        P(("dp", "row"), "col"),
        P("col"),
        P("col"),
        P("col", "row"),
        P("row", "col"),
        P("col", None),
        P(None, "col", "row"),
        P(None, "col", "row"),
        P(None, "row", "col"),
    )
    return jax.shard_map(local, mesh=mesh, in_specs=in_specs, out_specs=out_specs, check_vma=False)
```

```python
import functools
import math

import jax
import jax.numpy as jnp
from jax import lax
from jax.experimental import pallas as pl
from jax.experimental.pallas import tpu as pltpu
from jax.sharding import PartitionSpec as P

f32 = jnp.float32
bf16 = jnp.bfloat16

HEAD = 128
GROUP_HEADS = 6
EPS = 1e-06
ROPE_BASE = 10000.0
MASKED = -1e30
BLOCK = 256


MESH = pl.DeviceIdType.MESH
VMEM = pltpu.VMEM
ANY = pl.BlockSpec(memory_space=pl.ANY)
WHOLE = pl.BlockSpec(memory_space=pltpu.VMEM)
HALF = 512
SIDE = 384


def flip(v, k):
    return lax.ppermute(v, ("row", "col"), [(i, i ^ k) for i in range(4)])


def dp_sizes():
    total = lax.axis_size("dp")
    cores = 2 if total % 2 == 0 else 1
    side = math.isqrt(total // cores)
    return side, side, cores


def dp_place():
    xs, zs, cs = dp_sizes()
    d = lax.axis_index("dp")
    return d // (zs * cs), (d // cs) % zs, d % cs


def by_col(col, mine, other, axis):
    return jnp.where(
        col == 0,
        jnp.concatenate([mine, other], axis=axis),
        jnp.concatenate([other, mine], axis=axis),
    )


def nt(a, b):
    return lax.dot_general(a, b, (((1,), (1,)), ((), ())), preferred_element_type=f32)


def nn(a, b):
    return lax.dot_general(a, b, (((1,), (0,)), ((), ())), preferred_element_type=f32)


def tn(a, b):
    return lax.dot_general(a, b, (((0,), (0,)), ((), ())), preferred_element_type=f32)


class Links:
    def __init__(self, send, recv):
        self.send, self.recv = send, recv
        self.used = 0
        self.dp = lax.axis_index("dp")
        self.row = lax.axis_index("row")
        self.col = lax.axis_index("col")
        self.xs, self.zs, self.cs = dp_sizes()
        self.x, self.z, self.core = dp_place()

    def group(self, k):
        row = 1 - self.row if k & 2 else self.row
        col = 1 - self.col if k & 1 else self.col
        return (self.dp, row, col)

    def other_core(self):
        return (self.dp + 1 - 2 * self.core, self.row, self.col)

    def place(self, axis, k):
        x, z = self.x, self.z
        if axis == 0:
            x = (x + k) % self.xs
        else:
            z = (z + k) % self.zs
        return ((x * self.zs + z) * self.cs + self.core, self.row, self.col)

    def greet(self, devices):
        barrier = pltpu.get_barrier_semaphore()
        for device in devices:
            pl.semaphore_signal(barrier, inc=1, device_id=device, device_id_type=MESH)
        pl.semaphore_wait(barrier, len(devices))

    def plane(self):
        return (
            ([self.other_core()] if self.cs == 2 else [])
            + [self.place(0, k) for k in range(1, self.xs)]
            + [self.place(1, k) for k in range(1, self.zs)]
        )

    def copy(self, src, dst, device):
        i = self.used
        self.used += 1
        return pltpu.make_async_remote_copy(
            src_ref=src,
            dst_ref=dst,
            send_sem=self.send.at[i],
            recv_sem=self.recv.at[i],
            device_id=device,
            device_id_type=MESH,
        )

    def go(self, src, dst, device):
        copy = self.copy(src, dst, device)
        copy.start()
        return copy


def at(start, size, step=16):
    return pl.ds(pl.multiple_of(start, step), size)


def gather_group(links, own, dst, wide):
    quarter = HALF // 2
    first = {}
    for k, order in ((2, (1, 0)), (3, (0, 1))):
        for h in order:
            first[k, h] = links.copy(own(h), dst(k, h), links.group(k))
    for key in ((2, 1), (3, 0), (2, 0), (3, 1)):
        first[key].start()
    relay = [
        links.copy(dst(3, 0), dst(1, 0), links.group(2)),
        links.copy(dst(2, 1), dst(1, 1), links.group(3)),
    ]

    def forward():
        first[3, 0].wait_recv()
        relay[0].start()
        first[2, 1].wait_recv()
        relay[1].start()

    def finish():
        first[2, 0].wait_recv()
        first[3, 1].wait_recv()
        for copy in relay:
            copy.wait()
        for copy in first.values():
            copy.wait_send()

    return forward, finish


def gather_inputs_kernel(
    tokens, qkv_weight, small, tokens_all, qkv_all, small_all, send, recv, local
):
    links = Links(send, recv)
    group = [links.group(k) for k in (1, 2, 3)]
    zs, cs = links.zs, links.cs
    links.greet(
        group
        + ([links.other_core()] if cs == 2 else [])
        + [links.place(1, k) for k in range(1, zs)]
    )
    width = tokens.shape[1]
    quarter = HALF // 2

    def own(h):
        return tokens.at[h * quarter : (h + 1) * quarter]

    def dst(k, h):
        rows = (HALF if k & 2 else 0) + h * quarter
        return tokens_all.at[rows : rows + quarter, (k & 1) * width : (k & 1) * width + width]

    share = width // (cs * zs)
    start = links.core * (width // cs) + links.z * share
    theirs = (1 - links.col) * SIDE
    rows = at(start, share)
    there = at(width + start, share)
    fetch = [
        links.copy(
            qkv_weight.at[rows, at(theirs, SIDE, 128)],
            qkv_all.at[there, 0:SIDE],
            links.group(1),
        ),
        links.copy(
            qkv_weight.at[rows, 2 * SIDE :], qkv_all.at[there, SIDE:], links.group(1)
        ),
    ]
    for copy in fetch:
        copy.start()
    little = links.go(small, small_all.at[:, width:], links.group(1))
    forward, finish = gather_group(links, own, dst, width)
    locals_ = [
        pltpu.make_async_copy(tokens, tokens_all.at[0:HALF, 0:width], local.at[0]),
        pltpu.make_async_copy(
            qkv_weight.at[:, at(links.col * SIDE, SIDE, 128)],
            qkv_all.at[0:width, 0:SIDE],
            local.at[1],
        ),
        pltpu.make_async_copy(
            qkv_weight.at[:, 2 * SIDE :], qkv_all.at[0:width, SIDE:], local.at[2]
        ),
        pltpu.make_async_copy(small, small_all.at[:, 0:width], local.at[3]),
    ]
    for copy in locals_:
        copy.start()
    for copy in fetch:
        copy.wait()
    spread = [
        links.go(qkv_all.at[there], qkv_all.at[there], links.place(1, k)) for k in range(1, zs)
    ]
    forward()
    for copy in spread:
        copy.wait()
    if cs == 2:
        block = qkv_all.at[at(width + links.core * (width // 2), width // 2)]
        links.go(block, block, links.other_core()).wait()
    little.wait()
    for copy in locals_:
        copy.wait()
    finish()


def gather_inputs(tokens, qkv_weight, small):
    width = tokens.shape[1]
    return pl.pallas_call(
        gather_inputs_kernel,
        out_shape=(
            jax.ShapeDtypeStruct((2 * HALF, 2 * width), bf16),
            jax.ShapeDtypeStruct((2 * width, SIDE + 2 * HEAD), bf16),
            jax.ShapeDtypeStruct((8, 2 * width), f32),
        ),
        in_specs=[ANY] * 3,
        out_specs=(ANY,) * 3,
        scratch_shapes=[
            pltpu.SemaphoreType.DMA((16,)),
            pltpu.SemaphoreType.DMA((16,)),
            pltpu.SemaphoreType.DMA((4,)),
        ],
        compiler_params=pltpu.CompilerParams(collective_id=0, has_side_effects=True),
        name="gather_inputs",
    )(tokens, qkv_weight, small)


def gather_context_kernel(context, context_all, send, recv, local):
    links = Links(send, recv)
    links.greet([links.group(k) for k in (1, 2, 3)])
    width = context.shape[1]

    def block(k, h):
        return context_all.at[h * HALF : (h + 1) * HALF, k * width : (k + 1) * width]

    mine = pltpu.make_async_copy(context, context_all.at[:, 0:width], local)
    mine.start()
    first = {}
    for k, h in ((2, 0), (3, 1), (2, 1), (3, 0)):
        first[k, 1 - h] = links.go(
            context.at[h * HALF : (h + 1) * HALF], block(k, 1 - h), links.group(k)
        )
    first[3, 0].wait_recv()
    relay = [links.go(block(3, 0), block(1, 1), links.group(2))]
    first[2, 1].wait_recv()
    relay.append(links.go(block(2, 1), block(1, 0), links.group(3)))
    mine.wait()
    first[2, 0].wait_recv()
    first[3, 1].wait_recv()
    for copy in relay:
        copy.wait()
    for copy in first.values():
        copy.wait_send()


def gather_context(context):
    rows, width = context.shape
    return pl.pallas_call(
        gather_context_kernel,
        out_shape=jax.ShapeDtypeStruct((rows, 4 * width), bf16),
        in_specs=[ANY],
        out_specs=ANY,
        scratch_shapes=[
            pltpu.SemaphoreType.DMA((6,)),
            pltpu.SemaphoreType.DMA((6,)),
            pltpu.SemaphoreType.DMA,
        ],
        compiler_params=pltpu.CompilerParams(collective_id=1, has_side_effects=True),
        name="gather_context",
    )(context)


def scatter_group(links, partial, near2, near3, far2, far3, out2, out3):
    width = partial.shape[1] // 2
    quarter = HALF // 2
    n2, n3 = links.group(2), links.group(3)
    start = [
        links.go(partial.at[0:quarter, width:], near2, n2),
        links.go(partial.at[quarter:HALF, width:], near3, n3),
    ]
    direct = [
        links.go(partial.at[HALF + quarter :, width:], far3.at[quarter:], n3),
        links.go(partial.at[HALF : HALF + quarter, 0:width], far2.at[0:quarter], n2),
    ]
    relay = [
        links.copy(out3, far3.at[0:quarter], n3),
        links.copy(out2, far2.at[quarter:], n2),
    ]

    def forward():
        start[0].wait_recv()
        out3[...] = (
            partial[HALF : HALF + quarter, width:].astype(f32) + near2[...].astype(f32)
        ).astype(bf16)
        relay[0].start()
        start[1].wait_recv()
        out2[...] = (
            partial[HALF + quarter :, 0:width].astype(f32) + near3[...].astype(f32)
        ).astype(bf16)
        relay[1].start()

    def finish():
        for copy in direct:
            copy.wait_recv()
        for copy in relay:
            copy.wait_recv()

    def total(rows):
        return (
            partial[rows, 0:width].astype(f32)
            + far2[rows].astype(f32)
            + far3[rows].astype(f32)
        )

    def sent():
        for copy in start + direct + relay:
            copy.wait_send()

    return forward, finish, total, sent


def norm_back_rows(grad, gain, values, scale, inner, width):
    return scale * (grad * gain - values * (scale * inner * (1.0 / width)))


def column(row_vector):
    return jnp.broadcast_to(row_vector, (128, row_vector.shape[1])).T


def half_swap(v):
    return jnp.concatenate([v[:, HALF:], v[:, :HALF]], axis=1)


def add_rows(out, a, b, total_rows, step):
    @pl.loop(0, total_rows // step)
    def _(i):
        rows = at(i * step, step, 16)
        out[rows] = (a[rows].astype(f32) + b[rows].astype(f32)).astype(bf16)


def reduce_kernel(
    partial,
    vectors,
    hidden,
    cot,
    scale,
    gain,
    gate_up,
    down,
    hidden_grad,
    hidden_low,
    vector_sums,
    gain_part,
    shard_up,
    shard_down,
    near2,
    near3,
    far2,
    far3,
    out2,
    out3,
    vec_in,
    low,
    core_up,
    core_down,
    sum_up,
    sum_down,
    in_up,
    in_down,
    part_up,
    part_down,
    in2_up,
    in2_down,
    peer_up,
    peer_down,
    send,
    recv,
    local,
):
    links = Links(send, recv)
    xs, zs, cs = links.xs, links.zs, links.cs
    sizes = (xs, zs)
    places = (links.x, links.z)
    links.greet([links.group(k) for k in (1, 2, 3)] + links.plane())
    width = partial.shape[1] // 2
    quarter = HALF // 2
    forward, finish, total, sent = scatter_group(
        links, partial, near2, near3, far2, far3, out2, out3
    )
    vec_copies = [links.go(vectors, vec_in.at[k - 1], links.group(k)) for k in (1, 2, 3)]
    core_copies = []
    if cs == 2:
        for ab in range(2):
            core_copies.append(
                (
                    links.go(
                        gate_up.at[1 - links.core, ab], core_up.at[ab], links.other_core()
                    ),
                    links.go(
                        down.at[1 - links.core, ab], core_down.at[ab], links.other_core()
                    ),
                )
            )
    up_rows, down_rows = gate_up.shape[2], down.shape[2]

    def core_step(ab):
        for copy in core_copies[ab] if cs == 2 else ():
            copy.wait_recv()
        for mine, came, out, rows in (
            (gate_up.at[links.core, ab], core_up.at[ab], sum_up.at[ab], up_rows),
            (down.at[links.core, ab], core_down.at[ab], sum_down.at[ab], down_rows),
        ):
            add_rows(out, mine, came, rows, 96)

    up1, down1 = up_rows // xs, down_rows // xs
    up2, down2 = up1 // zs, down1 // zs
    first_copies, second_copies = {}, {}

    def first_send(ab):
        n, place = sizes[ab], places[ab]
        for k in range(1, n):
            j = (place + k) % n
            first_copies[ab, k] = (
                links.go(
                    sum_up.at[ab, at(j * up1, up1)], in_up.at[ab, k - 1], links.place(ab, k)
                ),
                links.go(
                    sum_down.at[ab, at(j * down1, down1)],
                    in_down.at[ab, k - 1],
                    links.place(ab, k),
                ),
            )

    def first_sum(ab):
        n, place = sizes[ab], places[ab]
        for k in range(1, n):
            for copy in first_copies[ab, k]:
                copy.wait_recv()
        for mine, came, out, rows, piece in (
            (sum_up, in_up, part_up, up1, up2),
            (sum_down, in_down, part_down, down1, down2),
        ):

            if piece % 16 == 0:

                @pl.loop(0, rows // piece)
                def _(j):
                    own = mine[ab, at(place * rows + j * piece, piece)].astype(f32)
                    for k in range(1, n):
                        own = own + came[ab, k - 1, at(j * piece, piece)].astype(f32)
                    out[ab, j, 0:piece] = own.astype(bf16)

            else:
                own = mine[ab, at(place * rows, rows)].astype(f32)
                for k in range(1, n):
                    own = own + came[ab, k - 1].astype(f32)
                for j in range(rows // piece):
                    out[ab, j, 0:piece] = own[j * piece : (j + 1) * piece].astype(bf16)

    def second_send(ab):
        n, place = sizes[1 - ab], places[1 - ab]
        for k in range(1, n):
            j = (place + k) % n
            second_copies[ab, k] = (
                links.go(part_up.at[ab, j], in2_up.at[ab, k - 1], links.place(1 - ab, k)),
                links.go(part_down.at[ab, j], in2_down.at[ab, k - 1], links.place(1 - ab, k)),
            )

    def second_sum(ab, out_up, out_down):
        n, place = sizes[1 - ab], places[1 - ab]
        for k in range(1, n):
            for copy in second_copies[ab, k]:
                copy.wait_recv()
        for mine, came, out in (
            (part_up, in2_up, out_up),
            (part_down, in2_down, out_down),
        ):
            value = mine[ab, place].astype(f32)
            for k in range(1, n):
                value = value + came[ab, k - 1].astype(f32)
            out[...] = value.astype(bf16)

    for ref in (part_up, part_down):
        piece = up2 if ref is part_up else down2
        if piece < ref.shape[2]:
            ref[:, :, piece:] = jnp.zeros(
                (2, ref.shape[1], ref.shape[2] - piece, ref.shape[3]), bf16
            )

    core_step(0)
    first_send(0)
    forward()
    core_step(1)
    first_send(1)

    for copy in vec_copies:
        copy.wait()
    vec = vectors[...] + vec_in[0] + half_swap(vec_in[1] + vec_in[2])
    vector_sums[...] = vec
    finish()
    inner = column(vec[6:7, 0:HALF])[:, 0:1]
    part = jnp.zeros((8, width), f32)
    for h in range(4):
        rows = slice(h * 128, (h + 1) * 128)
        grad = total(rows)
        values = hidden[rows]
        scale_rows = scale[rows, 0:1]
        back = norm_back_rows(
            grad, gain[0:1, :], values, scale_rows, inner[rows], 2 * width
        )
        back = back + cot[rows].astype(f32)
        hidden_grad[rows] = back
        low[rows] = back.astype(bf16)
        part = part + jnp.sum(
            (grad * values * scale_rows).reshape(16, 8, width), axis=0
        )
    gain_part[...] = jnp.broadcast_to(jnp.sum(part, axis=0, keepdims=True), (8, width))

    def own(h):
        return low.at[h * quarter : (h + 1) * quarter]

    def dst(k, h):
        rows = (HALF if k & 2 else 0) + h * quarter
        return hidden_low.at[rows : rows + quarter, (k & 1) * width : (k & 1) * width + width]

    mine = pltpu.make_async_copy(low, hidden_low.at[0:HALF, 0:width], local)
    mine.start()
    forward_low, finish_low = gather_group(links, own, dst, width)
    first_sum(0)
    second_send(0)
    first_sum(1)
    second_send(1)
    forward_low()
    second_sum(0, shard_up.at[0], shard_down.at[0])
    second_sum(1, peer_up, peer_down)
    peer = [
        links.go(peer_up, shard_up.at[1], links.group(1)),
        links.go(peer_down, shard_down.at[1], links.group(1)),
    ]
    mine.wait()
    finish_low()
    for copy in peer:
        copy.wait()
    sent()
    for pair in core_copies:
        for copy in pair:
            copy.wait_send()
    for copies in (first_copies, second_copies):
        for pair in copies.values():
            for copy in pair:
                copy.wait_send()


def pad16(n):
    return -(-n // 16) * 16


def reduce_step(partial, vectors, hidden, cot, scale, gain, gate_up, down):
    xs, zs, cs = dp_sizes()
    width = hidden.shape[1]
    up_rows, down_rows = gate_up.shape[2], down.shape[2]
    up1, down1 = up_rows // xs, down_rows // xs
    up2, down2 = pad16(up1 // zs), pad16(down1 // zs)
    n1, n2 = max(xs - 1, 1), max(zs - 1, 1)
    quarter = HALF // 2
    return pl.pallas_call(
        reduce_kernel,
        out_shape=(
            jax.ShapeDtypeStruct((HALF, width), f32),
            jax.ShapeDtypeStruct((2 * HALF, 2 * width), bf16),
            jax.ShapeDtypeStruct(vectors.shape, f32),
            jax.ShapeDtypeStruct((8, width), f32),
            jax.ShapeDtypeStruct((2, up2, SIDE), bf16),
            jax.ShapeDtypeStruct((2, down2, SIDE), bf16),
        ),
        in_specs=[WHOLE] * 8,
        out_specs=(WHOLE, ANY, WHOLE, WHOLE, WHOLE, WHOLE),
        scratch_shapes=[
            VMEM((quarter, width), bf16),
            VMEM((quarter, width), bf16),
            VMEM((HALF, width), bf16),
            VMEM((HALF, width), bf16),
            VMEM((quarter, width), bf16),
            VMEM((quarter, width), bf16),
            VMEM((3,) + vectors.shape, f32),
            VMEM((HALF, width), bf16),
            VMEM((2, up_rows, SIDE), bf16),
            VMEM((2, down_rows, SIDE), bf16),
            VMEM((2, up_rows, SIDE), bf16),
            VMEM((2, down_rows, SIDE), bf16),
            VMEM((2, n1, up1, SIDE), bf16),
            VMEM((2, n1, down1, SIDE), bf16),
            VMEM((2, zs, up2, SIDE), bf16),
            VMEM((2, zs, down2, SIDE), bf16),
            VMEM((2, n2, up2, SIDE), bf16),
            VMEM((2, n2, down2, SIDE), bf16),
            VMEM((up2, SIDE), bf16),
            VMEM((down2, SIDE), bf16),
            pltpu.SemaphoreType.DMA((48,)),
            pltpu.SemaphoreType.DMA((48,)),
            pltpu.SemaphoreType.DMA,
        ],
        compiler_params=pltpu.CompilerParams(
            collective_id=2, has_side_effects=True, vmem_limit_bytes=56 * 2**20
        ),
        name="reduce_step",
    )(partial, vectors, hidden, cot, scale, gain, gate_up, down)


def final_kernel(
    partial,
    vectors,
    tokens,
    scale,
    gain,
    hidden_grad,
    router_part,
    layer_partial,
    hidden,
    qkv_part,
    out_part,
    small,
    input_grad,
    layer_out,
    small_out,
    sums,
    near2,
    near3,
    far2,
    far3,
    out2,
    out3,
    lnear2,
    lnear3,
    lfar2,
    lfar3,
    lout2,
    lout3,
    vec_in,
    small_own,
    small_in,
    core_in,
    core_sum,
    in1,
    part,
    in2,
    own_shard,
    peer_shard,
    send,
    recv,
    local,
):
    links = Links(send, recv)
    xs, zs, cs = links.xs, links.zs, links.cs
    sizes, places = (xs, zs), (links.x, links.z)
    links.greet([links.group(k) for k in (1, 2, 3)] + links.plane())
    width = partial.shape[1] // 2
    forward, finish, total, sent = scatter_group(
        links, partial, near2, near3, far2, far3, out2, out3
    )
    vec_copies = [links.go(vectors, vec_in.at[k - 1], links.group(k)) for k in (1, 2, 3)]
    small_copies = [links.go(small, small_in.at[k - 1], links.group(k)) for k in (1, 2, 3)]
    qkv_cols = qkv_part.shape[1]
    core_copies = []
    if cs == 2:
        for ab in range(2):
            first = ab * width + (1 - links.core) * SIDE
            core_copies.append(
                (
                    links.go(
                        qkv_part.at[at(first, SIDE)],
                        core_in.at[ab, :, 0:qkv_cols],
                        links.other_core(),
                    ),
                    links.go(
                        out_part.at[:, at(first, SIDE, 128)],
                        core_in.at[ab, :, qkv_cols:],
                        links.other_core(),
                    ),
                )
            )
    n_first = SIDE // xs
    piece = n_first // zs
    pad = part.shape[2]
    first_copies, second_copies = {}, {}
    if piece < pad:
        part[:, :, piece:] = jnp.zeros((2, zs, pad - piece, part.shape[3]), bf16)

    def core_step(ab):
        first = ab * width + links.core * SIDE
        for copy in core_copies[ab] if cs == 2 else ():
            copy.wait_recv()
        mine = qkv_part[at(first, SIDE)].astype(f32)
        core_sum[ab, :, 0:qkv_cols] = (
            mine + core_in[ab, :, 0:qkv_cols].astype(f32)
        ).astype(bf16)
        mine = out_part[:, at(first, SIDE, 128)].astype(f32)
        core_sum[ab, :, qkv_cols:] = (mine + core_in[ab, :, qkv_cols:].astype(f32)).astype(
            bf16
        )

    def first_send(ab):
        n, place = sizes[ab], places[ab]
        for k in range(1, n):
            j = (place + k) % n
            first_copies[ab, k] = links.go(
                core_sum.at[ab, at(j * n_first, n_first)],
                in1.at[ab, k - 1],
                links.place(ab, k),
            )

    def first_sum(ab):
        n, place = sizes[ab], places[ab]
        for k in range(1, n):
            first_copies[ab, k].wait_recv()

        own = core_sum[ab, at(place * n_first, n_first)].astype(f32)
        for k in range(1, n):
            own = own + in1[ab, k - 1].astype(f32)
        for j in range(zs):
            part[ab, j, 0:piece] = own[j * piece : (j + 1) * piece].astype(bf16)

    def second_send(ab):
        n, place = sizes[1 - ab], places[1 - ab]
        for k in range(1, n):
            j = (place + k) % n
            second_copies[ab, k] = links.go(
                part.at[ab, j], in2.at[ab, k - 1], links.place(1 - ab, k)
            )

    def second_sum(ab, out):
        n, place = sizes[1 - ab], places[1 - ab]
        value = part[ab, place].astype(f32)
        for k in range(1, n):
            second_copies[ab, k].wait_recv()
            value = value + in2[ab, k - 1].astype(f32)
        out[...] = value.astype(bf16)

    core_step(0)
    first_send(0)
    core_step(1)
    first_send(1)
    forward()
    lforward, lfinish, ltotal, lsent = scatter_group(
        links, layer_partial, lnear2, lnear3, lfar2, lfar3, lout2, lout3
    )
    for copy in small_copies:
        copy.wait()

    def swapped(v):
        return jnp.concatenate([v[:, width:], v[:, :width]], axis=1)

    group_sum = small[...] + small_in[1] + swapped(small_in[0] + small_in[2])
    rows = lax.broadcasted_iota(jnp.int32, (8, width), 0)
    small_own[0] = jnp.where(rows < 6, small[:, 0:width], group_sum[:, 0:width])
    stage_copies = []

    def small_stage(stage):
        axis_sizes = (cs, xs, zs)
        base = (0, 1, xs)[stage]
        n = axis_sizes[stage]
        copies = []
        for k in range(1, n):
            device = links.other_core() if stage == 0 else links.place(stage - 1, k)
            copies.append(
                links.go(small_own.at[stage], small_in.at[3 + base + k - 1, :, 0:width], device)
            )

        def done():
            value = small_own[stage]
            for k in range(1, n):
                copies[k - 1].wait()
                value = value + small_in[3 + base + k - 1, :, 0:width]
            small_own[stage + 1] = value

        return done

    done = small_stage(0)
    first_sum(0)
    second_send(0)
    done()
    done = small_stage(1)
    first_sum(1)
    second_send(1)
    done()
    done = small_stage(2)
    second_sum(1, peer_shard)
    peer = links.go(peer_shard, own_shard.at[1], links.group(1))
    second_sum(0, own_shard.at[0])
    done()
    small_out[...] = small_own[3]

    gather_copies = []

    def index(ab, x, z):
        return (x * zs + z) if ab == 0 else (z * xs + x)

    home = []
    for ab in range(2):
        if ab == 1:
            peer.wait()
        here = sums.at[links.core, ab, index(ab, links.x, links.z)]
        mine = pltpu.make_async_copy(own_shard.at[ab], here, local.at[ab])
        mine.start()
        home.append(mine)
        for k in range(1, sizes[1 - ab]):
            gather_copies.append(links.go(own_shard.at[ab], here, links.place(1 - ab, k)))
    lforward()

    for copy in vec_copies:
        copy.wait()
    vec = vectors[...] + vec_in[0] + half_swap(vec_in[1] + vec_in[2])
    inner = column(vec[6:7, 0:HALF])[:, 0:1]
    finish()
    for h in range(4):
        rows = slice(h * 128, (h + 1) * 128)
        grad = total(rows) + router_part[rows]
        back = norm_back_rows(
            grad,
            gain[0:1, :],
            tokens[rows].astype(f32),
            scale[rows, 0:1],
            inner[rows],
            2 * width,
        )
        input_grad[rows] = hidden_grad[rows] + back

    for copy in gather_copies:
        copy.wait()
    for copy in home:
        copy.wait()
    second = []
    for ab in range(2):
        first = (links.x if ab == 0 else links.z) * sizes[1 - ab]
        block = sums.at[links.core, ab, pl.ds(first, sizes[1 - ab])]
        for k in range(1, sizes[ab]):
            second.append(links.go(block, block, links.place(ab, k)))
    for copy in second:
        copy.wait()
    last = None
    if cs == 2:
        block = sums.at[links.core]
        last = links.go(block, block, links.other_core())
    lfinish()
    for h in range(4):
        rows = slice(h * 128, (h + 1) * 128)
        layer_out[rows] = (hidden[rows] + ltotal(rows)).astype(bf16)
    if last is not None:
        last.wait()
    sent()
    lsent()
    for pair in core_copies:
        for copy in pair:
            copy.wait_send()
    for copies in (first_copies, second_copies):
        for copy in copies.values():
            copy.wait_send()


def final_step(
    partial,
    vectors,
    tokens,
    scale,
    gain,
    hidden_grad,
    router_part,
    layer_partial,
    hidden,
    qkv_part,
    out_part,
    small,
):
    xs, zs, cs = dp_sizes()
    width = hidden.shape[1]
    quarter = HALF // 2
    cols = qkv_part.shape[1] + SIDE
    pad = pad16(SIDE // (xs * zs))
    n1, n2 = max(xs - 1, 1), max(zs - 1, 1)
    group_buffers = [
        VMEM((quarter, width), bf16),
        VMEM((quarter, width), bf16),
        VMEM((HALF, width), bf16),
        VMEM((HALF, width), bf16),
        VMEM((quarter, width), bf16),
        VMEM((quarter, width), bf16),
    ]
    return pl.pallas_call(
        final_kernel,
        out_shape=(
            jax.ShapeDtypeStruct((HALF, width), f32),
            jax.ShapeDtypeStruct((HALF, width), bf16),
            jax.ShapeDtypeStruct((8, width), f32),
            jax.ShapeDtypeStruct((cs, 2, xs * zs, pad, cols), bf16),
        ),
        in_specs=[WHOLE] * 12,
        out_specs=(WHOLE, WHOLE, WHOLE, ANY),
        scratch_shapes=group_buffers
        + group_buffers
        + [
            VMEM((3,) + vectors.shape, f32),
            VMEM((4, 8, width), f32),
            VMEM((3 + 1 + xs + zs, 8, 2 * width), f32),
            VMEM((2, SIDE, cols), bf16),
            VMEM((2, SIDE, cols), bf16),
            VMEM((2, n1, SIDE // xs, cols), bf16),
            VMEM((2, zs, pad, cols), bf16),
            VMEM((2, n2, pad, cols), bf16),
            VMEM((2, pad, cols), bf16),
            VMEM((pad, cols), bf16),
            pltpu.SemaphoreType.DMA((64,)),
            pltpu.SemaphoreType.DMA((64,)),
            pltpu.SemaphoreType.DMA((2,)),
        ],
        compiler_params=pltpu.CompilerParams(
            collective_id=3, has_side_effects=True, vmem_limit_bytes=56 * 2**20
        ),
        name="final_step",
    )(
        partial,
        vectors,
        tokens,
        scale,
        gain,
        hidden_grad,
        router_part,
        layer_partial,
        hidden,
        qkv_part,
        out_part,
        small,
    )


def swap_halves(v):
    half = v.shape[-1] // 2
    return jnp.concatenate([v[..., half:], v[..., :half]], axis=-1)


def project_kernel(
    tok, small, weight, routes, cosine, sine, normed_ref, q_ref, k_ref, v_ref, gates_ref, scale_ref
):
    x = tok[...].astype(f32)
    rows, width = x.shape
    scale = lax.rsqrt(jnp.sum(x * x, axis=1, keepdims=True) * (1.0 / width) + EPS)
    normed = (x * scale * small[6:7, :]).astype(bf16)
    normed_ref[...] = normed
    scale_ref[...] = jnp.broadcast_to(scale, scale_ref.shape)
    router = jnp.concatenate([small[...], jnp.zeros((120, width), f32)], axis=0).astype(bf16)
    logits = nt(normed, router)
    lanes = lax.broadcasted_iota(jnp.int32, (rows, 128), 1)
    chosen = lanes == routes[:, 0:1]
    for j in range(1, routes.shape[1]):
        chosen = chosen | (lanes == routes[:, j : j + 1])
    masked = jnp.where(chosen, logits, MASKED)
    raised = jnp.exp(masked - jnp.max(masked, axis=1, keepdims=True))
    raised = jnp.where(chosen, raised, 0.0)
    gates_ref[...] = raised / jnp.sum(raised, axis=1, keepdims=True)
    projected = nn(normed, weight[...])
    for h in range(4):
        part = projected[:, h * HEAD : (h + 1) * HEAD]
        turned = (part * cosine[...] + swap_halves(part) * sine[...]).astype(bf16)
        if h < 3:
            q_ref[:, h * HEAD : (h + 1) * HEAD] = turned
        else:
            k_ref[...] = turned
    v_ref[...] = projected[:, 4 * HEAD :].astype(bf16)


def project(tokens_all, small, weight, routes, cosine, sine):
    total, width = tokens_all.shape
    step = 256

    def rows(cols):
        return pl.BlockSpec((step, cols), lambda i: (i, 0))

    def whole(shape):
        return pl.BlockSpec(shape, lambda i: (0,) * len(shape))

    return pl.pallas_call(
        project_kernel,
        grid=(total // step,),
        out_shape=(
            jax.ShapeDtypeStruct((total, width), bf16),
            jax.ShapeDtypeStruct((total, SIDE), bf16),
            jax.ShapeDtypeStruct((total, HEAD), bf16),
            jax.ShapeDtypeStruct((total, HEAD), bf16),
            jax.ShapeDtypeStruct((total, 128), f32),
            jax.ShapeDtypeStruct((total, 128), f32),
        ),
        in_specs=[
            rows(width),
            whole(small.shape),
            whole(weight.shape),
            rows(routes.shape[1]),
            rows(HEAD),
            rows(HEAD),
        ],
        out_specs=(rows(width), rows(SIDE), rows(HEAD), rows(HEAD), rows(128), rows(128)),
        compiler_params=pltpu.CompilerParams(vmem_limit_bytes=32 * 2**20),
        cost_estimate=pl.CostEstimate(
            flops=2 * total * width * 640, bytes_accessed=10 * 2**20, transcendentals=0
        ),
        name="project",
    )(tokens_all, small, weight, routes, cosine, sine)


def mix_kernel(ctx, tok, weight, small, normed_ref, hidden_ref, scale_ref):
    hidden = tok[...].astype(f32) + nn(ctx[...], weight[...])
    width = hidden.shape[1]
    scale = lax.rsqrt(jnp.sum(hidden * hidden, axis=1, keepdims=True) * (1.0 / width) + EPS)
    normed_ref[...] = (hidden * scale * small[7:8, :]).astype(bf16)
    scale_ref[...] = jnp.broadcast_to(scale, scale_ref.shape)

    @pl.when(pl.program_id(0) < 2)
    def _():
        hidden_ref[...] = hidden[:, : width // 2]


def mix(context_all, tokens_all, weight, small):
    total, width = tokens_all.shape
    step = 256

    def rows(cols):
        return pl.BlockSpec((step, cols), lambda i: (i, 0))

    def whole(shape):
        return pl.BlockSpec(shape, lambda i: (0,) * len(shape))

    return pl.pallas_call(
        mix_kernel,
        grid=(total // step,),
        out_shape=(
            jax.ShapeDtypeStruct((total, width), bf16),
            jax.ShapeDtypeStruct((total // 2, width // 2), f32),
            jax.ShapeDtypeStruct((total, 128), f32),
        ),
        in_specs=[rows(width), rows(width), whole(weight.shape), whole(small.shape)],
        out_specs=(
            rows(width),
            pl.BlockSpec((step, width // 2), lambda i: (jnp.minimum(i, 1), 0)),
            rows(128),
        ),
        compiler_params=pltpu.CompilerParams(vmem_limit_bytes=40 * 2**20),
        cost_estimate=pl.CostEstimate(
            flops=2 * total * width * width, bytes_accessed=14 * 2**20, transcendentals=0
        ),
        name="mix",
    )(context_all, tokens_all, weight, small)


def experts_kernel(
    normed, cot, gate_up, down, gates, weighted_ref, grad_ref, back_ref, out_ref, vec_ref
):
    col = lax.axis_index("col")
    count, _, both = gate_up.shape
    hidden = both // 2
    rows = normed.shape[0]
    lanes = lax.broadcasted_iota(jnp.int32, (rows, 128), 1)
    vec = jnp.zeros((rows, 128), f32)
    inner = jnp.zeros((rows, 1), f32)
    back = out = None
    x, y = normed[...], cot[...]
    for e in range(count):
        here = lanes == col * count + e
        gate = jnp.sum(jnp.where(here, gates[...], 0.0), axis=1, keepdims=True)
        both_pre = nn(x, gate_up[e])
        gate_pre, up_pre = both_pre[:, :hidden], both_pre[:, hidden:]
        sigmoid = 1.0 / (1.0 + jnp.exp(-gate_pre))
        silu = gate_pre * sigmoid
        activated = silu * up_pre
        weighted = (gate * activated).astype(bf16)
        weighted_ref[:, e * hidden : (e + 1) * hidden] = weighted
        down_e = down[e * hidden : (e + 1) * hidden]
        weighted_grad = nt(y, down_e)
        vec = vec + jnp.where(
            here, jnp.sum(activated * weighted_grad, axis=1, keepdims=True), 0.0
        )
        g = gate * weighted_grad
        gate_grad = g * up_pre * (sigmoid * (1.0 + gate_pre * (1.0 - sigmoid)))
        up_grad = g * silu
        inner = inner + jnp.sum(gate_grad * gate_pre + up_grad * up_pre, axis=1, keepdims=True)
        grads = jnp.concatenate([gate_grad, up_grad], axis=1).astype(bf16)
        grad_ref[e] = grads
        back_e = nt(grads, gate_up[e])
        out_e = nn(weighted, down_e)
        back = back_e if back is None else back + back_e
        out = out_e if out is None else out + out_e
    back_ref[...] = back.astype(bf16)
    out_ref[...] = out.astype(bf16)
    vec = jnp.where(lanes == 6, inner, vec)
    vec_ref[...] = vec.T[0:8, :]


def experts_step(normed, cot, gate_up, down, gates):
    total, width = normed.shape
    step = 256
    count, _, both = gate_up.shape

    def rows(cols):
        return pl.BlockSpec((step, cols), lambda i: (i, 0))

    def whole(shape):
        return pl.BlockSpec(shape, lambda i: (0,) * len(shape))

    return pl.pallas_call(
        experts_kernel,
        grid=(total // step,),
        out_shape=(
            jax.ShapeDtypeStruct((total, down.shape[0]), bf16),
            jax.ShapeDtypeStruct((count, total, both), bf16),
            jax.ShapeDtypeStruct((total, width), bf16),
            jax.ShapeDtypeStruct((total, width), bf16),
            jax.ShapeDtypeStruct((8, total), f32),
        ),
        in_specs=[
            rows(width),
            rows(width),
            whole(gate_up.shape),
            whole(down.shape),
            rows(128),
        ],
        out_specs=(
            rows(down.shape[0]),
            pl.BlockSpec((count, step, both), lambda i: (0, i, 0)),
            rows(width),
            rows(width),
            pl.BlockSpec((8, step), lambda i: (0, i)),
        ),
        compiler_params=pltpu.CompilerParams(vmem_limit_bytes=58 * 2**20),
        cost_estimate=pl.CostEstimate(
            flops=6 * total * width * count * both, bytes_accessed=26 * 2**20, transcendentals=0
        ),
        name="experts",
    )(normed, cot, gate_up, down, gates)


def expert_grads_kernel(normed, grads, weighted, cot, up_ref, down_ref):
    width = normed.shape[1]
    half = width // 2
    hidden = weighted.shape[1]
    for ab in range(2):
        part = tn(normed[:, ab * half : (ab + 1) * half], grads[0])
        for which in range(2):
            up_ref[which, ab] = part[:, which * hidden : (which + 1) * hidden].astype(bf16)
    part = tn(weighted[...], cot[...])
    for ab in range(2):
        for which in range(2):
            first = ab * half + which * hidden
            down_ref[which, ab] = part[:, first : first + hidden].astype(bf16)


def expert_grads(normed, grads, weighted, cot):
    total, width = normed.shape
    count, _, both = grads.shape
    hidden = both // 2
    half = width // 2

    def whole(shape):
        return pl.BlockSpec(shape, lambda e: (0,) * len(shape))

    return pl.pallas_call(
        expert_grads_kernel,
        grid=(count,),
        out_shape=(
            jax.ShapeDtypeStruct((2, 2, count * half, hidden), bf16),
            jax.ShapeDtypeStruct((2, 2, count * hidden, hidden), bf16),
        ),
        in_specs=[
            whole(normed.shape),
            pl.BlockSpec((1, total, both), lambda e: (e, 0, 0)),
            pl.BlockSpec((total, hidden), lambda e: (0, e)),
            whole(cot.shape),
        ],
        out_specs=(
            pl.BlockSpec((2, 2, half, hidden), lambda e: (0, 0, e, 0)),
            pl.BlockSpec((2, 2, hidden, hidden), lambda e: (0, 0, e, 0)),
        ),
        compiler_params=pltpu.CompilerParams(vmem_limit_bytes=56 * 2**20),
        cost_estimate=pl.CostEstimate(
            flops=3 * total * width * count * both, bytes_accessed=24 * 2**20, transcendentals=0
        ),
        name="expert_grads",
    )(normed, grads, weighted, cot)


def window(i, block):
    first = max(0, (i + 1) * block - 512 - block)
    return first, (i + 1) * block


def own_places(ref, out, row, half):
    for h in range(2):
        start = pl.multiple_of(half * jnp.bitwise_xor(row, h), half)
        out[h * half : (h + 1) * half] = ref[pl.ds(start, half)]


def allowed_keys(segk_ref, segq_ref, i, first, last):
    block = BLOCK
    width = last - first
    keys = lax.broadcasted_iota(jnp.int32, (width, block), 0) + first
    queries = lax.broadcasted_iota(jnp.int32, (width, block), 1) + i * block
    same = segk_ref[first:last] == segq_ref[:, i * block : (i + 1) * block]
    return (keys <= queries) & same


def attend_kernel(heads, q_ref, k_ref, v_ref, segk_ref, segq_ref, o_ref, lse_ref, q, k, vt):
    row = lax.axis_index("row")
    total = q_ref.shape[0]
    half = total // 2
    own_places(q_ref, q, row, half)
    own_places(k_ref, k, row, half)
    for h in range(2):
        start = pl.multiple_of(half * jnp.bitwise_xor(row, h), half)
        vt[:, h * half : (h + 1) * half] = v_ref[pl.ds(start, half)].astype(f32).T.astype(bf16)
    for i in range(total // BLOCK):
        first, last = window(i, BLOCK)
        here = slice(i * BLOCK, (i + 1) * BLOCK)
        allowed = allowed_keys(segk_ref, segq_ref, i, first, last)
        place = i * BLOCK // half
        start = pl.multiple_of(
            half * jnp.bitwise_xor(row, place) + (i * BLOCK - place * half), BLOCK
        )
        for h in range(heads):
            s = nt(k[first:last], q[here, h * HEAD : (h + 1) * HEAD]) * (HEAD**-0.5)
            s = jnp.where(allowed, s, MASKED)
            top = jnp.max(s, axis=0, keepdims=True)
            p = jnp.exp(s - top)
            total_p = jnp.sum(p, axis=0, keepdims=True)
            p = (p * (1.0 / total_p)).astype(bf16)
            ot = nn(vt[:, first:last], p)
            o_ref[pl.ds(start, BLOCK), h * HEAD : (h + 1) * HEAD] = ot.T.astype(bf16)
            lse_ref[h : h + 1, here] = top + jnp.log(total_p)


def attend(q, k, v, seg):
    total, width = q.shape
    heads = width // HEAD
    return pl.pallas_call(
        functools.partial(attend_kernel, heads),
        out_shape=(
            jax.ShapeDtypeStruct((total, width), bf16),
            jax.ShapeDtypeStruct((8, total), f32),
        ),
        in_specs=[WHOLE] * 5,
        out_specs=(WHOLE, WHOLE),
        scratch_shapes=[
            VMEM((total, width), bf16),
            VMEM((total, HEAD), bf16),
            VMEM((HEAD, total), bf16),
        ],
        compiler_params=pltpu.CompilerParams(vmem_limit_bytes=32 * 2**20),
        cost_estimate=pl.CostEstimate(
            flops=2 * heads * total * total * HEAD * 2,
            bytes_accessed=6 * total * width,
            transcendentals=heads * total * total,
        ),
        name="attend",
    )(q, k, v, seg.reshape(total, 1), seg.reshape(1, total))


def attend_back_kernel(
    heads,
    q_ref,
    k_ref,
    v_ref,
    hidden_low,
    out_weight,
    segk_ref,
    segq_ref,
    lse_ref,
    cos_ref,
    sin_ref,
    grad_ref,
    vec_ref,
    q,
    k,
    v,
    kt,
    do,
    dk,
    dv,
):
    row = lax.axis_index("row")
    total = q_ref.shape[0]
    half = total // 2
    scale = HEAD**-0.5
    own_places(q_ref, q, row, half)
    own_places(k_ref, k, row, half)
    own_places(v_ref, v, row, half)
    for h in range(2):
        start = pl.multiple_of(half * jnp.bitwise_xor(row, h), half)
        do[h * half : (h + 1) * half] = nt(
            hidden_low[pl.ds(start, half)], out_weight[...]
        ).astype(bf16)
    kt[...] = k[...].astype(f32).T.astype(bf16)
    dk[...] = jnp.zeros_like(dk)
    dv[...] = jnp.zeros_like(dv)

    def back(grad, rows):
        return grad * cos_ref[rows] - swap_halves(grad) * sin_ref[rows]

    inners = []
    for i in range(total // BLOCK):
        first, last = window(i, BLOCK)
        here = slice(i * BLOCK, (i + 1) * BLOCK)
        allowed = allowed_keys(segk_ref, segq_ref, i, first, last)
        place = i * BLOCK // half
        start = pl.multiple_of(
            half * jnp.bitwise_xor(row, place) + (i * BLOCK - place * half), BLOCK
        )
        rows = pl.ds(start, BLOCK)
        inner_q = jnp.zeros((BLOCK, 1), f32)
        for h in range(heads):
            cols = slice(h * HEAD, (h + 1) * HEAD)
            s = nt(k[first:last], q[here, cols]) * scale
            s = jnp.where(allowed, s, MASKED)
            p = jnp.exp(s - lse_ref[h : h + 1, here])
            dp = nt(v[first:last], do[here, cols])
            inner = jnp.sum(dp * p, axis=0, keepdims=True)
            ds = (p * (dp - inner)).astype(bf16)
            dq = (nn(kt[:, first:last], ds) * scale).T
            inner_q = inner_q + jnp.sum(dq * q[here, cols].astype(f32), axis=1, keepdims=True)
            grad_ref[rows, cols] = back(dq, rows).astype(bf16)
            dk[first:last] += nn(ds, q[here, cols]) * scale
            dv[first:last] += nn(p.astype(bf16), do[here, cols])
        inners.append(inner_q)
    width = heads * HEAD
    for i in range(total // BLOCK):
        here = slice(i * BLOCK, (i + 1) * BLOCK)
        place = i * BLOCK // half
        start = pl.multiple_of(
            half * jnp.bitwise_xor(row, place) + (i * BLOCK - place * half), BLOCK
        )
        rows = pl.ds(start, BLOCK)
        key_grad, value_grad = dk[here], dv[here]
        inner = inners[i] + jnp.sum(
            key_grad * k[here].astype(f32) + value_grad * v[here].astype(f32),
            axis=1,
            keepdims=True,
        )
        grad_ref[rows, width : width + HEAD] = back(key_grad, rows).astype(bf16)
        grad_ref[rows, width + HEAD :] = value_grad.astype(bf16)
        vec_ref[:, rows] = jnp.broadcast_to(inner, (BLOCK, 128)).T[0:8, :]


def attend_back(q, k, v, hidden_low, out_weight, seg, lse, cosine, sine):
    total, width = q.shape
    heads = width // HEAD
    return pl.pallas_call(
        functools.partial(attend_back_kernel, heads),
        out_shape=(
            jax.ShapeDtypeStruct((total, width + 2 * HEAD), bf16),
            jax.ShapeDtypeStruct((8, total), f32),
        ),
        in_specs=[WHOLE] * 10,
        out_specs=(WHOLE, WHOLE),
        scratch_shapes=[
            VMEM((total, width), bf16),
            VMEM((total, HEAD), bf16),
            VMEM((total, HEAD), bf16),
            VMEM((HEAD, total), bf16),
            VMEM((total, width), bf16),
            VMEM((total, HEAD), f32),
            VMEM((total, HEAD), f32),
        ],
        compiler_params=pltpu.CompilerParams(vmem_limit_bytes=48 * 2**20),
        cost_estimate=pl.CostEstimate(
            flops=5 * heads * total * total * HEAD * 2,
            bytes_accessed=10 * total * width,
            transcendentals=heads * total * total,
        ),
        name="attend_back",
    )(
        q,
        k,
        v,
        hidden_low,
        out_weight,
        seg.reshape(total, 1),
        seg.reshape(1, total),
        lse,
        cosine,
        sine,
    )


def attn_grads_kernel(
    grads,
    qkv_weight,
    normed,
    context,
    hidden_low,
    small,
    gates,
    vec_sums,
    vec_part,
    ffn_part,
    partial_ref,
    qkv_ref,
    out_ref,
    vec_ref,
    router_ref,
    small_ref,
):
    total, width = normed.shape
    half = width // 2
    row = lax.axis_index("row")
    col = lax.axis_index("col")
    rows = 256
    for i in range(total // rows):
        here = slice(i * rows, (i + 1) * rows)
        partial_ref[here] = nt(grads[here], qkv_weight[...]).astype(bf16)
    gate_rows = gates[...].T[0:8, :]
    sums = vec_sums[...]
    mask = lax.broadcasted_iota(jnp.int32, sums.shape, 0) < 6
    sums = jnp.where(mask, sums, 0.0)
    logits_grad = gate_rows * (sums - jnp.sum(gate_rows * sums, axis=0, keepdims=True))
    logits_low = jnp.where(mask, logits_grad, 0.0).astype(bf16)
    router = jnp.where(
        lax.broadcasted_iota(jnp.int32, (8, width), 0) < 6, small[...], 0.0
    )
    router_grad = nn(logits_low, normed[...])
    router_ref[...] = tn(logits_low[:, 0:HALF], router[:, 0:half].astype(bf16))
    pieces = []
    for i in range(width // rows):
        here = slice(i * rows, (i + 1) * rows)
        part = tn(normed[:, here], grads[...])
        qkv_ref[here] = part.astype(bf16)
        gain_sum = jnp.sum(part * qkv_weight[here].astype(f32), axis=1, keepdims=True)
        pieces.append(jnp.broadcast_to(gain_sum, (rows, 128)).T[0:8, :])
    out_ref[...] = tn(context[...], hidden_low[...]).astype(bf16)
    gain_row = jnp.concatenate(pieces, axis=1)
    once = jnp.where((row == 0) & (col == 0), 1.0, 0.0)
    gain_row = gain_row + once * jnp.sum(router_grad * router, axis=0, keepdims=True)
    gain_row = gain_row / small[6:7, :]
    ffn = jnp.concatenate([ffn_part[...], jnp.zeros((8, half), f32)], axis=1)
    index = lax.broadcasted_iota(jnp.int32, (8, width), 0)
    small_ref[...] = jnp.where(
        index < 6, router_grad, jnp.where(index == 6, gain_row, ffn)
    )
    logit_rows = nt(router.astype(bf16), normed[...])
    router_inner = jnp.sum(
        logits_low.astype(f32) * logit_rows, axis=0, keepdims=True
    )
    vec_ref[...] = vec_part[...] + once * router_inner


def attn_grads(
    grads, qkv_weight, normed, context, hidden_low, small, gates, vec_sums, vec_part, ffn_part
):
    total, width = normed.shape
    return pl.pallas_call(
        attn_grads_kernel,
        out_shape=(
            jax.ShapeDtypeStruct((total, width), bf16),
            jax.ShapeDtypeStruct(qkv_weight.shape, bf16),
            jax.ShapeDtypeStruct((context.shape[1], width), bf16),
            jax.ShapeDtypeStruct((8, total), f32),
            jax.ShapeDtypeStruct((HALF, width // 2), f32),
            jax.ShapeDtypeStruct((8, width), f32),
        ),
        in_specs=[WHOLE] * 10,
        out_specs=(WHOLE,) * 6,
        compiler_params=pltpu.CompilerParams(vmem_limit_bytes=56 * 2**20),
        cost_estimate=pl.CostEstimate(
            flops=2 * total * width * (640 * 2 + 384), bytes_accessed=24 * 2**20, transcendentals=0
        ),
        name="attn_grads",
    )(grads, qkv_weight, normed, context, hidden_low, small, gates, vec_sums, vec_part, ffn_part)


def turn_tables(places):
    steps_up = jnp.arange(HEAD // 2, dtype=f32) * (2.0 / HEAD)
    inverse = jnp.exp(-math.log(ROPE_BASE) * steps_up)
    angles = places[:, None] * inverse[None, :]
    cosine, sine = jnp.cos(angles), jnp.sin(angles)
    return (
        jnp.concatenate([cosine, cosine], axis=1),
        jnp.concatenate([-sine, sine], axis=1),
    )


def gather4(x):
    half = x.shape[0] // 2
    a = flip(x, 2)
    b = flip(x, 3)
    c = jnp.concatenate([flip(b[:half], 2), flip(a[half:], 3)], axis=0)
    return x, c, a, b


def two_by_two(blocks):
    return jnp.concatenate(
        [
            jnp.concatenate([blocks[0], blocks[1]], axis=1),
            jnp.concatenate([blocks[2], blocks[3]], axis=1),
        ],
        axis=0,
    )


def local(
    tokens,
    cotangent,
    attn_gain,
    ffn_gain,
    qkv_weight,
    out_weight,
    router_weight,
    gate_weight,
    up_weight,
    down_weight,
    routes,
    segments,
):
    row = lax.axis_index("row")
    col = lax.axis_index("col")
    dp = lax.axis_index("dp")
    dp_count = lax.axis_size("dp")
    xs, zs, cs = dp_sizes()
    own_rows, own_width = tokens.shape
    total = 2 * own_rows
    experts, _, hidden = gate_weight.shape
    own_experts = experts // 2
    hid = own_experts * hidden
    other_col = 1 - col

    rolled = jnp.where(col == 0, out_weight, jnp.roll(out_weight, SIDE, axis=0))
    share = own_width // dp_count

    def dp_rows(v, count):
        return lax.dynamic_slice_in_dim(v, dp * count, count, v.ndim - 2)

    out_piece = dp_rows(rolled, share)
    out_pieces = jnp.concatenate([flip(out_piece, 1), flip(out_piece, 2), flip(out_piece, 3)], 0)

    def expert_half(v, which):
        return lax.dynamic_slice_in_dim(v, which * own_experts, own_experts, 0)

    gate_up_piece = jnp.concatenate(
        [
            dp_rows(expert_half(gate_weight, other_col), share),
            dp_rows(expert_half(up_weight, other_col), share),
        ],
        axis=2,
    ).reshape(own_experts * share, own_width)
    down_share = hid // dp_count
    down_piece = dp_rows(expert_half(down_weight, other_col).reshape(hid, own_width), down_share)
    expert_pieces = flip(jnp.concatenate([gate_up_piece, down_piece], axis=0), 1)
    gathered = lax.all_gather(
        jnp.concatenate([out_pieces, expert_pieces], axis=0), "dp", axis=0, tiled=False
    )
    out_other = (
        gathered[:, : 3 * share]
        .reshape(dp_count, 3, share, own_width)
        .transpose(1, 0, 2, 3)
        .reshape(3, own_width, own_width)
    )
    gate_up_other = (
        gathered[:, 3 * share : 3 * share + own_experts * share]
        .reshape(dp_count, own_experts, share, own_width)
        .transpose(1, 0, 2, 3)
        .reshape(own_experts, own_width, own_width)
    )
    down_other = gathered[:, (3 + own_experts) * share :].reshape(hid, own_width)

    o1, o2, o3 = out_other[0], out_other[1], out_other[2]
    out_local = jnp.concatenate(
        [
            jnp.concatenate([rolled, o2], axis=0),
            jnp.concatenate([o1[SIDE:], o1[:SIDE], o3[SIDE:], o3[:SIDE]], axis=0),
        ],
        axis=1,
    )
    gate_up_own = jnp.concatenate(
        [expert_half(gate_weight, col), expert_half(up_weight, col)], axis=2
    )
    gate_up_local = jnp.concatenate([gate_up_own, gate_up_other], axis=1)
    down_local = jnp.concatenate(
        [expert_half(down_weight, col).reshape(hid, own_width), down_other], axis=1
    )

    def own_order(v):
        return jnp.where(row == 0, v, jnp.roll(v, own_rows, axis=0))

    routes_local = own_order(routes)
    cosine, sine = turn_tables(own_order(jnp.arange(total, dtype=f32)))
    small = jnp.concatenate(
        [router_weight.T.astype(f32), attn_gain[None], ffn_gain[None]], axis=0
    )

    tokens_all, qkv_local, small_all = gather_inputs(tokens, qkv_weight, small)
    normed_one, queries, keys, values, gates, scale_one = project(
        tokens_all, small_all, qkv_local, routes_local, cosine, sine
    )
    context, lse = attend(queries, keys, values, segments)
    context_all = gather_context(context)
    cot_all = two_by_two(gather4(cotangent))
    normed_two, hidden_own, scale_two = mix(context_all, tokens_all, out_local, small_all)
    weighted, pre_grads, normed_two_part, layer_part, expert_vec = experts_step(
        normed_two, cot_all, gate_up_local, down_local, gates
    )
    gate_up_grads, down_grads = expert_grads(normed_two, pre_grads, weighted, cot_all)
    hidden_grad, hidden_low, vec_sums, ffn_part, shard_up, shard_down = reduce_step(
        normed_two_part,
        expert_vec,
        hidden_own,
        cotangent,
        scale_two,
        ffn_gain[None],
        gate_up_grads,
        down_grads,
    )
    up_rows = own_experts * own_width // (xs * zs)
    down_rows = hid // (xs * zs)
    expert_sums = lax.all_gather(
        jnp.concatenate([shard_up[:, :up_rows], shard_down[:, :down_rows]], axis=1),
        "dp",
        axis=0,
        tiled=False,
    ).reshape(xs, zs, cs, 2, up_rows + down_rows, SIDE)

    projected_grad, vec_part = attend_back(
        queries, keys, values, hidden_low, out_local[:SIDE], segments, lse, cosine, sine
    )
    input_part, qkv_part, out_part, input_vec, router_part, small_part = attn_grads(
        projected_grad,
        qkv_local,
        normed_one,
        context,
        hidden_low,
        small_all,
        gates,
        vec_sums,
        vec_part,
        ffn_part,
    )
    input_grad, layer_out, small_sums, attn_sums = final_step(
        input_part,
        input_vec,
        tokens,
        scale_one,
        attn_gain[None],
        hidden_grad,
        router_part,
        layer_part,
        hidden_own,
        qkv_part,
        out_part,
        small_part,
    )
    router_grad = small_sums[:experts].T
    attn_gain_grad = small_sums[6]
    ffn_gain_grad = small_sums[7]

    def spread(v, swap):
        v = v.transpose(1, 0, 2, 3) if swap else v
        return v.reshape(-1, v.shape[-1])

    def expert_out(rows, which):
        which = which % cs
        return [spread(expert_sums[:, :, which, ab, rows], ab == 1) for ab in range(2)]

    def gate_or_up(which):
        mine, other = expert_out(slice(0, up_rows), which)
        shape = (own_experts, own_width, hidden)
        return by_col(col, mine.reshape(shape), other.reshape(shape), 0).astype(f32)

    gate_grad = gate_or_up(0)
    up_grad = gate_or_up(1)
    down_mine, down_peer = [
        jnp.concatenate(list(parts), axis=1)
        for parts in zip(
            expert_out(slice(up_rows, None), 0), expert_out(slice(up_rows, None), 1)
        )
    ]
    shape = (own_experts, hidden, own_width)
    down_grad = by_col(col, down_mine.reshape(shape), down_peer.reshape(shape), 0).astype(f32)

    attn_rows = SIDE // (xs * zs)
    qkv_cols = SIDE + 2 * HEAD

    def attn_out(ab):
        block = attn_sums[:, ab, :, :attn_rows]
        qkv = block[..., :qkv_cols].reshape(own_width * cs // 2, qkv_cols)
        out = block[..., qkv_cols:].transpose(1, 2, 0, 3).reshape(SIDE, SIDE * cs)
        return qkv.astype(f32), out.astype(f32)

    qkv_mine, out_mine = attn_out(0)
    qkv_peer, out_peer = attn_out(1)
    qkv_grad = jnp.concatenate(
        [
            by_col(col, qkv_mine[:, :SIDE], qkv_peer[:, :SIDE], 1),
            qkv_mine[:, SIDE:] + qkv_peer[:, SIDE:],
        ],
        axis=1,
    )
    out_grad = by_col(col, out_mine, out_peer, 0)
    return (
        layer_out,
        input_grad,
        attn_gain_grad,
        ffn_gain_grad,
        qkv_grad,
        out_grad,
        router_grad,
        gate_grad,
        up_grad,
        down_grad,
    )


def solution(mesh):
    in_specs = (
        P(("dp", "row"), "col"),
        P(("dp", "row"), "col"),
        P("col"),
        P("col"),
        P("col", "row"),
        P("row", "col"),
        P("col", None),
        P(None, "col", "row"),
        P(None, "col", "row"),
        P(None, "row", "col"),
        P("dp", None),
        P("dp"),
    )
    out_specs = (
        P(("dp", "row"), "col"),
        P(("dp", "row"), "col"),
        P("col"),
        P("col"),
        P("col", "row"),
        P("row", "col"),
        P("col", None),
        P(None, "col", "row"),
        P(None, "col", "row"),
        P(None, "row", "col"),
    )
    return jax.shard_map(local, mesh=mesh, in_specs=in_specs, out_specs=out_specs, check_vma=False)
```

```python
import functools
import math

import jax
import jax.numpy as jnp
from jax import lax
from jax.experimental import pallas as pl
from jax.experimental.pallas import tpu as pltpu
from jax.sharding import PartitionSpec as P

f32 = jnp.float32
bf16 = jnp.bfloat16

HEAD = 128
GROUP_HEADS = 6
EPS = 1e-06
ROPE_BASE = 10000.0
MASKED = -1e30
BLOCK = 256


MESH = pl.DeviceIdType.MESH
VMEM = pltpu.VMEM
ANY = pl.BlockSpec(memory_space=pl.ANY)
WHOLE = pl.BlockSpec(memory_space=pltpu.VMEM)
HALF = 512
SIDE = 384


def flip(v, k):
    return lax.ppermute(v, ("row", "col"), [(i, i ^ k) for i in range(4)])


def dp_sizes():
    total = lax.axis_size("dp")
    cores = 2 if total % 2 == 0 else 1
    side = math.isqrt(total // cores)
    return side, side, cores


def dp_place():
    xs, zs, cs = dp_sizes()
    d = lax.axis_index("dp")
    return d // (zs * cs), (d // cs) % zs, d % cs


def nt(a, b):
    return lax.dot_general(a, b, (((1,), (1,)), ((), ())), preferred_element_type=f32)


def nn(a, b):
    return lax.dot_general(a, b, (((1,), (0,)), ((), ())), preferred_element_type=f32)


def tn(a, b):
    return lax.dot_general(a, b, (((0,), (0,)), ((), ())), preferred_element_type=f32)


class Links:
    def __init__(self, send, recv):
        self.send, self.recv = send, recv
        self.used = 0
        self.dp = lax.axis_index("dp")
        self.row = lax.axis_index("row")
        self.col = lax.axis_index("col")
        self.xs, self.zs, self.cs = dp_sizes()
        self.x, self.z, self.core = dp_place()

    def group(self, k):
        row = 1 - self.row if k & 2 else self.row
        col = 1 - self.col if k & 1 else self.col
        return (self.dp, row, col)

    def other_core(self):
        return (self.dp + 1 - 2 * self.core, self.row, self.col)

    def place(self, axis, k):
        x, z = self.x, self.z
        if axis == 0:
            x = (x + k) % self.xs
        else:
            z = (z + k) % self.zs
        return ((x * self.zs + z) * self.cs + self.core, self.row, self.col)

    def greet(self, devices):
        barrier = pltpu.get_barrier_semaphore()
        for device in devices:
            pl.semaphore_signal(barrier, inc=1, device_id=device, device_id_type=MESH)
        pl.semaphore_wait(barrier, len(devices))

    def plane(self):
        return (
            ([self.other_core()] if self.cs == 2 else [])
            + [self.place(0, k) for k in range(1, self.xs)]
            + [self.place(1, k) for k in range(1, self.zs)]
        )

    def copy(self, src, dst, device):
        i = self.used
        self.used += 1
        return pltpu.make_async_remote_copy(
            src_ref=src,
            dst_ref=dst,
            send_sem=self.send.at[i],
            recv_sem=self.recv.at[i],
            device_id=device,
            device_id_type=MESH,
        )

    def go(self, src, dst, device):
        copy = self.copy(src, dst, device)
        copy.start()
        return copy


def at(start, size, step=16):
    return pl.ds(pl.multiple_of(start, step), size)


def gather_group(links, own, dst, wide):
    quarter = HALF // 2
    first = {}
    for k, order in ((2, (1, 0)), (3, (0, 1))):
        for h in order:
            first[k, h] = links.copy(own(h), dst(k, h), links.group(k))
    for key in ((2, 1), (3, 0), (2, 0), (3, 1)):
        first[key].start()
    relay = [
        links.copy(dst(3, 0), dst(1, 0), links.group(2)),
        links.copy(dst(2, 1), dst(1, 1), links.group(3)),
    ]

    def forward():
        first[3, 0].wait_recv()
        relay[0].start()
        first[2, 1].wait_recv()
        relay[1].start()

    def finish():
        first[2, 0].wait_recv()
        first[3, 1].wait_recv()
        for copy in relay:
            copy.wait()
        for copy in first.values():
            copy.wait_send()

    return forward, finish


def unit_rows():
    xs, zs, _ = dp_sizes()
    return 768 // (xs * zs), min(SIDE, 768 // (xs * zs))


def down_units(hid):
    xs, zs, _ = dp_sizes()
    return -(-(hid // unit_rows()[1]) // (xs * zs))


def swap_units_kernel(out_weight, gate_weight, up_weight, down_weight, units, send, recv):
    links = Links(send, recv)
    links.greet([links.group(k) for k in (1, 2, 3)])
    rows, down_rows = unit_rows()
    pieces = links.xs * links.zs
    place = links.x * links.zs + links.z
    lanes = at(links.core * SIDE, SIDE, 128)
    copies = []
    for k in (1, 2, 3):
        col = 1 - links.col if k & 1 else links.col
        index = (place + col * (pieces // 2)) % pieces
        copies.append(
            links.go(
                out_weight.at[index, :, lanes],
                units.at[(k - 1) * rows : k * rows],
                links.group(k),
            )
        )
    count = gate_weight.shape[0] // 2
    first = (1 - links.col) * count
    for e in range(count):
        i = links.used
        links.used += 1
        to = units.at[(3 + e) * rows : (4 + e) * rows]
        either = [
            pltpu.make_async_remote_copy(
                src_ref=weight.at[first + e, place],
                dst_ref=to,
                send_sem=links.send.at[i],
                recv_sem=links.recv.at[i],
                device_id=links.group(1),
                device_id_type=MESH,
            )
            for weight in (gate_weight, up_weight)
        ]
        for which in range(2):

            @pl.when(links.core == which)
            def _(copy=either[which]):
                copy.start()

        copies.append(either[0])
    blocks = down_weight.shape[0] // 2
    for j in range(down_units(blocks * down_rows)):
        index = jnp.minimum(j * pieces + place, blocks - 1)
        start = (3 + count) * rows + j * down_rows
        copies.append(
            links.go(
                down_weight.at[(1 - links.col) * blocks + index, :, lanes],
                units.at[start : start + down_rows],
                links.group(1),
            )
        )
    for copy in copies:
        copy.wait()


def swap_units(out_weight, gate_weight, up_weight, down_weight):
    xs, zs, _ = dp_sizes()
    pieces = xs * zs
    rows, down_rows = unit_rows()
    experts, width, hidden = gate_weight.shape
    hid = experts // 2 * hidden
    total = (3 + experts // 2) * rows + down_units(hid) * down_rows
    return pl.pallas_call(
        swap_units_kernel,
        out_shape=jax.ShapeDtypeStruct((total, SIDE), bf16),
        in_specs=[ANY] * 4,
        out_specs=ANY,
        scratch_shapes=[
            pltpu.SemaphoreType.DMA((12,)),
            pltpu.SemaphoreType.DMA((12,)),
        ],
        compiler_params=pltpu.CompilerParams(collective_id=4, has_side_effects=True),
        name="swap_units",
    )(
        out_weight.reshape(pieces, rows, width),
        gate_weight.reshape(experts, pieces, rows, hidden),
        up_weight.reshape(experts, pieces, rows, hidden),
        down_weight.reshape(-1, down_rows, width),
    )


def gather_inputs_kernel(
    tokens, qkv_weight, small, tokens_all, qkv_all, small_all, send, recv, local
):
    links = Links(send, recv)
    group = [links.group(k) for k in (1, 2, 3)]
    zs, cs = links.zs, links.cs
    links.greet(
        group
        + ([links.other_core()] if cs == 2 else [])
        + [links.place(1, k) for k in range(1, zs)]
    )
    width = tokens.shape[1]
    quarter = HALF // 2

    def own(h):
        return tokens.at[h * quarter : (h + 1) * quarter]

    def dst(k, h):
        rows = (HALF if k & 2 else 0) + h * quarter
        return tokens_all.at[rows : rows + quarter, (k & 1) * width : (k & 1) * width + width]

    share = width // (cs * zs)
    start = links.core * (width // cs) + links.z * share
    theirs = (1 - links.col) * SIDE
    rows = at(start, share)
    there = at(width + start, share)
    fetch = [
        links.copy(
            qkv_weight.at[rows, at(theirs, SIDE, 128)],
            qkv_all.at[there, 0:SIDE],
            links.group(1),
        ),
        links.copy(
            qkv_weight.at[rows, 2 * SIDE :], qkv_all.at[there, SIDE:], links.group(1)
        ),
    ]
    for copy in fetch:
        copy.start()
    little = links.go(small, small_all.at[:, width:], links.group(1))
    forward, finish = gather_group(links, own, dst, width)
    locals_ = [
        pltpu.make_async_copy(tokens, tokens_all.at[0:HALF, 0:width], local.at[0]),
        pltpu.make_async_copy(
            qkv_weight.at[:, at(links.col * SIDE, SIDE, 128)],
            qkv_all.at[0:width, 0:SIDE],
            local.at[1],
        ),
        pltpu.make_async_copy(
            qkv_weight.at[:, 2 * SIDE :], qkv_all.at[0:width, SIDE:], local.at[2]
        ),
        pltpu.make_async_copy(small, small_all.at[:, 0:width], local.at[3]),
    ]
    for copy in locals_:
        copy.start()
    for copy in fetch:
        copy.wait()
    spread = [
        links.go(qkv_all.at[there], qkv_all.at[there], links.place(1, k)) for k in range(1, zs)
    ]
    forward()
    for copy in spread:
        copy.wait()
    if cs == 2:
        block = qkv_all.at[at(width + links.core * (width // 2), width // 2)]
        links.go(block, block, links.other_core()).wait()
    little.wait()
    for copy in locals_:
        copy.wait()
    finish()


def gather_inputs(tokens, qkv_weight, small):
    width = tokens.shape[1]
    return pl.pallas_call(
        gather_inputs_kernel,
        out_shape=(
            jax.ShapeDtypeStruct((2 * HALF, 2 * width), bf16),
            jax.ShapeDtypeStruct((2 * width, SIDE + 2 * HEAD), bf16),
            jax.ShapeDtypeStruct((8, 2 * width), f32),
        ),
        in_specs=[WHOLE] * 3,
        out_specs=(ANY,) * 3,
        scratch_shapes=[
            pltpu.SemaphoreType.DMA((16,)),
            pltpu.SemaphoreType.DMA((16,)),
            pltpu.SemaphoreType.DMA((4,)),
        ],
        compiler_params=pltpu.CompilerParams(collective_id=0, has_side_effects=True),
        name="gather_inputs",
    )(tokens, qkv_weight, small)


def gather_context_kernel(context, context_all, send, recv, local):
    links = Links(send, recv)
    links.greet([links.group(k) for k in (1, 2, 3)])
    width = context.shape[1]

    def block(k, h):
        return context_all.at[h * HALF : (h + 1) * HALF, k * width : (k + 1) * width]

    mine = pltpu.make_async_copy(context, context_all.at[:, 0:width], local)
    mine.start()
    first = {}
    for k, h in ((2, 0), (3, 1), (2, 1), (3, 0)):
        first[k, 1 - h] = links.go(
            context.at[h * HALF : (h + 1) * HALF], block(k, 1 - h), links.group(k)
        )
    first[3, 0].wait_recv()
    relay = [links.go(block(3, 0), block(1, 1), links.group(2))]
    first[2, 1].wait_recv()
    relay.append(links.go(block(2, 1), block(1, 0), links.group(3)))
    mine.wait()
    first[2, 0].wait_recv()
    first[3, 1].wait_recv()
    for copy in relay:
        copy.wait()
    for copy in first.values():
        copy.wait_send()


def gather_context(context):
    rows, width = context.shape
    return pl.pallas_call(
        gather_context_kernel,
        out_shape=jax.ShapeDtypeStruct((rows, 4 * width), bf16),
        in_specs=[WHOLE],
        out_specs=ANY,
        scratch_shapes=[
            pltpu.SemaphoreType.DMA((6,)),
            pltpu.SemaphoreType.DMA((6,)),
            pltpu.SemaphoreType.DMA,
        ],
        compiler_params=pltpu.CompilerParams(collective_id=1, has_side_effects=True),
        name="gather_context",
    )(context)


def scatter_group(links, partial, near2, near3, far2, far3, out2, out3):
    width = partial.shape[1] // 2
    quarter = HALF // 2
    n2, n3 = links.group(2), links.group(3)
    start = [
        links.go(partial.at[0:quarter, width:], near2, n2),
        links.go(partial.at[quarter:HALF, width:], near3, n3),
    ]
    direct = [
        links.go(partial.at[HALF + quarter :, width:], far3.at[quarter:], n3),
        links.go(partial.at[HALF : HALF + quarter, 0:width], far2.at[0:quarter], n2),
    ]
    relay = [
        links.copy(out3, far3.at[0:quarter], n3),
        links.copy(out2, far2.at[quarter:], n2),
    ]

    def forward():
        start[0].wait_recv()
        out3[...] = (
            partial[HALF : HALF + quarter, width:].astype(f32) + near2[...].astype(f32)
        ).astype(bf16)
        relay[0].start()
        start[1].wait_recv()
        out2[...] = (
            partial[HALF + quarter :, 0:width].astype(f32) + near3[...].astype(f32)
        ).astype(bf16)
        relay[1].start()

    def finish():
        for copy in direct:
            copy.wait_recv()
        for copy in relay:
            copy.wait_recv()

    def total(rows):
        return (
            partial[rows, 0:width].astype(f32)
            + far2[rows].astype(f32)
            + far3[rows].astype(f32)
        )

    def sent():
        for copy in start + direct + relay:
            copy.wait_send()

    return forward, finish, total, sent


def norm_back_rows(grad, gain, values, scale, inner, width):
    return scale * (grad * gain - values * (scale * inner * (1.0 / width)))


def column(row_vector):
    return jnp.broadcast_to(row_vector, (128, row_vector.shape[1])).T


def half_swap(v):
    return jnp.concatenate([v[:, HALF:], v[:, :HALF]], axis=1)


def add_rows(out, a, b, total_rows, step):
    @pl.loop(0, total_rows // step)
    def _(i):
        rows = at(i * step, step, 16)
        out[rows] = (a[rows].astype(f32) + b[rows].astype(f32)).astype(bf16)


def reduce_kernel(
    partial,
    vectors,
    hidden,
    cot,
    scale,
    gain,
    gate_up,
    down,
    hidden_grad,
    hidden_low,
    vector_sums,
    gain_part,
    shard_up,
    shard_down,
    near2,
    near3,
    far2,
    far3,
    out2,
    out3,
    vec_in,
    low,
    core_up,
    core_down,
    sum_up,
    sum_down,
    in_up,
    in_down,
    part_up,
    part_down,
    in2_up,
    in2_down,
    peer_up,
    peer_down,
    send,
    recv,
    local,
):
    links = Links(send, recv)
    xs, zs, cs = links.xs, links.zs, links.cs
    sizes = (xs, zs)
    places = (links.x, links.z)
    links.greet([links.group(k) for k in (1, 2, 3)] + links.plane())
    width = partial.shape[1] // 2
    quarter = HALF // 2
    forward, finish, total, sent = scatter_group(
        links, partial, near2, near3, far2, far3, out2, out3
    )
    vec_copies = [links.go(vectors, vec_in.at[k - 1], links.group(k)) for k in (1, 2, 3)]
    core_copies = []
    if cs == 2:
        for ab in range(2):
            core_copies.append(
                (
                    links.go(
                        gate_up.at[1 - links.core, ab], core_up.at[ab], links.other_core()
                    ),
                    links.go(
                        down.at[1 - links.core, ab], core_down.at[ab], links.other_core()
                    ),
                )
            )
    up_rows, down_rows = gate_up.shape[2], down.shape[2]

    def core_step(ab):
        for copy in core_copies[ab] if cs == 2 else ():
            copy.wait_recv()
        for mine, came, out, rows in (
            (gate_up.at[links.core, ab], core_up.at[ab], sum_up.at[ab], up_rows),
            (down.at[links.core, ab], core_down.at[ab], sum_down.at[ab], down_rows),
        ):
            add_rows(out, mine, came, rows, 96)

    up1, down1 = up_rows // xs, down_rows // xs
    up2, down2 = up1 // zs, down1 // zs
    first_copies, second_copies = {}, {}

    def first_send(ab):
        n, place = sizes[ab], places[ab]
        for k in range(1, n):
            j = (place + k) % n
            first_copies[ab, k] = (
                links.go(
                    sum_up.at[ab, at(j * up1, up1)], in_up.at[ab, k - 1], links.place(ab, k)
                ),
                links.go(
                    sum_down.at[ab, at(j * down1, down1)],
                    in_down.at[ab, k - 1],
                    links.place(ab, k),
                ),
            )

    def first_sum(ab):
        n, place = sizes[ab], places[ab]
        for k in range(1, n):
            for copy in first_copies[ab, k]:
                copy.wait_recv()
        for mine, came, out, rows, piece in (
            (sum_up, in_up, part_up, up1, up2),
            (sum_down, in_down, part_down, down1, down2),
        ):

            if piece % 16 == 0:

                @pl.loop(0, rows // piece)
                def _(j):
                    own = mine[ab, at(place * rows + j * piece, piece)].astype(f32)
                    for k in range(1, n):
                        own = own + came[ab, k - 1, at(j * piece, piece)].astype(f32)
                    out[ab, j, 0:piece] = own.astype(bf16)

            else:
                own = mine[ab, at(place * rows, rows)].astype(f32)
                for k in range(1, n):
                    own = own + came[ab, k - 1].astype(f32)
                for j in range(rows // piece):
                    out[ab, j, 0:piece] = own[j * piece : (j + 1) * piece].astype(bf16)

    def second_send(ab):
        n, place = sizes[1 - ab], places[1 - ab]
        for k in range(1, n):
            j = (place + k) % n
            second_copies[ab, k] = (
                links.go(part_up.at[ab, j], in2_up.at[ab, k - 1], links.place(1 - ab, k)),
                links.go(part_down.at[ab, j], in2_down.at[ab, k - 1], links.place(1 - ab, k)),
            )

    def second_sum(ab, out_up, out_down):
        n, place = sizes[1 - ab], places[1 - ab]
        for k in range(1, n):
            for copy in second_copies[ab, k]:
                copy.wait_recv()
        for mine, came, out in (
            (part_up, in2_up, out_up),
            (part_down, in2_down, out_down),
        ):
            value = mine[ab, place].astype(f32)
            for k in range(1, n):
                value = value + came[ab, k - 1].astype(f32)
            out[...] = value.astype(bf16)

    for ref in (part_up, part_down):
        piece = up2 if ref is part_up else down2
        if piece < ref.shape[2]:
            ref[:, :, piece:] = jnp.zeros(
                (2, ref.shape[1], ref.shape[2] - piece, ref.shape[3]), bf16
            )

    core_step(0)
    first_send(0)
    forward()
    core_step(1)
    first_send(1)

    for copy in vec_copies:
        copy.wait()
    vec = vectors[...] + vec_in[0] + half_swap(vec_in[1] + vec_in[2])
    vector_sums[...] = vec
    finish()
    inner = column(vec[6:7, 0:HALF])[:, 0:1]
    part = jnp.zeros((8, width), f32)
    for h in range(4):
        rows = slice(h * 128, (h + 1) * 128)
        grad = total(rows)
        values = hidden[rows]
        scale_rows = scale[rows, 0:1]
        back = norm_back_rows(
            grad, gain[0:1, :], values, scale_rows, inner[rows], 2 * width
        )
        back = back + cot[rows].astype(f32)
        hidden_grad[rows] = back
        low[rows] = back.astype(bf16)
        part = part + jnp.sum(
            (grad * values * scale_rows).reshape(16, 8, width), axis=0
        )
    gain_part[...] = jnp.broadcast_to(jnp.sum(part, axis=0, keepdims=True), (8, width))

    def own(h):
        return low.at[h * quarter : (h + 1) * quarter]

    def dst(k, h):
        rows = (HALF if k & 2 else 0) + h * quarter
        return hidden_low.at[rows : rows + quarter, (k & 1) * width : (k & 1) * width + width]

    mine = pltpu.make_async_copy(low, hidden_low.at[0:HALF, 0:width], local)
    mine.start()
    forward_low, finish_low = gather_group(links, own, dst, width)
    first_sum(0)
    second_send(0)
    first_sum(1)
    second_send(1)
    forward_low()
    second_sum(0, shard_up.at[0], shard_down.at[0])
    second_sum(1, peer_up, peer_down)
    peer = [
        links.go(peer_up, shard_up.at[1], links.group(1)),
        links.go(peer_down, shard_down.at[1], links.group(1)),
    ]
    mine.wait()
    finish_low()
    for copy in peer:
        copy.wait()
    sent()
    for pair in core_copies:
        for copy in pair:
            copy.wait_send()
    for copies in (first_copies, second_copies):
        for pair in copies.values():
            for copy in pair:
                copy.wait_send()


def pad16(n):
    return -(-n // 16) * 16


def reduce_step(partial, vectors, hidden, cot, scale, gain, gate_up, down):
    xs, zs, cs = dp_sizes()
    width = hidden.shape[1]
    up_rows, down_rows = gate_up.shape[2], down.shape[2]
    up1, down1 = up_rows // xs, down_rows // xs
    up2, down2 = pad16(up1 // zs), pad16(down1 // zs)
    n1, n2 = max(xs - 1, 1), max(zs - 1, 1)
    quarter = HALF // 2
    return pl.pallas_call(
        reduce_kernel,
        out_shape=(
            jax.ShapeDtypeStruct((HALF, width), f32),
            jax.ShapeDtypeStruct((2 * HALF, 2 * width), bf16),
            jax.ShapeDtypeStruct(vectors.shape, f32),
            jax.ShapeDtypeStruct((8, width), f32),
            jax.ShapeDtypeStruct((2, up2, SIDE), bf16),
            jax.ShapeDtypeStruct((2, down2, SIDE), bf16),
        ),
        in_specs=[WHOLE] * 8,
        out_specs=(WHOLE, ANY, WHOLE, WHOLE, WHOLE, WHOLE),
        scratch_shapes=[
            VMEM((quarter, width), bf16),
            VMEM((quarter, width), bf16),
            VMEM((HALF, width), bf16),
            VMEM((HALF, width), bf16),
            VMEM((quarter, width), bf16),
            VMEM((quarter, width), bf16),
            VMEM((3,) + vectors.shape, f32),
            VMEM((HALF, width), bf16),
            VMEM((2, up_rows, SIDE), bf16),
            VMEM((2, down_rows, SIDE), bf16),
            VMEM((2, up_rows, SIDE), bf16),
            VMEM((2, down_rows, SIDE), bf16),
            VMEM((2, n1, up1, SIDE), bf16),
            VMEM((2, n1, down1, SIDE), bf16),
            VMEM((2, zs, up2, SIDE), bf16),
            VMEM((2, zs, down2, SIDE), bf16),
            VMEM((2, n2, up2, SIDE), bf16),
            VMEM((2, n2, down2, SIDE), bf16),
            VMEM((up2, SIDE), bf16),
            VMEM((down2, SIDE), bf16),
            pltpu.SemaphoreType.DMA((48,)),
            pltpu.SemaphoreType.DMA((48,)),
            pltpu.SemaphoreType.DMA,
        ],
        compiler_params=pltpu.CompilerParams(
            collective_id=2, has_side_effects=True, vmem_limit_bytes=56 * 2**20
        ),
        name="reduce_step",
    )(partial, vectors, hidden, cot, scale, gain, gate_up, down)


def final_kernel(
    partial,
    vectors,
    tokens,
    scale,
    gain,
    hidden_grad,
    router_part,
    qkv_part,
    out_part,
    small,
    input_grad,
    small_out,
    sums,
    near2,
    near3,
    far2,
    far3,
    out2,
    out3,
    vec_in,
    small_own,
    small_in,
    core_in,
    core_sum,
    in1,
    part,
    in2,
    own_shard,
    peer_shard,
    send,
    recv,
    local,
):
    links = Links(send, recv)
    xs, zs, cs = links.xs, links.zs, links.cs
    sizes, places = (xs, zs), (links.x, links.z)
    links.greet([links.group(k) for k in (1, 2, 3)] + links.plane())
    width = partial.shape[1] // 2
    forward, finish, total, sent = scatter_group(
        links, partial, near2, near3, far2, far3, out2, out3
    )
    vec_copies = [links.go(vectors, vec_in.at[k - 1], links.group(k)) for k in (1, 2, 3)]
    small_copies = [links.go(small, small_in.at[k - 1], links.group(k)) for k in (1, 2, 3)]
    qkv_cols = qkv_part.shape[1]
    core_copies = []
    if cs == 2:
        for ab in range(2):
            first = ab * width + (1 - links.core) * SIDE
            core_copies.append(
                (
                    links.go(
                        qkv_part.at[at(first, SIDE)],
                        core_in.at[ab, :, 0:qkv_cols],
                        links.other_core(),
                    ),
                    links.go(
                        out_part.at[:, at(first, SIDE, 128)],
                        core_in.at[ab, :, qkv_cols:],
                        links.other_core(),
                    ),
                )
            )
    n_first = SIDE // xs
    piece = n_first // zs
    pad = part.shape[2]
    first_copies, second_copies = {}, {}
    if piece < pad:
        part[:, :, piece:] = jnp.zeros((2, zs, pad - piece, part.shape[3]), bf16)

    def core_step(ab):
        first = ab * width + links.core * SIDE
        for copy in core_copies[ab] if cs == 2 else ():
            copy.wait_recv()
        mine = qkv_part[at(first, SIDE)].astype(f32)
        core_sum[ab, :, 0:qkv_cols] = (
            mine + core_in[ab, :, 0:qkv_cols].astype(f32)
        ).astype(bf16)
        mine = out_part[:, at(first, SIDE, 128)].astype(f32)
        core_sum[ab, :, qkv_cols:] = (mine + core_in[ab, :, qkv_cols:].astype(f32)).astype(
            bf16
        )

    def first_send(ab):
        n, place = sizes[ab], places[ab]
        for k in range(1, n):
            j = (place + k) % n
            first_copies[ab, k] = links.go(
                core_sum.at[ab, at(j * n_first, n_first)],
                in1.at[ab, k - 1],
                links.place(ab, k),
            )

    def first_sum(ab):
        n, place = sizes[ab], places[ab]
        for k in range(1, n):
            first_copies[ab, k].wait_recv()

        own = core_sum[ab, at(place * n_first, n_first)].astype(f32)
        for k in range(1, n):
            own = own + in1[ab, k - 1].astype(f32)
        for j in range(zs):
            part[ab, j, 0:piece] = own[j * piece : (j + 1) * piece].astype(bf16)

    def second_send(ab):
        n, place = sizes[1 - ab], places[1 - ab]
        for k in range(1, n):
            j = (place + k) % n
            second_copies[ab, k] = links.go(
                part.at[ab, j], in2.at[ab, k - 1], links.place(1 - ab, k)
            )

    def second_sum(ab, out):
        n, place = sizes[1 - ab], places[1 - ab]
        value = part[ab, place].astype(f32)
        for k in range(1, n):
            second_copies[ab, k].wait_recv()
            value = value + in2[ab, k - 1].astype(f32)
        out[...] = value.astype(bf16)

    core_step(0)
    first_send(0)
    core_step(1)
    first_send(1)
    forward()
    for copy in small_copies:
        copy.wait()

    def swapped(v):
        return jnp.concatenate([v[:, width:], v[:, :width]], axis=1)

    group_sum = small[...] + small_in[1] + swapped(small_in[0] + small_in[2])
    rows = lax.broadcasted_iota(jnp.int32, (8, width), 0)
    small_own[0] = jnp.where(rows < 6, small[:, 0:width], group_sum[:, 0:width])
    stage_copies = []

    def small_stage(stage):
        axis_sizes = (cs, xs, zs)
        base = (0, 1, xs)[stage]
        n = axis_sizes[stage]
        copies = []
        for k in range(1, n):
            device = links.other_core() if stage == 0 else links.place(stage - 1, k)
            copies.append(
                links.go(small_own.at[stage], small_in.at[3 + base + k - 1, :, 0:width], device)
            )

        def done():
            value = small_own[stage]
            for k in range(1, n):
                copies[k - 1].wait()
                value = value + small_in[3 + base + k - 1, :, 0:width]
            small_own[stage + 1] = value

        return done

    done = small_stage(0)
    first_sum(0)
    second_send(0)
    done()
    done = small_stage(1)
    first_sum(1)
    second_send(1)
    done()
    done = small_stage(2)
    second_sum(1, peer_shard)
    peer = links.go(peer_shard, own_shard.at[1], links.group(1))
    second_sum(0, own_shard.at[0])
    done()
    small_out[...] = small_own[3]

    gather_copies = []

    def index(ab, x, z):
        return (x * zs + z) if ab == 0 else (z * xs + x)

    home = []
    for ab in range(2):
        if ab == 1:
            peer.wait()
        here = sums.at[links.core, ab, index(ab, links.x, links.z)]
        mine = pltpu.make_async_copy(own_shard.at[ab], here, local.at[ab])
        mine.start()
        home.append(mine)
        for k in range(1, sizes[1 - ab]):
            gather_copies.append(links.go(own_shard.at[ab], here, links.place(1 - ab, k)))

    for copy in vec_copies:
        copy.wait()
    vec = vectors[...] + vec_in[0] + half_swap(vec_in[1] + vec_in[2])
    inner = column(vec[6:7, 0:HALF])[:, 0:1]
    finish()
    for h in range(4):
        rows = slice(h * 128, (h + 1) * 128)
        grad = total(rows) + router_part[rows]
        back = norm_back_rows(
            grad,
            gain[0:1, :],
            tokens[rows].astype(f32),
            scale[rows, 0:1],
            inner[rows],
            2 * width,
        )
        input_grad[rows] = hidden_grad[rows] + back

    for copy in gather_copies:
        copy.wait()
    for copy in home:
        copy.wait()
    second = []
    for ab in range(2):
        first = (links.x if ab == 0 else links.z) * sizes[1 - ab]
        block = sums.at[links.core, ab, pl.ds(first, sizes[1 - ab])]
        for k in range(1, sizes[ab]):
            second.append(links.go(block, block, links.place(ab, k)))
    for copy in second:
        copy.wait()
    last = None
    if cs == 2:
        block = sums.at[links.core]
        last = links.go(block, block, links.other_core())
    if last is not None:
        last.wait()
    sent()
    for pair in core_copies:
        for copy in pair:
            copy.wait_send()
    for copies in (first_copies, second_copies):
        for copy in copies.values():
            copy.wait_send()


def final_step(
    partial,
    vectors,
    tokens,
    scale,
    gain,
    hidden_grad,
    router_part,
    qkv_part,
    out_part,
    small,
):
    xs, zs, cs = dp_sizes()
    width = hidden_grad.shape[1]
    quarter = HALF // 2
    cols = qkv_part.shape[1] + SIDE
    pad = pad16(SIDE // (xs * zs))
    n1, n2 = max(xs - 1, 1), max(zs - 1, 1)
    group_buffers = [
        VMEM((quarter, width), bf16),
        VMEM((quarter, width), bf16),
        VMEM((HALF, width), bf16),
        VMEM((HALF, width), bf16),
        VMEM((quarter, width), bf16),
        VMEM((quarter, width), bf16),
    ]
    return pl.pallas_call(
        final_kernel,
        out_shape=(
            jax.ShapeDtypeStruct((HALF, width), f32),
            jax.ShapeDtypeStruct((8, width), f32),
            jax.ShapeDtypeStruct((cs, 2, xs * zs, pad, cols), bf16),
        ),
        in_specs=[WHOLE] * 10,
        out_specs=(WHOLE, WHOLE, ANY),
        scratch_shapes=group_buffers
        + [
            VMEM((3,) + vectors.shape, f32),
            VMEM((4, 8, width), f32),
            VMEM((3 + 1 + xs + zs, 8, 2 * width), f32),
            VMEM((2, SIDE, cols), bf16),
            VMEM((2, SIDE, cols), bf16),
            VMEM((2, n1, SIDE // xs, cols), bf16),
            VMEM((2, zs, pad, cols), bf16),
            VMEM((2, n2, pad, cols), bf16),
            VMEM((2, pad, cols), bf16),
            VMEM((pad, cols), bf16),
            pltpu.SemaphoreType.DMA((64,)),
            pltpu.SemaphoreType.DMA((64,)),
            pltpu.SemaphoreType.DMA((2,)),
        ],
        compiler_params=pltpu.CompilerParams(
            collective_id=3, has_side_effects=True, vmem_limit_bytes=56 * 2**20
        ),
        name="final_step",
    )(
        partial,
        vectors,
        tokens,
        scale,
        gain,
        hidden_grad,
        router_part,
        qkv_part,
        out_part,
        small,
    )


def swap_halves(v):
    half = v.shape[-1] // 2
    return jnp.concatenate([v[..., half:], v[..., :half]], axis=-1)


def project_kernel(
    tok, small, weight, routes, cosine, sine, normed_ref, q_ref, k_ref, v_ref, gates_ref, scale_ref
):
    x = tok[...].astype(f32)
    rows, width = x.shape
    scale = lax.rsqrt(jnp.sum(x * x, axis=1, keepdims=True) * (1.0 / width) + EPS)
    normed = (x * scale * small[6:7, :]).astype(bf16)
    normed_ref[...] = normed
    scale_ref[...] = jnp.broadcast_to(scale, scale_ref.shape)
    router = jnp.concatenate([small[...], jnp.zeros((120, width), f32)], axis=0).astype(bf16)
    logits = nt(normed, router)
    lanes = lax.broadcasted_iota(jnp.int32, (rows, 128), 1)
    chosen = lanes == routes[:, 0:1]
    for j in range(1, routes.shape[1]):
        chosen = chosen | (lanes == routes[:, j : j + 1])
    masked = jnp.where(chosen, logits, MASKED)
    raised = jnp.exp(masked - jnp.max(masked, axis=1, keepdims=True))
    raised = jnp.where(chosen, raised, 0.0)
    gates_ref[...] = raised / jnp.sum(raised, axis=1, keepdims=True)
    projected = nn(normed, weight[...])
    for h in range(4):
        part = projected[:, h * HEAD : (h + 1) * HEAD]
        turned = (part * cosine[...] + swap_halves(part) * sine[...]).astype(bf16)
        if h < 3:
            q_ref[:, h * HEAD : (h + 1) * HEAD] = turned
        else:
            k_ref[...] = turned
    v_ref[...] = projected[:, 4 * HEAD :].astype(bf16)


def project(tokens_all, small, weight, routes, cosine, sine):
    total, width = tokens_all.shape
    step = 256

    def rows(cols):
        return pl.BlockSpec((step, cols), lambda i: (i, 0))

    def whole(shape):
        return pl.BlockSpec(shape, lambda i: (0,) * len(shape))

    return pl.pallas_call(
        project_kernel,
        grid=(total // step,),
        out_shape=(
            jax.ShapeDtypeStruct((total, width), bf16),
            jax.ShapeDtypeStruct((total, SIDE), bf16),
            jax.ShapeDtypeStruct((total, HEAD), bf16),
            jax.ShapeDtypeStruct((total, HEAD), bf16),
            jax.ShapeDtypeStruct((total, 128), f32),
            jax.ShapeDtypeStruct((total, 128), f32),
        ),
        in_specs=[
            rows(width),
            whole(small.shape),
            whole(weight.shape),
            rows(routes.shape[1]),
            rows(HEAD),
            rows(HEAD),
        ],
        out_specs=(rows(width), rows(SIDE), rows(HEAD), rows(HEAD), rows(128), rows(128)),
        compiler_params=pltpu.CompilerParams(vmem_limit_bytes=32 * 2**20),
        cost_estimate=pl.CostEstimate(
            flops=2 * total * width * 640, bytes_accessed=10 * 2**20, transcendentals=0
        ),
        name="project",
    )(tokens_all, small, weight, routes, cosine, sine)


def mix_kernel(
    ctx,
    tok,
    small,
    out_weight,
    units,
    normed_ref,
    hidden_ref,
    scale_ref,
    quarter_ref,
    weight,
    sem,
):
    pieces, rows = weight.shape[1:3]
    full = weight.shape[3]
    width = full // 2

    @pl.when(pl.program_id(0) == 0)
    def _():
        col = lax.axis_index("col")
        half = pieces // 2
        copies = []

        def fetch(src, dst):
            copy = pltpu.make_async_copy(src, dst, sem.at[len(copies)])
            copy.start()
            copies.append(copy)

        for h in range(2):
            which = col if h == 0 else 1 - col
            fetch(
                out_weight.at[pl.ds(which * half, half)],
                weight.at[0, h * half : (h + 1) * half, :, 0:width],
            )
        for k in (1, 2, 3):
            for core in range(2):
                first = (k & 1) * width + core * SIDE
                fetch(
                    units.at[:, core, (k - 1) * rows : k * rows],
                    weight.at[k // 2, :, :, first : first + SIDE],
                )
        for copy in copies:
            copy.wait()
        quarter_ref[...] = weight[0, 0:half].reshape(SIDE, full)

    hidden = tok[...].astype(f32) + nn(ctx[...], weight[...].reshape(full, full))
    scale = lax.rsqrt(jnp.sum(hidden * hidden, axis=1, keepdims=True) * (1.0 / full) + EPS)
    normed_ref[...] = (hidden * scale * small[7:8, :]).astype(bf16)
    scale_ref[...] = jnp.broadcast_to(scale, scale_ref.shape)

    @pl.when(pl.program_id(0) == 0)
    def _():
        hidden_ref[...] = hidden[:, :width]


def mix(context_all, tokens_all, small, out_weight, units):
    total, width = tokens_all.shape
    step = HALF
    pieces = units.shape[0]
    rows_unit = width // 2 // pieces

    def rows(cols):
        return pl.BlockSpec((step, cols), lambda i: (i, 0))

    def whole(shape):
        return pl.BlockSpec(shape, lambda i: (0,) * len(shape))

    return pl.pallas_call(
        mix_kernel,
        grid=(total // step,),
        out_shape=(
            jax.ShapeDtypeStruct((total, width), bf16),
            jax.ShapeDtypeStruct((HALF, width // 2), f32),
            jax.ShapeDtypeStruct((total, 128), f32),
            jax.ShapeDtypeStruct((SIDE, width), bf16),
        ),
        in_specs=[rows(width), rows(width), whole(small.shape), ANY, ANY],
        out_specs=(
            rows(width),
            whole((HALF, width // 2)),
            rows(128),
            whole((SIDE, width)),
        ),
        scratch_shapes=[
            VMEM((2, pieces, rows_unit, width), bf16),
            pltpu.SemaphoreType.DMA((8,)),
        ],
        compiler_params=pltpu.CompilerParams(vmem_limit_bytes=48 * 2**20),
        cost_estimate=pl.CostEstimate(
            flops=2 * total * width * width, bytes_accessed=14 * 2**20, transcendentals=0
        ),
        name="mix",
    )(context_all, tokens_all, small, out_weight, units)


def experts_kernel(
    normed,
    cot_own,
    cot_1a,
    cot_1b,
    cot_2,
    cot_3,
    gates,
    gate_weight,
    up_weight,
    down_weight,
    units,
    weighted_ref,
    grad_ref,
    back_ref,
    vec_ref,
    cot,
    own_ref,
    o1a,
    o1b,
    o2a,
    o2b,
    o3a,
    o3b,
    gate_up,
    down,
    sem,
):
    col = lax.axis_index("col")
    step = pl.program_id(0)
    count, _, pieces, unit, both = gate_up.shape
    blocks, down_unit, full = down.shape
    width = full // 2
    hidden = both // 2
    rows = normed.shape[0]
    quarter = HALF // 2
    copies = []

    def fetch(src, dst):
        copies.append(pltpu.make_async_copy(src, dst, sem.at[len(copies)]))

    for e in range(count):
        for which, weight in enumerate((gate_weight, up_weight)):
            cols = slice(which * hidden, (which + 1) * hidden)
            fetch(weight.at[col * count + e], gate_up.at[e, 0, :, :, cols])
            fetch(
                units.at[:, which, (3 + e) * unit : (4 + e) * unit], gate_up.at[e, 1, :, :, cols]
            )
    fetch(down_weight.at[pl.ds(col * blocks, blocks)], down.at[:, :, 0:width])
    for j in range(-(-blocks // pieces)):
        n = min(pieces, blocks - j * pieces)
        start = (3 + count) * unit + j * down_unit
        for core in range(2):
            first = width + core * SIDE
            fetch(
                units.at[0:n, core, start : start + down_unit],
                down.at[j * pieces : j * pieces + n, :, first : first + SIDE],
            )

    @pl.when(step == 0)
    def _():
        for copy in copies:
            copy.start()
        cot[:, :width] = cot_own[...]
        cot[0:quarter, width:] = cot_1a[...]
        cot[quarter:, width:] = cot_1b[...]
        for copy in copies:
            copy.wait()

    @pl.when(step == 1)
    def _():
        cot[:, :width] = cot_2[...]
        cot[:, width:] = cot_3[...]

    lanes = lax.broadcasted_iota(jnp.int32, (rows, 128), 1)
    vec = jnp.zeros((rows, 128), f32)
    inner = jnp.zeros((rows, 1), f32)
    back = out = None
    x, y = normed[...], cot[...]
    for e in range(count):
        weight = gate_up[e].reshape(full, both)
        down_e = down[...].reshape(count, hidden, full)[e]
        here = lanes == col * count + e
        gate = jnp.sum(jnp.where(here, gates[...], 0.0), axis=1, keepdims=True)
        both_pre = nn(x, weight)
        gate_pre, up_pre = both_pre[:, :hidden], both_pre[:, hidden:]
        sigmoid = 1.0 / (1.0 + jnp.exp(-gate_pre))
        silu = gate_pre * sigmoid
        activated = silu * up_pre
        weighted = (gate * activated).astype(bf16)
        weighted_ref[:, e * hidden : (e + 1) * hidden] = weighted
        weighted_grad = nt(y, down_e)
        vec = vec + jnp.where(
            here, jnp.sum(activated * weighted_grad, axis=1, keepdims=True), 0.0
        )
        g = gate * weighted_grad
        gate_grad = g * up_pre * (sigmoid * (1.0 + gate_pre * (1.0 - sigmoid)))
        up_grad = g * silu
        inner = inner + jnp.sum(gate_grad * gate_pre + up_grad * up_pre, axis=1, keepdims=True)
        grads = jnp.concatenate([gate_grad, up_grad], axis=1).astype(bf16)
        grad_ref[e] = grads
        back_e = nt(grads, weight)
        out_e = nn(weighted, down_e)
        back = back_e if back is None else back + back_e
        out = out_e if out is None else out + out_e
    back_ref[...] = back.astype(bf16)
    vec = jnp.where(lanes == 6, inner, vec)
    vec_ref[...] = vec.T[0:8, :]

    @pl.when(step == 0)
    def _():
        own_ref[...] = out[:, :width]
        o1a[...] = out[:quarter, width:].astype(bf16)
        o1b[...] = out[quarter:, width:].astype(bf16)

    @pl.when(step == 1)
    def _():
        o2a[...] = out[:quarter, :width].astype(bf16)
        o2b[...] = out[quarter:, :width].astype(bf16)
        o3a[...] = out[:quarter, width:].astype(bf16)
        o3b[...] = out[quarter:, width:].astype(bf16)


def experts_step(normed, cot_blocks, gates, gate_weight, up_weight, down_weight, units):
    total, width = normed.shape
    step = HALF
    experts, own_width, hidden = gate_weight.shape
    count = experts // 2
    both = 2 * hidden
    hid = count * hidden
    pieces = units.shape[0]
    unit, down_unit = unit_rows()
    quarter = jax.ShapeDtypeStruct((HALF // 2, own_width), bf16)

    def rows(cols):
        return pl.BlockSpec((step, cols), lambda i: (i, 0))

    def whole(shape):
        return pl.BlockSpec(shape, lambda i: (0,) * len(shape))

    return pl.pallas_call(
        experts_kernel,
        grid=(total // step,),
        out_shape=(
            jax.ShapeDtypeStruct((total, hid), bf16),
            jax.ShapeDtypeStruct((count, total, both), bf16),
            jax.ShapeDtypeStruct((total, width), bf16),
            jax.ShapeDtypeStruct((8, total), f32),
            jax.ShapeDtypeStruct((total, width), bf16),
            jax.ShapeDtypeStruct((HALF, own_width), f32),
        )
        + (quarter,) * 6,
        in_specs=[rows(width)]
        + [whole(block.shape) for block in cot_blocks]
        + [rows(128)]
        + [ANY] * 4,
        out_specs=(
            rows(hid),
            pl.BlockSpec((count, step, both), lambda i: (0, i, 0)),
            rows(width),
            pl.BlockSpec((8, step), lambda i: (0, i)),
            rows(width),
            whole((HALF, own_width)),
        )
        + (whole(quarter.shape),) * 6,
        scratch_shapes=[
            VMEM((count, 2, pieces, unit, both), bf16),
            VMEM((hid // down_unit, down_unit, width), bf16),
            pltpu.SemaphoreType.DMA((24,)),
        ],
        compiler_params=pltpu.CompilerParams(vmem_limit_bytes=60 * 2**20),
        cost_estimate=pl.CostEstimate(
            flops=6 * total * width * count * both, bytes_accessed=26 * 2**20, transcendentals=0
        ),
        name="experts",
    )(
        normed,
        *cot_blocks,
        gates,
        gate_weight.reshape(experts, pieces, unit, hidden),
        up_weight.reshape(experts, pieces, unit, hidden),
        down_weight.reshape(-1, down_unit, own_width),
        units,
    )


def expert_grads_kernel(normed, grads, weighted, cot, up_ref, down_ref, normed_t):
    width = normed.shape[1]
    half = width // 2
    hidden = weighted.shape[1]

    @pl.when(pl.program_id(0) == 0)
    def _():
        for i in range(4):
            rows = slice(i * 256, (i + 1) * 256)
            normed_t[:, rows] = normed[rows].T

    for ab in range(2):
        part = nn(normed_t[ab * half : (ab + 1) * half], grads[0])
        for which in range(2):
            up_ref[which, ab] = part[:, which * hidden : (which + 1) * hidden].astype(bf16)
    part = tn(weighted[...], cot[...])
    for ab in range(2):
        for which in range(2):
            first = ab * half + which * hidden
            down_ref[which, ab] = part[:, first : first + hidden].astype(bf16)


def expert_grads(normed, grads, weighted, cot):
    total, width = normed.shape
    count, _, both = grads.shape
    hidden = both // 2
    half = width // 2

    def whole(shape):
        return pl.BlockSpec(shape, lambda e: (0,) * len(shape))

    return pl.pallas_call(
        expert_grads_kernel,
        grid=(count,),
        out_shape=(
            jax.ShapeDtypeStruct((2, 2, count * half, hidden), bf16),
            jax.ShapeDtypeStruct((2, 2, count * hidden, hidden), bf16),
        ),
        in_specs=[
            whole(normed.shape),
            pl.BlockSpec((1, total, both), lambda e: (e, 0, 0)),
            pl.BlockSpec((total, hidden), lambda e: (0, e)),
            whole(cot.shape),
        ],
        out_specs=(
            pl.BlockSpec((2, 2, half, hidden), lambda e: (0, 0, e, 0)),
            pl.BlockSpec((2, 2, hidden, hidden), lambda e: (0, 0, e, 0)),
        ),
        scratch_shapes=[VMEM((width, total), bf16)],
        compiler_params=pltpu.CompilerParams(vmem_limit_bytes=56 * 2**20),
        cost_estimate=pl.CostEstimate(
            flops=3 * total * width * count * both, bytes_accessed=24 * 2**20, transcendentals=0
        ),
        name="expert_grads",
    )(normed, grads, weighted, cot)


def window(i, block):
    first = max(0, (i + 1) * block - 512 - block)
    return first, (i + 1) * block


def own_places(ref, out, row, half):
    for h in range(2):
        start = pl.multiple_of(half * jnp.bitwise_xor(row, h), half)
        out[h * half : (h + 1) * half] = ref[pl.ds(start, half)]


def allowed_keys(segk_ref, segq_ref, i, first, last):
    block = BLOCK
    width = last - first
    keys = lax.broadcasted_iota(jnp.int32, (width, block), 0) + first
    queries = lax.broadcasted_iota(jnp.int32, (width, block), 1) + i * block
    same = segk_ref[first:last] == segq_ref[:, i * block : (i + 1) * block]
    return (keys <= queries) & same


def attend_kernel(heads, q_ref, k_ref, v_ref, segk_ref, segq_ref, o_ref, lse_ref, q, k, vt):
    row = lax.axis_index("row")
    total = q_ref.shape[0]
    half = total // 2
    own_places(q_ref, q, row, half)
    own_places(k_ref, k, row, half)
    for h in range(2):
        start = pl.multiple_of(half * jnp.bitwise_xor(row, h), half)
        vt[:, h * half : (h + 1) * half] = v_ref[pl.ds(start, half)].astype(f32).T.astype(bf16)
    for i in range(total // BLOCK):
        first, last = window(i, BLOCK)
        here = slice(i * BLOCK, (i + 1) * BLOCK)
        allowed = allowed_keys(segk_ref, segq_ref, i, first, last)
        place = i * BLOCK // half
        start = pl.multiple_of(
            half * jnp.bitwise_xor(row, place) + (i * BLOCK - place * half), BLOCK
        )
        for h in range(heads):
            s = nt(k[first:last], q[here, h * HEAD : (h + 1) * HEAD]) * (HEAD**-0.5)
            s = jnp.where(allowed, s, MASKED)
            top = jnp.max(s, axis=0, keepdims=True)
            p = jnp.exp(s - top)
            total_p = jnp.sum(p, axis=0, keepdims=True)
            p = (p * (1.0 / total_p)).astype(bf16)
            ot = nn(vt[:, first:last], p)
            o_ref[pl.ds(start, BLOCK), h * HEAD : (h + 1) * HEAD] = ot.T.astype(bf16)
            lse_ref[h : h + 1, here] = top + jnp.log(total_p)


def attend(q, k, v, seg):
    total, width = q.shape
    heads = width // HEAD
    return pl.pallas_call(
        functools.partial(attend_kernel, heads),
        out_shape=(
            jax.ShapeDtypeStruct((total, width), bf16),
            jax.ShapeDtypeStruct((8, total), f32),
        ),
        in_specs=[WHOLE] * 5,
        out_specs=(WHOLE, WHOLE),
        scratch_shapes=[
            VMEM((total, width), bf16),
            VMEM((total, HEAD), bf16),
            VMEM((HEAD, total), bf16),
        ],
        compiler_params=pltpu.CompilerParams(vmem_limit_bytes=32 * 2**20),
        cost_estimate=pl.CostEstimate(
            flops=2 * heads * total * total * HEAD * 2,
            bytes_accessed=6 * total * width,
            transcendentals=heads * total * total,
        ),
        name="attend",
    )(q, k, v, seg.reshape(total, 1), seg.reshape(1, total))


def attend_back_kernel(
    heads,
    q_ref,
    k_ref,
    v_ref,
    hidden_low,
    out_weight,
    segk_ref,
    segq_ref,
    lse_ref,
    cos_ref,
    sin_ref,
    grad_ref,
    vec_ref,
    q,
    k,
    v,
    kt,
    do,
    dk,
    dv,
):
    row = lax.axis_index("row")
    total = q_ref.shape[0]
    half = total // 2
    scale = HEAD**-0.5
    own_places(q_ref, q, row, half)
    own_places(k_ref, k, row, half)
    own_places(v_ref, v, row, half)
    for h in range(2):
        start = pl.multiple_of(half * jnp.bitwise_xor(row, h), half)
        do[h * half : (h + 1) * half] = nt(
            hidden_low[pl.ds(start, half)], out_weight[...]
        ).astype(bf16)
    kt[...] = k[...].astype(f32).T.astype(bf16)
    dk[...] = jnp.zeros_like(dk)
    dv[...] = jnp.zeros_like(dv)

    def back(grad, rows):
        return grad * cos_ref[rows] - swap_halves(grad) * sin_ref[rows]

    inners = []
    for i in range(total // BLOCK):
        first, last = window(i, BLOCK)
        here = slice(i * BLOCK, (i + 1) * BLOCK)
        allowed = allowed_keys(segk_ref, segq_ref, i, first, last)
        place = i * BLOCK // half
        start = pl.multiple_of(
            half * jnp.bitwise_xor(row, place) + (i * BLOCK - place * half), BLOCK
        )
        rows = pl.ds(start, BLOCK)
        inner_q = jnp.zeros((BLOCK, 1), f32)
        for h in range(heads):
            cols = slice(h * HEAD, (h + 1) * HEAD)
            s = nt(k[first:last], q[here, cols]) * scale
            s = jnp.where(allowed, s, MASKED)
            p = jnp.exp(s - lse_ref[h : h + 1, here])
            dp = nt(v[first:last], do[here, cols])
            inner = jnp.sum(dp * p, axis=0, keepdims=True)
            ds = (p * (dp - inner)).astype(bf16)
            dq = (nn(kt[:, first:last], ds) * scale).T
            inner_q = inner_q + jnp.sum(dq * q[here, cols].astype(f32), axis=1, keepdims=True)
            grad_ref[rows, cols] = back(dq, rows).astype(bf16)
            dk[first:last] += nn(ds, q[here, cols]) * scale
            dv[first:last] += nn(p.astype(bf16), do[here, cols])
        inners.append(inner_q)
    width = heads * HEAD
    for i in range(total // BLOCK):
        here = slice(i * BLOCK, (i + 1) * BLOCK)
        place = i * BLOCK // half
        start = pl.multiple_of(
            half * jnp.bitwise_xor(row, place) + (i * BLOCK - place * half), BLOCK
        )
        rows = pl.ds(start, BLOCK)
        key_grad, value_grad = dk[here], dv[here]
        inner = inners[i] + jnp.sum(
            key_grad * k[here].astype(f32) + value_grad * v[here].astype(f32),
            axis=1,
            keepdims=True,
        )
        grad_ref[rows, width : width + HEAD] = back(key_grad, rows).astype(bf16)
        grad_ref[rows, width + HEAD :] = value_grad.astype(bf16)
        vec_ref[:, rows] = jnp.broadcast_to(inner, (BLOCK, 128)).T[0:8, :]


def attend_back(q, k, v, hidden_low, out_weight, seg, lse, cosine, sine):
    total, width = q.shape
    heads = width // HEAD
    return pl.pallas_call(
        functools.partial(attend_back_kernel, heads),
        out_shape=(
            jax.ShapeDtypeStruct((total, width + 2 * HEAD), bf16),
            jax.ShapeDtypeStruct((8, total), f32),
        ),
        in_specs=[WHOLE] * 10,
        out_specs=(WHOLE, WHOLE),
        scratch_shapes=[
            VMEM((total, width), bf16),
            VMEM((total, HEAD), bf16),
            VMEM((total, HEAD), bf16),
            VMEM((HEAD, total), bf16),
            VMEM((total, width), bf16),
            VMEM((total, HEAD), f32),
            VMEM((total, HEAD), f32),
        ],
        compiler_params=pltpu.CompilerParams(vmem_limit_bytes=48 * 2**20),
        cost_estimate=pl.CostEstimate(
            flops=5 * heads * total * total * HEAD * 2,
            bytes_accessed=10 * total * width,
            transcendentals=heads * total * total,
        ),
        name="attend_back",
    )(
        q,
        k,
        v,
        hidden_low,
        out_weight,
        seg.reshape(total, 1),
        seg.reshape(1, total),
        lse,
        cosine,
        sine,
    )


def attn_grads_kernel(
    grads,
    qkv_weight,
    normed,
    context,
    hidden_low,
    small,
    gates,
    vec_sums,
    vec_part,
    ffn_part,
    partial_ref,
    qkv_ref,
    out_ref,
    vec_ref,
    router_ref,
    small_ref,
):
    total, width = normed.shape
    half = width // 2
    row = lax.axis_index("row")
    col = lax.axis_index("col")
    rows = 256
    for i in range(total // rows):
        here = slice(i * rows, (i + 1) * rows)
        partial_ref[here] = nt(grads[here], qkv_weight[...]).astype(bf16)
    gate_rows = gates[...].T[0:8, :]
    sums = vec_sums[...]
    mask = lax.broadcasted_iota(jnp.int32, sums.shape, 0) < 6
    sums = jnp.where(mask, sums, 0.0)
    logits_grad = gate_rows * (sums - jnp.sum(gate_rows * sums, axis=0, keepdims=True))
    logits_low = jnp.where(mask, logits_grad, 0.0).astype(bf16)
    router = jnp.where(
        lax.broadcasted_iota(jnp.int32, (8, width), 0) < 6, small[...], 0.0
    )
    router_grad = nn(logits_low, normed[...])
    router_ref[...] = tn(logits_low[:, 0:HALF], router[:, 0:half].astype(bf16))
    pieces = []
    for i in range(width // rows):
        here = slice(i * rows, (i + 1) * rows)
        part = tn(normed[:, here], grads[...])
        qkv_ref[here] = part.astype(bf16)
        gain_sum = jnp.sum(part * qkv_weight[here].astype(f32), axis=1, keepdims=True)
        pieces.append(jnp.broadcast_to(gain_sum, (rows, 128)).T[0:8, :])
    out_ref[...] = tn(context[...], hidden_low[...]).astype(bf16)
    gain_row = jnp.concatenate(pieces, axis=1)
    once = jnp.where((row == 0) & (col == 0), 1.0, 0.0)
    gain_row = gain_row + once * jnp.sum(router_grad * router, axis=0, keepdims=True)
    gain_row = gain_row / small[6:7, :]
    ffn = jnp.concatenate([ffn_part[...], jnp.zeros((8, half), f32)], axis=1)
    index = lax.broadcasted_iota(jnp.int32, (8, width), 0)
    small_ref[...] = jnp.where(
        index < 6, router_grad, jnp.where(index == 6, gain_row, ffn)
    )
    logit_rows = nt(router.astype(bf16), normed[...])
    router_inner = jnp.sum(
        logits_low.astype(f32) * logit_rows, axis=0, keepdims=True
    )
    vec_ref[...] = vec_part[...] + once * router_inner


def attn_grads(
    grads, qkv_weight, normed, context, hidden_low, small, gates, vec_sums, vec_part, ffn_part
):
    total, width = normed.shape
    return pl.pallas_call(
        attn_grads_kernel,
        out_shape=(
            jax.ShapeDtypeStruct((total, width), bf16),
            jax.ShapeDtypeStruct(qkv_weight.shape, bf16),
            jax.ShapeDtypeStruct((context.shape[1], width), bf16),
            jax.ShapeDtypeStruct((8, total), f32),
            jax.ShapeDtypeStruct((HALF, width // 2), f32),
            jax.ShapeDtypeStruct((8, width), f32),
        ),
        in_specs=[WHOLE] * 10,
        out_specs=(WHOLE,) * 6,
        compiler_params=pltpu.CompilerParams(vmem_limit_bytes=56 * 2**20),
        cost_estimate=pl.CostEstimate(
            flops=2 * total * width * (640 * 2 + 384), bytes_accessed=24 * 2**20, transcendentals=0
        ),
        name="attn_grads",
    )(grads, qkv_weight, normed, context, hidden_low, small, gates, vec_sums, vec_part, ffn_part)


def expert_finish_kernel(col_ref, by_x, by_z, gate_ref, up_ref, down_ref):
    ab = pl.program_id(0)
    rows = gate_ref.shape[0]
    down_rows = down_ref.shape[0]

    def write(block):
        pieces = block.shape[0]
        step, down_step = rows // pieces, down_rows // pieces
        for p in range(pieces):
            here = slice(p * step, (p + 1) * step)
            gate_ref[here] = block[p, 0, 0, 0:step].astype(f32)
            up_ref[here] = block[p, 1, 0, 0:step].astype(f32)
            here = slice(p * down_step, (p + 1) * down_step)
            for core in range(2):
                down_ref[here, core * SIDE : (core + 1) * SIDE] = block[
                    p, core, 0, step : step + down_step
                ].astype(f32)

    @pl.when(ab == 0)
    def _():
        write(by_x.at[0])

    @pl.when(ab == 1)
    def _():
        write(by_z.at[:, 0])


def expert_finish(sums, col, up_rows, down_rows):
    xs, zs, cs = dp_sizes()
    piece = sums.shape[-2]

    def half(ab, col_ref):
        return jnp.where(ab == 0, col_ref[0], 1 - col_ref[0])

    def out_spec(rows, cols):
        return pl.BlockSpec(
            (rows, cols), lambda ab, j, col_ref: (half(ab, col_ref) * xs + j, 0)
        )

    return pl.pallas_call(
        expert_finish_kernel,
        grid_spec=pltpu.PrefetchScalarGridSpec(
            num_scalar_prefetch=1,
            grid=(2, xs),
            in_specs=[
                pl.BlockSpec(
                    (1, zs, cs, 1, piece, SIDE),
                    lambda ab, j, col_ref: (jnp.where(ab == 0, j, xs - 1), 0, 0, 0, 0, 0),
                ),
                pl.BlockSpec(
                    (xs, 1, cs, 1, piece, SIDE),
                    lambda ab, j, col_ref: (0, jnp.where(ab == 0, 0, j), 0, 1, 0, 0),
                ),
            ],
            out_specs=(
                out_spec(up_rows * zs, SIDE),
                out_spec(up_rows * zs, SIDE),
                out_spec(down_rows * zs, 2 * SIDE),
            ),
        ),
        out_shape=(
            jax.ShapeDtypeStruct((2 * up_rows * xs * zs, SIDE), f32),
            jax.ShapeDtypeStruct((2 * up_rows * xs * zs, SIDE), f32),
            jax.ShapeDtypeStruct((2 * down_rows * xs * zs, 2 * SIDE), f32),
        ),
        compiler_params=pltpu.CompilerParams(vmem_limit_bytes=48 * 2**20),
        name="expert_finish",
    )(col.reshape(1), sums, sums)


def attn_finish_kernel(sums, qkv_ref, out_ref):
    col = lax.axis_index("col")
    cores, _, pieces = sums.shape[:3]
    rows = SIDE // pieces
    cols = SIDE + 2 * HEAD
    for core in range(cores):
        kept = None
        here = slice(core * SIDE, (core + 1) * SIDE)
        for ab in range(2):
            half = col if ab == 0 else 1 - col
            block = sums[core, ab].astype(f32)[:, 0:rows].reshape(SIDE, cols + SIDE)
            qkv_ref[here, at(half * SIDE, SIDE, 128)] = block[:, 0:SIDE]
            out_ref[at(half * SIDE, SIDE), here] = block[:, cols:]
            pair = block[:, SIDE:cols]
            kept = pair if kept is None else kept + pair
        qkv_ref[here, 2 * SIDE :] = kept


def attn_finish(sums):
    return pl.pallas_call(
        attn_finish_kernel,
        out_shape=(
            jax.ShapeDtypeStruct((2 * SIDE, 2 * SIDE + 2 * HEAD), f32),
            jax.ShapeDtypeStruct((2 * SIDE, 2 * SIDE), f32),
        ),
        in_specs=[WHOLE],
        out_specs=(WHOLE, WHOLE),
        compiler_params=pltpu.CompilerParams(vmem_limit_bytes=48 * 2**20),
        name="attn_finish",
    )(sums)


def turn_tables(places):
    steps_up = jnp.arange(HEAD // 2, dtype=f32) * (2.0 / HEAD)
    inverse = jnp.exp(-math.log(ROPE_BASE) * steps_up)
    angles = places[:, None] * inverse[None, :]
    cosine, sine = jnp.cos(angles), jnp.sin(angles)
    return (
        jnp.concatenate([cosine, cosine], axis=1),
        jnp.concatenate([-sine, sine], axis=1),
    )


def local(
    tokens,
    cotangent,
    attn_gain,
    ffn_gain,
    qkv_weight,
    out_weight,
    router_weight,
    gate_weight,
    up_weight,
    down_weight,
    routes,
    segments,
):
    row = lax.axis_index("row")
    col = lax.axis_index("col")
    xs, zs, cs = dp_sizes()
    own_rows, own_width = tokens.shape
    total = 2 * own_rows
    quarter = own_rows // 2
    experts, _, hidden = gate_weight.shape
    own_experts = experts // 2
    hid = own_experts * hidden
    pieces = xs * zs

    units = swap_units(out_weight, gate_weight, up_weight, down_weight)
    units = lax.all_gather(units, "dp", axis=0, tiled=False)
    units = units.reshape((pieces, cs) + units.shape[1:])

    def own_order(v):
        return jnp.where(row == 0, v, jnp.roll(v, own_rows, axis=0))

    routes_local = own_order(routes)
    cosine, sine = turn_tables(own_order(jnp.arange(total, dtype=f32)))
    small = jnp.concatenate(
        [router_weight.T.astype(f32), attn_gain[None], ffn_gain[None]], axis=0
    )

    tokens_all, qkv_local, small_all = gather_inputs(tokens, qkv_weight, small)
    cot_own, tokens_all = lax.optimization_barrier((cotangent, tokens_all))
    cot_2 = flip(cot_own, 2)
    cot_3 = flip(cot_own, 3)
    normed_one, queries, keys, values, gates, scale_one = project(
        tokens_all, small_all, qkv_local, routes_local, cosine, sine
    )
    context, lse = attend(queries, keys, values, segments)
    cot_1a = flip(cot_3[:quarter], 2)
    cot_1b = flip(cot_2[quarter:], 3)
    context_all = gather_context(context)
    normed_two, hidden_own, scale_two, out_quarter = mix(
        context_all, tokens_all, small_all, out_weight.reshape(pieces, -1, own_width), units
    )
    (
        weighted,
        pre_grads,
        normed_two_part,
        expert_vec,
        cot_all,
        layer_own,
        o1a,
        o1b,
        o2a,
        o2b,
        o3a,
        o3b,
    ) = experts_step(
        normed_two,
        (cot_own, cot_1a, cot_1b, cot_2, cot_3),
        gates,
        gate_weight,
        up_weight,
        down_weight,
        units,
    )
    pass_3 = flip(o1a, 2)
    pass_2 = flip(o1b, 3)
    far_3b = flip(o3b, 3)
    far_2a = flip(o2a, 2)
    gate_up_grads, down_grads = expert_grads(normed_two, pre_grads, weighted, cot_all)
    hidden_grad, hidden_low, vec_sums, ffn_part, shard_up, shard_down = reduce_step(
        normed_two_part,
        expert_vec,
        hidden_own,
        cotangent,
        scale_two,
        ffn_gain[None],
        gate_up_grads,
        down_grads,
    )
    up_rows = own_experts * own_width // pieces
    down_rows = hid // pieces
    expert_sums = lax.all_gather(
        jnp.concatenate([shard_up[:, :up_rows], shard_down[:, :down_rows]], axis=1),
        "dp",
        axis=0,
        tiled=False,
    ).reshape(xs, zs, cs, 2, up_rows + down_rows, SIDE)
    far_3a = flip((o3a.astype(f32) + pass_3.astype(f32)).astype(bf16), 3)
    far_2b = flip((o2b.astype(f32) + pass_2.astype(f32)).astype(bf16), 2)

    projected_grad, vec_part = attend_back(
        queries, keys, values, hidden_low, out_quarter, segments, lse, cosine, sine
    )
    input_part, qkv_part, out_part, input_vec, router_part, small_part = attn_grads(
        projected_grad,
        qkv_local,
        normed_one,
        context,
        hidden_low,
        small_all,
        gates,
        vec_sums,
        vec_part,
        ffn_part,
    )
    layer_out = (
        hidden_own
        + layer_own
        + jnp.concatenate([far_2a, far_2b], axis=0).astype(f32)
        + jnp.concatenate([far_3a, far_3b], axis=0).astype(f32)
    ).astype(bf16)
    input_grad, small_sums, attn_sums = final_step(
        input_part,
        input_vec,
        tokens,
        scale_one,
        attn_gain[None],
        hidden_grad,
        router_part,
        qkv_part,
        out_part,
        small_part,
    )
    router_grad = small_sums[:experts].T
    attn_gain_grad = small_sums[6]
    ffn_gain_grad = small_sums[7]
    qkv_grad, out_grad = attn_finish(attn_sums)
    gate_grad, up_grad, down_grad = expert_finish(expert_sums, col, up_rows, down_rows)
    gate_grad = gate_grad.reshape(experts, own_width, hidden)
    up_grad = up_grad.reshape(experts, own_width, hidden)
    down_grad = down_grad.reshape(experts, hidden, own_width)
    return (
        layer_out,
        input_grad,
        attn_gain_grad,
        ffn_gain_grad,
        qkv_grad,
        out_grad,
        router_grad,
        gate_grad,
        up_grad,
        down_grad,
    )


def solution(mesh):
    in_specs = (
        P(("dp", "row"), "col"),
        P(("dp", "row"), "col"),
        P("col"),
        P("col"),
        P("col", "row"),
        P("row", "col"),
        P("col", None),
        P(None, "col", "row"),
        P(None, "col", "row"),
        P(None, "row", "col"),
        P("dp", None),
        P("dp"),
    )
    out_specs = (
        P(("dp", "row"), "col"),
        P(("dp", "row"), "col"),
        P("col"),
        P("col"),
        P("col", "row"),
        P("row", "col"),
        P("col", None),
        P(None, "col", "row"),
        P(None, "col", "row"),
        P(None, "row", "col"),
    )
    return jax.shard_map(local, mesh=mesh, in_specs=in_specs, out_specs=out_specs, check_vma=False)
```

```python
import functools
import math

import jax
import jax.numpy as jnp
from jax import lax
from jax.experimental import pallas as pl
from jax.experimental.pallas import tpu as pltpu
from jax.sharding import PartitionSpec as P

f32 = jnp.float32
bf16 = jnp.bfloat16

HEAD = 128
GROUP_HEADS = 6
EPS = 1e-06
ROPE_BASE = 10000.0
MASKED = -1e30
BLOCK = 256


MESH = pl.DeviceIdType.MESH
VMEM = pltpu.VMEM
ANY = pl.BlockSpec(memory_space=pl.ANY)
WHOLE = pl.BlockSpec(memory_space=pltpu.VMEM)
HALF = 512
SIDE = 384


def flip(v, k):
    return lax.ppermute(v, ("row", "col"), [(i, i ^ k) for i in range(4)])


def dp_sizes():
    total = lax.axis_size("dp")
    cores = 2 if total % 2 == 0 else 1
    side = math.isqrt(total // cores)
    return side, side, cores


def dp_place():
    xs, zs, cs = dp_sizes()
    d = lax.axis_index("dp")
    return d // (zs * cs), (d // cs) % zs, d % cs


def nt(a, b):
    return lax.dot_general(a, b, (((1,), (1,)), ((), ())), preferred_element_type=f32)


def nn(a, b):
    return lax.dot_general(a, b, (((1,), (0,)), ((), ())), preferred_element_type=f32)


def tn(a, b):
    return lax.dot_general(a, b, (((0,), (0,)), ((), ())), preferred_element_type=f32)


class Links:
    def __init__(self, send, recv):
        self.send, self.recv = send, recv
        self.used = 0
        self.dp = lax.axis_index("dp")
        self.row = lax.axis_index("row")
        self.col = lax.axis_index("col")
        self.xs, self.zs, self.cs = dp_sizes()
        self.x, self.z, self.core = dp_place()

    def group(self, k):
        row = 1 - self.row if k & 2 else self.row
        col = 1 - self.col if k & 1 else self.col
        return (self.dp, row, col)

    def other_core(self):
        return (self.dp + 1 - 2 * self.core, self.row, self.col)

    def place(self, axis, k):
        x, z = self.x, self.z
        if axis == 0:
            x = (x + k) % self.xs
        else:
            z = (z + k) % self.zs
        return ((x * self.zs + z) * self.cs + self.core, self.row, self.col)

    def greet(self, devices):
        barrier = pltpu.get_barrier_semaphore()
        for device in devices:
            pl.semaphore_signal(barrier, inc=1, device_id=device, device_id_type=MESH)
        pl.semaphore_wait(barrier, len(devices))

    def plane(self):
        return (
            ([self.other_core()] if self.cs == 2 else [])
            + [self.place(0, k) for k in range(1, self.xs)]
            + [self.place(1, k) for k in range(1, self.zs)]
        )

    def copy(self, src, dst, device):
        i = self.used
        self.used += 1
        return pltpu.make_async_remote_copy(
            src_ref=src,
            dst_ref=dst,
            send_sem=self.send.at[i],
            recv_sem=self.recv.at[i],
            device_id=device,
            device_id_type=MESH,
        )

    def go(self, src, dst, device):
        copy = self.copy(src, dst, device)
        copy.start()
        return copy


def at(start, size, step=16):
    return pl.ds(pl.multiple_of(start, step), size)


class Fetch:
    def __init__(self, sems):
        self.sems = sems
        self.used = 0
        self.named = {}

    def start(self, name, *pairs):
        copies = self.named.setdefault(name, [])
        for src, dst in pairs:
            copy = pltpu.make_async_copy(src, dst, self.sems.at[self.used])
            self.used += 1
            copy.start()
            copies.append(copy)

    def wait(self, *names):
        for name in names:
            for copy in self.named.pop(name):
                copy.wait()


def pad16(n):
    return -(-n // 16) * 16


class PlaneSum:
    def __init__(self, links, part, came, in1, piece, in2, shard, peer, sums=None, local=None):
        self.links, self.part, self.came, self.in1 = links, part, came, in1
        self.piece, self.in2, self.shard, self.peer = piece, in2, shard, peer
        self.sums, self.local = sums, local
        self.sizes = (links.xs, links.zs)
        self.places = (links.x, links.z)
        self.sent = []
        self.first, self.second, self.core = {}, {}, {}
        rows = came.shape[1]
        self.rows1 = rows // links.xs
        self.rows2 = self.rows1 // links.zs
        self.home, self.spread1, self.spread2 = {}, {}, {}

    def start(self):
        kept, rows = self.rows2, self.piece.shape[2]
        if kept < rows:
            shape = self.piece.shape
            self.piece[:, :, kept:] = jnp.zeros(shape[:2] + (rows - kept, shape[3]), bf16)

    def core_send(self, ab, rows=None):
        if self.links.cs == 1:
            return
        src, dst = self.part(ab, 1 - self.links.core), self.came.at[ab]
        if rows is not None:
            src, dst = src.at[rows], dst.at[rows]
        copy = self.links.go(src, dst, self.links.other_core())
        self.core.setdefault(ab, []).append(copy)
        self.sent.append(copy)

    def first_send(self, ab):
        for copy in self.core.get(ab, []):
            copy.wait_recv()
        mine, total = self.part(ab, self.links.core), self.came.at[ab]
        rows = total.shape[0]
        step = 96

        @pl.loop(0, rows // step)
        def _(i):
            here = at(i * step, step)
            total[here] = (total[here].astype(f32) + mine[here].astype(f32)).astype(bf16)

        n, place = self.sizes[ab], self.places[ab]
        for k in range(1, n):
            j = (place + k) % n
            copy = self.links.go(
                self.came.at[ab, at(j * self.rows1, self.rows1)],
                self.in1.at[ab, k - 1],
                self.links.place(ab, k),
            )
            self.first[ab, k] = copy
            self.sent.append(copy)

    def second_send(self, ab):
        n, place = self.sizes[ab], self.places[ab]
        for k in range(1, n):
            self.first[ab, k].wait_recv()
        rows, piece = self.rows1, self.rows2
        if piece % 16 == 0:

            @pl.loop(0, rows // piece)
            def _(j):
                own = self.came[ab, at(place * rows + j * piece, piece)].astype(f32)
                for k in range(1, n):
                    own = own + self.in1[ab, k - 1, at(j * piece, piece)].astype(f32)
                self.piece[ab, j, 0:piece] = own.astype(bf16)

        else:
            own = self.came[ab, at(place * rows, rows)].astype(f32)
            for k in range(1, n):
                own = own + self.in1[ab, k - 1].astype(f32)
            for j in range(rows // piece):
                self.piece[ab, j, 0:piece] = own[j * piece : (j + 1) * piece].astype(bf16)
        n, place = self.sizes[1 - ab], self.places[1 - ab]
        for k in range(1, n):
            j = (place + k) % n
            copy = self.links.go(
                self.piece.at[ab, j], self.in2.at[ab, k - 1], self.links.place(1 - ab, k)
            )
            self.second[ab, k] = copy
            self.sent.append(copy)

    def last_sum(self, ab):
        n, place = self.sizes[1 - ab], self.places[1 - ab]
        value = self.piece[ab, place].astype(f32)
        for k in range(1, n):
            self.second[ab, k].wait_recv()
            value = value + self.in2[ab, k - 1].astype(f32)
        if ab == 0:
            self.shard[0] = value.astype(bf16)
        else:
            self.peer[...] = value.astype(bf16)
            self.swap = self.links.go(self.peer, self.shard.at[1], self.links.group(1))

    def gather_near(self, ab):
        links = self.links
        if ab == 1:
            self.swap.wait()
        x, z = links.x, links.z
        index = (x * links.zs + z) if ab == 0 else (z * links.xs + x)
        here = self.sums.at[links.core, ab, index]
        copy = pltpu.make_async_copy(self.shard.at[ab], here, self.local.at[ab])
        copy.start()
        self.home[ab] = copy
        self.spread1[ab] = [
            links.go(self.shard.at[ab], here, links.place(1 - ab, k))
            for k in range(1, self.sizes[1 - ab])
        ]

    def gather_far(self, ab):
        links = self.links
        for copy in self.spread1[ab]:
            copy.wait()
        self.home[ab].wait()
        n = self.sizes[1 - ab]
        first = (links.x if ab == 0 else links.z) * n
        block = self.sums.at[links.core, ab, pl.ds(first, n)]
        self.spread2[ab] = [
            links.go(block, block, links.place(ab, k)) for k in range(1, self.sizes[ab])
        ]

    def gather_core(self):
        links = self.links
        for ab in range(2):
            for copy in self.spread2[ab]:
                copy.wait()
        if links.cs == 2:
            block = self.sums.at[links.core]
            self.last = links.go(block, block, links.other_core())

    def done(self):
        for copy in self.sent:
            copy.wait_send()
        if self.sums is None:
            self.swap.wait()
        elif self.links.cs == 2:
            self.last.wait()


def plane_scratch(rows, width):
    xs, zs, _ = dp_sizes()
    n1, n2 = max(xs - 1, 1), max(zs - 1, 1)
    pad = pad16(rows // (xs * zs))
    return [
        VMEM((2, rows, width), bf16),
        VMEM((2, n1, rows // xs, width), bf16),
        VMEM((2, zs, pad, width), bf16),
        VMEM((2, n2, pad, width), bf16),
        VMEM((pad, width), bf16),
    ]


def gather_group(links, own, dst, wide):
    quarter = HALF // 2
    first = {}
    for k, order in ((2, (1, 0)), (3, (0, 1))):
        for h in order:
            first[k, h] = links.copy(own(h), dst(k, h), links.group(k))
    for key in ((2, 1), (3, 0), (2, 0), (3, 1)):
        first[key].start()
    relay = [
        links.copy(dst(3, 0), dst(1, 0), links.group(2)),
        links.copy(dst(2, 1), dst(1, 1), links.group(3)),
    ]

    def forward():
        first[3, 0].wait_recv()
        relay[0].start()
        first[2, 1].wait_recv()
        relay[1].start()

    def finish():
        first[2, 0].wait_recv()
        first[3, 1].wait_recv()
        for copy in relay:
            copy.wait()
        for copy in first.values():
            copy.wait_send()

    return forward, finish


def unit_rows():
    xs, zs, _ = dp_sizes()
    return 768 // (xs * zs), min(SIDE, 768 // (xs * zs))


def down_units(hid):
    xs, zs, _ = dp_sizes()
    return -(-(hid // unit_rows()[1]) // (xs * zs))


def swap_units_kernel(out_weight, gate_weight, up_weight, down_weight, units, send, recv):
    links = Links(send, recv)
    links.greet([links.group(k) for k in (1, 2, 3)])
    rows, down_rows = unit_rows()
    pieces = links.xs * links.zs
    place = links.x * links.zs + links.z
    lanes = at(links.core * SIDE, SIDE, 128)
    copies = []
    for k in (1, 2, 3):
        col = 1 - links.col if k & 1 else links.col
        index = (place + col * (pieces // 2)) % pieces
        copies.append(
            links.go(
                out_weight.at[index, :, lanes],
                units.at[(k - 1) * rows : k * rows],
                links.group(k),
            )
        )
    count = gate_weight.shape[0] // 2
    first = (1 - links.col) * count
    for e in range(count):
        i = links.used
        links.used += 1
        to = units.at[(3 + e) * rows : (4 + e) * rows]
        either = [
            pltpu.make_async_remote_copy(
                src_ref=weight.at[first + e, place],
                dst_ref=to,
                send_sem=links.send.at[i],
                recv_sem=links.recv.at[i],
                device_id=links.group(1),
                device_id_type=MESH,
            )
            for weight in (gate_weight, up_weight)
        ]
        for which in range(2):

            @pl.when(links.core == which)
            def _(copy=either[which]):
                copy.start()

        copies.append(either[0])
    blocks = down_weight.shape[0] // 2
    for j in range(down_units(blocks * down_rows)):
        index = jnp.minimum(j * pieces + place, blocks - 1)
        start = (3 + count) * rows + j * down_rows
        copies.append(
            links.go(
                down_weight.at[(1 - links.col) * blocks + index, :, lanes],
                units.at[start : start + down_rows],
                links.group(1),
            )
        )
    for copy in copies:
        copy.wait()


def swap_units(out_weight, gate_weight, up_weight, down_weight):
    xs, zs, _ = dp_sizes()
    pieces = xs * zs
    rows, down_rows = unit_rows()
    experts, width, hidden = gate_weight.shape
    hid = experts // 2 * hidden
    total = (3 + experts // 2) * rows + down_units(hid) * down_rows
    return pl.pallas_call(
        swap_units_kernel,
        out_shape=jax.ShapeDtypeStruct((total, SIDE), bf16),
        in_specs=[ANY] * 4,
        out_specs=ANY,
        scratch_shapes=[
            pltpu.SemaphoreType.DMA((12,)),
            pltpu.SemaphoreType.DMA((12,)),
        ],
        compiler_params=pltpu.CompilerParams(collective_id=4, has_side_effects=True),
        name="swap_units",
    )(
        out_weight.reshape(pieces, rows, width),
        gate_weight.reshape(experts, pieces, rows, hidden),
        up_weight.reshape(experts, pieces, rows, hidden),
        down_weight.reshape(-1, down_rows, width),
    )


def gather_inputs_kernel(
    tokens, qkv_weight, small, tokens_all, qkv_all, small_all, send, recv, local
):
    links = Links(send, recv)
    group = [links.group(k) for k in (1, 2, 3)]
    zs, cs = links.zs, links.cs
    links.greet(
        group
        + ([links.other_core()] if cs == 2 else [])
        + [links.place(1, k) for k in range(1, zs)]
    )
    width = tokens.shape[1]
    quarter = HALF // 2

    def own(h):
        return tokens.at[h * quarter : (h + 1) * quarter]

    def dst(k, h):
        rows = (HALF if k & 2 else 0) + h * quarter
        return tokens_all.at[rows : rows + quarter, (k & 1) * width : (k & 1) * width + width]

    share = width // (cs * zs)
    start = links.core * (width // cs) + links.z * share
    theirs = (1 - links.col) * SIDE
    rows = at(start, share)
    there = at(width + start, share)
    fetch = [
        links.copy(
            qkv_weight.at[rows, at(theirs, SIDE, 128)],
            qkv_all.at[there, 0:SIDE],
            links.group(1),
        ),
        links.copy(
            qkv_weight.at[rows, 2 * SIDE :], qkv_all.at[there, SIDE:], links.group(1)
        ),
    ]
    for copy in fetch:
        copy.start()
    little = links.go(small, small_all.at[:, width:], links.group(1))
    forward, finish = gather_group(links, own, dst, width)
    locals_ = [
        pltpu.make_async_copy(tokens, tokens_all.at[0:HALF, 0:width], local.at[0]),
        pltpu.make_async_copy(
            qkv_weight.at[:, at(links.col * SIDE, SIDE, 128)],
            qkv_all.at[0:width, 0:SIDE],
            local.at[1],
        ),
        pltpu.make_async_copy(
            qkv_weight.at[:, 2 * SIDE :], qkv_all.at[0:width, SIDE:], local.at[2]
        ),
        pltpu.make_async_copy(small, small_all.at[:, 0:width], local.at[3]),
    ]
    for copy in locals_:
        copy.start()
    for copy in fetch:
        copy.wait()
    spread = [
        links.go(qkv_all.at[there], qkv_all.at[there], links.place(1, k)) for k in range(1, zs)
    ]
    forward()
    for copy in spread:
        copy.wait()
    if cs == 2:
        block = qkv_all.at[at(width + links.core * (width // 2), width // 2)]
        links.go(block, block, links.other_core()).wait()
    little.wait()
    for copy in locals_:
        copy.wait()
    finish()


def gather_inputs(tokens, qkv_weight, small):
    width = tokens.shape[1]
    return pl.pallas_call(
        gather_inputs_kernel,
        out_shape=(
            jax.ShapeDtypeStruct((2 * HALF, 2 * width), bf16),
            jax.ShapeDtypeStruct((2 * width, SIDE + 2 * HEAD), bf16),
            jax.ShapeDtypeStruct((8, 2 * width), f32),
        ),
        in_specs=[WHOLE] * 3,
        out_specs=(ANY,) * 3,
        scratch_shapes=[
            pltpu.SemaphoreType.DMA((16,)),
            pltpu.SemaphoreType.DMA((16,)),
            pltpu.SemaphoreType.DMA((4,)),
        ],
        compiler_params=pltpu.CompilerParams(collective_id=0, has_side_effects=True),
        name="gather_inputs",
    )(tokens, qkv_weight, small)


def gather_context_kernel(context, context_all, send, recv, local):
    links = Links(send, recv)
    links.greet([links.group(k) for k in (1, 2, 3)])
    width = context.shape[1]

    def block(k, h):
        return context_all.at[h * HALF : (h + 1) * HALF, k * width : (k + 1) * width]

    mine = pltpu.make_async_copy(context, context_all.at[:, 0:width], local)
    mine.start()
    first = {}
    for k, h in ((2, 0), (3, 1), (2, 1), (3, 0)):
        first[k, 1 - h] = links.go(
            context.at[h * HALF : (h + 1) * HALF], block(k, 1 - h), links.group(k)
        )
    first[3, 0].wait_recv()
    relay = [links.go(block(3, 0), block(1, 1), links.group(2))]
    first[2, 1].wait_recv()
    relay.append(links.go(block(2, 1), block(1, 0), links.group(3)))
    mine.wait()
    first[2, 0].wait_recv()
    first[3, 1].wait_recv()
    for copy in relay:
        copy.wait()
    for copy in first.values():
        copy.wait_send()


def gather_context(context):
    rows, width = context.shape
    return pl.pallas_call(
        gather_context_kernel,
        out_shape=jax.ShapeDtypeStruct((rows, 4 * width), bf16),
        in_specs=[WHOLE],
        out_specs=ANY,
        scratch_shapes=[
            pltpu.SemaphoreType.DMA((6,)),
            pltpu.SemaphoreType.DMA((6,)),
            pltpu.SemaphoreType.DMA,
        ],
        compiler_params=pltpu.CompilerParams(collective_id=1, has_side_effects=True),
        name="gather_context",
    )(context)


def scatter_group(links, blocks, mine, pass2, pass3, near2, near3, far2, far3, out2, out3):
    quarter = HALF // 2
    n2, n3 = links.group(2), links.group(3)
    start, direct = [], []

    def send_own_rows():
        start.append(links.go(blocks(1, 0), near2, n2))
        start.append(links.go(blocks(1, 1), near3, n3))

    def send_other_rows():
        direct.append(links.go(blocks(3, 1), far3.at[quarter:], n3))
        direct.append(links.go(blocks(2, 0), far2.at[0:quarter], n2))

    relay = [
        links.copy(out3, far3.at[0:quarter], n3),
        links.copy(out2, far2.at[quarter:], n2),
    ]

    def forward():
        start[0].wait_recv()
        out3[...] = (pass3[...].astype(f32) + near2[...].astype(f32)).astype(bf16)
        relay[0].start()
        start[1].wait_recv()
        out2[...] = (pass2[...].astype(f32) + near3[...].astype(f32)).astype(bf16)
        relay[1].start()

    def finish():
        for copy in direct + relay:
            copy.wait_recv()

    def total(rows):
        return mine[rows].astype(f32) + far2[rows].astype(f32) + far3[rows].astype(f32)

    def sent():
        for copy in start + direct + relay:
            copy.wait_send()

    return send_own_rows, send_other_rows, forward, finish, total, sent


def group_scratch(width):
    quarter = HALF // 2
    return [
        VMEM((quarter, width), bf16),
        VMEM((quarter, width), bf16),
        VMEM((HALF, width), bf16),
        VMEM((HALF, width), bf16),
        VMEM((quarter, width), bf16),
        VMEM((quarter, width), bf16),
    ]


def norm_back_rows(grad, gain, values, scale, inner, width):
    return scale * (grad * gain - values * (scale * inner * (1.0 / width)))


def column(row_vector):
    return jnp.broadcast_to(row_vector, (128, row_vector.shape[1])).T


def half_swap(v):
    return jnp.concatenate([v[:, HALF:], v[:, :HALF]], axis=1)


def reduce_kernel(
    partial,
    vectors,
    hidden_h,
    cot_h,
    scale_h,
    gain,
    normed_h,
    grads_h,
    weighted_h,
    cot_all_h,
    hidden_grad,
    hidden_low,
    vector_sums,
    gain_part,
    shard_up,
    shard_down,
    hidden,
    cot,
    scale,
    normed,
    grads,
    weighted,
    cot_all,
    normed_t,
    mine_p,
    pass2,
    pass3,
    near2,
    near3,
    far2,
    far3,
    out2,
    out3,
    vec_in,
    low,
    up_part,
    down_part,
    *rest,
):
    up_scratch, down_scratch = rest[0:5], rest[5:10]
    send, recv, sems, local = rest[10:]
    links = Links(send, recv)
    width = hidden_grad.shape[1]
    quarter = HALF // 2
    count, _, both = grads.shape
    side = both // 2
    fetch = Fetch(sems)
    fetch.start("normed", (normed_h, normed))
    fetch.start("grads", *[(grads_h.at[e], grads.at[e]) for e in range(count)])
    fetch.start("down", (weighted_h, weighted), (cot_all_h, cot_all))
    fetch.start(
        "pass",
        (partial.at[HALF + quarter :, 0:width], pass2),
        (partial.at[HALF : HALF + quarter, width:], pass3),
    )
    fetch.start(
        "own",
        (partial.at[0:HALF, 0:width], mine_p),
        (hidden_h, hidden),
        (cot_h, cot),
        (scale_h.at[0:HALF], scale),
    )
    links.greet([links.group(k) for k in (1, 2, 3)] + links.plane())

    def blocks(k, h):
        first = (HALF if k & 2 else 0) + h * quarter
        cols = slice((k & 1) * width, (k & 1) * width + width)
        return partial.at[first : first + quarter, cols]

    own_rows, other_rows, forward, finish, total, sent = scatter_group(
        links, blocks, mine_p, pass2, pass3, near2, near3, far2, far3, out2, out3
    )
    own_rows()
    other_rows()
    vec_copies = [links.go(vectors, vec_in.at[k - 1], links.group(k)) for k in (1, 2, 3)]

    up = PlaneSum(
        links, lambda ab, core: up_part.at[core, ab], *up_scratch[:4], shard_up, up_scratch[4]
    )
    down = PlaneSum(
        links,
        lambda ab, core: down_part.at[core, ab],
        *down_scratch[:4],
        shard_down,
        down_scratch[4],
    )
    up.start()
    down.start()
    fetch.wait("normed")
    for i in range(4):
        rows = slice(i * 256, (i + 1) * 256)
        normed_t[:, rows] = normed[rows].T
    fetch.wait("grads")
    for e in range(count):
        rows = slice(e * width, (e + 1) * width)
        for ab in range(2):
            part = nn(normed_t[ab * width : (ab + 1) * width], grads[e])
            for which in range(2):
                up_part[which, ab, rows] = part[:, which * side : (which + 1) * side].astype(
                    bf16
                )
            up.core_send(ab, rows)
        if e == 0:
            fetch.wait("down", "pass")
        rows = slice(e * side, (e + 1) * side)
        part = tn(weighted[:, rows], cot_all[...])
        for ab in range(2):
            for which in range(2):
                first = ab * width + which * side
                down_part[which, ab, rows] = part[:, first : first + side].astype(bf16)
            down.core_send(ab, rows)
        if e == 1:
            forward()
    for ab in range(2):
        up.first_send(ab)
        down.first_send(ab)

    for copy in vec_copies:
        copy.wait()
    vec = vectors[...] + vec_in[0] + half_swap(vec_in[1] + vec_in[2])
    vector_sums[...] = vec
    fetch.wait("own")
    inner = column(vec[6:7, 0:HALF])[:, 0:1]
    part = jnp.zeros((8, width), f32)
    finish()
    for h in range(4):
        rows = slice(h * 128, (h + 1) * 128)
        grad = total(rows)
        values = hidden[rows]
        scale_rows = scale[rows, 0:1]
        back = norm_back_rows(grad, gain[0:1, :], values, scale_rows, inner[rows], 2 * width)
        back = back + cot[rows].astype(f32)
        hidden_grad[rows] = back
        low[rows] = back.astype(bf16)
        part = part + jnp.sum((grad * values * scale_rows).reshape(16, 8, width), axis=0)
    gain_part[...] = jnp.broadcast_to(jnp.sum(part, axis=0, keepdims=True), (8, width))

    def own(h):
        return low.at[h * quarter : (h + 1) * quarter]

    def dst(k, h):
        rows = (HALF if k & 2 else 0) + h * quarter
        return hidden_low.at[rows : rows + quarter, (k & 1) * width : (k & 1) * width + width]

    mine = pltpu.make_async_copy(low, hidden_low.at[0:HALF, 0:width], local)
    mine.start()
    forward_low, finish_low = gather_group(links, own, dst, width)
    forward_low()
    for ab in range(2):
        up.second_send(ab)
        down.second_send(ab)
    for ab in (1, 0):
        up.last_sum(ab)
        down.last_sum(ab)
    mine.wait()
    finish_low()
    sent()
    up.done()
    down.done()


def reduce_step(
    partial, vectors, hidden, cot, scale, gain, normed, grads, weighted, cot_all
):
    xs, zs, _ = dp_sizes()
    width = hidden.shape[1]
    count, total, both = grads.shape
    side = both // 2
    up_rows, down_rows = count * width, count * side
    quarter = HALF // 2
    return pl.pallas_call(
        reduce_kernel,
        out_shape=(
            jax.ShapeDtypeStruct((HALF, width), f32),
            jax.ShapeDtypeStruct((2 * HALF, 2 * width), bf16),
            jax.ShapeDtypeStruct(vectors.shape, f32),
            jax.ShapeDtypeStruct((8, width), f32),
            jax.ShapeDtypeStruct((2, pad16(up_rows // (xs * zs)), side), bf16),
            jax.ShapeDtypeStruct((2, pad16(down_rows // (xs * zs)), side), bf16),
        ),
        in_specs=[ANY, WHOLE, ANY, ANY, ANY, WHOLE, ANY, ANY, ANY, ANY],
        out_specs=(WHOLE, ANY, WHOLE, WHOLE, WHOLE, WHOLE),
        scratch_shapes=[
            VMEM((HALF, width), f32),
            VMEM((HALF, width), bf16),
            VMEM((HALF, 128), f32),
            VMEM(normed.shape, bf16),
            VMEM(grads.shape, bf16),
            VMEM(weighted.shape, bf16),
            VMEM(cot_all.shape, bf16),
            VMEM((2 * width, total), bf16),
            VMEM((HALF, width), bf16),
            VMEM((quarter, width), bf16),
            VMEM((quarter, width), bf16),
        ]
        + group_scratch(width)
        + [
            VMEM((3,) + vectors.shape, f32),
            VMEM((HALF, width), bf16),
            VMEM((2, 2, up_rows, side), bf16),
            VMEM((2, 2, down_rows, side), bf16),
        ]
        + plane_scratch(up_rows, side)
        + plane_scratch(down_rows, side)
        + [
            pltpu.SemaphoreType.DMA((64,)),
            pltpu.SemaphoreType.DMA((64,)),
            pltpu.SemaphoreType.DMA((16,)),
            pltpu.SemaphoreType.DMA,
        ],
        compiler_params=pltpu.CompilerParams(
            collective_id=2, has_side_effects=True, vmem_limit_bytes=60 * 2**20
        ),
        name="reduce_step",
    )(partial, vectors, hidden, cot, scale, gain, normed, grads, weighted, cot_all)


def attn_back_kernel(
    heads,
    q_h,
    k_h,
    v_h,
    lse,
    segk_ref,
    segq_ref,
    cos_h,
    sin_h,
    context_h,
    hidden_low_h,
    out_weight,
    qkv_h,
    normed_h,
    small_all,
    gates,
    vec_sums,
    ffn_part,
    tokens_h,
    scale_h,
    gain,
    hidden_grad_h,
    input_grad,
    small_out,
    qkv_sums,
    out_sums,
    q,
    k,
    v,
    cos_ref,
    sin_ref,
    context,
    hidden_low,
    qkv,
    normed,
    tokens,
    scale,
    hidden_grad,
    kt,
    do,
    dk,
    dv,
    grads,
    partial,
    qkv_part,
    out_part,
    near2,
    near3,
    far2,
    far3,
    out2,
    out3,
    vec_own,
    vec_in,
    small,
    small_own,
    small_in,
    qkv_shard,
    out_shard,
    *rest,
):
    qkv_scratch, out_scratch = rest[0:5], rest[5:10]
    send, recv, sems, local = rest[10:]
    links = Links(send, recv)
    xs, zs, cs = links.xs, links.zs, links.cs
    row = links.row
    total, full = normed.shape
    width = full // 2
    quarter = HALF // 2
    head_scale = HEAD**-0.5
    fetch = Fetch(sems)
    fetch.start("out", (context_h, context), (hidden_low_h, hidden_low))
    for src, dst in ((q_h, q), (k_h, k), (v_h, v)):
        fetch.start(
            "attention",
            *[
                (
                    src.at[at(HALF * jnp.bitwise_xor(row, h), HALF)],
                    dst.at[h * HALF : (h + 1) * HALF],
                )
                for h in range(2)
            ],
        )
    fetch.start("turn", (cos_h, cos_ref), (sin_h, sin_ref))
    fetch.start("normed", (normed_h, normed))
    fetch.start("qkv", (qkv_h, qkv))
    fetch.start(
        "own",
        (tokens_h, tokens),
        (scale_h.at[0:HALF], scale),
        (hidden_grad_h, hidden_grad),
    )
    links.greet([links.group(k) for k in (1, 2, 3)] + links.plane())

    out_sum = PlaneSum(
        links,
        lambda ab, core: out_part.at[:, at(ab * width + core * SIDE, SIDE, 128)],
        *out_scratch[:4],
        out_shard,
        out_scratch[4],
        out_sums,
        local.at[0],
    )
    qkv_sum = PlaneSum(
        links,
        lambda ab, core: qkv_part.at[at(ab * width + core * SIDE, SIDE)],
        *qkv_scratch[:4],
        qkv_shard,
        qkv_scratch[4],
        qkv_sums,
        local.at[1],
    )
    out_sum.start()
    qkv_sum.start()
    fetch.wait("out")
    out_part[...] = tn(context[...], hidden_low[...]).astype(bf16)
    for ab in range(2):
        out_sum.core_send(ab)

    for h in range(2):
        rows = at(HALF * jnp.bitwise_xor(row, h), HALF)
        do[h * HALF : (h + 1) * HALF] = nt(hidden_low[rows], out_weight[...]).astype(bf16)
    fetch.wait("attention", "turn")
    kt[...] = k[...].astype(f32).T.astype(bf16)
    dk[...] = jnp.zeros_like(dk)
    dv[...] = jnp.zeros_like(dv)

    def back(grad, rows):
        return grad * cos_ref[rows] - swap_halves(grad) * sin_ref[rows]

    def rows_of(i):
        place = i * BLOCK // HALF
        return at(HALF * jnp.bitwise_xor(row, place) + (i * BLOCK - place * HALF), BLOCK, BLOCK)

    inners = []
    for i in range(total // BLOCK):
        first, last = window(i, BLOCK)
        here = slice(i * BLOCK, (i + 1) * BLOCK)
        allowed = allowed_keys(segk_ref, segq_ref, i, first, last)
        rows = rows_of(i)
        inner_q = jnp.zeros((BLOCK, 1), f32)
        for h in range(heads):
            cols = slice(h * HEAD, (h + 1) * HEAD)
            s = nt(k[first:last], q[here, cols]) * head_scale
            s = jnp.where(allowed, s, MASKED)
            p = jnp.exp(s - lse[h : h + 1, here])
            dp = nt(v[first:last], do[here, cols])
            inner = jnp.sum(dp * p, axis=0, keepdims=True)
            ds = (p * (dp - inner)).astype(bf16)
            dq = (nn(kt[:, first:last], ds) * head_scale).T
            inner_q = inner_q + jnp.sum(dq * q[here, cols].astype(f32), axis=1, keepdims=True)
            grads[rows, cols] = back(dq, rows).astype(bf16)
            dk[first:last] += nn(ds, q[here, cols]) * head_scale
            dv[first:last] += nn(p.astype(bf16), do[here, cols])
        inners.append(inner_q)
        if i == 1:
            for ab in range(2):
                out_sum.first_send(ab)
    for ab in range(2):
        out_sum.second_send(ab)

    gate_rows = gates[...].T[0:8, :]
    sums = vec_sums[...]
    mask = lax.broadcasted_iota(jnp.int32, sums.shape, 0) < 6
    sums = jnp.where(mask, sums, 0.0)
    logits_grad = gate_rows * (sums - jnp.sum(gate_rows * sums, axis=0, keepdims=True))
    logits_low = jnp.where(mask, logits_grad, 0.0).astype(bf16)
    router = jnp.where(
        lax.broadcasted_iota(jnp.int32, (8, full), 0) < 6, small_all[...], 0.0
    )
    router_low = router.astype(bf16)
    once = jnp.where((row == 0) & (links.col == 0), 1.0, 0.0)
    fetch.wait("normed")
    router_grad = nn(logits_low, normed[...])
    router_inner = once * jnp.sum(
        logits_low.astype(f32) * nt(router_low, normed[...]), axis=0, keepdims=True
    )
    for i in range(total // BLOCK):
        here = slice(i * BLOCK, (i + 1) * BLOCK)
        rows = rows_of(i)
        key_grad, value_grad = dk[here], dv[here]
        inner = inners[i] + jnp.sum(
            key_grad * k[here].astype(f32) + value_grad * v[here].astype(f32),
            axis=1,
            keepdims=True,
        )
        grads[rows, heads * HEAD : (heads + 1) * HEAD] = back(key_grad, rows).astype(bf16)
        grads[rows, (heads + 1) * HEAD :] = value_grad.astype(bf16)
        vec_own[:, rows] = jnp.broadcast_to(inner, (BLOCK, 128)).T[0:8, :]
    vec_own[...] += router_inner
    vec_copies = [links.go(vec_own, vec_in.at[k - 1], links.group(k)) for k in (1, 2, 3)]

    def blocks(k, h):
        first = (HALF if k & 2 else 0) + h * quarter
        cols = slice((k & 1) * width, (k & 1) * width + width)
        return partial.at[first : first + quarter, cols]

    own_rows, other_rows, forward, finish, sum_rows, sent = scatter_group(
        links,
        blocks,
        partial.at[0:HALF, 0:width],
        partial.at[HALF + quarter :, 0:width],
        partial.at[HALF : HALF + quarter, width:],
        near2,
        near3,
        far2,
        far3,
        out2,
        out3,
    )
    fetch.wait("qkv")
    partial[0:HALF] = nt(grads[0:HALF], qkv[...]).astype(bf16)
    own_rows()
    partial[HALF:] = nt(grads[HALF:], qkv[...]).astype(bf16)
    other_rows()

    gain_sums = {}
    for mine in (False, True):
        which = links.core if mine else 1 - links.core
        for ab in range(2):
            first = ab * width + which * SIDE
            part = tn(normed[:, at(first, SIDE, 128)], grads[...])
            rows = at(first, SIDE)
            qkv_part[rows] = part.astype(bf16)
            gain_sum = jnp.sum(part * qkv[rows].astype(f32), axis=1, keepdims=True)
            gain_sums[mine, ab] = jnp.broadcast_to(gain_sum, (SIDE, 128)).T[0:8, :]
            if not mine:
                qkv_sum.core_send(ab)
    for ab in range(2):
        out_sum.last_sum(1 - ab)
    forward()
    for ab in range(2):
        qkv_sum.first_send(ab)
    for ab in range(2):
        out_sum.gather_near(ab)

    halves = []
    for ab in range(2):
        a, b = gain_sums[True, ab], gain_sums[False, ab]
        first = links.core == 0
        halves.append(jnp.concatenate([jnp.where(first, a, b), jnp.where(first, b, a)], axis=1))
    gain_row = jnp.concatenate(halves, axis=1)
    gain_row = gain_row + once * jnp.sum(router_grad * router, axis=0, keepdims=True)
    gain_row = gain_row / small_all[6:7, :]
    ffn = jnp.concatenate([ffn_part[...], jnp.zeros((8, width), f32)], axis=1)
    index = lax.broadcasted_iota(jnp.int32, (8, full), 0)
    small[...] = jnp.where(index < 6, router_grad, jnp.where(index == 6, gain_row, ffn))
    small_copies = [links.go(small, small_in.at[k - 1], links.group(k)) for k in (1, 2, 3)]

    stages = []

    def small_stage(stage):
        axis_sizes = (cs, xs, zs)
        base = 3 + (0, 1, xs)[stage]
        copies = []
        for k in range(1, axis_sizes[stage]):
            device = links.other_core() if stage == 0 else links.place(stage - 1, k)
            there = small_in.at[base + k - 1, :, 0:width]
            copies.append((links.go(small_own.at[stage], there, device), there))

        def done():
            value = small_own[stage]
            for copy, there in copies:
                copy.wait()
                value = value + there[...]
            small_own[stage + 1] = value

        return done

    for ab in range(2):
        qkv_sum.second_send(ab)
    for copy in small_copies:
        copy.wait()

    def swapped(v):
        return jnp.concatenate([v[:, width:], v[:, :width]], axis=1)

    group_sum = small[...] + small_in[1] + swapped(small_in[0] + small_in[2])
    eight = lax.broadcasted_iota(jnp.int32, (8, width), 0)
    small_own[0] = jnp.where(eight < 6, small[:, 0:width], group_sum[:, 0:width])
    done = small_stage(0)
    for ab in range(2):
        out_sum.gather_far(ab)
    for ab in (1, 0):
        qkv_sum.last_sum(ab)
    done()
    done = small_stage(1)
    qkv_sum.gather_near(0)
    qkv_sum.gather_near(1)
    done()
    done = small_stage(2)

    for copy in vec_copies:
        copy.wait()
    vec = vec_own[...] + vec_in[0] + half_swap(vec_in[1] + vec_in[2])
    inner = column(vec[6:7, 0:HALF])[:, 0:1]
    fetch.wait("own")
    qkv_sum.gather_far(0)
    qkv_sum.gather_far(1)
    out_sum.gather_core()
    finish()
    for h in range(4):
        rows = slice(h * 128, (h + 1) * 128)
        grad = sum_rows(rows) + tn(logits_low[:, rows], router_low[:, 0:width])
        input_grad[rows] = hidden_grad[rows] + norm_back_rows(
            grad,
            gain[0:1, :],
            tokens[rows].astype(f32),
            scale[rows, 0:1],
            inner[rows],
            full,
        )
    done()
    small_out[...] = small_own[3]
    qkv_sum.gather_core()
    sent()
    out_sum.done()
    qkv_sum.done()


def attn_back(
    q,
    k,
    v,
    lse,
    seg,
    cosine,
    sine,
    context,
    hidden_low,
    out_weight,
    qkv_weight,
    normed,
    small_all,
    gates,
    vec_sums,
    ffn_part,
    tokens,
    scale,
    gain,
    hidden_grad,
):
    xs, zs, cs = dp_sizes()
    total, full = normed.shape
    width = full // 2
    heads = q.shape[1] // HEAD
    cols = qkv_weight.shape[1]
    pad = pad16(SIDE // (xs * zs))
    return pl.pallas_call(
        functools.partial(attn_back_kernel, heads),
        out_shape=(
            jax.ShapeDtypeStruct((HALF, width), f32),
            jax.ShapeDtypeStruct((8, width), f32),
            jax.ShapeDtypeStruct((cs, 2, xs * zs, pad, cols), bf16),
            jax.ShapeDtypeStruct((cs, 2, xs * zs, pad, SIDE), bf16),
        ),
        in_specs=[ANY] * 3
        + [WHOLE] * 3
        + [ANY] * 4
        + [WHOLE]
        + [ANY] * 2
        + [WHOLE] * 4
        + [ANY] * 2
        + [WHOLE, ANY],
        out_specs=(WHOLE, WHOLE, ANY, ANY),
        scratch_shapes=[
            VMEM(q.shape, bf16),
            VMEM(k.shape, bf16),
            VMEM(v.shape, bf16),
            VMEM(cosine.shape, f32),
            VMEM(sine.shape, f32),
            VMEM(context.shape, bf16),
            VMEM(hidden_low.shape, bf16),
            VMEM(qkv_weight.shape, bf16),
            VMEM(normed.shape, bf16),
            VMEM(tokens.shape, bf16),
            VMEM((HALF, 128), f32),
            VMEM(hidden_grad.shape, f32),
            VMEM((HEAD, total), bf16),
            VMEM(q.shape, bf16),
            VMEM(k.shape, f32),
            VMEM(v.shape, f32),
            VMEM((total, cols), bf16),
            VMEM((total, full), bf16),
            VMEM((full, cols), bf16),
            VMEM((SIDE, full), bf16),
        ]
        + group_scratch(width)
        + [
            VMEM((8, total), f32),
            VMEM((3, 8, total), f32),
            VMEM((8, full), f32),
            VMEM((4, 8, width), f32),
            VMEM((3 + 1 + xs + zs, 8, full), f32),
            VMEM((2, pad, cols), bf16),
            VMEM((2, pad, SIDE), bf16),
        ]
        + plane_scratch(SIDE, cols)
        + plane_scratch(SIDE, SIDE)
        + [
            pltpu.SemaphoreType.DMA((96,)),
            pltpu.SemaphoreType.DMA((96,)),
            pltpu.SemaphoreType.DMA((16,)),
            pltpu.SemaphoreType.DMA((2, 2)),
        ],
        compiler_params=pltpu.CompilerParams(
            collective_id=3, has_side_effects=True, vmem_limit_bytes=60 * 2**20
        ),
        name="attn_back",
    )(
        q,
        k,
        v,
        lse,
        seg.reshape(total, 1),
        seg.reshape(1, total),
        cosine,
        sine,
        context,
        hidden_low,
        out_weight,
        qkv_weight,
        normed,
        small_all,
        gates,
        vec_sums,
        ffn_part,
        tokens,
        scale,
        gain,
        hidden_grad,
    )


def swap_halves(v):
    half = v.shape[-1] // 2
    return jnp.concatenate([v[..., half:], v[..., :half]], axis=-1)


def project_kernel(
    tok, small, weight, routes, cosine, sine, normed_ref, q_ref, k_ref, v_ref, gates_ref, scale_ref
):
    x = tok[...].astype(f32)
    rows, width = x.shape
    scale = lax.rsqrt(jnp.sum(x * x, axis=1, keepdims=True) * (1.0 / width) + EPS)
    normed = (x * scale * small[6:7, :]).astype(bf16)
    normed_ref[...] = normed
    scale_ref[...] = jnp.broadcast_to(scale, scale_ref.shape)
    router = jnp.concatenate([small[...], jnp.zeros((120, width), f32)], axis=0).astype(bf16)
    logits = nt(normed, router)
    lanes = lax.broadcasted_iota(jnp.int32, (rows, 128), 1)
    chosen = lanes == routes[:, 0:1]
    for j in range(1, routes.shape[1]):
        chosen = chosen | (lanes == routes[:, j : j + 1])
    masked = jnp.where(chosen, logits, MASKED)
    raised = jnp.exp(masked - jnp.max(masked, axis=1, keepdims=True))
    raised = jnp.where(chosen, raised, 0.0)
    gates_ref[...] = raised / jnp.sum(raised, axis=1, keepdims=True)
    projected = nn(normed, weight[...])
    for h in range(4):
        part = projected[:, h * HEAD : (h + 1) * HEAD]
        turned = (part * cosine[...] + swap_halves(part) * sine[...]).astype(bf16)
        if h < 3:
            q_ref[:, h * HEAD : (h + 1) * HEAD] = turned
        else:
            k_ref[...] = turned
    v_ref[...] = projected[:, 4 * HEAD :].astype(bf16)


def project(tokens_all, small, weight, routes, cosine, sine):
    total, width = tokens_all.shape
    step = 256

    def rows(cols):
        return pl.BlockSpec((step, cols), lambda i: (i, 0))

    def whole(shape):
        return pl.BlockSpec(shape, lambda i: (0,) * len(shape))

    return pl.pallas_call(
        project_kernel,
        grid=(total // step,),
        out_shape=(
            jax.ShapeDtypeStruct((total, width), bf16),
            jax.ShapeDtypeStruct((total, SIDE), bf16),
            jax.ShapeDtypeStruct((total, HEAD), bf16),
            jax.ShapeDtypeStruct((total, HEAD), bf16),
            jax.ShapeDtypeStruct((total, 128), f32),
            jax.ShapeDtypeStruct((total, 128), f32),
        ),
        in_specs=[
            rows(width),
            whole(small.shape),
            whole(weight.shape),
            rows(routes.shape[1]),
            rows(HEAD),
            rows(HEAD),
        ],
        out_specs=(rows(width), rows(SIDE), rows(HEAD), rows(HEAD), rows(128), rows(128)),
        compiler_params=pltpu.CompilerParams(vmem_limit_bytes=32 * 2**20),
        cost_estimate=pl.CostEstimate(
            flops=2 * total * width * 640, bytes_accessed=10 * 2**20, transcendentals=0
        ),
        name="project",
    )(tokens_all, small, weight, routes, cosine, sine)


def mix_kernel(
    ctx,
    tok,
    small,
    out_weight,
    units,
    normed_ref,
    hidden_ref,
    scale_ref,
    quarter_ref,
    weight,
    sem,
):
    pieces, rows = weight.shape[1:3]
    full = weight.shape[3]
    width = full // 2

    @pl.when(pl.program_id(0) == 0)
    def _():
        col = lax.axis_index("col")
        half = pieces // 2
        copies = []

        def fetch(src, dst):
            copy = pltpu.make_async_copy(src, dst, sem.at[len(copies)])
            copy.start()
            copies.append(copy)

        for h in range(2):
            which = col if h == 0 else 1 - col
            fetch(
                out_weight.at[pl.ds(which * half, half)],
                weight.at[0, h * half : (h + 1) * half, :, 0:width],
            )
        for k in (1, 2, 3):
            for core in range(2):
                first = (k & 1) * width + core * SIDE
                fetch(
                    units.at[:, core, (k - 1) * rows : k * rows],
                    weight.at[k // 2, :, :, first : first + SIDE],
                )
        for copy in copies:
            copy.wait()
        quarter_ref[...] = weight[0, 0:half].reshape(SIDE, full)

    hidden = tok[...].astype(f32) + nn(ctx[...], weight[...].reshape(full, full))
    scale = lax.rsqrt(jnp.sum(hidden * hidden, axis=1, keepdims=True) * (1.0 / full) + EPS)
    normed_ref[...] = (hidden * scale * small[7:8, :]).astype(bf16)
    scale_ref[...] = jnp.broadcast_to(scale, scale_ref.shape)

    @pl.when(pl.program_id(0) == 0)
    def _():
        hidden_ref[...] = hidden[:, :width]


def mix(context_all, tokens_all, small, out_weight, units):
    total, width = tokens_all.shape
    step = HALF
    pieces = units.shape[0]
    rows_unit = width // 2 // pieces

    def rows(cols):
        return pl.BlockSpec((step, cols), lambda i: (i, 0))

    def whole(shape):
        return pl.BlockSpec(shape, lambda i: (0,) * len(shape))

    return pl.pallas_call(
        mix_kernel,
        grid=(total // step,),
        out_shape=(
            jax.ShapeDtypeStruct((total, width), bf16),
            jax.ShapeDtypeStruct((HALF, width // 2), f32),
            jax.ShapeDtypeStruct((total, 128), f32),
            jax.ShapeDtypeStruct((SIDE, width), bf16),
        ),
        in_specs=[rows(width), rows(width), whole(small.shape), ANY, ANY],
        out_specs=(
            rows(width),
            whole((HALF, width // 2)),
            rows(128),
            whole((SIDE, width)),
        ),
        scratch_shapes=[
            VMEM((2, pieces, rows_unit, width), bf16),
            pltpu.SemaphoreType.DMA((8,)),
        ],
        compiler_params=pltpu.CompilerParams(vmem_limit_bytes=48 * 2**20),
        cost_estimate=pl.CostEstimate(
            flops=2 * total * width * width, bytes_accessed=14 * 2**20, transcendentals=0
        ),
        name="mix",
    )(context_all, tokens_all, small, out_weight, units)


def experts_kernel(
    normed,
    cot_own,
    cot_1a,
    cot_1b,
    cot_2,
    cot_3,
    gates,
    gate_weight,
    up_weight,
    down_weight,
    units,
    weighted_ref,
    grad_ref,
    back_ref,
    vec_ref,
    cot,
    own_ref,
    o1a,
    o1b,
    o2a,
    o2b,
    o3a,
    o3b,
    gate_up,
    down,
    sem,
):
    col = lax.axis_index("col")
    step = pl.program_id(0)
    count, _, pieces, unit, both = gate_up.shape
    blocks, down_unit, full = down.shape
    width = full // 2
    hidden = both // 2
    rows = normed.shape[0]
    quarter = HALF // 2
    copies = []

    def fetch(src, dst):
        copies.append(pltpu.make_async_copy(src, dst, sem.at[len(copies)]))

    for e in range(count):
        for which, weight in enumerate((gate_weight, up_weight)):
            cols = slice(which * hidden, (which + 1) * hidden)
            fetch(weight.at[col * count + e], gate_up.at[e, 0, :, :, cols])
            fetch(
                units.at[:, which, (3 + e) * unit : (4 + e) * unit], gate_up.at[e, 1, :, :, cols]
            )
    fetch(down_weight.at[pl.ds(col * blocks, blocks)], down.at[:, :, 0:width])
    for j in range(-(-blocks // pieces)):
        n = min(pieces, blocks - j * pieces)
        start = (3 + count) * unit + j * down_unit
        for core in range(2):
            first = width + core * SIDE
            fetch(
                units.at[0:n, core, start : start + down_unit],
                down.at[j * pieces : j * pieces + n, :, first : first + SIDE],
            )

    @pl.when(step == 0)
    def _():
        for copy in copies:
            copy.start()
        cot[:, :width] = cot_own[...]
        cot[0:quarter, width:] = cot_1a[...]
        cot[quarter:, width:] = cot_1b[...]
        for copy in copies:
            copy.wait()

    @pl.when(step == 1)
    def _():
        cot[:, :width] = cot_2[...]
        cot[:, width:] = cot_3[...]

    lanes = lax.broadcasted_iota(jnp.int32, (rows, 128), 1)
    vec = jnp.zeros((rows, 128), f32)
    inner = jnp.zeros((rows, 1), f32)
    back = out = None
    x, y = normed[...], cot[...]
    for e in range(count):
        weight = gate_up[e].reshape(full, both)
        down_e = down[...].reshape(count, hidden, full)[e]
        here = lanes == col * count + e
        gate = jnp.sum(jnp.where(here, gates[...], 0.0), axis=1, keepdims=True)
        both_pre = nn(x, weight)
        gate_pre, up_pre = both_pre[:, :hidden], both_pre[:, hidden:]
        sigmoid = 1.0 / (1.0 + jnp.exp(-gate_pre))
        silu = gate_pre * sigmoid
        activated = silu * up_pre
        weighted = (gate * activated).astype(bf16)
        weighted_ref[:, e * hidden : (e + 1) * hidden] = weighted
        weighted_grad = nt(y, down_e)
        vec = vec + jnp.where(
            here, jnp.sum(activated * weighted_grad, axis=1, keepdims=True), 0.0
        )
        g = gate * weighted_grad
        gate_grad = g * up_pre * (sigmoid * (1.0 + gate_pre * (1.0 - sigmoid)))
        up_grad = g * silu
        inner = inner + jnp.sum(gate_grad * gate_pre + up_grad * up_pre, axis=1, keepdims=True)
        grads = jnp.concatenate([gate_grad, up_grad], axis=1).astype(bf16)
        grad_ref[e] = grads
        back_e = nt(grads, weight)
        out_e = nn(weighted, down_e)
        back = back_e if back is None else back + back_e
        out = out_e if out is None else out + out_e
    back_ref[...] = back.astype(bf16)
    vec = jnp.where(lanes == 6, inner, vec)
    vec_ref[...] = vec.T[0:8, :]

    @pl.when(step == 0)
    def _():
        own_ref[...] = out[:, :width]
        o1a[...] = out[:quarter, width:].astype(bf16)
        o1b[...] = out[quarter:, width:].astype(bf16)

    @pl.when(step == 1)
    def _():
        o2a[...] = out[:quarter, :width].astype(bf16)
        o2b[...] = out[quarter:, :width].astype(bf16)
        o3a[...] = out[:quarter, width:].astype(bf16)
        o3b[...] = out[quarter:, width:].astype(bf16)


def experts_step(normed, cot_blocks, gates, gate_weight, up_weight, down_weight, units):
    total, width = normed.shape
    step = HALF
    experts, own_width, hidden = gate_weight.shape
    count = experts // 2
    both = 2 * hidden
    hid = count * hidden
    pieces = units.shape[0]
    unit, down_unit = unit_rows()
    quarter = jax.ShapeDtypeStruct((HALF // 2, own_width), bf16)

    def rows(cols):
        return pl.BlockSpec((step, cols), lambda i: (i, 0))

    def whole(shape):
        return pl.BlockSpec(shape, lambda i: (0,) * len(shape))

    return pl.pallas_call(
        experts_kernel,
        grid=(total // step,),
        out_shape=(
            jax.ShapeDtypeStruct((total, hid), bf16),
            jax.ShapeDtypeStruct((count, total, both), bf16),
            jax.ShapeDtypeStruct((total, width), bf16),
            jax.ShapeDtypeStruct((8, total), f32),
            jax.ShapeDtypeStruct((total, width), bf16),
            jax.ShapeDtypeStruct((HALF, own_width), f32),
        )
        + (quarter,) * 6,
        in_specs=[rows(width)]
        + [whole(block.shape) for block in cot_blocks]
        + [rows(128)]
        + [ANY] * 4,
        out_specs=(
            rows(hid),
            pl.BlockSpec((count, step, both), lambda i: (0, i, 0)),
            rows(width),
            pl.BlockSpec((8, step), lambda i: (0, i)),
            rows(width),
            whole((HALF, own_width)),
        )
        + (whole(quarter.shape),) * 6,
        scratch_shapes=[
            VMEM((count, 2, pieces, unit, both), bf16),
            VMEM((hid // down_unit, down_unit, width), bf16),
            pltpu.SemaphoreType.DMA((24,)),
        ],
        compiler_params=pltpu.CompilerParams(vmem_limit_bytes=60 * 2**20),
        cost_estimate=pl.CostEstimate(
            flops=6 * total * width * count * both, bytes_accessed=26 * 2**20, transcendentals=0
        ),
        name="experts",
    )(
        normed,
        *cot_blocks,
        gates,
        gate_weight.reshape(experts, pieces, unit, hidden),
        up_weight.reshape(experts, pieces, unit, hidden),
        down_weight.reshape(-1, down_unit, own_width),
        units,
    )


def window(i, block):
    first = max(0, (i + 1) * block - 512 - block)
    return first, (i + 1) * block


def own_places(ref, out, row, half):
    for h in range(2):
        start = pl.multiple_of(half * jnp.bitwise_xor(row, h), half)
        out[h * half : (h + 1) * half] = ref[pl.ds(start, half)]


def allowed_keys(segk_ref, segq_ref, i, first, last):
    block = BLOCK
    width = last - first
    keys = lax.broadcasted_iota(jnp.int32, (width, block), 0) + first
    queries = lax.broadcasted_iota(jnp.int32, (width, block), 1) + i * block
    same = segk_ref[first:last] == segq_ref[:, i * block : (i + 1) * block]
    return (keys <= queries) & same


def attend_kernel(heads, q_ref, k_ref, v_ref, segk_ref, segq_ref, o_ref, lse_ref, q, k, vt):
    row = lax.axis_index("row")
    total = q_ref.shape[0]
    half = total // 2
    own_places(q_ref, q, row, half)
    own_places(k_ref, k, row, half)
    for h in range(2):
        start = pl.multiple_of(half * jnp.bitwise_xor(row, h), half)
        vt[:, h * half : (h + 1) * half] = v_ref[pl.ds(start, half)].astype(f32).T.astype(bf16)
    for i in range(total // BLOCK):
        first, last = window(i, BLOCK)
        here = slice(i * BLOCK, (i + 1) * BLOCK)
        allowed = allowed_keys(segk_ref, segq_ref, i, first, last)
        place = i * BLOCK // half
        start = pl.multiple_of(
            half * jnp.bitwise_xor(row, place) + (i * BLOCK - place * half), BLOCK
        )
        for h in range(heads):
            s = nt(k[first:last], q[here, h * HEAD : (h + 1) * HEAD]) * (HEAD**-0.5)
            s = jnp.where(allowed, s, MASKED)
            top = jnp.max(s, axis=0, keepdims=True)
            p = jnp.exp(s - top)
            total_p = jnp.sum(p, axis=0, keepdims=True)
            p = (p * (1.0 / total_p)).astype(bf16)
            ot = nn(vt[:, first:last], p)
            o_ref[pl.ds(start, BLOCK), h * HEAD : (h + 1) * HEAD] = ot.T.astype(bf16)
            lse_ref[h : h + 1, here] = top + jnp.log(total_p)


def attend(q, k, v, seg):
    total, width = q.shape
    heads = width // HEAD
    return pl.pallas_call(
        functools.partial(attend_kernel, heads),
        out_shape=(
            jax.ShapeDtypeStruct((total, width), bf16),
            jax.ShapeDtypeStruct((8, total), f32),
        ),
        in_specs=[WHOLE] * 5,
        out_specs=(WHOLE, WHOLE),
        scratch_shapes=[
            VMEM((total, width), bf16),
            VMEM((total, HEAD), bf16),
            VMEM((HEAD, total), bf16),
        ],
        compiler_params=pltpu.CompilerParams(vmem_limit_bytes=32 * 2**20),
        cost_estimate=pl.CostEstimate(
            flops=2 * heads * total * total * HEAD * 2,
            bytes_accessed=6 * total * width,
            transcendentals=heads * total * total,
        ),
        name="attend",
    )(q, k, v, seg.reshape(total, 1), seg.reshape(1, total))


def expert_finish_kernel(col_ref, by_x, by_z, gate_ref, up_ref, down_ref):
    ab = pl.program_id(0)
    rows = gate_ref.shape[0]
    down_rows = down_ref.shape[0]

    def write(block):
        pieces = block.shape[0]
        step, down_step = rows // pieces, down_rows // pieces
        for p in range(pieces):
            here = slice(p * step, (p + 1) * step)
            gate_ref[here] = block[p, 0, 0, 0:step].astype(f32)
            up_ref[here] = block[p, 1, 0, 0:step].astype(f32)
            here = slice(p * down_step, (p + 1) * down_step)
            for core in range(2):
                down_ref[here, core * SIDE : (core + 1) * SIDE] = block[
                    p, core, 0, step : step + down_step
                ].astype(f32)

    @pl.when(ab == 0)
    def _():
        write(by_x.at[0])

    @pl.when(ab == 1)
    def _():
        write(by_z.at[:, 0])


def expert_finish(sums, col, up_rows, down_rows):
    xs, zs, cs = dp_sizes()
    piece = sums.shape[-2]

    def half(ab, col_ref):
        return jnp.where(ab == 0, col_ref[0], 1 - col_ref[0])

    def out_spec(rows, cols):
        return pl.BlockSpec(
            (rows, cols), lambda ab, j, col_ref: (half(ab, col_ref) * xs + j, 0)
        )

    return pl.pallas_call(
        expert_finish_kernel,
        grid_spec=pltpu.PrefetchScalarGridSpec(
            num_scalar_prefetch=1,
            grid=(2, xs),
            in_specs=[
                pl.BlockSpec(
                    (1, zs, cs, 1, piece, SIDE),
                    lambda ab, j, col_ref: (jnp.where(ab == 0, j, xs - 1), 0, 0, 0, 0, 0),
                ),
                pl.BlockSpec(
                    (xs, 1, cs, 1, piece, SIDE),
                    lambda ab, j, col_ref: (0, jnp.where(ab == 0, 0, j), 0, 1, 0, 0),
                ),
            ],
            out_specs=(
                out_spec(up_rows * zs, SIDE),
                out_spec(up_rows * zs, SIDE),
                out_spec(down_rows * zs, 2 * SIDE),
            ),
        ),
        out_shape=(
            jax.ShapeDtypeStruct((2 * up_rows * xs * zs, SIDE), f32),
            jax.ShapeDtypeStruct((2 * up_rows * xs * zs, SIDE), f32),
            jax.ShapeDtypeStruct((2 * down_rows * xs * zs, 2 * SIDE), f32),
        ),
        compiler_params=pltpu.CompilerParams(vmem_limit_bytes=48 * 2**20),
        name="expert_finish",
    )(col.reshape(1), sums, sums)


def attn_finish_kernel(qkv_sums, out_sums, qkv_ref, out_ref):
    col = lax.axis_index("col")
    cores, _, pieces = qkv_sums.shape[:3]
    rows = SIDE // pieces
    cols = SIDE + 2 * HEAD
    for core in range(cores):
        kept = None
        here = slice(core * SIDE, (core + 1) * SIDE)
        for ab in range(2):
            half = col if ab == 0 else 1 - col
            block = qkv_sums[core, ab].astype(f32)[:, 0:rows].reshape(SIDE, cols)
            qkv_ref[here, at(half * SIDE, SIDE, 128)] = block[:, 0:SIDE]
            out_ref[at(half * SIDE, SIDE), here] = (
                out_sums[core, ab].astype(f32)[:, 0:rows].reshape(SIDE, SIDE)
            )
            pair = block[:, SIDE:cols]
            kept = pair if kept is None else kept + pair
        qkv_ref[here, 2 * SIDE :] = kept


def attn_finish(qkv_sums, out_sums):
    return pl.pallas_call(
        attn_finish_kernel,
        out_shape=(
            jax.ShapeDtypeStruct((2 * SIDE, 2 * SIDE + 2 * HEAD), f32),
            jax.ShapeDtypeStruct((2 * SIDE, 2 * SIDE), f32),
        ),
        in_specs=[WHOLE, WHOLE],
        out_specs=(WHOLE, WHOLE),
        compiler_params=pltpu.CompilerParams(vmem_limit_bytes=48 * 2**20),
        name="attn_finish",
    )(qkv_sums, out_sums)


def turn_tables(places):
    steps_up = jnp.arange(HEAD // 2, dtype=f32) * (2.0 / HEAD)
    inverse = jnp.exp(-math.log(ROPE_BASE) * steps_up)
    angles = places[:, None] * inverse[None, :]
    cosine, sine = jnp.cos(angles), jnp.sin(angles)
    return (
        jnp.concatenate([cosine, cosine], axis=1),
        jnp.concatenate([-sine, sine], axis=1),
    )


def local(
    tokens,
    cotangent,
    attn_gain,
    ffn_gain,
    qkv_weight,
    out_weight,
    router_weight,
    gate_weight,
    up_weight,
    down_weight,
    routes,
    segments,
):
    row = lax.axis_index("row")
    col = lax.axis_index("col")
    xs, zs, cs = dp_sizes()
    own_rows, own_width = tokens.shape
    total = 2 * own_rows
    quarter = own_rows // 2
    experts, _, hidden = gate_weight.shape
    own_experts = experts // 2
    hid = own_experts * hidden
    pieces = xs * zs

    units = swap_units(out_weight, gate_weight, up_weight, down_weight)
    units = lax.all_gather(units, "dp", axis=0, tiled=False)
    units = units.reshape((pieces, cs) + units.shape[1:])

    def own_order(v):
        return jnp.where(row == 0, v, jnp.roll(v, own_rows, axis=0))

    routes_local = own_order(routes)
    cosine, sine = turn_tables(own_order(jnp.arange(total, dtype=f32)))
    small = jnp.concatenate(
        [router_weight.T.astype(f32), attn_gain[None], ffn_gain[None]], axis=0
    )

    tokens_all, qkv_local, small_all = gather_inputs(tokens, qkv_weight, small)
    cot_own, tokens_all = lax.optimization_barrier((cotangent, tokens_all))
    cot_2 = flip(cot_own, 2)
    cot_3 = flip(cot_own, 3)
    normed_one, queries, keys, values, gates, scale_one = project(
        tokens_all, small_all, qkv_local, routes_local, cosine, sine
    )
    context, lse = attend(queries, keys, values, segments)
    cot_1a = flip(cot_3[:quarter], 2)
    cot_1b = flip(cot_2[quarter:], 3)
    context_all = gather_context(context)
    normed_two, hidden_own, scale_two, out_quarter = mix(
        context_all, tokens_all, small_all, out_weight.reshape(pieces, -1, own_width), units
    )
    (
        weighted,
        pre_grads,
        normed_two_part,
        expert_vec,
        cot_all,
        layer_own,
        o1a,
        o1b,
        o2a,
        o2b,
        o3a,
        o3b,
    ) = experts_step(
        normed_two,
        (cot_own, cot_1a, cot_1b, cot_2, cot_3),
        gates,
        gate_weight,
        up_weight,
        down_weight,
        units,
    )
    pass_3 = flip(o1a, 2)
    pass_2 = flip(o1b, 3)
    far_3b = flip(o3b, 3)
    far_2a = flip(o2a, 2)
    hidden_grad, hidden_low, vec_sums, ffn_part, shard_up, shard_down = reduce_step(
        normed_two_part,
        expert_vec,
        hidden_own,
        cotangent,
        scale_two,
        ffn_gain[None],
        normed_two,
        pre_grads,
        weighted,
        cot_all,
    )
    up_rows = own_experts * own_width // pieces
    down_rows = hid // pieces
    expert_sums = lax.all_gather(
        jnp.concatenate([shard_up[:, :up_rows], shard_down[:, :down_rows]], axis=1),
        "dp",
        axis=0,
        tiled=False,
    ).reshape(xs, zs, cs, 2, up_rows + down_rows, SIDE)
    far_3a = flip((o3a.astype(f32) + pass_3.astype(f32)).astype(bf16), 3)
    far_2b = flip((o2b.astype(f32) + pass_2.astype(f32)).astype(bf16), 2)

    layer_out = (
        hidden_own
        + layer_own
        + jnp.concatenate([far_2a, far_2b], axis=0).astype(f32)
        + jnp.concatenate([far_3a, far_3b], axis=0).astype(f32)
    ).astype(bf16)
    input_grad, small_sums, qkv_sums, out_sums = attn_back(
        queries,
        keys,
        values,
        lse,
        segments,
        cosine,
        sine,
        context,
        hidden_low,
        out_quarter,
        qkv_local,
        normed_one,
        small_all,
        gates,
        vec_sums,
        ffn_part,
        tokens,
        scale_one,
        attn_gain[None],
        hidden_grad,
    )
    router_grad = small_sums[:experts].T
    attn_gain_grad = small_sums[6]
    ffn_gain_grad = small_sums[7]
    qkv_grad, out_grad = attn_finish(qkv_sums, out_sums)
    gate_grad, up_grad, down_grad = expert_finish(expert_sums, col, up_rows, down_rows)
    gate_grad = gate_grad.reshape(experts, own_width, hidden)
    up_grad = up_grad.reshape(experts, own_width, hidden)
    down_grad = down_grad.reshape(experts, hidden, own_width)
    return (
        layer_out,
        input_grad,
        attn_gain_grad,
        ffn_gain_grad,
        qkv_grad,
        out_grad,
        router_grad,
        gate_grad,
        up_grad,
        down_grad,
    )


def solution(mesh):
    in_specs = (
        P(("dp", "row"), "col"),
        P(("dp", "row"), "col"),
        P("col"),
        P("col"),
        P("col", "row"),
        P("row", "col"),
        P("col", None),
        P(None, "col", "row"),
        P(None, "col", "row"),
        P(None, "row", "col"),
        P("dp", None),
        P("dp"),
    )
    out_specs = (
        P(("dp", "row"), "col"),
        P(("dp", "row"), "col"),
        P("col"),
        P("col"),
        P("col", "row"),
        P("row", "col"),
        P("col", None),
        P(None, "col", "row"),
        P(None, "col", "row"),
        P(None, "row", "col"),
    )
    return jax.shard_map(local, mesh=mesh, in_specs=in_specs, out_specs=out_specs, check_vma=False)
```

```python
import functools
import math

import jax
import jax.numpy as jnp
from jax import lax
from jax.experimental import pallas as pl
from jax.experimental.pallas import tpu as pltpu
from jax.sharding import PartitionSpec as P

f32 = jnp.float32
bf16 = jnp.bfloat16

HEAD = 128
GROUP_HEADS = 6
EPS = 1e-06
ROPE_BASE = 10000.0
MASKED = -1e30
BLOCK = 256


MESH = pl.DeviceIdType.MESH
VMEM = pltpu.VMEM
ANY = pl.BlockSpec(memory_space=pl.ANY)
WHOLE = pl.BlockSpec(memory_space=pltpu.VMEM)
HALF = 512
SIDE = 384


def dp_sizes():
    total = lax.axis_size("dp")
    cores = 2 if total % 2 == 0 else 1
    side = math.isqrt(total // cores)
    return side, side, cores


def dp_place():
    xs, zs, cs = dp_sizes()
    d = lax.axis_index("dp")
    return d // (zs * cs), (d // cs) % zs, d % cs


def nt(a, b):
    return lax.dot_general(a, b, (((1,), (1,)), ((), ())), preferred_element_type=f32)


def nn(a, b):
    return lax.dot_general(a, b, (((1,), (0,)), ((), ())), preferred_element_type=f32)


def tn(a, b):
    return lax.dot_general(a, b, (((0,), (0,)), ((), ())), preferred_element_type=f32)


class Links:
    def __init__(self, send, recv):
        self.send, self.recv = send, recv
        self.used = 0
        self.dp = lax.axis_index("dp")
        self.row = lax.axis_index("row")
        self.col = lax.axis_index("col")
        self.xs, self.zs, self.cs = dp_sizes()
        self.x, self.z, self.core = dp_place()

    def group(self, k):
        row = 1 - self.row if k & 2 else self.row
        col = 1 - self.col if k & 1 else self.col
        return (self.dp, row, col)

    def other_core(self):
        return (self.dp + 1 - 2 * self.core, self.row, self.col)

    def place(self, axis, k):
        x, z = self.x, self.z
        if axis == 0:
            x = (x + k) % self.xs
        else:
            z = (z + k) % self.zs
        return ((x * self.zs + z) * self.cs + self.core, self.row, self.col)

    def greet(self, devices):
        barrier = pltpu.get_barrier_semaphore()
        for device in devices:
            pl.semaphore_signal(barrier, inc=1, device_id=device, device_id_type=MESH)
        pl.semaphore_wait(barrier, len(devices))

    def plane(self):
        return (
            ([self.other_core()] if self.cs == 2 else [])
            + [self.place(0, k) for k in range(1, self.xs)]
            + [self.place(1, k) for k in range(1, self.zs)]
        )

    def copy(self, src, dst, device):
        i = self.used
        self.used += 1
        return pltpu.make_async_remote_copy(
            src_ref=src,
            dst_ref=dst,
            send_sem=self.send.at[i],
            recv_sem=self.recv.at[i],
            device_id=device,
            device_id_type=MESH,
        )

    def go(self, src, dst, device):
        copy = self.copy(src, dst, device)
        copy.start()
        return copy


def at(start, size, step=16):
    return pl.ds(pl.multiple_of(start, step), size)


class Fetch:
    def __init__(self, sems):
        self.sems = sems
        self.used = 0
        self.named = {}

    def start(self, name, *pairs):
        copies = self.named.setdefault(name, [])
        for src, dst in pairs:
            copy = pltpu.make_async_copy(src, dst, self.sems.at[self.used])
            self.used += 1
            copy.start()
            copies.append(copy)

    def wait(self, *names):
        for name in names:
            for copy in self.named.pop(name):
                copy.wait()


def pad16(n):
    return -(-n // 16) * 16


class PlaneSum:
    def __init__(self, links, part, came, in1, piece, in2, shard, peer, sums=None, local=None):
        self.links, self.part, self.came, self.in1 = links, part, came, in1
        self.piece, self.in2, self.shard, self.peer = piece, in2, shard, peer
        self.sums, self.local = sums, local
        self.sizes = (links.xs, links.zs)
        self.places = (links.x, links.z)
        self.sent = []
        self.first, self.second, self.core = {}, {}, {}
        rows = came.shape[1]
        self.rows1 = rows // links.xs
        self.rows2 = self.rows1 // links.zs
        self.home, self.spread1, self.spread2 = {}, {}, {}

    def start(self):
        kept, rows = self.rows2, self.piece.shape[2]
        if kept < rows:
            shape = self.piece.shape
            self.piece[:, :, kept:] = jnp.zeros(shape[:2] + (rows - kept, shape[3]), bf16)

    def core_send(self, ab, rows=None):
        if self.links.cs == 1:
            return
        src, dst = self.part(ab, 1 - self.links.core), self.came.at[ab]
        if rows is not None:
            src, dst = src.at[rows], dst.at[rows]
        copy = self.links.go(src, dst, self.links.other_core())
        self.core.setdefault(ab, []).append(copy)
        self.sent.append(copy)

    def first_send(self, ab):
        for copy in self.core.get(ab, []):
            copy.wait_recv()
        mine, total = self.part(ab, self.links.core), self.came.at[ab]
        rows = total.shape[0]
        step = 96

        @pl.loop(0, rows // step)
        def _(i):
            here = at(i * step, step)
            total[here] = (total[here].astype(f32) + mine[here].astype(f32)).astype(bf16)

        n, place = self.sizes[ab], self.places[ab]
        for k in range(1, n):
            j = (place + k) % n
            copy = self.links.go(
                self.came.at[ab, at(j * self.rows1, self.rows1)],
                self.in1.at[ab, k - 1],
                self.links.place(ab, k),
            )
            self.first[ab, k] = copy
            self.sent.append(copy)

    def second_send(self, ab):
        n, place = self.sizes[ab], self.places[ab]
        for k in range(1, n):
            self.first[ab, k].wait_recv()
        rows, piece = self.rows1, self.rows2
        if piece % 16 == 0:

            @pl.loop(0, rows // piece)
            def _(j):
                own = self.came[ab, at(place * rows + j * piece, piece)].astype(f32)
                for k in range(1, n):
                    own = own + self.in1[ab, k - 1, at(j * piece, piece)].astype(f32)
                self.piece[ab, j, 0:piece] = own.astype(bf16)

        else:
            own = self.came[ab, at(place * rows, rows)].astype(f32)
            for k in range(1, n):
                own = own + self.in1[ab, k - 1].astype(f32)
            for j in range(rows // piece):
                self.piece[ab, j, 0:piece] = own[j * piece : (j + 1) * piece].astype(bf16)
        n, place = self.sizes[1 - ab], self.places[1 - ab]
        for k in range(1, n):
            j = (place + k) % n
            copy = self.links.go(
                self.piece.at[ab, j], self.in2.at[ab, k - 1], self.links.place(1 - ab, k)
            )
            self.second[ab, k] = copy
            self.sent.append(copy)

    def last_sum(self, ab):
        n, place = self.sizes[1 - ab], self.places[1 - ab]
        value = self.piece[ab, place].astype(f32)
        for k in range(1, n):
            self.second[ab, k].wait_recv()
            value = value + self.in2[ab, k - 1].astype(f32)
        if ab == 0:
            self.shard[0] = value.astype(bf16)
        else:
            self.peer[...] = value.astype(bf16)
            self.swap = self.links.go(self.peer, self.shard.at[1], self.links.group(1))

    def gather_near(self, ab):
        links = self.links
        if ab == 1:
            self.swap.wait()
        x, z = links.x, links.z
        index = (x * links.zs + z) if ab == 0 else (z * links.xs + x)
        here = self.sums.at[links.core, ab, index]
        copy = pltpu.make_async_copy(self.shard.at[ab], here, self.local.at[ab])
        copy.start()
        self.home[ab] = copy
        self.spread1[ab] = [
            links.go(self.shard.at[ab], here, links.place(1 - ab, k))
            for k in range(1, self.sizes[1 - ab])
        ]

    def gather_far(self, ab):
        links = self.links
        for copy in self.spread1[ab]:
            copy.wait()
        self.home[ab].wait()
        n = self.sizes[1 - ab]
        first = (links.x if ab == 0 else links.z) * n
        block = self.sums.at[links.core, ab, pl.ds(first, n)]
        self.spread2[ab] = [
            links.go(block, block, links.place(ab, k)) for k in range(1, self.sizes[ab])
        ]

    def gather_core(self):
        links = self.links
        for ab in range(2):
            for copy in self.spread2[ab]:
                copy.wait()
        if links.cs == 2:
            block = self.sums.at[links.core]
            self.last = links.go(block, block, links.other_core())

    def done(self):
        for copy in self.sent:
            copy.wait_send()
        if self.sums is None:
            self.swap.wait()
        elif self.links.cs == 2:
            self.last.wait()


def plane_scratch(rows, width):
    xs, zs, _ = dp_sizes()
    n1, n2 = max(xs - 1, 1), max(zs - 1, 1)
    pad = pad16(rows // (xs * zs))
    return [
        VMEM((2, rows, width), bf16),
        VMEM((2, n1, rows // xs, width), bf16),
        VMEM((2, zs, pad, width), bf16),
        VMEM((2, n2, pad, width), bf16),
        VMEM((pad, width), bf16),
    ]


def gather_group(links, own, dst):
    first = {}
    for k, order in ((2, (1, 0)), (3, (0, 1))):
        for h in order:
            first[k, h] = links.copy(own(h), dst(k, h), links.group(k))
    for key in ((2, 1), (3, 0), (2, 0), (3, 1)):
        first[key].start()
    relay = [
        links.copy(dst(3, 0), dst(1, 0), links.group(2)),
        links.copy(dst(2, 1), dst(1, 1), links.group(3)),
    ]

    def forward():
        first[3, 0].wait_recv()
        relay[0].start()
        first[2, 1].wait_recv()
        relay[1].start()

    def near():
        first[2, 0].wait_recv()
        first[3, 1].wait_recv()

    def far():
        for copy in relay:
            copy.wait_recv()

    def sent():
        for copy in list(first.values()) + relay:
            copy.wait_send()

    return forward, near, far, sent


def unit_rows():
    xs, zs, _ = dp_sizes()
    return 768 // (xs * zs), min(SIDE, 768 // (xs * zs))


def down_units(hid):
    xs, zs, _ = dp_sizes()
    return -(-(hid // unit_rows()[1]) // (xs * zs))


class Units:
    def __init__(self, links, units, out_weight, gate_weight, up_weight, down_weight):
        self.links, self.units = links, units
        rows, down_rows = unit_rows()
        xs, zs = links.xs, links.zs
        pieces = xs * zs
        place = links.x * zs + links.z
        lanes = at(links.core * SIDE, SIDE, 128)
        home = units.at[links.core, links.x, links.z]
        self.out_rows = 3 * rows
        self.cut = 4 * rows
        self.total = units.shape[3]
        self.fetch = []
        for k in (1, 2, 3):
            col = 1 - links.col if k & 1 else links.col
            index = (place + col * (pieces // 2)) % pieces
            self.fetch.append(
                links.go(
                    out_weight.at[index, :, lanes],
                    home.at[(k - 1) * rows : k * rows],
                    links.group(k),
                )
            )
        count = gate_weight.shape[0] // 2
        first = (1 - links.col) * count
        for e in range(count):
            i = links.used
            links.used += 1
            to = home.at[(3 + e) * rows : (4 + e) * rows]
            either = [
                pltpu.make_async_remote_copy(
                    src_ref=weight.at[first + e, place],
                    dst_ref=to,
                    send_sem=links.send.at[i],
                    recv_sem=links.recv.at[i],
                    device_id=links.group(1),
                    device_id_type=MESH,
                )
                for weight in (gate_weight, up_weight)
            ]
            for which in range(2):

                @pl.when(links.core == which)
                def _(copy=either[which]):
                    copy.start()

            self.fetch.append(either[0])
        blocks = down_weight.shape[0] // 2
        for j in range(down_units(blocks * down_rows)):
            index = jnp.minimum(j * pieces + place, blocks - 1)
            start = (3 + count) * rows + j * down_rows
            self.fetch.append(
                links.go(
                    down_weight.at[(1 - links.col) * blocks + index, :, lanes],
                    home.at[start : start + down_rows],
                    links.group(1),
                )
            )

    def near(self):
        for copy in self.fetch:
            copy.wait()
        links = self.links
        home = self.units.at[links.core, links.x, links.z]
        self.first = []
        for rows, axis, n in (
            (slice(0, self.cut), 1, links.zs),
            (slice(self.cut, self.total), 0, links.xs),
        ):
            for k in range(1, n):
                self.first.append(links.go(home.at[rows], home.at[rows], links.place(axis, k)))

    def far(self):
        for copy in self.first:
            copy.wait()
        links, units = self.links, self.units
        self.second = []
        line = units.at[links.core, links.x, :, 0 : self.cut]
        for k in range(1, links.xs):
            self.second.append(links.go(line, line, links.place(0, k)))
        line = units.at[links.core, :, links.z, self.cut : self.total]
        for k in range(1, links.zs):
            self.second.append(links.go(line, line, links.place(1, k)))

    def swap(self):
        for copy in self.second:
            copy.wait()
        links = self.links
        self.last = []
        for rows in (slice(0, self.out_rows), slice(self.out_rows, self.total)):
            block = self.units.at[links.core, :, :, rows]
            self.last.append(links.go(block, block, links.other_core()))

    def wait_out(self):
        self.last[0].wait()

    def done(self):
        self.last[1].wait()


def forward_kernel(
    heads,
    tokens,
    cot_h,
    qkv_weight,
    small,
    routes,
    cosine,
    sine,
    segk_ref,
    segq_ref,
    out_weight,
    gate_weight,
    up_weight,
    down_weight,
    normed_h,
    q_h,
    k_h,
    v_h,
    context_h,
    qkv_h,
    normed_two_h,
    quarter_h,
    cot_2,
    cot_3,
    units,
    lse,
    gates_ref,
    scale_one,
    small_all,
    hidden_own,
    scale_two,
    tokens_all,
    qkv_all,
    normed,
    q,
    k,
    v,
    vt,
    contexts,
    weight,
    hidden,
    normed_two,
    send,
    recv,
    sems,
):
    links = Links(send, recv)
    row, col = links.row, links.col
    zs, cs = links.zs, links.cs
    total, full = normed.shape
    width = full // 2
    quarter = HALF // 2
    links.greet([links.group(k) for k in (1, 2, 3)] + links.plane())

    def own(h):
        return tokens.at[h * quarter : (h + 1) * quarter]

    def dst(k, h):
        rows = (HALF if k & 2 else 0) + h * quarter
        return tokens_all.at[rows : rows + quarter, (k & 1) * width : (k & 1) * width + width]

    share = width // (cs * zs)
    start = links.core * (width // cs) + links.z * share
    there = at(width + start, share)
    fetch_qkv = [
        links.go(
            qkv_weight.at[at(start, share), at((1 - col) * SIDE, SIDE, 128)],
            qkv_all.at[there, 0:SIDE],
            links.group(1),
        ),
        links.go(
            qkv_weight.at[at(start, share), 2 * SIDE :], qkv_all.at[there, SIDE:], links.group(1)
        ),
        links.go(small, small_all.at[:, width:], links.group(1)),
    ]
    forward, near, far, tokens_sent = gather_group(links, own, dst)
    shares = Units(links, units, out_weight, gate_weight, up_weight, down_weight)
    fetch = Fetch(sems)
    pieces = weight.shape[1]
    half = pieces // 2
    fetch.start(
        "weight",
        *[
            (
                out_weight.at[pl.ds((col if h == 0 else 1 - col) * half, half)],
                weight.at[0, h * half : (h + 1) * half, :, 0:width],
            )
            for h in range(2)
        ],
    )
    tokens_all[0:HALF, 0:width] = tokens[...]
    qkv_all[0:width, 0:SIDE] = qkv_weight[:, at(col * SIDE, SIDE, 128)]
    qkv_all[0:width, SIDE:] = qkv_weight[:, 2 * SIDE :]
    small_all[:, 0:width] = small[...]
    for copy in fetch_qkv:
        copy.wait()
    spread = [
        links.go(qkv_all.at[there], qkv_all.at[there], links.place(1, k)) for k in range(1, zs)
    ]
    forward()
    shares.near()
    for copy in spread:
        copy.wait()
    if cs == 2:
        block = qkv_all.at[at(width + links.core * (width // 2), width // 2)]
        swap_qkv = links.go(block, block, links.other_core())
        swap_qkv.wait()
    near()

    def project(i):
        rows = slice(i * BLOCK, (i + 1) * BLOCK)
        place = i * BLOCK // HALF
        here = at(
            HALF * jnp.bitwise_xor(row, place) + (i * BLOCK - place * HALF), BLOCK, BLOCK
        )
        x = tokens_all[rows].astype(f32)
        scale = lax.rsqrt(jnp.sum(x * x, axis=1, keepdims=True) * (1.0 / full) + EPS)
        low = (x * scale * small_all[6:7, :]).astype(bf16)
        normed[rows] = low
        scale_one[rows] = jnp.broadcast_to(scale, (BLOCK, 128))
        router = jnp.concatenate([small_all[...], jnp.zeros((120, full), f32)], axis=0)
        logits = nt(low, router.astype(bf16))
        lanes = lax.broadcasted_iota(jnp.int32, (BLOCK, 128), 1)
        chosen = lanes == routes[rows, 0:1]
        for j in range(1, routes.shape[1]):
            chosen = chosen | (lanes == routes[rows, j : j + 1])
        masked = jnp.where(chosen, logits, MASKED)
        raised = jnp.exp(masked - jnp.max(masked, axis=1, keepdims=True))
        raised = jnp.where(chosen, raised, 0.0)
        gates_ref[rows] = raised / jnp.sum(raised, axis=1, keepdims=True)
        projected = nn(low, qkv_all[...])
        for h in range(heads + 1):
            part = projected[:, h * HEAD : (h + 1) * HEAD]
            turned = (part * cosine[rows] + swap_halves(part) * sine[rows]).astype(bf16)
            if h < heads:
                q[here, h * HEAD : (h + 1) * HEAD] = turned
            else:
                k[here] = turned
        v[here] = projected[:, (heads + 1) * HEAD :].astype(bf16)

    project(2)
    project(3)
    far()
    cot_copies = [
        links.go(
            cot_h.at[h * quarter : (h + 1) * quarter],
            out.at[h * quarter : (h + 1) * quarter],
            links.group(k),
        )
        for k, out, h in ((2, cot_2, 1), (3, cot_3, 0), (2, cot_2, 0), (3, cot_3, 1))
    ]
    project(0)
    project(1)
    shares.far()
    fetch.start("out", (normed, normed_h), (q, q_h), (k, k_h), (v, v_h), (qkv_all, qkv_h))

    vt[...] = v[...].astype(f32).T.astype(bf16)

    def block(j, h, head):
        first = j * SIDE + head * HEAD
        return contexts.at[h * HALF : (h + 1) * HALF, first : first + HEAD]

    sends, relays = {}, []
    for head in range(heads):
        cols = slice(head * HEAD, (head + 1) * HEAD)
        for i in range(total // BLOCK):
            first, last = window(i, BLOCK)
            here = slice(i * BLOCK, (i + 1) * BLOCK)
            allowed = allowed_keys(segk_ref, segq_ref, i, first, last)
            place = i * BLOCK // HALF
            rows = at(
                HALF * jnp.bitwise_xor(row, place) + (i * BLOCK - place * HALF), BLOCK, BLOCK
            )
            s = nt(k[first:last], q[here, cols]) * (HEAD**-0.5)
            s = jnp.where(allowed, s, MASKED)
            top = jnp.max(s, axis=0, keepdims=True)
            p = jnp.exp(s - top)
            total_p = jnp.sum(p, axis=0, keepdims=True)
            p = (p * (1.0 / total_p)).astype(bf16)
            ot = nn(vt[:, first:last], p)
            contexts[rows, cols] = ot.T.astype(bf16)
            lse[head : head + 1, here] = top + jnp.log(total_p)
        for j, h in ((2, 0), (3, 1), (2, 1), (3, 0)):
            sends[j, 1 - h, head] = links.go(
                block(0, h, head), block(j, 1 - h, head), links.group(j)
            )
    lse[heads:, :] = jnp.zeros((8 - heads, total), f32)
    fetch.start("context", (contexts.at[:, 0:SIDE], context_h))
    shares.swap()
    for head in range(heads):
        sends[3, 0, head].wait_recv()
        relays.append(links.go(block(3, 0, head), block(1, 1, head), links.group(2)))
        sends[2, 1, head].wait_recv()
        relays.append(links.go(block(2, 1, head), block(1, 0, head), links.group(3)))

    shares.wait_out()
    rows = weight.shape[2]
    for j in (1, 2, 3):
        for core in range(2):
            first = (j & 1) * width + core * SIDE
            fetch.start(
                "weight",
                *[
                    (
                        units.at[core, x, :, (j - 1) * rows : j * rows],
                        weight.at[j // 2, x * zs : (x + 1) * zs, :, first : first + SIDE],
                    )
                    for x in range(links.xs)
                ],
            )
    for head in range(heads):
        sends[2, 0, head].wait_recv()
        sends[3, 1, head].wait_recv()
    fetch.wait("weight")
    w_own = weight[0, 0:half].reshape(SIDE, full)
    w_far = weight[1].reshape(width, full)
    fetch.start("quarter", (weight.at[0, 0:half], quarter_h))
    for i in range(2):
        rows = slice(i * HALF, (i + 1) * HALF)
        hidden[rows] = (
            tokens_all[rows].astype(f32)
            + nn(contexts[rows, 0:SIDE], w_own)
            + nn(contexts[rows, 2 * SIDE :], w_far)
        )
    for copy in relays:
        copy.wait_recv()
    w_peer = weight[0, half:].reshape(SIDE, full)
    for i in range(2):
        rows = slice(i * HALF, (i + 1) * HALF)
        value = hidden[rows] + nn(contexts[rows, SIDE : 2 * SIDE], w_peer)
        scale = lax.rsqrt(jnp.sum(value * value, axis=1, keepdims=True) * (1.0 / full) + EPS)
        normed_two[rows] = (value * scale * small_all[7:8, :]).astype(bf16)
        scale_two[rows] = jnp.broadcast_to(scale, (HALF, 128))
        if i == 0:
            hidden_own[...] = value[:, 0:width]
        fetch.start("out", (normed_two.at[rows], normed_two_h.at[rows]))
    tokens_sent()
    for copy in relays + list(sends.values()):
        copy.wait_send()
    for copy in cot_copies:
        copy.wait()
    shares.done()
    fetch.wait("out", "context", "quarter")


def forward_step(
    tokens,
    cot,
    qkv_weight,
    small,
    routes,
    cosine,
    sine,
    seg,
    out_weight,
    gate_weight,
    up_weight,
    down_weight,
):
    xs, zs, cs = dp_sizes()
    pieces = xs * zs
    rows, down_rows = unit_rows()
    width = tokens.shape[1]
    full, total = 2 * width, 2 * HALF
    heads = SIDE // HEAD
    experts, _, hidden = gate_weight.shape
    hid = experts // 2 * hidden
    unit_total = (3 + experts // 2) * rows + down_units(hid) * down_rows
    out = [
        jax.ShapeDtypeStruct((total, full), bf16),
        jax.ShapeDtypeStruct((total, SIDE), bf16),
        jax.ShapeDtypeStruct((total, HEAD), bf16),
        jax.ShapeDtypeStruct((total, HEAD), bf16),
        jax.ShapeDtypeStruct((total, SIDE), bf16),
        jax.ShapeDtypeStruct((full, SIDE + 2 * HEAD), bf16),
        jax.ShapeDtypeStruct((total, full), bf16),
        jax.ShapeDtypeStruct((pieces // 2, rows, full), bf16),
        jax.ShapeDtypeStruct((HALF, width), bf16),
        jax.ShapeDtypeStruct((HALF, width), bf16),
        jax.ShapeDtypeStruct((cs, xs, zs, unit_total, SIDE), bf16),
        jax.ShapeDtypeStruct((8, total), f32),
        jax.ShapeDtypeStruct((total, 128), f32),
        jax.ShapeDtypeStruct((total, 128), f32),
        jax.ShapeDtypeStruct((8, full), f32),
        jax.ShapeDtypeStruct((HALF, width), f32),
        jax.ShapeDtypeStruct((total, 128), f32),
    ]
    return pl.pallas_call(
        functools.partial(forward_kernel, heads),
        out_shape=tuple(out),
        in_specs=[WHOLE, ANY] + [WHOLE] * 7 + [ANY] * 4,
        out_specs=(ANY,) * 11 + (WHOLE,) * 6,
        scratch_shapes=[
            VMEM((total, full), bf16),
            VMEM((full, SIDE + 2 * HEAD), bf16),
            VMEM((total, full), bf16),
            VMEM((total, SIDE), bf16),
            VMEM((total, HEAD), bf16),
            VMEM((total, HEAD), bf16),
            VMEM((HEAD, total), bf16),
            VMEM((total, full), bf16),
            VMEM((2, pieces, rows, full), bf16),
            VMEM((total, full), f32),
            VMEM((total, full), bf16),
            pltpu.SemaphoreType.DMA((80,)),
            pltpu.SemaphoreType.DMA((80,)),
            pltpu.SemaphoreType.DMA((48,)),
        ],
        compiler_params=pltpu.CompilerParams(
            collective_id=0, has_side_effects=True, vmem_limit_bytes=60 * 2**20
        ),
        name="forward_step",
    )(
        tokens,
        cot,
        qkv_weight,
        small,
        routes,
        cosine,
        sine,
        seg.reshape(total, 1),
        seg.reshape(1, total),
        out_weight.reshape(pieces, rows, width),
        gate_weight.reshape(experts, pieces, rows, hidden),
        up_weight.reshape(experts, pieces, rows, hidden),
        down_weight.reshape(-1, down_rows, width),
    )


def scatter_group(links, blocks, mine, pass2, pass3, near2, near3, far2, far3, out2, out3):
    quarter = HALF // 2
    n2, n3 = links.group(2), links.group(3)
    start, direct = [], []

    def send_own_rows():
        start.append(links.go(blocks(1, 0), near2, n2))
        start.append(links.go(blocks(1, 1), near3, n3))

    def send_other_rows():
        direct.append(links.go(blocks(3, 1), far3.at[quarter:], n3))
        direct.append(links.go(blocks(2, 0), far2.at[0:quarter], n2))

    relay = [
        links.copy(out3, far3.at[0:quarter], n3),
        links.copy(out2, far2.at[quarter:], n2),
    ]

    def forward():
        start[0].wait_recv()
        out3[...] = (pass3[...].astype(f32) + near2[...].astype(f32)).astype(bf16)
        relay[0].start()
        start[1].wait_recv()
        out2[...] = (pass2[...].astype(f32) + near3[...].astype(f32)).astype(bf16)
        relay[1].start()

    def finish():
        for copy in direct + relay:
            copy.wait_recv()

    def total(rows):
        return mine[rows].astype(f32) + far2[rows].astype(f32) + far3[rows].astype(f32)

    def sent():
        for copy in start + direct + relay:
            copy.wait_send()

    return send_own_rows, send_other_rows, forward, finish, total, sent


def group_scratch(width):
    quarter = HALF // 2
    return [
        VMEM((quarter, width), bf16),
        VMEM((quarter, width), bf16),
        VMEM((HALF, width), bf16),
        VMEM((HALF, width), bf16),
        VMEM((quarter, width), bf16),
        VMEM((quarter, width), bf16),
    ]


def norm_back_rows(grad, gain, values, scale, inner, width):
    return scale * (grad * gain - values * (scale * inner * (1.0 / width)))


def column(row_vector):
    return jnp.broadcast_to(row_vector, (128, row_vector.shape[1])).T


def half_swap(v):
    return jnp.concatenate([v[:, HALF:], v[:, :HALF]], axis=1)


def reduce_kernel(
    partial,
    vectors,
    hidden_h,
    cot_h,
    scale_h,
    gain,
    normed_h,
    grads_h,
    weighted_h,
    cot_all_h,
    hidden_grad,
    hidden_low,
    vector_sums,
    gain_part,
    shard_up,
    shard_down,
    hidden,
    cot,
    scale,
    normed,
    grads,
    weighted,
    cot_all,
    normed_t,
    mine_p,
    pass2,
    pass3,
    near2,
    near3,
    far2,
    far3,
    out2,
    out3,
    vec_in,
    low,
    up_part,
    down_part,
    *rest,
):
    up_scratch, down_scratch = rest[0:5], rest[5:10]
    send, recv, sems, local = rest[10:]
    links = Links(send, recv)
    width = hidden_grad.shape[1]
    quarter = HALF // 2
    count, _, both = grads.shape
    side = both // 2
    fetch = Fetch(sems)
    fetch.start("normed", (normed_h, normed))
    fetch.start("grads", *[(grads_h.at[e], grads.at[e]) for e in range(count)])
    fetch.start("down", (weighted_h, weighted), (cot_all_h, cot_all))
    fetch.start(
        "pass",
        (partial.at[HALF + quarter :, 0:width], pass2),
        (partial.at[HALF : HALF + quarter, width:], pass3),
    )
    fetch.start(
        "own",
        (partial.at[0:HALF, 0:width], mine_p),
        (hidden_h, hidden),
        (cot_h, cot),
        (scale_h.at[0:HALF], scale),
    )
    links.greet([links.group(k) for k in (1, 2, 3)] + links.plane())

    def blocks(k, h):
        first = (HALF if k & 2 else 0) + h * quarter
        cols = slice((k & 1) * width, (k & 1) * width + width)
        return partial.at[first : first + quarter, cols]

    own_rows, other_rows, forward, finish, total, sent = scatter_group(
        links, blocks, mine_p, pass2, pass3, near2, near3, far2, far3, out2, out3
    )
    own_rows()
    other_rows()
    vec_copies = [links.go(vectors, vec_in.at[k - 1], links.group(k)) for k in (1, 2, 3)]

    up = PlaneSum(
        links, lambda ab, core: up_part.at[core, ab], *up_scratch[:4], shard_up, up_scratch[4]
    )
    down = PlaneSum(
        links,
        lambda ab, core: down_part.at[core, ab],
        *down_scratch[:4],
        shard_down,
        down_scratch[4],
    )
    up.start()
    down.start()
    fetch.wait("normed")
    for i in range(4):
        rows = slice(i * 256, (i + 1) * 256)
        normed_t[:, rows] = normed[rows].T
    fetch.wait("grads")
    for e in range(count):
        rows = slice(e * width, (e + 1) * width)
        for ab in range(2):
            part = nn(normed_t[ab * width : (ab + 1) * width], grads[e])
            for which in range(2):
                up_part[which, ab, rows] = part[:, which * side : (which + 1) * side].astype(
                    bf16
                )
            up.core_send(ab, rows)
        if e == 0:
            fetch.wait("down", "pass")
        rows = slice(e * side, (e + 1) * side)
        part = tn(weighted[:, rows], cot_all[...])
        for ab in range(2):
            for which in range(2):
                first = ab * width + which * side
                down_part[which, ab, rows] = part[:, first : first + side].astype(bf16)
            down.core_send(ab, rows)
        if e == 1:
            forward()
    for ab in range(2):
        up.first_send(ab)
        down.first_send(ab)

    for copy in vec_copies:
        copy.wait()
    vec = vectors[...] + vec_in[0] + half_swap(vec_in[1] + vec_in[2])
    vector_sums[...] = vec
    fetch.wait("own")
    inner = column(vec[6:7, 0:HALF])[:, 0:1]
    part = jnp.zeros((8, width), f32)
    finish()
    for h in range(4):
        rows = slice(h * 128, (h + 1) * 128)
        grad = total(rows)
        values = hidden[rows]
        scale_rows = scale[rows, 0:1]
        back = norm_back_rows(grad, gain[0:1, :], values, scale_rows, inner[rows], 2 * width)
        back = back + cot[rows].astype(f32)
        hidden_grad[rows] = back
        low[rows] = back.astype(bf16)
        part = part + jnp.sum((grad * values * scale_rows).reshape(16, 8, width), axis=0)
    gain_part[...] = jnp.broadcast_to(jnp.sum(part, axis=0, keepdims=True), (8, width))

    def own(h):
        return low.at[h * quarter : (h + 1) * quarter]

    def dst(k, h):
        rows = (HALF if k & 2 else 0) + h * quarter
        return hidden_low.at[rows : rows + quarter, (k & 1) * width : (k & 1) * width + width]

    mine = pltpu.make_async_copy(low, hidden_low.at[0:HALF, 0:width], local)
    mine.start()
    forward_low, near_low, far_low, low_sent = gather_group(links, own, dst)
    forward_low()
    for ab in range(2):
        up.second_send(ab)
        down.second_send(ab)
    for ab in (1, 0):
        up.last_sum(ab)
        down.last_sum(ab)
    mine.wait()
    near_low()
    far_low()
    low_sent()
    sent()
    up.done()
    down.done()


def reduce_step(
    partial, vectors, hidden, cot, scale, gain, normed, grads, weighted, cot_all
):
    xs, zs, _ = dp_sizes()
    width = hidden.shape[1]
    count, total, both = grads.shape
    side = both // 2
    up_rows, down_rows = count * width, count * side
    quarter = HALF // 2
    return pl.pallas_call(
        reduce_kernel,
        out_shape=(
            jax.ShapeDtypeStruct((HALF, width), f32),
            jax.ShapeDtypeStruct((2 * HALF, 2 * width), bf16),
            jax.ShapeDtypeStruct(vectors.shape, f32),
            jax.ShapeDtypeStruct((8, width), f32),
            jax.ShapeDtypeStruct((2, pad16(up_rows // (xs * zs)), side), bf16),
            jax.ShapeDtypeStruct((2, pad16(down_rows // (xs * zs)), side), bf16),
        ),
        in_specs=[ANY, WHOLE, ANY, ANY, ANY, WHOLE, ANY, ANY, ANY, ANY],
        out_specs=(WHOLE, ANY, WHOLE, WHOLE, WHOLE, WHOLE),
        scratch_shapes=[
            VMEM((HALF, width), f32),
            VMEM((HALF, width), bf16),
            VMEM((HALF, 128), f32),
            VMEM(normed.shape, bf16),
            VMEM(grads.shape, bf16),
            VMEM(weighted.shape, bf16),
            VMEM(cot_all.shape, bf16),
            VMEM((2 * width, total), bf16),
            VMEM((HALF, width), bf16),
            VMEM((quarter, width), bf16),
            VMEM((quarter, width), bf16),
        ]
        + group_scratch(width)
        + [
            VMEM((3,) + vectors.shape, f32),
            VMEM((HALF, width), bf16),
            VMEM((2, 2, up_rows, side), bf16),
            VMEM((2, 2, down_rows, side), bf16),
        ]
        + plane_scratch(up_rows, side)
        + plane_scratch(down_rows, side)
        + [
            pltpu.SemaphoreType.DMA((64,)),
            pltpu.SemaphoreType.DMA((64,)),
            pltpu.SemaphoreType.DMA((16,)),
            pltpu.SemaphoreType.DMA,
        ],
        compiler_params=pltpu.CompilerParams(
            collective_id=2, has_side_effects=True, vmem_limit_bytes=60 * 2**20
        ),
        name="reduce_step",
    )(partial, vectors, hidden, cot, scale, gain, normed, grads, weighted, cot_all)


def attn_back_kernel(
    heads,
    q_h,
    k_h,
    v_h,
    lse,
    segk_ref,
    segq_ref,
    cos_h,
    sin_h,
    context_h,
    hidden_low_h,
    out_weight,
    qkv_h,
    normed_h,
    small_all,
    gates,
    vec_sums,
    ffn_part,
    tokens_h,
    scale_h,
    gain,
    hidden_grad_h,
    layer_h,
    hidden_h,
    input_grad,
    layer_out,
    small_out,
    qkv_sums,
    out_sums,
    q,
    k,
    v,
    cos_ref,
    sin_ref,
    context,
    hidden_low,
    qkv,
    normed,
    tokens,
    scale,
    hidden_grad,
    kt,
    do,
    dk,
    dv,
    grads,
    partial,
    qkv_part,
    out_part,
    near2,
    near3,
    far2,
    far3,
    out2,
    out3,
    layer_mine,
    layer_pass2,
    layer_pass3,
    hidden,
    lnear2,
    lnear3,
    lfar2,
    lfar3,
    lout2,
    lout3,
    vec_own,
    vec_in,
    small,
    small_own,
    small_in,
    qkv_shard,
    out_shard,
    *rest,
):
    qkv_scratch, out_scratch = rest[0:5], rest[5:10]
    send, recv, sems, local = rest[10:]
    links = Links(send, recv)
    xs, zs, cs = links.xs, links.zs, links.cs
    row = links.row
    total, full = normed.shape
    width = full // 2
    quarter = HALF // 2
    head_scale = HEAD**-0.5
    fetch = Fetch(sems)
    fetch.start("out", (context_h, context), (hidden_low_h, hidden_low))
    fetch.start("attention", (q_h, q), (k_h, k), (v_h, v))
    fetch.start("turn", (cos_h, cos_ref), (sin_h, sin_ref))
    fetch.start("normed", (normed_h, normed))
    fetch.start("qkv", (qkv_h, qkv))
    fetch.start(
        "own",
        (tokens_h, tokens),
        (scale_h.at[0:HALF], scale),
        (hidden_grad_h, hidden_grad),
    )
    fetch.start(
        "layer",
        (layer_h.at[0:HALF, 0:width], layer_mine),
        (layer_h.at[HALF + quarter :, 0:width], layer_pass2),
        (layer_h.at[HALF : HALF + quarter, width:], layer_pass3),
        (hidden_h, hidden),
    )
    links.greet([links.group(k) for k in (1, 2, 3)] + links.plane())

    def layer_blocks(k, h):
        first = (HALF if k & 2 else 0) + h * quarter
        cols = slice((k & 1) * width, (k & 1) * width + width)
        return layer_h.at[first : first + quarter, cols]

    layer_own, layer_other, layer_forward, layer_finish, layer_total, layer_sent = scatter_group(
        links,
        layer_blocks,
        layer_mine,
        layer_pass2,
        layer_pass3,
        lnear2,
        lnear3,
        lfar2,
        lfar3,
        lout2,
        lout3,
    )
    layer_own()
    layer_other()

    out_sum = PlaneSum(
        links,
        lambda ab, core: out_part.at[:, at(ab * width + core * SIDE, SIDE, 128)],
        *out_scratch[:4],
        out_shard,
        out_scratch[4],
        out_sums,
        local.at[0],
    )
    qkv_sum = PlaneSum(
        links,
        lambda ab, core: qkv_part.at[at(ab * width + core * SIDE, SIDE)],
        *qkv_scratch[:4],
        qkv_shard,
        qkv_scratch[4],
        qkv_sums,
        local.at[1],
    )
    out_sum.start()
    qkv_sum.start()
    fetch.wait("out")
    out_part[...] = tn(context[...], hidden_low[...]).astype(bf16)
    for ab in range(2):
        out_sum.core_send(ab)

    for h in range(2):
        rows = at(HALF * jnp.bitwise_xor(row, h), HALF)
        do[h * HALF : (h + 1) * HALF] = nt(hidden_low[rows], out_weight[...]).astype(bf16)
    fetch.wait("attention", "turn")
    kt[...] = k[...].astype(f32).T.astype(bf16)
    dk[...] = jnp.zeros_like(dk)
    dv[...] = jnp.zeros_like(dv)

    def back(grad, rows):
        return grad * cos_ref[rows] - swap_halves(grad) * sin_ref[rows]

    def rows_of(i):
        place = i * BLOCK // HALF
        return at(HALF * jnp.bitwise_xor(row, place) + (i * BLOCK - place * HALF), BLOCK, BLOCK)

    inners = []
    for i in range(total // BLOCK):
        first, last = window(i, BLOCK)
        here = slice(i * BLOCK, (i + 1) * BLOCK)
        allowed = allowed_keys(segk_ref, segq_ref, i, first, last)
        rows = rows_of(i)
        inner_q = jnp.zeros((BLOCK, 1), f32)
        for h in range(heads):
            cols = slice(h * HEAD, (h + 1) * HEAD)
            s = nt(k[first:last], q[here, cols]) * head_scale
            s = jnp.where(allowed, s, MASKED)
            p = jnp.exp(s - lse[h : h + 1, here])
            dp = nt(v[first:last], do[here, cols])
            inner = jnp.sum(dp * p, axis=0, keepdims=True)
            ds = (p * (dp - inner)).astype(bf16)
            dq = (nn(kt[:, first:last], ds) * head_scale).T
            inner_q = inner_q + jnp.sum(dq * q[here, cols].astype(f32), axis=1, keepdims=True)
            grads[rows, cols] = back(dq, rows).astype(bf16)
            dk[first:last] += nn(ds, q[here, cols]) * head_scale
            dv[first:last] += nn(p.astype(bf16), do[here, cols])
        inners.append(inner_q)
        if i == 1:
            for ab in range(2):
                out_sum.first_send(ab)
            fetch.wait("layer")
            layer_forward()
    for ab in range(2):
        out_sum.second_send(ab)

    gate_rows = gates[...].T[0:8, :]
    sums = vec_sums[...]
    mask = lax.broadcasted_iota(jnp.int32, sums.shape, 0) < 6
    sums = jnp.where(mask, sums, 0.0)
    logits_grad = gate_rows * (sums - jnp.sum(gate_rows * sums, axis=0, keepdims=True))
    logits_low = jnp.where(mask, logits_grad, 0.0).astype(bf16)
    router = jnp.where(
        lax.broadcasted_iota(jnp.int32, (8, full), 0) < 6, small_all[...], 0.0
    )
    router_low = router.astype(bf16)
    once = jnp.where((row == 0) & (links.col == 0), 1.0, 0.0)
    fetch.wait("normed")
    router_grad = nn(logits_low, normed[...])
    router_inner = once * jnp.sum(
        logits_low.astype(f32) * nt(router_low, normed[...]), axis=0, keepdims=True
    )
    for i in range(total // BLOCK):
        here = slice(i * BLOCK, (i + 1) * BLOCK)
        rows = rows_of(i)
        key_grad, value_grad = dk[here], dv[here]
        inner = inners[i] + jnp.sum(
            key_grad * k[here].astype(f32) + value_grad * v[here].astype(f32),
            axis=1,
            keepdims=True,
        )
        grads[rows, heads * HEAD : (heads + 1) * HEAD] = back(key_grad, rows).astype(bf16)
        grads[rows, (heads + 1) * HEAD :] = value_grad.astype(bf16)
        vec_own[:, rows] = jnp.broadcast_to(inner, (BLOCK, 128)).T[0:8, :]
    vec_own[...] += router_inner
    vec_copies = [links.go(vec_own, vec_in.at[k - 1], links.group(k)) for k in (1, 2, 3)]

    def blocks(k, h):
        first = (HALF if k & 2 else 0) + h * quarter
        cols = slice((k & 1) * width, (k & 1) * width + width)
        return partial.at[first : first + quarter, cols]

    own_rows, other_rows, forward, finish, sum_rows, sent = scatter_group(
        links,
        blocks,
        partial.at[0:HALF, 0:width],
        partial.at[HALF + quarter :, 0:width],
        partial.at[HALF : HALF + quarter, width:],
        near2,
        near3,
        far2,
        far3,
        out2,
        out3,
    )
    fetch.wait("qkv")
    partial[0:HALF] = nt(grads[0:HALF], qkv[...]).astype(bf16)
    own_rows()
    partial[HALF:] = nt(grads[HALF:], qkv[...]).astype(bf16)
    other_rows()

    gain_sums = {}
    for mine in (False, True):
        which = links.core if mine else 1 - links.core
        for ab in range(2):
            first = ab * width + which * SIDE
            part = tn(normed[:, at(first, SIDE, 128)], grads[...])
            rows = at(first, SIDE)
            qkv_part[rows] = part.astype(bf16)
            gain_sum = jnp.sum(part * qkv[rows].astype(f32), axis=1, keepdims=True)
            gain_sums[mine, ab] = jnp.broadcast_to(gain_sum, (SIDE, 128)).T[0:8, :]
            if not mine:
                qkv_sum.core_send(ab)
    for ab in range(2):
        out_sum.last_sum(1 - ab)
    forward()
    for ab in range(2):
        qkv_sum.first_send(ab)
    for ab in range(2):
        out_sum.gather_near(ab)

    halves = []
    for ab in range(2):
        a, b = gain_sums[True, ab], gain_sums[False, ab]
        first = links.core == 0
        halves.append(jnp.concatenate([jnp.where(first, a, b), jnp.where(first, b, a)], axis=1))
    gain_row = jnp.concatenate(halves, axis=1)
    gain_row = gain_row + once * jnp.sum(router_grad * router, axis=0, keepdims=True)
    gain_row = gain_row / small_all[6:7, :]
    ffn = jnp.concatenate([ffn_part[...], jnp.zeros((8, width), f32)], axis=1)
    index = lax.broadcasted_iota(jnp.int32, (8, full), 0)
    small[...] = jnp.where(index < 6, router_grad, jnp.where(index == 6, gain_row, ffn))
    small_copies = [links.go(small, small_in.at[k - 1], links.group(k)) for k in (1, 2, 3)]

    stages = []

    def small_stage(stage):
        axis_sizes = (cs, xs, zs)
        base = 3 + (0, 1, xs)[stage]
        copies = []
        for k in range(1, axis_sizes[stage]):
            device = links.other_core() if stage == 0 else links.place(stage - 1, k)
            there = small_in.at[base + k - 1, :, 0:width]
            copies.append((links.go(small_own.at[stage], there, device), there))

        def done():
            value = small_own[stage]
            for copy, there in copies:
                copy.wait()
                value = value + there[...]
            small_own[stage + 1] = value

        return done

    layer_finish()
    for h in range(4):
        rows = slice(h * 128, (h + 1) * 128)
        layer_out[rows] = (hidden[rows] + layer_total(rows)).astype(bf16)
    for ab in range(2):
        qkv_sum.second_send(ab)
    for copy in small_copies:
        copy.wait()

    def swapped(v):
        return jnp.concatenate([v[:, width:], v[:, :width]], axis=1)

    group_sum = small[...] + small_in[1] + swapped(small_in[0] + small_in[2])
    eight = lax.broadcasted_iota(jnp.int32, (8, width), 0)
    small_own[0] = jnp.where(eight < 6, small[:, 0:width], group_sum[:, 0:width])
    done = small_stage(0)
    for ab in range(2):
        out_sum.gather_far(ab)
    for ab in (1, 0):
        qkv_sum.last_sum(ab)
    done()
    done = small_stage(1)
    qkv_sum.gather_near(0)
    qkv_sum.gather_near(1)
    done()
    done = small_stage(2)

    for copy in vec_copies:
        copy.wait()
    vec = vec_own[...] + vec_in[0] + half_swap(vec_in[1] + vec_in[2])
    inner = column(vec[6:7, 0:HALF])[:, 0:1]
    fetch.wait("own")
    qkv_sum.gather_far(0)
    qkv_sum.gather_far(1)
    out_sum.gather_core()
    finish()
    for h in range(4):
        rows = slice(h * 128, (h + 1) * 128)
        grad = sum_rows(rows) + tn(logits_low[:, rows], router_low[:, 0:width])
        input_grad[rows] = hidden_grad[rows] + norm_back_rows(
            grad,
            gain[0:1, :],
            tokens[rows].astype(f32),
            scale[rows, 0:1],
            inner[rows],
            full,
        )
    done()
    small_out[...] = small_own[3]
    qkv_sum.gather_core()
    sent()
    layer_sent()
    out_sum.done()
    qkv_sum.done()


def attn_back(
    q,
    k,
    v,
    lse,
    seg,
    cosine,
    sine,
    context,
    hidden_low,
    out_weight,
    qkv_weight,
    normed,
    small_all,
    gates,
    vec_sums,
    ffn_part,
    tokens,
    scale,
    gain,
    hidden_grad,
    layer_part,
    hidden,
):
    xs, zs, cs = dp_sizes()
    total, full = normed.shape
    width = full // 2
    quarter = HALF // 2
    heads = q.shape[1] // HEAD
    cols = qkv_weight.shape[1]
    pad = pad16(SIDE // (xs * zs))
    return pl.pallas_call(
        functools.partial(attn_back_kernel, heads),
        out_shape=(
            jax.ShapeDtypeStruct((HALF, width), f32),
            jax.ShapeDtypeStruct((HALF, width), bf16),
            jax.ShapeDtypeStruct((8, width), f32),
            jax.ShapeDtypeStruct((cs, 2, xs * zs, pad, cols), bf16),
            jax.ShapeDtypeStruct((cs, 2, xs * zs, pad, SIDE), bf16),
        ),
        in_specs=[ANY] * 3
        + [WHOLE] * 3
        + [ANY] * 4
        + [WHOLE]
        + [ANY] * 2
        + [WHOLE] * 4
        + [ANY] * 2
        + [WHOLE] + [ANY] * 3,
        out_specs=(WHOLE, WHOLE, WHOLE, ANY, ANY),
        scratch_shapes=[
            VMEM(q.shape, bf16),
            VMEM(k.shape, bf16),
            VMEM(v.shape, bf16),
            VMEM(cosine.shape, f32),
            VMEM(sine.shape, f32),
            VMEM(context.shape, bf16),
            VMEM(hidden_low.shape, bf16),
            VMEM(qkv_weight.shape, bf16),
            VMEM(normed.shape, bf16),
            VMEM(tokens.shape, bf16),
            VMEM((HALF, 128), f32),
            VMEM(hidden_grad.shape, f32),
            VMEM((HEAD, total), bf16),
            VMEM(q.shape, bf16),
            VMEM(k.shape, f32),
            VMEM(v.shape, f32),
            VMEM((total, cols), bf16),
            VMEM((total, full), bf16),
            VMEM((full, cols), bf16),
            VMEM((SIDE, full), bf16),
        ]
        + group_scratch(width)
        + [
            VMEM((HALF, width), bf16),
            VMEM((quarter, width), bf16),
            VMEM((quarter, width), bf16),
            VMEM((HALF, width), f32),
        ]
        + group_scratch(width)
        + [
            VMEM((8, total), f32),
            VMEM((3, 8, total), f32),
            VMEM((8, full), f32),
            VMEM((4, 8, width), f32),
            VMEM((3 + 1 + xs + zs, 8, full), f32),
            VMEM((2, pad, cols), bf16),
            VMEM((2, pad, SIDE), bf16),
        ]
        + plane_scratch(SIDE, cols)
        + plane_scratch(SIDE, SIDE)
        + [
            pltpu.SemaphoreType.DMA((96,)),
            pltpu.SemaphoreType.DMA((96,)),
            pltpu.SemaphoreType.DMA((24,)),
            pltpu.SemaphoreType.DMA((2, 2)),
        ],
        compiler_params=pltpu.CompilerParams(
            collective_id=3, has_side_effects=True, vmem_limit_bytes=60 * 2**20
        ),
        name="attn_back",
    )(
        q,
        k,
        v,
        lse,
        seg.reshape(total, 1),
        seg.reshape(1, total),
        cosine,
        sine,
        context,
        hidden_low,
        out_weight,
        qkv_weight,
        normed,
        small_all,
        gates,
        vec_sums,
        ffn_part,
        tokens,
        scale,
        gain,
        hidden_grad,
        layer_part,
        hidden,
    )


def swap_halves(v):
    half = v.shape[-1] // 2
    return jnp.concatenate([v[..., half:], v[..., :half]], axis=-1)


def experts_kernel(
    normed_h,
    cot_own,
    cot_2,
    cot_3,
    gates,
    gate_weight,
    up_weight,
    down_weight,
    units,
    weighted_h,
    grads_h,
    back_h,
    out_h,
    cot_all_h,
    vec_ref,
    normed,
    cot,
    gate_up,
    down,
    weighted,
    grads,
    back,
    out,
    send,
    recv,
    sems,
):
    links = Links(send, recv)
    col = links.col
    count, _, pieces, unit, both = gate_up.shape
    blocks, down_unit, full = down.shape
    width = full // 2
    hidden = both // 2
    quarter = HALF // 2
    other, own = slice(HALF, 2 * HALF), slice(0, HALF)
    fetch = Fetch(sems)
    fetch.start("normed", (normed_h.at[other], normed.at[other]))
    for e in range(count):
        for which, weight in enumerate((gate_weight, up_weight)):
            cols = slice(which * hidden, (which + 1) * hidden)
            fetch.start(
                ("gate_up", e),
                (weight.at[col * count + e], gate_up.at[e, 0, :, :, cols]),
                (
                    units.at[which, :, (3 + e) * unit : (4 + e) * unit],
                    gate_up.at[e, 1, :, :, cols],
                ),
            )
    fetch.start(
        "cot",
        (cot_2, cot.at[other, 0:width]),
        (cot_3, cot.at[other, width:]),
        (cot_own, cot.at[own, 0:width]),
    )
    fetch.start("down", (down_weight.at[pl.ds(col * blocks, blocks)], down.at[:, :, 0:width]))
    for j in range(-(-blocks // pieces)):
        n = min(pieces, blocks - j * pieces)
        start = (3 + count) * unit + j * down_unit
        for core in range(2):
            first = width + core * SIDE
            fetch.start(
                "down",
                (
                    units.at[core, 0:n, start : start + down_unit],
                    down.at[j * pieces : j * pieces + n, :, first : first + SIDE],
                ),
            )
    fetch.start("normed_own", (normed_h.at[own], normed.at[own]))
    links.greet([links.group(2), links.group(3)])
    relays = [
        links.go(cot_3.at[0:quarter], cot.at[0:quarter, width:], links.group(2)),
        links.go(cot_2.at[quarter:], cot.at[quarter:HALF, width:], links.group(3)),
    ]
    fetch.wait("normed")
    for step, rows in enumerate((other, own)):
        if step == 1:
            fetch.wait("normed_own")
        x = normed[rows]
        lanes = lax.broadcasted_iota(jnp.int32, (HALF, 128), 1)
        vec = jnp.zeros((HALF, 128), f32)
        inner = jnp.zeros((HALF, 1), f32)
        pres = []
        for e in range(count):
            if step == 0:
                fetch.wait(("gate_up", e))
            pres.append(nn(x, gate_up[e].reshape(full, both)))
        if step == 0:
            fetch.wait("cot", "down")
        else:
            for copy in relays:
                copy.wait_recv()
        y = cot[rows]
        for e in range(count):
            down_e = down[...].reshape(count, hidden, full)[e]
            here = lanes == col * count + e
            gate = jnp.sum(jnp.where(here, gates[rows], 0.0), axis=1, keepdims=True)
            gate_pre, up_pre = pres[e][:, :hidden], pres[e][:, hidden:]
            sigmoid = 1.0 / (1.0 + jnp.exp(-gate_pre))
            silu = gate_pre * sigmoid
            activated = silu * up_pre
            weighted[rows, e * hidden : (e + 1) * hidden] = (gate * activated).astype(bf16)
            weighted_grad = nt(y, down_e)
            vec = vec + jnp.where(
                here, jnp.sum(activated * weighted_grad, axis=1, keepdims=True), 0.0
            )
            g = gate * weighted_grad
            gate_grad = g * up_pre * (sigmoid * (1.0 + gate_pre * (1.0 - sigmoid)))
            up_grad = g * silu
            inner = inner + jnp.sum(
                gate_grad * gate_pre + up_grad * up_pre, axis=1, keepdims=True
            )
            grads[e, rows] = jnp.concatenate([gate_grad, up_grad], axis=1).astype(bf16)
        fetch.start("out", *[(grads.at[e, rows], grads_h.at[e, rows]) for e in range(count)])
        fetch.start("out", (weighted.at[rows], weighted_h.at[rows]))
        fetch.start("out", (cot.at[rows], cot_all_h.at[rows]))
        total = None
        for e in range(count):
            term = nt(grads[e, rows], gate_up[e].reshape(full, both))
            total = term if total is None else total + term
        back[rows] = total.astype(bf16)
        fetch.start("out", (back.at[rows], back_h.at[rows]))
        out[rows] = nn(weighted[rows], down[...].reshape(count * hidden, full)).astype(bf16)
        fetch.start("out", (out.at[rows], out_h.at[rows]))
        vec = jnp.where(lanes == 6, inner, vec)
        vec_ref[:, rows] = vec.T[0:8, :]
    for copy in relays:
        copy.wait_send()
    fetch.wait("out")


def experts_step(
    normed, cot_own, cot_2, cot_3, gates, gate_weight, up_weight, down_weight, units
):
    total, width = normed.shape
    experts, own_width, hidden = gate_weight.shape
    count = experts // 2
    both = 2 * hidden
    hid = count * hidden
    pieces = units.shape[1]
    unit, down_unit = unit_rows()
    return pl.pallas_call(
        experts_kernel,
        out_shape=(
            jax.ShapeDtypeStruct((total, hid), bf16),
            jax.ShapeDtypeStruct((count, total, both), bf16),
            jax.ShapeDtypeStruct((total, width), bf16),
            jax.ShapeDtypeStruct((total, width), bf16),
            jax.ShapeDtypeStruct((total, width), bf16),
            jax.ShapeDtypeStruct((8, total), f32),
        ),
        in_specs=[ANY] * 4 + [WHOLE] + [ANY] * 4,
        out_specs=(ANY,) * 5 + (WHOLE,),
        scratch_shapes=[
            VMEM((total, width), bf16),
            VMEM((total, width), bf16),
            VMEM((count, 2, pieces, unit, both), bf16),
            VMEM((hid // down_unit, down_unit, width), bf16),
            VMEM((total, hid), bf16),
            VMEM((count, total, both), bf16),
            VMEM((total, width), bf16),
            VMEM((total, width), bf16),
            pltpu.SemaphoreType.DMA((2,)),
            pltpu.SemaphoreType.DMA((2,)),
            pltpu.SemaphoreType.DMA((48,)),
        ],
        compiler_params=pltpu.CompilerParams(
            collective_id=1, has_side_effects=True, vmem_limit_bytes=60 * 2**20
        ),
        name="experts",
    )(
        normed,
        cot_own,
        cot_2,
        cot_3,
        gates,
        gate_weight.reshape(experts, pieces, unit, hidden),
        up_weight.reshape(experts, pieces, unit, hidden),
        down_weight.reshape(-1, down_unit, own_width),
        units,
    )


def window(i, block):
    first = max(0, (i + 1) * block - 512 - block)
    return first, (i + 1) * block


def allowed_keys(segk_ref, segq_ref, i, first, last):
    block = BLOCK
    width = last - first
    keys = lax.broadcasted_iota(jnp.int32, (width, block), 0) + first
    queries = lax.broadcasted_iota(jnp.int32, (width, block), 1) + i * block
    same = segk_ref[first:last] == segq_ref[:, i * block : (i + 1) * block]
    return (keys <= queries) & same


def expert_finish_kernel(col_ref, by_x, by_z, gate_ref, up_ref, down_ref):
    ab = pl.program_id(0)
    rows = gate_ref.shape[0]
    down_rows = down_ref.shape[0]

    def write(block):
        pieces = block.shape[0]
        step, down_step = rows // pieces, down_rows // pieces
        for p in range(pieces):
            here = slice(p * step, (p + 1) * step)
            gate_ref[here] = block[p, 0, 0, 0:step].astype(f32)
            up_ref[here] = block[p, 1, 0, 0:step].astype(f32)
            here = slice(p * down_step, (p + 1) * down_step)
            for core in range(2):
                down_ref[here, core * SIDE : (core + 1) * SIDE] = block[
                    p, core, 0, step : step + down_step
                ].astype(f32)

    @pl.when(ab == 0)
    def _():
        write(by_x.at[0])

    @pl.when(ab == 1)
    def _():
        write(by_z.at[:, 0])


def expert_finish(sums, col, up_rows, down_rows):
    xs, zs, cs = dp_sizes()
    piece = sums.shape[-2]

    def half(ab, col_ref):
        return jnp.where(ab == 0, col_ref[0], 1 - col_ref[0])

    def out_spec(rows, cols):
        return pl.BlockSpec(
            (rows, cols), lambda ab, j, col_ref: (half(ab, col_ref) * xs + j, 0)
        )

    return pl.pallas_call(
        expert_finish_kernel,
        grid_spec=pltpu.PrefetchScalarGridSpec(
            num_scalar_prefetch=1,
            grid=(2, xs),
            in_specs=[
                pl.BlockSpec(
                    (1, zs, cs, 1, piece, SIDE),
                    lambda ab, j, col_ref: (jnp.where(ab == 0, j, xs - 1), 0, 0, 0, 0, 0),
                ),
                pl.BlockSpec(
                    (xs, 1, cs, 1, piece, SIDE),
                    lambda ab, j, col_ref: (0, jnp.where(ab == 0, 0, j), 0, 1, 0, 0),
                ),
            ],
            out_specs=(
                out_spec(up_rows * zs, SIDE),
                out_spec(up_rows * zs, SIDE),
                out_spec(down_rows * zs, 2 * SIDE),
            ),
        ),
        out_shape=(
            jax.ShapeDtypeStruct((2 * up_rows * xs * zs, SIDE), f32),
            jax.ShapeDtypeStruct((2 * up_rows * xs * zs, SIDE), f32),
            jax.ShapeDtypeStruct((2 * down_rows * xs * zs, 2 * SIDE), f32),
        ),
        compiler_params=pltpu.CompilerParams(vmem_limit_bytes=48 * 2**20),
        name="expert_finish",
    )(col.reshape(1), sums, sums)


def attn_finish_kernel(qkv_sums, out_sums, qkv_ref, out_ref):
    col = lax.axis_index("col")
    cores, _, pieces = qkv_sums.shape[:3]
    rows = SIDE // pieces
    cols = SIDE + 2 * HEAD
    for core in range(cores):
        kept = None
        here = slice(core * SIDE, (core + 1) * SIDE)
        for ab in range(2):
            half = col if ab == 0 else 1 - col
            block = qkv_sums[core, ab].astype(f32)[:, 0:rows].reshape(SIDE, cols)
            qkv_ref[here, at(half * SIDE, SIDE, 128)] = block[:, 0:SIDE]
            out_ref[at(half * SIDE, SIDE), here] = (
                out_sums[core, ab].astype(f32)[:, 0:rows].reshape(SIDE, SIDE)
            )
            pair = block[:, SIDE:cols]
            kept = pair if kept is None else kept + pair
        qkv_ref[here, 2 * SIDE :] = kept


def attn_finish(qkv_sums, out_sums):
    return pl.pallas_call(
        attn_finish_kernel,
        out_shape=(
            jax.ShapeDtypeStruct((2 * SIDE, 2 * SIDE + 2 * HEAD), f32),
            jax.ShapeDtypeStruct((2 * SIDE, 2 * SIDE), f32),
        ),
        in_specs=[WHOLE, WHOLE],
        out_specs=(WHOLE, WHOLE),
        compiler_params=pltpu.CompilerParams(vmem_limit_bytes=48 * 2**20),
        name="attn_finish",
    )(qkv_sums, out_sums)


def turn_tables(places):
    steps_up = jnp.arange(HEAD // 2, dtype=f32) * (2.0 / HEAD)
    inverse = jnp.exp(-math.log(ROPE_BASE) * steps_up)
    angles = places[:, None] * inverse[None, :]
    cosine, sine = jnp.cos(angles), jnp.sin(angles)
    return (
        jnp.concatenate([cosine, cosine], axis=1),
        jnp.concatenate([-sine, sine], axis=1),
    )


def local(
    tokens,
    cotangent,
    attn_gain,
    ffn_gain,
    qkv_weight,
    out_weight,
    router_weight,
    gate_weight,
    up_weight,
    down_weight,
    routes,
    segments,
):
    row = lax.axis_index("row")
    col = lax.axis_index("col")
    xs, zs, cs = dp_sizes()
    own_rows, own_width = tokens.shape
    total = 2 * own_rows
    experts, _, hidden = gate_weight.shape
    own_experts = experts // 2
    hid = own_experts * hidden
    pieces = xs * zs

    def own_order(v):
        return jnp.where(row == 0, v, jnp.roll(v, own_rows, axis=0))

    routes_local = own_order(routes)
    cosine, sine = turn_tables(own_order(jnp.arange(total, dtype=f32)))
    small = jnp.concatenate(
        [router_weight.T.astype(f32), attn_gain[None], ffn_gain[None]], axis=0
    )

    (
        normed_one,
        queries,
        keys,
        values,
        context,
        qkv_local,
        normed_two,
        out_quarter,
        cot_2,
        cot_3,
        units,
        lse,
        gates,
        scale_one,
        small_all,
        hidden_own,
        scale_two,
    ) = forward_step(
        tokens,
        cotangent,
        qkv_weight,
        small,
        routes_local,
        cosine,
        sine,
        segments,
        out_weight,
        gate_weight,
        up_weight,
        down_weight,
    )
    weighted, pre_grads, normed_two_part, layer_part, cot_all, expert_vec = experts_step(
        normed_two,
        cotangent,
        cot_2,
        cot_3,
        gates,
        gate_weight,
        up_weight,
        down_weight,
        units.reshape((cs, pieces) + units.shape[3:]),
    )
    hidden_grad, hidden_low, vec_sums, ffn_part, shard_up, shard_down = reduce_step(
        normed_two_part,
        expert_vec,
        hidden_own,
        cotangent,
        scale_two,
        ffn_gain[None],
        normed_two,
        pre_grads,
        weighted,
        cot_all,
    )
    up_rows = own_experts * own_width // pieces
    down_rows = hid // pieces
    expert_sums = lax.all_gather(
        jnp.concatenate([shard_up[:, :up_rows], shard_down[:, :down_rows]], axis=1),
        "dp",
        axis=0,
        tiled=False,
    ).reshape(xs, zs, cs, 2, up_rows + down_rows, SIDE)
    input_grad, layer_out, small_sums, qkv_sums, out_sums = attn_back(
        queries,
        keys,
        values,
        lse,
        segments,
        cosine,
        sine,
        context,
        hidden_low,
        out_quarter.reshape(SIDE, 2 * own_width),
        qkv_local,
        normed_one,
        small_all,
        gates,
        vec_sums,
        ffn_part,
        tokens,
        scale_one,
        attn_gain[None],
        hidden_grad,
        layer_part,
        hidden_own,
    )
    router_grad = small_sums[:experts].T
    attn_gain_grad = small_sums[6]
    ffn_gain_grad = small_sums[7]
    qkv_grad, out_grad = attn_finish(qkv_sums, out_sums)
    gate_grad, up_grad, down_grad = expert_finish(expert_sums, col, up_rows, down_rows)
    gate_grad = gate_grad.reshape(experts, own_width, hidden)
    up_grad = up_grad.reshape(experts, own_width, hidden)
    down_grad = down_grad.reshape(experts, hidden, own_width)
    return (
        layer_out,
        input_grad,
        attn_gain_grad,
        ffn_gain_grad,
        qkv_grad,
        out_grad,
        router_grad,
        gate_grad,
        up_grad,
        down_grad,
    )


def solution(mesh):
    in_specs = (
        P(("dp", "row"), "col"),
        P(("dp", "row"), "col"),
        P("col"),
        P("col"),
        P("col", "row"),
        P("row", "col"),
        P("col", None),
        P(None, "col", "row"),
        P(None, "col", "row"),
        P(None, "row", "col"),
        P("dp", None),
        P("dp"),
    )
    out_specs = (
        P(("dp", "row"), "col"),
        P(("dp", "row"), "col"),
        P("col"),
        P("col"),
        P("col", "row"),
        P("row", "col"),
        P("col", None),
        P(None, "col", "row"),
        P(None, "col", "row"),
        P(None, "row", "col"),
    )
    return jax.shard_map(local, mesh=mesh, in_specs=in_specs, out_specs=out_specs, check_vma=False)
```

```python
import functools
import math

import jax
import jax.numpy as jnp
import numpy as np
from jax import lax
from jax.experimental import pallas as pl
from jax.experimental.pallas import tpu as pltpu
from jax.sharding import PartitionSpec as P

f32 = jnp.float32
bf16 = jnp.bfloat16

HEAD = 128
GROUP_HEADS = 6
EPS = 1e-06
ROPE_BASE = 10000.0
MASKED = -1e30
BLOCK = 256


MESH = pl.DeviceIdType.MESH
VMEM = pltpu.VMEM
ANY = pl.BlockSpec(memory_space=pl.ANY)
WHOLE = pl.BlockSpec(memory_space=pltpu.VMEM)
HALF = 512
SIDE = 384


def dp_sizes():
    total = lax.axis_size("dp")
    cores = 2 if total % 2 == 0 else 1
    side = math.isqrt(total // cores)
    return side, side, cores


def dp_place():
    xs, zs, cs = dp_sizes()
    d = lax.axis_index("dp")
    return d // (zs * cs), (d // cs) % zs, d % cs


def nt(a, b):
    return lax.dot_general(a, b, (((1,), (1,)), ((), ())), preferred_element_type=f32)


def nn(a, b):
    return lax.dot_general(a, b, (((1,), (0,)), ((), ())), preferred_element_type=f32)


def tn(a, b):
    return lax.dot_general(a, b, (((0,), (0,)), ((), ())), preferred_element_type=f32)


class Links:
    def __init__(self, send, recv):
        self.send, self.recv = send, recv
        self.used = 0
        self.dp = lax.axis_index("dp")
        self.row = lax.axis_index("row")
        self.col = lax.axis_index("col")
        self.xs, self.zs, self.cs = dp_sizes()
        self.x, self.z, self.core = dp_place()

    def group(self, k):
        row = 1 - self.row if k & 2 else self.row
        col = 1 - self.col if k & 1 else self.col
        return (self.dp, row, col)

    def other_core(self):
        return (self.dp + 1 - 2 * self.core, self.row, self.col)

    def place(self, axis, k):
        x, z = self.x, self.z
        if axis == 0:
            x = (x + k) % self.xs
        else:
            z = (z + k) % self.zs
        return ((x * self.zs + z) * self.cs + self.core, self.row, self.col)

    def greet(self, devices):
        barrier = pltpu.get_barrier_semaphore()
        for device in devices:
            pl.semaphore_signal(barrier, inc=1, device_id=device, device_id_type=MESH)
        pl.semaphore_wait(barrier, len(devices))

    def plane(self):
        return (
            ([self.other_core()] if self.cs == 2 else [])
            + [self.place(0, k) for k in range(1, self.xs)]
            + [self.place(1, k) for k in range(1, self.zs)]
        )

    def copy(self, src, dst, device):
        i = self.used
        self.used += 1
        return pltpu.make_async_remote_copy(
            src_ref=src,
            dst_ref=dst,
            send_sem=self.send.at[i],
            recv_sem=self.recv.at[i],
            device_id=device,
            device_id_type=MESH,
        )

    def go(self, src, dst, device):
        copy = self.copy(src, dst, device)
        copy.start()
        return copy


def at(start, size, step=16):
    return pl.ds(pl.multiple_of(start, step), size)


class Fetch:
    def __init__(self, sems):
        self.sems = sems
        self.used = 0
        self.named = {}

    def start(self, name, *pairs):
        copies = self.named.setdefault(name, [])
        for src, dst in pairs:
            copy = pltpu.make_async_copy(src, dst, self.sems.at[self.used])
            self.used += 1
            copy.start()
            copies.append(copy)

    def wait(self, *names):
        for name in names:
            for copy in self.named.pop(name):
                copy.wait()


def pad16(n):
    return -(-n // 16) * 16


class PlaneSum:
    def __init__(self, links, parts, came, in1, piece, in2, peer, shard, groups=1, fold=False):
        self.links, self.parts, self.came, self.in1 = links, parts, came, in1
        self.fold = fold
        self.piece, self.in2, self.peer, self.shard = piece, in2, peer, shard
        self.sizes = (links.xs, links.zs)
        self.places = (links.x, links.z)
        self.sent = []
        self.first, self.second, self.core = {}, {}, {}
        self.groups = groups
        self.group_rows = came.shape[1] // groups
        self.chunk = self.group_rows // links.xs
        self.rows2 = groups * self.chunk // links.zs

    def start(self):
        kept, rows = self.rows2 * (2 if self.fold else 1), self.piece.shape[2]
        if kept < rows:
            shape = self.piece.shape
            self.piece[:, :, kept:] = jnp.zeros(shape[:2] + (rows - kept, shape[3]), bf16)

    def core_send(self, ab, g=0, which=0):
        if self.links.cs == 1:
            return
        rows = slice(g * self.group_rows, (g + 1) * self.group_rows)
        cols, part = self.parts(ab, 1 - self.links.core)[which]
        copy = self.links.go(
            part.at[rows], self.came.at[ab, rows, cols], self.links.other_core()
        )
        self.core.setdefault((ab, g), []).append(copy)
        self.sent.append(copy)

    def first_send(self, ab, g=0):
        for copy in self.core.get((ab, g), []):
            copy.wait_recv()
        total = self.came.at[ab]
        step = 96
        for cols, mine in self.parts(ab, self.links.core):

            @pl.loop(0, self.group_rows // step)
            def _(i):
                here = at(g * self.group_rows + i * step, step)
                total[here, cols] = (
                    total[here, cols].astype(f32) + mine[here].astype(f32)
                ).astype(bf16)

        n, place = self.sizes[ab], self.places[ab]
        for k in range(1, n):
            j = (place + k) % n
            copy = self.links.go(
                self.came.at[ab, at(g * self.group_rows + j * self.chunk, self.chunk)],
                self.in1.at[ab, k - 1, g * self.chunk : (g + 1) * self.chunk],
                self.links.place(ab, k),
            )
            self.first[ab, g, k] = copy
            self.sent.append(copy)

    def second_send(self, ab):
        n, place = self.sizes[ab], self.places[ab]
        owns = []
        for g in range(self.groups):
            own = self.came[ab, at(g * self.group_rows + place * self.chunk, self.chunk)].astype(
                f32
            )
            for k in range(1, n):
                self.first[ab, g, k].wait_recv()
                own = own + self.in1[ab, k - 1, g * self.chunk : (g + 1) * self.chunk].astype(
                    f32
                )
            owns.append(own)
        own = owns[0] if self.groups == 1 else jnp.concatenate(owns, axis=0)
        kept = self.rows2
        n, place = self.sizes[1 - ab], self.places[1 - ab]
        for j in range(n):
            block = own[j * kept : (j + 1) * kept]
            if self.fold:
                middle = block.shape[1] // 2
                block = jnp.concatenate([block[:, :middle], block[:, middle:]], axis=0)
            self.piece[ab, j, 0 : block.shape[0]] = block.astype(bf16)
        for k in range(1, n):
            j = (place + k) % n
            copy = self.links.go(
                self.piece.at[ab, j], self.in2.at[ab, k - 1], self.links.place(1 - ab, k)
            )
            self.second[ab, k] = copy
            self.sent.append(copy)

    def last_sum(self, ab):
        n, place = self.sizes[1 - ab], self.places[1 - ab]
        value = self.piece[ab, place].astype(f32)
        for k in range(1, n):
            self.second[ab, k].wait_recv()
            value = value + self.in2[ab, k - 1].astype(f32)
        if ab == 0:
            self.shard[0] = value.astype(bf16)
        else:
            self.peer[...] = value.astype(bf16)
            self.swap = self.links.go(self.peer, self.shard.at[1], self.links.group(1))

    def wait_peer(self):
        self.swap.wait()

    def done(self):
        for copy in self.sent:
            copy.wait_send()


class PlaneGather:
    def __init__(self, links, shard, sums, local):
        self.links, self.shard, self.sums, self.local = links, shard, sums, local
        self.sizes = (links.xs, links.zs)
        self.home, self.first, self.second, self.last = {}, {}, [], []

    def near(self, ab):
        links = self.links
        x, z = links.x, links.z
        index = (x * links.zs + z) if ab == 0 else (z * links.xs + x)
        here = self.sums.at[links.core, ab, index]
        copy = pltpu.make_async_copy(self.shard.at[ab], here, self.local.at[ab])
        copy.start()
        self.home[ab] = copy
        self.first[ab] = [
            links.go(self.shard.at[ab], here, links.place(1 - ab, k))
            for k in range(1, self.sizes[1 - ab])
        ]

    def far(self, ab, rows=slice(None)):
        links = self.links
        if ab in self.home:
            for copy in self.first[ab]:
                copy.wait()
            self.home.pop(ab).wait()
        n = self.sizes[1 - ab]
        first = (links.x if ab == 0 else links.z) * n
        block = self.sums.at[links.core, ab, pl.ds(first, n), rows]
        self.second.append(
            [links.go(block, block, links.place(ab, k)) for k in range(1, self.sizes[ab])]
        )

    def swap(self, rows=slice(None), count=2):
        links = self.links
        for copies in self.second[:count]:
            for copy in copies:
                copy.wait()
        del self.second[:count]
        if links.cs == 2:
            block = self.sums.at[links.core, :, :, rows]
            self.last.append(links.go(block, block, links.other_core()))

    def done(self):
        for copy in self.last:
            copy.wait()


def plane_scratch(rows, width, fold=False):
    xs, zs, _ = dp_sizes()
    n1, n2 = max(xs - 1, 1), max(zs - 1, 1)
    kept = rows // (xs * zs)
    shape = (2 * kept, width // 2) if fold else (pad16(kept), width)
    return [
        VMEM((2, rows, width), bf16),
        VMEM((2, n1, rows // xs, width), bf16),
        VMEM((2, zs) + shape, bf16),
        VMEM((2, n2) + shape, bf16),
        VMEM(shape, bf16),
    ]


def gather_group(links, own, dst):
    first = {}
    for k, order in ((2, (1, 0)), (3, (0, 1))):
        for h in order:
            first[k, h] = links.copy(own(h), dst(k, h), links.group(k))
    for key in ((2, 1), (3, 0), (2, 0), (3, 1)):
        first[key].start()
    relay = [
        links.copy(dst(3, 0), dst(1, 0), links.group(2)),
        links.copy(dst(2, 1), dst(1, 1), links.group(3)),
    ]

    def forward():
        first[3, 0].wait_recv()
        relay[0].start()
        first[2, 1].wait_recv()
        relay[1].start()

    def near():
        first[2, 0].wait_recv()
        first[3, 1].wait_recv()

    def far():
        for copy in relay:
            copy.wait_recv()

    def sent():
        for copy in list(first.values()) + relay:
            copy.wait_send()

    return forward, near, far, sent


def unit_rows():
    xs, zs, _ = dp_sizes()
    return 768 // (xs * zs), min(SIDE, 768 // (xs * zs))


def down_units(hid):
    xs, zs, _ = dp_sizes()
    return -(-(hid // unit_rows()[1]) // (xs * zs))


class Units:
    def __init__(self, links, units, out_weight, gate_weight, up_weight, down_weight):
        self.links, self.units = links, units
        rows, down_rows = unit_rows()
        xs, zs = links.xs, links.zs
        pieces = xs * zs
        place = links.x * zs + links.z
        lanes = at(links.core * SIDE, SIDE, 128)
        home = units.at[links.core, links.x, links.z]
        self.out_rows = 3 * rows
        self.cut = 4 * rows
        self.total = units.shape[3]
        self.fetch = []
        for k in (1, 2, 3):
            col = 1 - links.col if k & 1 else links.col
            index = (place + col * (pieces // 2)) % pieces
            self.fetch.append(
                links.go(
                    out_weight.at[index, :, lanes],
                    home.at[(k - 1) * rows : k * rows],
                    links.group(k),
                )
            )
        count = gate_weight.shape[0] // 2
        first = (1 - links.col) * count
        for e in range(count):
            i = links.used
            links.used += 1
            to = home.at[(3 + e) * rows : (4 + e) * rows]
            either = [
                pltpu.make_async_remote_copy(
                    src_ref=weight.at[first + e, place],
                    dst_ref=to,
                    send_sem=links.send.at[i],
                    recv_sem=links.recv.at[i],
                    device_id=links.group(1),
                    device_id_type=MESH,
                )
                for weight in (gate_weight, up_weight)
            ]
            for which in range(2):

                @pl.when(links.core == which)
                def _(copy=either[which]):
                    copy.start()

            self.fetch.append(either[0])
        blocks = down_weight.shape[0] // 2
        for j in range(down_units(blocks * down_rows)):
            index = jnp.minimum(j * pieces + place, blocks - 1)
            start = (3 + count) * rows + j * down_rows
            self.fetch.append(
                links.go(
                    down_weight.at[(1 - links.col) * blocks + index, :, lanes],
                    home.at[start : start + down_rows],
                    links.group(1),
                )
            )

    def near(self):
        for copy in self.fetch:
            copy.wait()
        links = self.links
        home = self.units.at[links.core, links.x, links.z]
        self.first = []
        for rows, axis, n in (
            (slice(0, self.cut), 1, links.zs),
            (slice(self.cut, self.total), 0, links.xs),
        ):
            for k in range(1, n):
                self.first.append(links.go(home.at[rows], home.at[rows], links.place(axis, k)))

    def far(self):
        for copy in self.first:
            copy.wait()
        links, units = self.links, self.units
        self.second = []
        line = units.at[links.core, links.x, :, 0 : self.cut]
        for k in range(1, links.xs):
            self.second.append(links.go(line, line, links.place(0, k)))
        line = units.at[links.core, :, links.z, self.cut : self.total]
        for k in range(1, links.zs):
            self.second.append(links.go(line, line, links.place(1, k)))

    def swap(self):
        for copy in self.second:
            copy.wait()
        links = self.links
        self.last = []
        for rows in (slice(0, self.out_rows), slice(self.out_rows, self.total)):
            block = self.units.at[links.core, :, :, rows]
            self.last.append(links.go(block, block, links.other_core()))

    def wait_out(self):
        self.last[0].wait()

    def done(self):
        self.last[1].wait()


def forward_kernel(
    heads,
    tokens,
    cot_h,
    qkv_weight,
    router_weight,
    attn_gain,
    ffn_gain,
    routes,
    cosine,
    sine,
    seg,
    out_weight,
    gate_weight,
    up_weight,
    down_weight,
    normed_h,
    q_h,
    k_h,
    v_h,
    context_h,
    qkv_h,
    normed_two_h,
    quarter_h,
    cot_2,
    cot_3,
    units,
    lse,
    gates_ref,
    scale_one,
    small_all,
    hidden_own,
    scale_two,
    tokens_all,
    qkv_all,
    normed,
    q,
    k,
    v,
    vt,
    contexts,
    weight,
    hidden,
    normed_two,
    small,
    segk,
    segq,
    route_cols,
    send,
    recv,
    sems,
):
    links = Links(send, recv)
    row, col = links.row, links.col
    zs, cs = links.zs, links.cs
    total, full = normed.shape
    width = full // 2
    quarter = HALF // 2
    small[0:6, :] = router_weight[...].astype(f32)
    small[6:7, :] = attn_gain[...].reshape(1, width)
    small[7:8, :] = ffn_gain[...].reshape(1, width)
    links.greet([links.group(k) for k in (1, 2, 3)] + links.plane())

    def own(h):
        return tokens.at[h * quarter : (h + 1) * quarter]

    def dst(k, h):
        rows = (HALF if k & 2 else 0) + h * quarter
        return tokens_all.at[rows : rows + quarter, (k & 1) * width : (k & 1) * width + width]

    share = width // (cs * zs)
    start = links.core * (width // cs) + links.z * share
    there = at(width + start, share)
    fetch_qkv = [
        links.go(
            qkv_weight.at[at(start, share), at((1 - col) * SIDE, SIDE, 128)],
            qkv_all.at[there, 0:SIDE],
            links.group(1),
        ),
        links.go(
            qkv_weight.at[at(start, share), 2 * SIDE :], qkv_all.at[there, SIDE:], links.group(1)
        ),
        links.go(small, small_all.at[:, width:], links.group(1)),
    ]
    shares = Units(links, units, out_weight, gate_weight, up_weight, down_weight)
    forward, near, far, tokens_sent = gather_group(links, own, dst)
    fetch = Fetch(sems)
    pieces = weight.shape[1]
    half = pieces // 2
    fetch.start(
        "weight",
        *[
            (
                out_weight.at[pl.ds((col if h == 0 else 1 - col) * half, half)],
                weight.at[0, h * half : (h + 1) * half, :, 0:width],
            )
            for h in range(2)
        ],
    )
    tokens_all[0:HALF, 0:width] = tokens[...]
    qkv_all[0:width, 0:SIDE] = qkv_weight[:, at(col * SIDE, SIDE, 128)]
    qkv_all[0:width, SIDE:] = qkv_weight[:, 2 * SIDE :]
    small_all[:, 0:width] = small[...]
    segq[...] = seg[...].astype(f32)
    segk[...] = column(segq[...])
    count = routes.shape[0]
    route_cols[...] = jnp.concatenate(
        [routes[...].astype(f32), jnp.zeros((128 - count, total), f32)], axis=0
    ).T
    for copy in fetch_qkv:
        copy.wait()
    spread = [
        links.go(qkv_all.at[there], qkv_all.at[there], links.place(1, k)) for k in range(1, zs)
    ]
    shares.near()
    forward()
    for copy in spread:
        copy.wait()
    if cs == 2:
        block = qkv_all.at[at(width + links.core * (width // 2), width // 2)]
        swap_qkv = links.go(block, block, links.other_core())
    shares.far()
    if cs == 2:
        swap_qkv.wait()
    near()

    def project(i):
        rows = slice(i * BLOCK, (i + 1) * BLOCK)
        place = i * BLOCK // HALF
        here = at(
            HALF * jnp.bitwise_xor(row, place) + (i * BLOCK - place * HALF), BLOCK, BLOCK
        )
        x = tokens_all[rows].astype(f32)
        scale = lax.rsqrt(jnp.sum(x * x, axis=1, keepdims=True) * (1.0 / full) + EPS)
        low = (x * scale * small_all[6:7, :]).astype(bf16)
        normed[rows] = low
        if i * BLOCK < HALF:
            scale_one[rows] = jnp.broadcast_to(scale, (BLOCK, 128))
        router = jnp.concatenate([small_all[...], jnp.zeros((120, full), f32)], axis=0)
        logits = nt(low, router.astype(bf16))
        lanes = lax.broadcasted_iota(jnp.int32, (BLOCK, 128), 1).astype(f32)
        chosen = lanes == route_cols[here, 0:1]
        for j in range(1, count):
            chosen = chosen | (lanes == route_cols[here, j : j + 1])
        masked = jnp.where(chosen, logits, MASKED)
        raised = jnp.exp(masked - jnp.max(masked, axis=1, keepdims=True))
        raised = jnp.where(chosen, raised, 0.0)
        gates_ref[rows] = raised / jnp.sum(raised, axis=1, keepdims=True)
        projected = nn(low, qkv_all[...])
        for h in range(heads + 1):
            part = projected[:, h * HEAD : (h + 1) * HEAD]
            turned = (part * cosine[here] + swap_halves(part) * sine[here]).astype(bf16)
            if h < heads:
                q[here, h * HEAD : (h + 1) * HEAD] = turned
            else:
                k[here] = turned
        v[here] = projected[:, (heads + 1) * HEAD :].astype(bf16)

    project(2)
    project(3)
    far()
    cot_copies = [
        links.go(cot_h.at[h * quarter : (h + 1) * quarter], out, links.group(k))
        for k, out, h in ((2, cot_2, 1), (3, cot_3, 0))
    ]
    project(0)
    project(1)
    fetch.start("out", (normed, normed_h), (q, q_h), (k, k_h), (v, v_h), (qkv_all, qkv_h))

    vt[...] = v[...].astype(f32).T.astype(bf16)

    def block(j, h, head):
        first = j * SIDE + head * HEAD
        return contexts.at[h * HALF : (h + 1) * HALF, first : first + HEAD]

    sends, relays = {}, []
    for head in range(heads):
        cols = slice(head * HEAD, (head + 1) * HEAD)
        for i in range(total // BLOCK):
            first, last = window(i, BLOCK)
            here = slice(i * BLOCK, (i + 1) * BLOCK)
            allowed = allowed_keys(segk, segq, i, first, last)
            place = i * BLOCK // HALF
            rows = at(
                HALF * jnp.bitwise_xor(row, place) + (i * BLOCK - place * HALF), BLOCK, BLOCK
            )
            s = nt(k[first:last], q[here, cols]) * (HEAD**-0.5)
            s = jnp.where(allowed, s, MASKED)
            top = jnp.max(s, axis=0, keepdims=True)
            p = jnp.exp(s - top)
            total_p = jnp.sum(p, axis=0, keepdims=True)
            p = (p * (1.0 / total_p)).astype(bf16)
            ot = nn(vt[:, first:last], p)
            contexts[rows, cols] = ot.T.astype(bf16)
            lse[head : head + 1, here] = top + jnp.log(total_p)
        for j, h in ((2, 0), (3, 1), (2, 1), (3, 0)):
            sends[j, 1 - h, head] = links.go(
                block(0, h, head), block(j, 1 - h, head), links.group(j)
            )
    lse[heads:, :] = jnp.zeros((8 - heads, total), f32)
    fetch.start("context", (contexts.at[:, 0:SIDE], context_h))
    shares.swap()
    for head in range(heads):
        sends[3, 0, head].wait_recv()
        relays.append(links.go(block(3, 0, head), block(1, 1, head), links.group(2)))
        sends[2, 1, head].wait_recv()
        relays.append(links.go(block(2, 1, head), block(1, 0, head), links.group(3)))

    shares.wait_out()
    rows = weight.shape[2]
    for j in (1, 2, 3):
        for core in range(2):
            first = (j & 1) * width + core * SIDE
            fetch.start(
                "weight",
                *[
                    (
                        units.at[core, x, :, (j - 1) * rows : j * rows],
                        weight.at[j // 2, x * zs : (x + 1) * zs, :, first : first + SIDE],
                    )
                    for x in range(links.xs)
                ],
            )
    for head in range(heads):
        sends[2, 0, head].wait_recv()
        sends[3, 1, head].wait_recv()
    fetch.wait("weight")
    w_own = weight[0, 0:half].reshape(SIDE, full)
    w_far = weight[1].reshape(width, full)
    fetch.start("quarter", (weight.at[0, 0:half], quarter_h))
    for i in range(2):
        rows = slice(i * HALF, (i + 1) * HALF)
        hidden[rows] = (
            tokens_all[rows].astype(f32)
            + nn(contexts[rows, 0:SIDE], w_own)
            + nn(contexts[rows, 2 * SIDE :], w_far)
        )
    for copy in relays:
        copy.wait_recv()
    w_peer = weight[0, half:].reshape(SIDE, full)
    for i in range(2):
        rows = slice(i * HALF, (i + 1) * HALF)
        value = hidden[rows] + nn(contexts[rows, SIDE : 2 * SIDE], w_peer)
        scale = lax.rsqrt(jnp.sum(value * value, axis=1, keepdims=True) * (1.0 / full) + EPS)
        normed_two[rows] = (value * scale * small_all[7:8, :]).astype(bf16)
        if i == 0:
            scale_two[...] = jnp.broadcast_to(scale, (HALF, 128))
            hidden_own[...] = value[:, 0:width]
        fetch.start("out", (normed_two.at[rows], normed_two_h.at[rows]))
    tokens_sent()
    for copy in relays + list(sends.values()):
        copy.wait_send()
    for copy in cot_copies:
        copy.wait()
    shares.done()
    fetch.wait("out", "context", "quarter")


def forward_step(
    tokens,
    cot,
    qkv_weight,
    router_weight,
    attn_gain,
    ffn_gain,
    routes,
    cosine,
    sine,
    seg,
    out_weight,
    gate_weight,
    up_weight,
    down_weight,
):
    xs, zs, cs = dp_sizes()
    pieces = xs * zs
    rows, down_rows = unit_rows()
    width = tokens.shape[1]
    full, total = 2 * width, 2 * HALF
    heads = SIDE // HEAD
    experts, _, hidden = gate_weight.shape
    hid = experts // 2 * hidden
    unit_total = (3 + experts // 2) * rows + down_units(hid) * down_rows
    out = [
        jax.ShapeDtypeStruct((total, full), bf16),
        jax.ShapeDtypeStruct((total, SIDE), bf16),
        jax.ShapeDtypeStruct((total, HEAD), bf16),
        jax.ShapeDtypeStruct((total, HEAD), bf16),
        jax.ShapeDtypeStruct((total, SIDE), bf16),
        jax.ShapeDtypeStruct((full, SIDE + 2 * HEAD), bf16),
        jax.ShapeDtypeStruct((total, full), bf16),
        jax.ShapeDtypeStruct((pieces // 2, rows, full), bf16),
        jax.ShapeDtypeStruct((HALF // 2, width), bf16),
        jax.ShapeDtypeStruct((HALF // 2, width), bf16),
        jax.ShapeDtypeStruct((cs, xs, zs, unit_total, SIDE), bf16),
        jax.ShapeDtypeStruct((8, total), f32),
        jax.ShapeDtypeStruct((total, 128), f32),
        jax.ShapeDtypeStruct((HALF, 128), f32),
        jax.ShapeDtypeStruct((8, full), f32),
        jax.ShapeDtypeStruct((HALF, width), f32),
        jax.ShapeDtypeStruct((HALF, 128), f32),
    ]
    return pl.pallas_call(
        functools.partial(forward_kernel, heads),
        out_shape=tuple(out),
        in_specs=[WHOLE, ANY] + [WHOLE] * 8 + [ANY] * 4,
        out_specs=(ANY,) * 11 + (WHOLE,) * 6,
        scratch_shapes=[
            VMEM((total, full), bf16),
            VMEM((full, SIDE + 2 * HEAD), bf16),
            VMEM((total, full), bf16),
            VMEM((total, SIDE), bf16),
            VMEM((total, HEAD), bf16),
            VMEM((total, HEAD), bf16),
            VMEM((HEAD, total), bf16),
            VMEM((total, full), bf16),
            VMEM((2, pieces, rows, full), bf16),
            VMEM((total, full), f32),
            VMEM((total, full), bf16),
            VMEM((8, width), f32),
            VMEM((total, 128), f32),
            VMEM((1, total), f32),
            VMEM((total, 128), f32),
            pltpu.SemaphoreType.DMA((80,)),
            pltpu.SemaphoreType.DMA((80,)),
            pltpu.SemaphoreType.DMA((48,)),
        ],
        compiler_params=pltpu.CompilerParams(
            collective_id=0, has_side_effects=True, vmem_limit_bytes=60 * 2**20
        ),
        name="forward_step",
    )(
        tokens,
        cot,
        qkv_weight,
        router_weight,
        attn_gain,
        ffn_gain,
        routes,
        cosine,
        sine,
        seg,
        out_weight.reshape(pieces, rows, width),
        gate_weight.reshape(experts, pieces, rows, hidden),
        up_weight.reshape(experts, pieces, rows, hidden),
        down_weight.reshape(-1, down_rows, width),
    )


def scatter_group(links, blocks, pass2, pass3, near2, near3, far, out2, out3):
    n2, n3 = links.group(2), links.group(3)
    start, direct = [], []

    def send_own_rows():
        start.append(links.go(blocks(1, 0), near2, n2))
        start.append(links.go(blocks(1, 1), near3, n3))

    def send_other_rows():
        direct.append(links.go(blocks(3, 1), far(3, 1), n3))
        direct.append(links.go(blocks(2, 0), far(2, 0), n2))

    relay = [links.copy(out3, far(3, 0), n3), links.copy(out2, far(2, 1), n2)]

    def forward():
        start[0].wait_recv()
        out3[...] = (pass3[...].astype(f32) + near2[...].astype(f32)).astype(bf16)
        relay[0].start()
        start[1].wait_recv()
        out2[...] = (pass2[...].astype(f32) + near3[...].astype(f32)).astype(bf16)
        relay[1].start()

    def finish():
        for copy in direct + relay:
            copy.wait_recv()

    def sent():
        for copy in start + direct + relay:
            copy.wait_send()

    return send_own_rows, send_other_rows, forward, finish, sent


def group_scratch(width):
    quarter = HALF // 2
    return [
        VMEM((quarter, width), bf16),
        VMEM((quarter, width), bf16),
        VMEM((HALF, width), bf16),
        VMEM((HALF, width), bf16),
        VMEM((quarter, width), bf16),
        VMEM((quarter, width), bf16),
    ]


def norm_back_rows(grad, gain, values, scale, inner, width):
    return scale * (grad * gain - values * (scale * inner * (1.0 / width)))


def column(row_vector):
    return jnp.broadcast_to(row_vector, (128, row_vector.shape[1])).T


def half_swap(v):
    return jnp.concatenate([v[:, HALF:], v[:, :HALF]], axis=1)


def reduce_kernel(
    partial,
    vectors,
    hidden_h,
    cot_h,
    scale_h,
    gain,
    normed_h,
    grads_h,
    weighted_h,
    cot_all_h,
    far_2,
    far_3,
    hidden_grad_h,
    hidden_low,
    vector_sums,
    gain_part,
    shard,
    hidden_grad,
    hidden,
    cot,
    scale,
    normed,
    grads,
    weighted,
    cot_all,
    normed_t,
    mine_p,
    pass2,
    pass3,
    near2,
    near3,
    far2,
    far3,
    out2,
    out3,
    vec_in,
    low,
    up_part,
    down_part,
    *rest,
):
    up_scratch, down_scratch = rest[0:5], rest[5:10]
    send, recv, sems, local = rest[10:]
    links = Links(send, recv)
    width = hidden_grad.shape[1]
    step = HALF // 4
    quarter = HALF // 2
    count, _, both = grads.shape
    side = both // 2
    fetch = Fetch(sems)
    fetch.start("normed", (normed_h, normed))
    fetch.start("grads", *[(grads_h.at[e], grads.at[e]) for e in range(count)])
    fetch.start("down", (weighted_h, weighted), (cot_all_h, cot_all))
    fetch.start(
        "pass",
        (partial.at[HALF + quarter :, 0:width], pass2),
        (partial.at[HALF : HALF + quarter, width:], pass3),
    )
    fetch.start(
        "own",
        (partial.at[0:HALF, 0:width], mine_p),
        (hidden_h, hidden),
        (cot_h, cot),
        (scale_h, scale),
        (far_2, far2.at[0:quarter]),
        (far_3, far3.at[quarter:]),
    )
    links.greet([links.group(k) for k in (1, 2, 3)] + links.plane())

    vec_copies = [links.go(vectors, vec_in.at[k - 1], links.group(k)) for k in (1, 2, 3)]

    def chunk(c):
        def blocks(k, h):
            first = (HALF if k & 2 else 0) + h * quarter + c * step
            cols = slice((k & 1) * width, (k & 1) * width + width)
            return partial.at[first : first + step, cols]

        def far(k, h):
            first = h * quarter + c * step
            return (far2 if k == 2 else far3).at[first : first + step]

        here = slice(c * step, (c + 1) * step)
        return scatter_group(
            links,
            blocks,
            pass2.at[here],
            pass3.at[here],
            near2.at[here],
            near3.at[here],
            far,
            out2.at[here],
            out3.at[here],
        )

    chunks = [chunk(c) for c in range(2)]
    own_rows, _, forward, finish, sent = [
        [functions[i] for functions in chunks] for i in range(5)
    ]
    own_rows[0]()
    own_rows[1]()

    kept = up_scratch[4].shape[0]
    up = PlaneSum(
        links,
        lambda ab, core: [(slice(None), up_part.at[core, ab])],
        *up_scratch,
        shard.at[:, 0:kept],
        count,
    )
    down = PlaneSum(
        links,
        lambda ab, core: [(slice(None), down_part.at[core, ab])],
        *down_scratch,
        shard.at[:, kept:],
        count,
    )
    up.start()
    down.start()
    fetch.wait("normed")
    for i in range(4):
        rows = slice(i * 256, (i + 1) * 256)
        normed_t[:, rows] = normed[rows].T
    state = {}

    def prepare():
        for copy in vec_copies:
            copy.wait()
        vec = vectors[...] + vec_in[0] + half_swap(vec_in[1] + vec_in[2])
        vector_sums[...] = vec
        fetch.wait("own")
        state["inner"] = column(vec[6:7, 0:HALF])[:, 0:1]
        state["part"] = jnp.zeros((8, width), f32)
        state["gain"] = gain[...].reshape(1, width)

    def norm_back(c):
        for h in range(2):
            first = h * quarter + c * step
            rows = slice(first, first + step)
            grad = mine_p[rows].astype(f32) + far2[rows].astype(f32) + far3[rows].astype(f32)
            values = hidden[rows]
            scale_rows = scale[rows, 0:1]
            back = norm_back_rows(
                grad, state["gain"], values, scale_rows, state["inner"][rows], 2 * width
            )
            back = back + cot[rows].astype(f32)
            hidden_grad[rows] = back
            low[rows] = back.astype(bf16)
            state["part"] = state["part"] + jnp.sum(
                (grad * values * scale_rows).reshape(step // 8, 8, width), axis=0
            )

    def gather(c):
        def own(h):
            first = h * quarter + c * step
            return low.at[first : first + step]

        def dst(k, h):
            first = (HALF if k & 2 else 0) + h * quarter + c * step
            cols = slice((k & 1) * width, (k & 1) * width + width)
            return hidden_low.at[first : first + step, cols]

        return gather_group(links, own, dst)

    gathers = []

    def finish_chunk(c):
        finish[c]()
        norm_back(c)
        gathers.append(gather(c))

    fetch.wait("grads", "down", "pass")
    pending = []
    for e in range(count):
        for ab in range(2):
            rows = slice(e * width, (e + 1) * width)
            part = nn(normed_t[ab * width : (ab + 1) * width], grads[e])
            for which in range(2):
                up_part[which, ab, rows] = part[:, which * side : (which + 1) * side].astype(
                    bf16
                )
            up.core_send(ab, e)
            rows = slice(e * side, (e + 1) * side)
            part = tn(weighted[:, rows], cot_all[:, ab * width : (ab + 1) * width])
            for which in range(2):
                down_part[which, ab, rows] = part[:, which * side : (which + 1) * side].astype(
                    bf16
                )
            down.core_send(ab, e)
            if e == 1:
                forward[ab]()
            if pending:
                up.first_send(*pending[0])
                down.first_send(*pending[0])
            pending[:] = [(ab, e)]
    prepare()
    finish_chunk(0)
    up.first_send(*pending[0])
    down.first_send(*pending[0])
    finish_chunk(1)
    keep = pltpu.make_async_copy(hidden_grad, hidden_grad_h, local.at[1])
    keep.start()
    gain_part[...] = jnp.broadcast_to(jnp.sum(state["part"], axis=0, keepdims=True), (8, width))
    mine = pltpu.make_async_copy(low, hidden_low.at[0:HALF, 0:width], local.at[0])
    mine.start()
    gathers[0][0]()
    for ab in range(2):
        up.second_send(ab)
        down.second_send(ab)
    gathers[1][0]()
    for ab in (1, 0):
        up.last_sum(ab)
        down.last_sum(ab)
    up.wait_peer()
    down.wait_peer()
    mine.wait()
    keep.wait()
    for c in range(2):
        for wait in gathers[c][1:]:
            wait()
        sent[c]()
    up.done()
    down.done()


def reduce_step(
    partial, vectors, hidden, cot, scale, gain, normed, grads, weighted, cot_all, far_2, far_3
):
    xs, zs, _ = dp_sizes()
    width = hidden.shape[1]
    count, total, both = grads.shape
    side = both // 2
    up_rows, down_rows = count * width, count * side
    quarter = HALF // 2
    return pl.pallas_call(
        reduce_kernel,
        out_shape=(
            jax.ShapeDtypeStruct((HALF, width), f32),
            jax.ShapeDtypeStruct((2 * HALF, 2 * width), bf16),
            jax.ShapeDtypeStruct(vectors.shape, f32),
            jax.ShapeDtypeStruct((8, width), f32),
            jax.ShapeDtypeStruct(
                (2, pad16(up_rows // (xs * zs)) + pad16(down_rows // (xs * zs)), side), bf16
            ),
        ),
        in_specs=[ANY, WHOLE, ANY, ANY, ANY, WHOLE] + [ANY] * 6,
        out_specs=(ANY, ANY, WHOLE, WHOLE, WHOLE),
        scratch_shapes=[
            VMEM((HALF, width), f32),
            VMEM((HALF, width), f32),
            VMEM((HALF, width), bf16),
            VMEM((HALF, 128), f32),
            VMEM(normed.shape, bf16),
            VMEM(grads.shape, bf16),
            VMEM(weighted.shape, bf16),
            VMEM(cot_all.shape, bf16),
            VMEM((2 * width, total), bf16),
            VMEM((HALF, width), bf16),
            VMEM((quarter, width), bf16),
            VMEM((quarter, width), bf16),
        ]
        + group_scratch(width)
        + [
            VMEM((3,) + vectors.shape, f32),
            VMEM((HALF, width), bf16),
            VMEM((2, 2, up_rows, side), bf16),
            VMEM((2, 2, down_rows, side), bf16),
        ]
        + plane_scratch(up_rows, side)
        + plane_scratch(down_rows, side)
        + [
            pltpu.SemaphoreType.DMA((112,)),
            pltpu.SemaphoreType.DMA((112,)),
            pltpu.SemaphoreType.DMA((16,)),
            pltpu.SemaphoreType.DMA((2,)),
        ],
        compiler_params=pltpu.CompilerParams(
            collective_id=2, has_side_effects=True, vmem_limit_bytes=60 * 2**20
        ),
        name="reduce_step",
    )(partial, vectors, hidden, cot, scale, gain, normed, grads, weighted, cot_all, far_2, far_3)


def attn_back_kernel(
    heads,
    q_h,
    k_h,
    v_h,
    lse,
    seg,
    cos_h,
    sin_h,
    context_h,
    hidden_low_h,
    out_weight,
    qkv_h,
    normed_h,
    small_all,
    gates,
    vec_sums,
    ffn_part,
    tokens_h,
    scale_h,
    gain,
    hidden_grad_h,
    layer_h,
    hidden_h,
    expert_shard,
    input_grad,
    layer_out,
    small_out,
    attn_sums,
    expert_sums,
    q,
    k,
    v,
    cos_ref,
    sin_ref,
    context,
    hidden_low,
    qkv,
    normed,
    tokens,
    scale,
    hidden_grad,
    kt,
    do,
    dk,
    dv,
    grads,
    partial,
    qkv_part,
    out_part,
    near2,
    near3,
    far2,
    far3,
    out2,
    out3,
    layer_mine,
    layer_pass2,
    layer_pass3,
    hidden,
    lnear2,
    lnear3,
    lfar2,
    lfar3,
    lout2,
    lout3,
    vec_own,
    vec_in,
    small_own,
    small_in,
    attn_shard,
    segk,
    segq,
    *rest,
):
    attn_scratch = rest[0:5]
    send, recv, sems, local = rest[5:]
    links = Links(send, recv)
    xs, zs, cs = links.xs, links.zs, links.cs
    row = links.row
    total, full = normed.shape
    width = full // 2
    quarter = HALF // 2
    head_scale = HEAD**-0.5
    fetch = Fetch(sems)
    fetch.start("out", (context_h, context), (hidden_low_h, hidden_low))
    fetch.start("attention", (q_h, q), (k_h, k), (v_h, v))
    fetch.start("turn", (cos_h, cos_ref), (sin_h, sin_ref))
    fetch.start("normed", (normed_h, normed))
    fetch.start("qkv", (qkv_h, qkv))
    fetch.start(
        "own",
        (tokens_h, tokens),
        (scale_h, scale),
        (hidden_grad_h, hidden_grad),
    )
    fetch.start(
        "layer",
        (layer_h.at[0:HALF, 0:width], layer_mine),
        (layer_h.at[HALF + quarter :, 0:width], layer_pass2),
        (layer_h.at[HALF : HALF + quarter, width:], layer_pass3),
        (hidden_h, hidden),
    )
    links.greet([links.group(k) for k in (1, 2, 3)] + links.plane())

    def layer_blocks(k, h):
        first = (HALF if k & 2 else 0) + h * quarter
        cols = slice((k & 1) * width, (k & 1) * width + width)
        return layer_h.at[first : first + quarter, cols]

    def halves_of(a, b):
        return lambda k, h: (a if k == 2 else b).at[h * quarter : (h + 1) * quarter]

    layer_own, layer_other, layer_forward, layer_finish, layer_sent = scatter_group(
        links,
        layer_blocks,
        layer_pass2,
        layer_pass3,
        lnear2,
        lnear3,
        halves_of(lfar2, lfar3),
        lout2,
        lout3,
    )
    layer_own()
    layer_other()
    segq[...] = seg[...].astype(f32)
    segk[...] = column(segq[...])

    cols_all = qkv.shape[1]

    def parts(ab, core):
        first = ab * width + core * SIDE
        return [
            (slice(0, cols_all), qkv_part.at[at(first, SIDE)]),
            (slice(cols_all, cols_all + SIDE), out_part.at[:, at(first, SIDE, 128)]),
        ]

    attn_sum = PlaneSum(links, parts, *attn_scratch, attn_shard, 1, True)
    attn_sum.start()
    attn_gather = PlaneGather(links, attn_shard, attn_sums, local.at[0])
    expert_gather = PlaneGather(links, expert_shard, expert_sums, local.at[1])
    expert_gather.near(0)
    expert_gather.near(1)
    piece_rows = expert_shard.shape[1]
    cuts = [pad16(piece_rows * i // 4) for i in range(4)] + [piece_rows]

    def spread(i):
        for ab in range(2):
            expert_gather.far(ab, slice(cuts[i], cuts[i + 1]))

    fetch.wait("out")
    out_part[...] = tn(context[...], hidden_low[...]).astype(bf16)
    for ab in range(2):
        attn_sum.core_send(ab, 0, 1)

    for h in range(2):
        rows = at(HALF * jnp.bitwise_xor(row, h), HALF)
        do[h * HALF : (h + 1) * HALF] = nt(hidden_low[rows], out_weight[...]).astype(bf16)
    fetch.wait("attention", "turn")
    spread(0)
    spread(1)
    kt[...] = k[...].astype(f32).T.astype(bf16)
    dk[...] = jnp.zeros_like(dk)
    dv[...] = jnp.zeros_like(dv)

    def back(grad, here):
        return grad * cos_ref[here] - swap_halves(grad) * sin_ref[here]

    def rows_of(i):
        place = i * BLOCK // HALF
        return at(HALF * jnp.bitwise_xor(row, place) + (i * BLOCK - place * HALF), BLOCK, BLOCK)

    inners = []
    for i in range(total // BLOCK):
        first, last = window(i, BLOCK)
        here = slice(i * BLOCK, (i + 1) * BLOCK)
        allowed = allowed_keys(segk, segq, i, first, last)
        rows = rows_of(i)
        inner_q = jnp.zeros((BLOCK, 1), f32)
        for h in range(heads):
            cols = slice(h * HEAD, (h + 1) * HEAD)
            s = nt(k[first:last], q[here, cols]) * head_scale
            s = jnp.where(allowed, s, MASKED)
            p = jnp.exp(s - lse[h : h + 1, here])
            dp = nt(v[first:last], do[here, cols])
            inner = jnp.sum(dp * p, axis=0, keepdims=True)
            ds = (p * (dp - inner)).astype(bf16)
            dq = (nn(kt[:, first:last], ds) * head_scale).T
            inner_q = inner_q + jnp.sum(dq * q[here, cols].astype(f32), axis=1, keepdims=True)
            grads[rows, cols] = back(dq, here).astype(bf16)
            dk[first:last] += nn(ds, q[here, cols]) * head_scale
            dv[first:last] += nn(p.astype(bf16), do[here, cols])
        inners.append(inner_q)

    gate_rows = gates[...].T[0:8, :]
    sums = vec_sums[...]
    mask = lax.broadcasted_iota(jnp.int32, sums.shape, 0) < 6
    sums = jnp.where(mask, sums, 0.0)
    logits_grad = gate_rows * (sums - jnp.sum(gate_rows * sums, axis=0, keepdims=True))
    logits_low = jnp.where(mask, logits_grad, 0.0).astype(bf16)
    router = jnp.where(
        lax.broadcasted_iota(jnp.int32, (8, full), 0) < 6, small_all[...], 0.0
    )
    router_low = router.astype(bf16)
    once = jnp.where((row == 0) & (links.col == 0), 1.0, 0.0)
    fetch.wait("normed")
    router_grad = nn(logits_low, normed[...])
    router_inner = once * jnp.sum(
        logits_low.astype(f32) * nt(router_low, normed[...]), axis=0, keepdims=True
    )
    for i in range(total // BLOCK):
        here = slice(i * BLOCK, (i + 1) * BLOCK)
        rows = rows_of(i)
        key_grad, value_grad = dk[here], dv[here]
        inner = inners[i] + jnp.sum(
            key_grad * k[here].astype(f32) + value_grad * v[here].astype(f32),
            axis=1,
            keepdims=True,
        )
        grads[rows, heads * HEAD : (heads + 1) * HEAD] = back(key_grad, here).astype(bf16)
        grads[rows, (heads + 1) * HEAD :] = value_grad.astype(bf16)
        vec_own[:, rows] = jnp.broadcast_to(inner, (BLOCK, 128)).T[0:8, :]
    vec_own[...] += router_inner
    vec_copies = [links.go(vec_own, vec_in.at[k - 1], links.group(k)) for k in (1, 2, 3)]

    def blocks(k, h):
        first = (HALF if k & 2 else 0) + h * quarter
        cols = slice((k & 1) * width, (k & 1) * width + width)
        return partial.at[first : first + quarter, cols]

    own_rows, other_rows, forward, finish, sent = scatter_group(
        links,
        blocks,
        partial.at[HALF + quarter :, 0:width],
        partial.at[HALF : HALF + quarter, width:],
        near2,
        near3,
        halves_of(far2, far3),
        out2,
        out3,
    )
    fetch.wait("qkv", "layer")
    layer_forward()
    partial[0:HALF] = nt(grads[0:HALF], qkv[...]).astype(bf16)
    own_rows()
    partial[HALF:] = nt(grads[HALF:], qkv[...]).astype(bf16)
    other_rows()

    gain_sums = {}
    for mine in (False, True):
        which = links.core if mine else 1 - links.core
        for ab in range(2):
            first = ab * width + which * SIDE
            part = tn(normed[:, at(first, SIDE, 128)], grads[...])
            rows = at(first, SIDE)
            qkv_part[rows] = part.astype(bf16)
            gain_sum = jnp.sum(part * qkv[rows].astype(f32), axis=1, keepdims=True)
            gain_sums[mine, ab] = jnp.broadcast_to(gain_sum, (SIDE, 128)).T[0:8, :]
            if not mine:
                attn_sum.core_send(ab, 0, 0)
    for ab in range(2):
        attn_sum.first_send(ab)
    spread(2)

    halves = []
    for ab in range(2):
        a, b = gain_sums[True, ab], gain_sums[False, ab]
        first = links.core == 0
        halves.append(jnp.concatenate([jnp.where(first, a, b), jnp.where(first, b, a)], axis=1))
    gain_row = jnp.concatenate(halves, axis=1)
    gain_row = gain_row + once * jnp.sum(router_grad * router, axis=0, keepdims=True)
    gain_row = gain_row / small_all[6:7, :]
    ffn = jnp.concatenate([ffn_part[...], jnp.zeros((8, width), f32)], axis=1)
    index = lax.broadcasted_iota(jnp.int32, (8, full), 0)
    small_own[0] = jnp.where(index < 6, router_grad, jnp.where(index == 6, gain_row, ffn))

    def small_stage(stage):
        if stage < 3:
            base = (0, 1, xs)[stage]
            devices = [
                links.other_core() if stage == 0 else links.place(stage - 1, k)
                for k in range(1, (cs, xs, zs)[stage])
            ]
        else:
            base = xs + zs - 1
            devices = [links.group(k) for k in (1, 2, 3)]
        copies = [
            (links.go(small_own.at[stage], small_in.at[base + i], device), base + i)
            for i, device in enumerate(devices)
        ]

        def done():
            value = small_own[stage]
            came = []
            for copy, i in copies:
                copy.wait()
                came.append(small_in[i])
            if stage < 3:
                for v in came:
                    value = value + v
                small_own[stage + 1] = value
            else:
                swap = came[0] + came[2]
                total_rows = (
                    value + came[1] + jnp.concatenate([swap[:, width:], swap[:, :width]], axis=1)
                )
                eight = lax.broadcasted_iota(jnp.int32, (8, width), 0)
                small_out[...] = jnp.where(
                    eight < 6, value[:, 0:width], total_rows[:, 0:width]
                )

        return done

    done = small_stage(0)
    layer_finish()
    for h in range(4):
        rows = slice(h * 128, (h + 1) * 128)
        layer_out[rows] = (
            hidden[rows]
            + layer_mine[rows].astype(f32)
            + lfar2[rows].astype(f32)
            + lfar3[rows].astype(f32)
        ).astype(bf16)
    done()
    done = small_stage(1)
    expert_gather.swap(slice(0, cuts[2]), 4)
    for ab in range(2):
        attn_sum.second_send(ab)
    spread(3)
    for ab in (1, 0):
        attn_sum.last_sum(ab)
    forward()
    attn_gather.near(0)
    for copy in vec_copies:
        copy.wait()
    vec = vec_own[...] + vec_in[0] + half_swap(vec_in[1] + vec_in[2])
    inner = column(vec[6:7, 0:HALF])[:, 0:1]
    fetch.wait("own")
    gain_in = gain[...].reshape(1, width)
    done()
    done = small_stage(2)
    attn_sum.wait_peer()
    attn_gather.near(1)
    attn_gather.far(0)
    expert_gather.swap(slice(cuts[2], piece_rows), 4)
    attn_gather.far(1)
    done()
    done = small_stage(3)
    finish()
    for h in range(4):
        rows = slice(h * 128, (h + 1) * 128)
        grad = (
            partial[rows, 0:width].astype(f32)
            + far2[rows].astype(f32)
            + far3[rows].astype(f32)
            + tn(logits_low[:, rows], router_low[:, 0:width])
        )
        input_grad[rows] = hidden_grad[rows] + norm_back_rows(
            grad,
            gain_in,
            tokens[rows].astype(f32),
            scale[rows, 0:1],
            inner[rows],
            full,
        )
    done()
    attn_gather.swap()
    sent()
    layer_sent()
    attn_sum.done()
    expert_gather.done()
    attn_gather.done()


def attn_back(
    q,
    k,
    v,
    lse,
    seg,
    cosine,
    sine,
    context,
    hidden_low,
    out_weight,
    qkv_weight,
    normed,
    small_all,
    gates,
    vec_sums,
    ffn_part,
    tokens,
    scale,
    gain,
    hidden_grad,
    layer_part,
    hidden,
    expert_shard,
):
    xs, zs, cs = dp_sizes()
    total, full = normed.shape
    width = full // 2
    quarter = HALF // 2
    heads = q.shape[1] // HEAD
    cols = qkv_weight.shape[1]
    piece = (2 * SIDE // (xs * zs), (cols + SIDE) // 2)
    return pl.pallas_call(
        functools.partial(attn_back_kernel, heads),
        out_shape=(
            jax.ShapeDtypeStruct((HALF, width), f32),
            jax.ShapeDtypeStruct((HALF, width), bf16),
            jax.ShapeDtypeStruct((8, width), f32),
            jax.ShapeDtypeStruct((cs, 2, xs * zs) + piece, bf16),
            jax.ShapeDtypeStruct((cs, 2, xs * zs) + expert_shard.shape[1:], bf16),
        ),
        in_specs=[ANY] * 3
        + [WHOLE] * 2
        + [ANY] * 4
        + [WHOLE]
        + [ANY] * 2
        + [WHOLE] * 4
        + [ANY] * 2
        + [WHOLE] + [ANY] * 3 + [WHOLE],
        out_specs=(WHOLE, WHOLE, WHOLE, ANY, ANY),
        scratch_shapes=[
            VMEM(q.shape, bf16),
            VMEM(k.shape, bf16),
            VMEM(v.shape, bf16),
            VMEM(cosine.shape, f32),
            VMEM(sine.shape, f32),
            VMEM(context.shape, bf16),
            VMEM(hidden_low.shape, bf16),
            VMEM(qkv_weight.shape, bf16),
            VMEM(normed.shape, bf16),
            VMEM(tokens.shape, bf16),
            VMEM((HALF, 128), f32),
            VMEM(hidden_grad.shape, f32),
            VMEM((HEAD, total), bf16),
            VMEM(q.shape, bf16),
            VMEM(k.shape, f32),
            VMEM(v.shape, f32),
            VMEM((total, cols), bf16),
            VMEM((total, full), bf16),
            VMEM((full, cols), bf16),
            VMEM((SIDE, full), bf16),
        ]
        + group_scratch(width)
        + [
            VMEM((HALF, width), bf16),
            VMEM((quarter, width), bf16),
            VMEM((quarter, width), bf16),
            VMEM((HALF, width), f32),
        ]
        + group_scratch(width)
        + [
            VMEM((8, total), f32),
            VMEM((3, 8, total), f32),
            VMEM((4, 8, full), f32),
            VMEM((xs + zs + 2, 8, full), f32),
            VMEM((2,) + piece, bf16),
            VMEM((total, 128), f32),
            VMEM((1, total), f32),
        ]
        + plane_scratch(SIDE, cols + SIDE, True)
        + [
            pltpu.SemaphoreType.DMA((112,)),
            pltpu.SemaphoreType.DMA((112,)),
            pltpu.SemaphoreType.DMA((24,)),
            pltpu.SemaphoreType.DMA((2, 2)),
        ],
        compiler_params=pltpu.CompilerParams(
            collective_id=3, has_side_effects=True, vmem_limit_bytes=60 * 2**20
        ),
        name="attn_back",
    )(
        q,
        k,
        v,
        lse,
        seg,
        cosine,
        sine,
        context,
        hidden_low,
        out_weight,
        qkv_weight,
        normed,
        small_all,
        gates,
        vec_sums,
        ffn_part,
        tokens,
        scale,
        gain,
        hidden_grad,
        layer_part,
        hidden,
        expert_shard,
    )


def swap_halves(v):
    half = v.shape[-1] // 2
    return jnp.concatenate([v[..., half:], v[..., :half]], axis=-1)


def experts_kernel(
    normed_h,
    cot_own,
    cot_2,
    cot_3,
    gates,
    gate_weight,
    up_weight,
    down_weight,
    units,
    weighted_h,
    grads_h,
    back_h,
    out_h,
    cot_all_h,
    far_2,
    far_3,
    vec_ref,
    normed,
    cot,
    gate_up,
    down,
    weighted,
    grads,
    back,
    out,
    send,
    recv,
    sems,
):
    links = Links(send, recv)
    col = links.col
    count, _, pieces, unit, both = gate_up.shape
    blocks, down_unit, full = down.shape
    width = full // 2
    hidden = both // 2
    quarter = HALF // 2
    other, own = slice(HALF, 2 * HALF), slice(0, HALF)
    fetch = Fetch(sems)
    fetch.start("normed", (normed_h.at[other], normed.at[other]))
    for e in range(count):
        for which, weight in enumerate((gate_weight, up_weight)):
            cols = slice(which * hidden, (which + 1) * hidden)
            fetch.start(
                ("gate_up", e),
                (weight.at[col * count + e], gate_up.at[e, 0, :, :, cols]),
                (
                    units.at[which, :, (3 + e) * unit : (4 + e) * unit],
                    gate_up.at[e, 1, :, :, cols],
                ),
            )
    fetch.start(
        "cot",
        (cot_2, cot.at[HALF + quarter :, 0:width]),
        (cot_3, cot.at[HALF : HALF + quarter, width:]),
        (cot_own, cot.at[own, 0:width]),
    )
    fetch.start("down", (down_weight.at[pl.ds(col * blocks, blocks)], down.at[:, :, 0:width]))
    for j in range(-(-blocks // pieces)):
        n = min(pieces, blocks - j * pieces)
        start = (3 + count) * unit + j * down_unit
        for core in range(2):
            first = width + core * SIDE
            fetch.start(
                "down",
                (
                    units.at[core, 0:n, start : start + down_unit],
                    down.at[j * pieces : j * pieces + n, :, first : first + SIDE],
                ),
            )
    fetch.start("normed_own", (normed_h.at[own], normed.at[own]))
    links.greet([links.group(2), links.group(3)])
    direct = [
        links.go(cot_own.at[0:quarter], cot.at[HALF : HALF + quarter, 0:width], links.group(2)),
        links.go(cot_own.at[quarter:], cot.at[HALF + quarter :, width:], links.group(3)),
    ]
    relays = [
        links.go(cot_3, cot.at[0:quarter, width:], links.group(2)),
        links.go(cot_2, cot.at[quarter:HALF, width:], links.group(3)),
    ]
    fetch.wait("normed")
    all_pres = [[], []]
    for e in range(count):
        fetch.wait(("gate_up", e))
        all_pres[0].append(nn(normed[other], gate_up[e].reshape(full, both)))
    fetch.wait("normed_own")
    for e in range(count):
        all_pres[1].append(nn(normed[own], gate_up[e].reshape(full, both)))
    for step, rows in enumerate((other, own)):
        lanes = lax.broadcasted_iota(jnp.int32, (HALF, 128), 1)
        vec = jnp.zeros((HALF, 128), f32)
        inner = jnp.zeros((HALF, 1), f32)
        pres = all_pres[step]
        if step == 0:
            fetch.wait("cot", "down")
            for copy in direct:
                copy.wait_recv()
        else:
            for copy in relays:
                copy.wait_recv()
        y = cot[rows]
        for e in range(count):
            down_e = down[...].reshape(count, hidden, full)[e]
            here = lanes == col * count + e
            gate = jnp.sum(jnp.where(here, gates[rows], 0.0), axis=1, keepdims=True)
            gate_pre, up_pre = pres[e][:, :hidden], pres[e][:, hidden:]
            sigmoid = 1.0 / (1.0 + jnp.exp(-gate_pre))
            silu = gate_pre * sigmoid
            activated = silu * up_pre
            weighted[rows, e * hidden : (e + 1) * hidden] = (gate * activated).astype(bf16)
            weighted_grad = nt(y, down_e)
            both_terms = activated * weighted_grad
            part = jnp.sum(both_terms, axis=1, keepdims=True)
            vec = vec + jnp.where(here, part, 0.0)
            slope = 1.0 + gate_pre * (1.0 - sigmoid)
            g = gate * weighted_grad
            gate_grad = g * up_pre * (sigmoid * slope)
            up_grad = g * silu
            inner = inner + gate * (
                part + jnp.sum(both_terms * slope, axis=1, keepdims=True)
            )
            grads[e, rows] = jnp.concatenate([gate_grad, up_grad], axis=1).astype(bf16)
        fetch.start("out", *[(grads.at[e, rows], grads_h.at[e, rows]) for e in range(count)])
        fetch.start("out", (weighted.at[rows], weighted_h.at[rows]))
        fetch.start("out", (cot.at[rows], cot_all_h.at[rows]))
        total = None
        for e in range(count):
            term = nt(grads[e, rows], gate_up[e].reshape(full, both))
            total = term if total is None else total + term
        back[rows] = total.astype(bf16)
        if step == 0:
            sums = [
                links.go(back.at[HALF + quarter :, width:], far_3, links.group(3)),
                links.go(back.at[HALF : HALF + quarter, 0:width], far_2, links.group(2)),
            ]
        fetch.start("out", (back.at[rows], back_h.at[rows]))
        out[rows] = nn(weighted[rows], down[...].reshape(count * hidden, full)).astype(bf16)
        fetch.start("out", (out.at[rows], out_h.at[rows]))
        vec = jnp.where(lanes == 6, inner, vec)
        vec_ref[:, rows] = vec.T[0:8, :]
    for copy in direct + relays:
        copy.wait_send()
    for copy in sums:
        copy.wait()
    fetch.wait("out")


def experts_step(
    normed, cot_own, cot_2, cot_3, gates, gate_weight, up_weight, down_weight, units
):
    total, width = normed.shape
    experts, own_width, hidden = gate_weight.shape
    count = experts // 2
    both = 2 * hidden
    hid = count * hidden
    pieces = units.shape[1]
    unit, down_unit = unit_rows()
    return pl.pallas_call(
        experts_kernel,
        out_shape=(
            jax.ShapeDtypeStruct((total, hid), bf16),
            jax.ShapeDtypeStruct((count, total, both), bf16),
            jax.ShapeDtypeStruct((total, width), bf16),
            jax.ShapeDtypeStruct((total, width), bf16),
            jax.ShapeDtypeStruct((total, width), bf16),
            jax.ShapeDtypeStruct((HALF // 2, own_width), bf16),
            jax.ShapeDtypeStruct((HALF // 2, own_width), bf16),
            jax.ShapeDtypeStruct((8, total), f32),
        ),
        in_specs=[ANY] * 4 + [WHOLE] + [ANY] * 4,
        out_specs=(ANY,) * 7 + (WHOLE,),
        scratch_shapes=[
            VMEM((total, width), bf16),
            VMEM((total, width), bf16),
            VMEM((count, 2, pieces, unit, both), bf16),
            VMEM((hid // down_unit, down_unit, width), bf16),
            VMEM((total, hid), bf16),
            VMEM((count, total, both), bf16),
            VMEM((total, width), bf16),
            VMEM((total, width), bf16),
            pltpu.SemaphoreType.DMA((6,)),
            pltpu.SemaphoreType.DMA((6,)),
            pltpu.SemaphoreType.DMA((48,)),
        ],
        compiler_params=pltpu.CompilerParams(
            collective_id=1, has_side_effects=True, vmem_limit_bytes=60 * 2**20
        ),
        name="experts",
    )(
        normed,
        cot_own,
        cot_2,
        cot_3,
        gates,
        gate_weight.reshape(experts, pieces, unit, hidden),
        up_weight.reshape(experts, pieces, unit, hidden),
        down_weight.reshape(-1, down_unit, own_width),
        units,
    )


def window(i, block):
    first = max(0, (i + 1) * block - 512 - block)
    return first, (i + 1) * block


def allowed_keys(segk, segq, i, first, last):
    width = last - first
    keys = lax.broadcasted_iota(jnp.int32, (width, BLOCK), 0) + first
    queries = lax.broadcasted_iota(jnp.int32, (width, BLOCK), 1) + i * BLOCK
    same = segk[first:last, 0:1] == segq[:, i * BLOCK : (i + 1) * BLOCK]
    return (keys <= queries) & same


def finish_kernel(
    col_ref,
    sums,
    input_ref,
    layer_ref,
    small,
    attn_h,
    gate_ref,
    up_ref,
    down_ref,
    input_out,
    layer_out,
    router_ref,
    attn_gain,
    ffn_gain,
    qkv_out,
    out_out,
    attn_sums,
    qkv_grad,
    out_grad,
    sems,
):
    ab, j = pl.program_id(0), pl.program_id(1)
    steps = pl.num_programs(1)
    count, rows = gate_ref.shape[1:3]
    down_rows = down_ref.shape[2]
    fetch = pltpu.make_async_copy(attn_h, attn_sums, sems.at[0])
    store = [
        pltpu.make_async_copy(qkv_grad, qkv_out, sems.at[1]),
        pltpu.make_async_copy(out_grad, out_out, sems.at[2]),
    ]

    @pl.when((ab == 0) & (j == 0))
    def _():
        fetch.start()

    cores, _, pieces = sums.shape[:3]
    step, down_step = count * rows // pieces, count * down_rows // pieces
    first = pad16(step)
    for which, ref in enumerate((gate_ref, up_ref)):
        block = sums[which, 0, :, 0:step].astype(f32)
        ref[0] = block.reshape(count, rows, SIDE)
    for core in range(cores):
        block = sums[core, 0, :, first : first + down_step].astype(f32)
        down_ref[0, :, :, core * SIDE : (core + 1) * SIDE] = block.reshape(
            count, down_rows, SIDE
        )
    input_out[...] = input_ref[...]
    layer_out[...] = layer_ref[...]

    @pl.when((ab == 1) & (j == 0))
    def _():
        fetch.wait()
        col = col_ref[0]
        cores, _, pieces = attn_sums.shape[:3]
        kept_rows = SIDE // pieces
        middle = attn_sums.shape[4]
        pair = middle - SIDE
        for core in range(cores):
            kept = None
            here = slice(core * SIDE, (core + 1) * SIDE)
            for part in range(2):
                half = col if part == 0 else 1 - col
                block = attn_sums[core, part].astype(f32)
                left = block[:, 0:kept_rows].reshape(SIDE, middle)
                right = block[:, kept_rows:].reshape(SIDE, middle)
                qkv_grad[here, at(half * SIDE, SIDE, 128)] = left[:, 0:SIDE]
                out_grad[at(half * SIDE, SIDE), here] = right[:, pair:]
                both = jnp.concatenate([left[:, SIDE:], right[:, 0:pair]], axis=1)
                kept = both if kept is None else kept + both
            qkv_grad[here, 2 * SIDE :] = kept
        for copy in store:
            copy.start()
        value = small[...]
        attn_gain[...] = value[6:7].reshape(attn_gain.shape)
        ffn_gain[...] = value[7:8].reshape(ffn_gain.shape)
        router_ref[...] = value[0 : router_ref.shape[0]]

    @pl.when((ab == 1) & (j == steps - 1))
    def _():
        for copy in store:
            copy.wait()


def finish_step(sums, input_grad, layer_out, small, attn_sums, col, experts):
    xs, zs, cs = dp_sizes()
    piece = sums.shape[-2]
    own_rows, width = input_grad.shape
    part = own_rows // (2 * xs)
    cols = SIDE + 2 * HEAD
    count = experts // 2

    def out_spec(rows, width):
        return pl.BlockSpec(
            (1, count, rows, width),
            lambda ab, j, col_ref: (jnp.where(ab == 0, col_ref[0], 1 - col_ref[0]), 0, j, 0),
        )

    rows_spec = pl.BlockSpec((part, width), lambda ab, j, col_ref: (ab * xs + j, 0))

    def whole(shape):
        return pl.BlockSpec(shape, lambda ab, j, col_ref: (0,) * len(shape))

    return pl.pallas_call(
        finish_kernel,
        grid_spec=pltpu.PrefetchScalarGridSpec(
            num_scalar_prefetch=1,
            grid=(2, xs),
            in_specs=[
                pl.BlockSpec(
                    (cs, 1, zs, piece, SIDE), lambda ab, j, col_ref: (0, ab, j, 0, 0)
                ),
                rows_spec,
                rows_spec,
                whole(small.shape),
                ANY,
            ],
            out_specs=(
                out_spec(width // xs, SIDE),
                out_spec(width // xs, SIDE),
                out_spec(SIDE // xs, width),
                rows_spec,
                rows_spec,
                whole((experts, width)),
                whole((width,)),
                whole((width,)),
                ANY,
                ANY,
            ),
            scratch_shapes=[
                VMEM(attn_sums.shape, bf16),
                VMEM((2 * SIDE, SIDE + cols), f32),
                VMEM((2 * SIDE, 2 * SIDE), f32),
                pltpu.SemaphoreType.DMA((3,)),
            ],
        ),
        out_shape=(
            jax.ShapeDtypeStruct((2, count, width, SIDE), f32),
            jax.ShapeDtypeStruct((2, count, width, SIDE), f32),
            jax.ShapeDtypeStruct((2, count, SIDE, width), f32),
            jax.ShapeDtypeStruct(input_grad.shape, f32),
            jax.ShapeDtypeStruct(layer_out.shape, bf16),
            jax.ShapeDtypeStruct((experts, width), f32),
            jax.ShapeDtypeStruct((width,), f32),
            jax.ShapeDtypeStruct((width,), f32),
            jax.ShapeDtypeStruct((2 * SIDE, SIDE + cols), f32),
            jax.ShapeDtypeStruct((2 * SIDE, 2 * SIDE), f32),
        ),
        compiler_params=pltpu.CompilerParams(vmem_limit_bytes=56 * 2**20),
        name="finish",
    )(col.reshape(1), sums, input_grad, layer_out, small, attn_sums)


def turn_tables(total):
    steps_up = np.arange(HEAD // 2, dtype=np.float32) * np.float32(2.0 / HEAD)
    inverse = np.exp(np.float32(-math.log(ROPE_BASE)) * steps_up)
    angles = (np.arange(total, dtype=np.float32)[:, None] * inverse[None, :]).astype(np.float64)
    cosine, sine = np.cos(angles), np.sin(angles)
    return (
        np.concatenate([cosine, cosine], axis=1).astype(np.float32),
        np.concatenate([-sine, sine], axis=1).astype(np.float32),
    )


def local(
    tokens,
    cotangent,
    attn_gain,
    ffn_gain,
    qkv_weight,
    out_weight,
    router_weight,
    gate_weight,
    up_weight,
    down_weight,
    routes,
    segments,
):
    col = lax.axis_index("col")
    xs, zs, cs = dp_sizes()
    own_rows, own_width = tokens.shape
    experts, _, hidden = gate_weight.shape
    pieces = xs * zs
    cosine, sine = turn_tables(2 * own_rows)
    seg = segments[None]
    (
        normed_one,
        queries,
        keys,
        values,
        context,
        qkv_local,
        normed_two,
        out_quarter,
        cot_2,
        cot_3,
        units,
        lse,
        gates,
        scale_one,
        small_all,
        hidden_own,
        scale_two,
    ) = forward_step(
        tokens,
        cotangent,
        qkv_weight,
        router_weight.T,
        attn_gain,
        ffn_gain,
        routes.T,
        cosine,
        sine,
        seg,
        out_weight,
        gate_weight,
        up_weight,
        down_weight,
    )
    (
        weighted,
        pre_grads,
        normed_two_part,
        layer_part,
        cot_all,
        far_2,
        far_3,
        expert_vec,
    ) = experts_step(
        normed_two,
        cotangent,
        cot_2,
        cot_3,
        gates,
        gate_weight,
        up_weight,
        down_weight,
        units.reshape((cs, pieces) + units.shape[3:]),
    )
    hidden_grad, hidden_low, vec_sums, ffn_part, shard = reduce_step(
        normed_two_part,
        expert_vec,
        hidden_own,
        cotangent,
        scale_two,
        ffn_gain,
        normed_two,
        pre_grads,
        weighted,
        cot_all,
        far_2,
        far_3,
    )
    input_grad, layer_out, small_sums, attn_sums, expert_sums = attn_back(
        queries,
        keys,
        values,
        lse,
        seg,
        cosine,
        sine,
        context,
        hidden_low,
        out_quarter.reshape(SIDE, 2 * own_width),
        qkv_local,
        normed_one,
        small_all,
        gates,
        vec_sums,
        ffn_part,
        tokens,
        scale_one,
        attn_gain,
        hidden_grad,
        layer_part,
        hidden_own,
        shard,
    )
    (
        gate_grad,
        up_grad,
        down_grad,
        input_grad,
        layer_out,
        router_grad,
        attn_gain_grad,
        ffn_gain_grad,
        qkv_grad,
        out_grad,
    ) = finish_step(
        expert_sums,
        input_grad,
        layer_out,
        small_sums,
        attn_sums,
        col,
        experts,
    )
    router_grad = router_grad.T
    gate_grad = gate_grad.reshape(experts, own_width, hidden)
    up_grad = up_grad.reshape(experts, own_width, hidden)
    down_grad = down_grad.reshape(experts, hidden, own_width)
    return (
        layer_out,
        input_grad,
        attn_gain_grad,
        ffn_gain_grad,
        qkv_grad,
        out_grad,
        router_grad,
        gate_grad,
        up_grad,
        down_grad,
    )


def solution(mesh):
    in_specs = (
        P(("dp", "row"), "col"),
        P(("dp", "row"), "col"),
        P("col"),
        P("col"),
        P("col", "row"),
        P("row", "col"),
        P("col", None),
        P(None, "col", "row"),
        P(None, "col", "row"),
        P(None, "row", "col"),
        P("dp", None),
        P("dp"),
    )
    out_specs = (
        P(("dp", "row"), "col"),
        P(("dp", "row"), "col"),
        P("col"),
        P("col"),
        P("col", "row"),
        P("row", "col"),
        P("col", None),
        P(None, "col", "row"),
        P(None, "col", "row"),
        P(None, "row", "col"),
    )
    return jax.shard_map(local, mesh=mesh, in_specs=in_specs, out_specs=out_specs, check_vma=False)
```

```python
import functools
import math

import jax
import jax.numpy as jnp
import numpy as np
from jax import lax
from jax.experimental import pallas as pl
from jax.experimental.pallas import tpu as pltpu
from jax.sharding import PartitionSpec as P

f32 = jnp.float32
bf16 = jnp.bfloat16

HEAD = 128
GROUP_HEADS = 6
EPS = 1e-06
ROPE_BASE = 10000.0
MASKED = -1e30
BLOCK = 256


MESH = pl.DeviceIdType.MESH
VMEM = pltpu.VMEM
ANY = pl.BlockSpec(memory_space=pl.ANY)
WHOLE = pl.BlockSpec(memory_space=pltpu.VMEM)
HALF = 512
SIDE = 384


def dp_sizes():
    total = lax.axis_size("dp")
    cores = 2 if total % 2 == 0 else 1
    side = math.isqrt(total // cores)
    return side, side, cores


def dp_place():
    xs, zs, cs = dp_sizes()
    d = lax.axis_index("dp")
    return d // (zs * cs), (d // cs) % zs, d % cs


def nt(a, b):
    return lax.dot_general(a, b, (((1,), (1,)), ((), ())), preferred_element_type=f32)


def nn(a, b):
    return lax.dot_general(a, b, (((1,), (0,)), ((), ())), preferred_element_type=f32)


def tn(a, b):
    return lax.dot_general(a, b, (((0,), (0,)), ((), ())), preferred_element_type=f32)


class Links:
    def __init__(self, send, recv):
        self.send, self.recv = send, recv
        self.used = 0
        self.dp = lax.axis_index("dp")
        self.row = lax.axis_index("row")
        self.col = lax.axis_index("col")
        self.xs, self.zs, self.cs = dp_sizes()
        self.x, self.z, self.core = dp_place()

    def group(self, k):
        row = 1 - self.row if k & 2 else self.row
        col = 1 - self.col if k & 1 else self.col
        return (self.dp, row, col)

    def other_core(self):
        return (self.dp + 1 - 2 * self.core, self.row, self.col)

    def place(self, axis, k):
        x, z = self.x, self.z
        if axis == 0:
            x = (x + k) % self.xs
        else:
            z = (z + k) % self.zs
        return ((x * self.zs + z) * self.cs + self.core, self.row, self.col)

    def greet(self, devices):
        barrier = pltpu.get_barrier_semaphore()
        for device in devices:
            pl.semaphore_signal(barrier, inc=1, device_id=device, device_id_type=MESH)
        pl.semaphore_wait(barrier, len(devices))

    def plane(self):
        return (
            ([self.other_core()] if self.cs == 2 else [])
            + [self.place(0, k) for k in range(1, self.xs)]
            + [self.place(1, k) for k in range(1, self.zs)]
        )

    def copy(self, src, dst, device):
        i = self.used
        self.used += 1
        return pltpu.make_async_remote_copy(
            src_ref=src,
            dst_ref=dst,
            send_sem=self.send.at[i],
            recv_sem=self.recv.at[i],
            device_id=device,
            device_id_type=MESH,
        )

    def go(self, src, dst, device):
        copy = self.copy(src, dst, device)
        copy.start()
        return copy


def at(start, size, step=16):
    return pl.ds(pl.multiple_of(start, step), size)


class Fetch:
    def __init__(self, sems):
        self.sems = sems
        self.used = 0
        self.named = {}

    def start(self, name, *pairs):
        copies = self.named.setdefault(name, [])
        for src, dst in pairs:
            copy = pltpu.make_async_copy(src, dst, self.sems.at[self.used])
            self.used += 1
            copy.start()
            copies.append(copy)

    def wait(self, *names):
        for name in names:
            for copy in self.named.pop(name):
                copy.wait()


def pad16(n):
    return -(-n // 16) * 16


class PlaneSum:
    def __init__(
        self, links, parts, came, in1, piece, in2, peer, shard, groups=1, fold=False, near=None
    ):
        self.links, self.parts, self.came, self.in1 = links, parts, came, in1
        self.fold, self.near = fold, near
        self.ring = {}
        self.piece, self.in2, self.peer, self.shard = piece, in2, peer, shard
        self.sizes = (links.xs, links.zs)
        self.places = (links.x, links.z)
        self.sent = []
        self.first, self.second, self.core = {}, {}, {}
        self.groups = groups
        self.group_rows = came.shape[1] // groups
        self.chunk = self.group_rows // links.xs
        self.rows2 = groups * self.chunk // links.zs

    def start(self):
        kept, rows = self.rows2 * (2 if self.fold else 1), self.piece.shape[2]
        if kept < rows:
            shape = self.piece.shape
            self.piece[:, :, kept:] = jnp.zeros(shape[:2] + (rows - kept, shape[3]), bf16)

    def core_send(self, ab, g=0, which=0):
        if self.links.cs == 1:
            return
        rows = slice(g * self.group_rows, (g + 1) * self.group_rows)
        cols, part = self.parts(ab, 1 - self.links.core)[which]
        copy = self.links.go(
            part.at[rows], self.came.at[ab, rows, cols], self.links.other_core()
        )
        self.core.setdefault((ab, g), []).append(copy)
        self.sent.append(copy)

    def first_send(self, ab, g=0, which=None):
        copies = self.core.get((ab, g), [])
        for copy in copies:
            copy.wait_recv()
        del copies[:]
        total = self.came.at[ab]
        step = 96
        parts = self.parts(ab, self.links.core)
        chosen = parts if which is None else [parts[which]]
        for cols, mine in chosen:

            @pl.loop(0, self.group_rows // step)
            def _(i):
                here = at(g * self.group_rows + i * step, step)
                total[here, cols] = (
                    total[here, cols].astype(f32) + mine[here].astype(f32)
                ).astype(bf16)

        n, place = self.sizes[ab], self.places[ab]
        if self.near is not None and n == 4:
            half = self.chunk // 2
            first = g * self.chunk
            right, left = self.links.place(ab, 1), self.links.place(ab, 3)

            def rows_of(j, h):
                start = g * self.group_rows + ((place + j) % n) * self.chunk + h * half
                return self.came.at[ab, at(start, half)]

            here = slice(g * half, (g + 1) * half)
            passed = [
                self.links.go(rows_of(2, 0), self.near.at[ab, 0, here], right),
                self.links.go(rows_of(2, 1), self.near.at[ab, 1, here], left),
            ]
            from_left, from_right = self.in1.at[ab, 0], self.in1.at[ab, 1]
            top, end = slice(first, first + half), slice(first + half, first + self.chunk)
            direct = [
                self.links.go(rows_of(1, 1), from_left.at[end], right),
                self.links.go(rows_of(3, 0), from_right.at[top], left),
            ]
            self.ring[ab, g] = (
                passed,
                rows_of,
                here,
                self.links.copy(rows_of(1, 0), from_left.at[top], right),
                self.links.copy(rows_of(3, 1), from_right.at[end], left),
            )
            self.sent += passed + direct
            self.first[ab, g, 1] = direct
            return
        cols = slice(None) if which is None else parts[which][0]
        for k in range(1, n):
            j = (place + k) % n
            copy = self.links.go(
                self.came.at[ab, at(g * self.group_rows + j * self.chunk, self.chunk), cols],
                self.in1.at[ab, k - 1, g * self.chunk : (g + 1) * self.chunk, cols],
                self.links.place(ab, k),
            )
            self.first.setdefault((ab, g, k), []).append(copy)
            self.sent.append(copy)

    def relay(self, ab, g=0):
        if (ab, g) not in self.ring:
            return
        passed, rows_of, here, to_right, to_left = self.ring[ab, g]
        for i, (j, h, copy) in enumerate(((1, 0, to_right), (3, 1, to_left))):
            passed[i].wait_recv()
            mine = rows_of(j, h)
            mine[...] = (mine[...].astype(f32) + self.near[ab, i, here].astype(f32)).astype(bf16)
            copy.start()
            self.sent.append(copy)
            self.first[ab, g, 2 + i] = [copy]

    def second_send(self, ab):
        n, place = self.sizes[ab], self.places[ab]
        owns = []
        for g in range(self.groups):
            own = self.came[ab, at(g * self.group_rows + place * self.chunk, self.chunk)].astype(
                f32
            )
            for k in range(1, n):
                for copy in self.first[ab, g, k]:
                    copy.wait_recv()
            for k in range(1, 3 if (ab, g) in self.ring else n):
                own = own + self.in1[ab, k - 1, g * self.chunk : (g + 1) * self.chunk].astype(
                    f32
                )
            owns.append(own)
        own = owns[0] if self.groups == 1 else jnp.concatenate(owns, axis=0)
        kept = self.rows2
        n, place = self.sizes[1 - ab], self.places[1 - ab]
        for j in range(n):
            block = own[j * kept : (j + 1) * kept]
            if self.fold:
                middle = block.shape[1] // 2
                block = jnp.concatenate([block[:, :middle], block[:, middle:]], axis=0)
            self.piece[ab, j, 0 : block.shape[0]] = block.astype(bf16)
        for k in range(1, n):
            j = (place + k) % n
            copy = self.links.go(
                self.piece.at[ab, j], self.in2.at[ab, k - 1], self.links.place(1 - ab, k)
            )
            self.second[ab, k] = copy
            self.sent.append(copy)

    def last_sum(self, ab):
        n, place = self.sizes[1 - ab], self.places[1 - ab]
        value = self.piece[ab, place].astype(f32)
        for k in range(1, n):
            self.second[ab, k].wait_recv()
            value = value + self.in2[ab, k - 1].astype(f32)
        if ab == 0:
            self.shard[0] = value.astype(bf16)
        else:
            self.peer[...] = value.astype(bf16)
            self.swap = self.links.go(self.peer, self.shard.at[1], self.links.group(1))

    def wait_peer(self):
        self.swap.wait()

    def done(self):
        for copy in self.sent:
            copy.wait_send()


class PlaneGather:
    def __init__(self, links, shard, sums, local):
        self.links, self.shard, self.sums, self.local = links, shard, sums, local
        self.relayed = []
        self.sizes = (links.xs, links.zs)
        self.home, self.first, self.second, self.last = {}, {}, [], []
        self.relays = []

    def near(self, ab):
        links = self.links
        x, z = links.x, links.z
        index = (x * links.zs + z) if ab == 0 else (z * links.xs + x)
        here = self.sums.at[links.core, ab, index]
        copy = pltpu.make_async_copy(self.shard.at[ab], here, self.local.at[ab])
        copy.start()
        self.home[ab] = copy
        self.first[ab] = [
            links.go(self.shard.at[ab], here, links.place(1 - ab, k))
            for k in range(1, self.sizes[1 - ab])
        ]

    def far(self, ab, rows=slice(None), ring=False):
        links = self.links
        if ab in self.home:
            for copy in self.first[ab]:
                copy.wait()
            self.home.pop(ab).wait()
        n = self.sizes[1 - ab]
        place = links.x if ab == 0 else links.z
        block = self.sums.at[links.core, ab, pl.ds(place * n, n), rows]
        ring = ring and self.sizes[ab] == 4
        copies = [
            links.go(block, block, links.place(ab, k))
            for k in ((1, 3) if ring else range(1, self.sizes[ab]))
        ]
        self.second.append(copies)
        if ring:
            self.relays.append((ab, rows, copies))

    def relay(self):
        links = self.links
        for ab, rows, copies in self.relays[:2]:
            n = self.sizes[1 - ab]
            place = links.x if ab == 0 else links.z
            half = n // 2
            passed = []
            for i, (k, to) in enumerate(((3, 1), (1, 3))):
                copies[i].wait_recv()
                first = ((place + k) % 4) * n + i * half
                block = self.sums.at[links.core, ab, pl.ds(first, half), rows]
                passed.append(links.go(block, block, links.place(ab, to)))
            self.relayed.append((copies, passed))
        del self.relays[:2]

    def swap(self, rows=slice(None), count=2):
        links = self.links
        for copies in self.second[:count]:
            passed = [p for c, p in self.relayed if c is copies]
            for copy in copies:
                copy.wait_send()
                if not passed:
                    copy.wait_recv()
            for copy in passed[0] if passed else ():
                copy.wait()
        del self.second[:count]
        if links.cs == 2:
            block = self.sums.at[links.core, :, :, rows]
            self.last.append(links.go(block, block, links.other_core()))

    def done(self):
        for copy in self.last:
            copy.wait()


def plane_scratch(rows, width, fold=False):
    xs, zs, _ = dp_sizes()
    n1, n2 = max(xs - 1, 1), max(zs - 1, 1)
    kept = rows // (xs * zs)
    shape = (2 * kept, width // 2) if fold else (pad16(kept), width)
    return [
        VMEM((2, rows, width), bf16),
        VMEM((2, n1, rows // xs, width), bf16),
        VMEM((2, zs) + shape, bf16),
        VMEM((2, n2) + shape, bf16),
        VMEM(shape, bf16),
    ]


def gather_group(links, own, dst):
    first = {}
    for k, order in ((2, (1, 0)), (3, (0, 1))):
        for h in order:
            first[k, h] = links.copy(own(h), dst(k, h), links.group(k))
    for key in ((2, 1), (3, 0), (2, 0), (3, 1)):
        first[key].start()
    relay = [
        links.copy(dst(3, 0), dst(1, 0), links.group(2)),
        links.copy(dst(2, 1), dst(1, 1), links.group(3)),
    ]

    def forward():
        first[3, 0].wait_recv()
        relay[0].start()
        first[2, 1].wait_recv()
        relay[1].start()

    def near():
        first[2, 0].wait_recv()
        first[3, 1].wait_recv()

    def far():
        for copy in relay:
            copy.wait_recv()

    def sent():
        for copy in list(first.values()) + relay:
            copy.wait_send()

    return forward, near, far, sent


def unit_rows():
    xs, zs, _ = dp_sizes()
    return 768 // (xs * zs), min(SIDE, 768 // (xs * zs))


def down_units(hid):
    xs, zs, _ = dp_sizes()
    return -(-(hid // unit_rows()[1]) // (xs * zs))


class Units:
    def __init__(self, links, units, out_weight, gate_weight, up_weight, down_weight):
        self.links, self.units = links, units
        rows, down_rows = unit_rows()
        xs, zs = links.xs, links.zs
        pieces = xs * zs
        place = links.x * zs + links.z
        lanes = at(links.core * SIDE, SIDE, 128)
        home = units.at[links.core, links.x, links.z]
        self.out_rows = 3 * rows
        self.cut = 4 * rows
        self.total = units.shape[3]
        self.fetch = []
        for k in (1, 2, 3):
            col = 1 - links.col if k & 1 else links.col
            index = (place + col * (pieces // 2)) % pieces
            self.fetch.append(
                links.go(
                    out_weight.at[index, :, lanes],
                    home.at[(k - 1) * rows : k * rows],
                    links.group(k),
                )
            )
        count = gate_weight.shape[0] // 2
        first = (1 - links.col) * count
        for e in range(count):
            i = links.used
            links.used += 1
            to = home.at[(3 + e) * rows : (4 + e) * rows]
            either = [
                pltpu.make_async_remote_copy(
                    src_ref=weight.at[first + e, place],
                    dst_ref=to,
                    send_sem=links.send.at[i],
                    recv_sem=links.recv.at[i],
                    device_id=links.group(1),
                    device_id_type=MESH,
                )
                for weight in (gate_weight, up_weight)
            ]
            for which in range(2):

                @pl.when(links.core == which)
                def _(copy=either[which]):
                    copy.start()

            self.fetch.append(either[0])
        blocks = down_weight.shape[0] // 2
        for j in range(down_units(blocks * down_rows)):
            index = jnp.minimum(j * pieces + place, blocks - 1)
            start = (3 + count) * rows + j * down_rows
            self.fetch.append(
                links.go(
                    down_weight.at[(1 - links.col) * blocks + index, :, lanes],
                    home.at[start : start + down_rows],
                    links.group(1),
                )
            )

    def near(self):
        for copy in self.fetch:
            copy.wait()
        links = self.links
        home = self.units.at[links.core, links.x, links.z]
        self.first = []
        for rows, axis, n in (
            (slice(0, self.cut), 1, links.zs),
            (slice(self.cut, self.total), 0, links.xs),
        ):
            for k in range(1, n):
                self.first.append(links.go(home.at[rows], home.at[rows], links.place(axis, k)))

    def far(self):
        for copy in self.first:
            copy.wait()
        links, units = self.links, self.units
        self.second = []
        line = units.at[links.core, links.x, :, 0 : self.cut]
        for k in range(1, links.xs):
            self.second.append(links.go(line, line, links.place(0, k)))
        line = units.at[links.core, :, links.z, self.cut : self.total]
        for k in range(1, links.zs):
            self.second.append(links.go(line, line, links.place(1, k)))

    def swap(self):
        for copy in self.second:
            copy.wait()
        links = self.links
        self.last = []
        for rows in (slice(0, self.out_rows), slice(self.out_rows, self.total)):
            block = self.units.at[links.core, :, :, rows]
            self.last.append(links.go(block, block, links.other_core()))

    def wait_out(self):
        self.last[0].wait()

    def done(self):
        self.last[1].wait()


def forward_kernel(
    heads,
    tokens,
    cot_h,
    qkv_weight,
    router_weight,
    attn_gain,
    ffn_gain,
    routes,
    cosine,
    sine,
    seg,
    out_weight,
    gate_weight,
    up_weight,
    down_weight,
    normed_h,
    q_h,
    k_h,
    v_h,
    context_h,
    qkv_h,
    normed_two_h,
    quarter_h,
    cot_2,
    cot_3,
    units,
    lse,
    gates_ref,
    scale_one,
    small_all,
    hidden_own,
    scale_two,
    tokens_all,
    qkv_all,
    normed,
    q,
    k,
    v,
    vt,
    contexts,
    weight,
    hidden,
    normed_two,
    small,
    segk,
    segq,
    route_cols,
    send,
    recv,
    sems,
):
    links = Links(send, recv)
    row, col = links.row, links.col
    zs, cs = links.zs, links.cs
    total, full = normed.shape
    width = full // 2
    quarter = HALF // 2
    small[0:6, :] = router_weight[...].astype(f32)
    small[6:7, :] = attn_gain[...].reshape(1, width)
    small[7:8, :] = ffn_gain[...].reshape(1, width)
    links.greet([links.group(k) for k in (1, 2, 3)] + links.plane())

    def own(h):
        return tokens.at[h * quarter : (h + 1) * quarter]

    def dst(k, h):
        rows = (HALF if k & 2 else 0) + h * quarter
        return tokens_all.at[rows : rows + quarter, (k & 1) * width : (k & 1) * width + width]

    share = width // (cs * zs)
    start = links.core * (width // cs) + links.z * share
    there = at(width + start, share)
    fetch_qkv = [
        links.go(
            qkv_weight.at[at(start, share), at((1 - col) * SIDE, SIDE, 128)],
            qkv_all.at[there, 0:SIDE],
            links.group(1),
        ),
        links.go(
            qkv_weight.at[at(start, share), 2 * SIDE :], qkv_all.at[there, SIDE:], links.group(1)
        ),
        links.go(small, small_all.at[:, width:], links.group(1)),
    ]
    shares = Units(links, units, out_weight, gate_weight, up_weight, down_weight)
    forward, near, far, tokens_sent = gather_group(links, own, dst)
    fetch = Fetch(sems)
    pieces = weight.shape[1]
    half = pieces // 2
    fetch.start(
        "weight",
        *[
            (
                out_weight.at[pl.ds((col if h == 0 else 1 - col) * half, half)],
                weight.at[0, h * half : (h + 1) * half, :, 0:width],
            )
            for h in range(2)
        ],
    )
    tokens_all[0:HALF, 0:width] = tokens[...]
    qkv_all[0:width, 0:SIDE] = qkv_weight[:, at(col * SIDE, SIDE, 128)]
    qkv_all[0:width, SIDE:] = qkv_weight[:, 2 * SIDE :]
    small_all[:, 0:width] = small[...]
    segq[...] = seg[...].astype(f32)
    segk[...] = column(segq[...])
    count = routes.shape[0]
    route_cols[...] = jnp.concatenate(
        [routes[...].astype(f32), jnp.zeros((128 - count, total), f32)], axis=0
    ).T
    for copy in fetch_qkv:
        copy.wait()
    spread = [
        links.go(qkv_all.at[there], qkv_all.at[there], links.place(1, k)) for k in range(1, zs)
    ]
    shares.near()
    forward()
    for copy in spread:
        copy.wait()
    if cs == 2:
        block = qkv_all.at[at(width + links.core * (width // 2), width // 2)]
        swap_qkv = links.go(block, block, links.other_core())
    shares.far()
    if cs == 2:
        swap_qkv.wait()
    near()

    def project(i):
        rows = slice(i * BLOCK, (i + 1) * BLOCK)
        place = i * BLOCK // HALF
        here = at(
            HALF * jnp.bitwise_xor(row, place) + (i * BLOCK - place * HALF), BLOCK, BLOCK
        )
        x = tokens_all[rows].astype(f32)
        scale = lax.rsqrt(jnp.sum(x * x, axis=1, keepdims=True) * (1.0 / full) + EPS)
        low = (x * scale * small_all[6:7, :]).astype(bf16)
        normed[rows] = low
        if i * BLOCK < HALF:
            scale_one[rows] = jnp.broadcast_to(scale, (BLOCK, 128))
        router = jnp.concatenate([small_all[...], jnp.zeros((120, full), f32)], axis=0)
        logits = nt(low, router.astype(bf16))
        lanes = lax.broadcasted_iota(jnp.int32, (BLOCK, 128), 1).astype(f32)
        chosen = lanes == route_cols[here, 0:1]
        for j in range(1, count):
            chosen = chosen | (lanes == route_cols[here, j : j + 1])
        masked = jnp.where(chosen, logits, MASKED)
        raised = jnp.exp(masked - jnp.max(masked, axis=1, keepdims=True))
        raised = jnp.where(chosen, raised, 0.0)
        gates_ref[rows] = raised / jnp.sum(raised, axis=1, keepdims=True)
        projected = nn(low, qkv_all[...])
        for h in range(heads + 1):
            part = projected[:, h * HEAD : (h + 1) * HEAD]
            turned = (part * cosine[here] + swap_halves(part) * sine[here]).astype(bf16)
            if h < heads:
                q[here, h * HEAD : (h + 1) * HEAD] = turned
            else:
                k[here] = turned
        v[here] = projected[:, (heads + 1) * HEAD :].astype(bf16)

    project(2)
    project(3)
    far()
    cot_copies = [
        links.go(cot_h.at[h * quarter : (h + 1) * quarter], out, links.group(k))
        for k, out, h in ((2, cot_2, 1), (3, cot_3, 0))
    ]
    project(0)
    project(1)
    fetch.start("out", (normed, normed_h), (q, q_h), (k, k_h), (v, v_h), (qkv_all, qkv_h))

    vt[...] = v[...].astype(f32).T.astype(bf16)

    def block(j, h, head):
        first = j * SIDE + head * HEAD
        return contexts.at[h * HALF : (h + 1) * HALF, first : first + HEAD]

    sends, relays = {}, []
    for head in range(heads):
        cols = slice(head * HEAD, (head + 1) * HEAD)
        for i in range(total // BLOCK):
            first, last = window(i, BLOCK)
            here = slice(i * BLOCK, (i + 1) * BLOCK)
            allowed = allowed_keys(segk, segq, i, first, last)
            place = i * BLOCK // HALF
            rows = at(
                HALF * jnp.bitwise_xor(row, place) + (i * BLOCK - place * HALF), BLOCK, BLOCK
            )
            s = nt(k[first:last], q[here, cols]) * (HEAD**-0.5)
            s = jnp.where(allowed, s, MASKED)
            top = jnp.max(s, axis=0, keepdims=True)
            p = jnp.exp(s - top)
            total_p = jnp.sum(p, axis=0, keepdims=True)
            p = (p * (1.0 / total_p)).astype(bf16)
            ot = nn(vt[:, first:last], p)
            contexts[rows, cols] = ot.T.astype(bf16)
            lse[head : head + 1, here] = top + jnp.log(total_p)
        for j, h in ((2, 0), (3, 1), (2, 1), (3, 0)):
            sends[j, 1 - h, head] = links.go(
                block(0, h, head), block(j, 1 - h, head), links.group(j)
            )
    lse[heads:, :] = jnp.zeros((8 - heads, total), f32)
    fetch.start("context", (contexts.at[:, 0:SIDE], context_h))
    shares.swap()
    for head in range(heads):
        sends[3, 0, head].wait_recv()
        relays.append(links.go(block(3, 0, head), block(1, 1, head), links.group(2)))
        sends[2, 1, head].wait_recv()
        relays.append(links.go(block(2, 1, head), block(1, 0, head), links.group(3)))

    shares.wait_out()
    rows = weight.shape[2]
    for j in (1, 2, 3):
        for core in range(2):
            first = (j & 1) * width + core * SIDE
            fetch.start(
                "weight",
                *[
                    (
                        units.at[core, x, :, (j - 1) * rows : j * rows],
                        weight.at[j // 2, x * zs : (x + 1) * zs, :, first : first + SIDE],
                    )
                    for x in range(links.xs)
                ],
            )
    for head in range(heads):
        sends[2, 0, head].wait_recv()
        sends[3, 1, head].wait_recv()
    fetch.wait("weight")
    w_own = weight[0, 0:half].reshape(SIDE, full)
    w_far = weight[1].reshape(width, full)
    fetch.start("quarter", (weight.at[0, 0:half], quarter_h))
    for i in range(2):
        rows = slice(i * HALF, (i + 1) * HALF)
        hidden[rows] = (
            tokens_all[rows].astype(f32)
            + nn(contexts[rows, 0:SIDE], w_own)
            + nn(contexts[rows, 2 * SIDE :], w_far)
        )
    for copy in relays:
        copy.wait_recv()
    w_peer = weight[0, half:].reshape(SIDE, full)
    for i in range(2):
        rows = slice(i * HALF, (i + 1) * HALF)
        value = hidden[rows] + nn(contexts[rows, SIDE : 2 * SIDE], w_peer)
        scale = lax.rsqrt(jnp.sum(value * value, axis=1, keepdims=True) * (1.0 / full) + EPS)
        normed_two[rows] = (value * scale * small_all[7:8, :]).astype(bf16)
        if i == 0:
            scale_two[...] = jnp.broadcast_to(scale, (HALF, 128))
            hidden_own[...] = value[:, 0:width]
        fetch.start("out", (normed_two.at[rows], normed_two_h.at[rows]))
    tokens_sent()
    for copy in relays + list(sends.values()):
        copy.wait_send()
    for copy in cot_copies:
        copy.wait()
    shares.done()
    fetch.wait("out", "context", "quarter")


def forward_step(
    tokens,
    cot,
    qkv_weight,
    router_weight,
    attn_gain,
    ffn_gain,
    routes,
    cosine,
    sine,
    seg,
    out_weight,
    gate_weight,
    up_weight,
    down_weight,
):
    xs, zs, cs = dp_sizes()
    pieces = xs * zs
    rows, down_rows = unit_rows()
    width = tokens.shape[1]
    full, total = 2 * width, 2 * HALF
    heads = SIDE // HEAD
    experts, _, hidden = gate_weight.shape
    hid = experts // 2 * hidden
    unit_total = (3 + experts // 2) * rows + down_units(hid) * down_rows
    out = [
        jax.ShapeDtypeStruct((total, full), bf16),
        jax.ShapeDtypeStruct((total, SIDE), bf16),
        jax.ShapeDtypeStruct((total, HEAD), bf16),
        jax.ShapeDtypeStruct((total, HEAD), bf16),
        jax.ShapeDtypeStruct((total, SIDE), bf16),
        jax.ShapeDtypeStruct((full, SIDE + 2 * HEAD), bf16),
        jax.ShapeDtypeStruct((total, full), bf16),
        jax.ShapeDtypeStruct((pieces // 2, rows, full), bf16),
        jax.ShapeDtypeStruct((HALF // 2, width), bf16),
        jax.ShapeDtypeStruct((HALF // 2, width), bf16),
        jax.ShapeDtypeStruct((cs, xs, zs, unit_total, SIDE), bf16),
        jax.ShapeDtypeStruct((8, total), f32),
        jax.ShapeDtypeStruct((total, 128), f32),
        jax.ShapeDtypeStruct((HALF, 128), f32),
        jax.ShapeDtypeStruct((8, full), f32),
        jax.ShapeDtypeStruct((HALF, width), f32),
        jax.ShapeDtypeStruct((HALF, 128), f32),
    ]
    return pl.pallas_call(
        functools.partial(forward_kernel, heads),
        out_shape=tuple(out),
        in_specs=[WHOLE, ANY] + [WHOLE] * 8 + [ANY] * 4,
        out_specs=(ANY,) * 11 + (WHOLE,) * 6,
        scratch_shapes=[
            VMEM((total, full), bf16),
            VMEM((full, SIDE + 2 * HEAD), bf16),
            VMEM((total, full), bf16),
            VMEM((total, SIDE), bf16),
            VMEM((total, HEAD), bf16),
            VMEM((total, HEAD), bf16),
            VMEM((HEAD, total), bf16),
            VMEM((total, full), bf16),
            VMEM((2, pieces, rows, full), bf16),
            VMEM((total, full), f32),
            VMEM((total, full), bf16),
            VMEM((8, width), f32),
            VMEM((total, 128), f32),
            VMEM((1, total), f32),
            VMEM((total, 128), f32),
            pltpu.SemaphoreType.DMA((80,)),
            pltpu.SemaphoreType.DMA((80,)),
            pltpu.SemaphoreType.DMA((48,)),
        ],
        compiler_params=pltpu.CompilerParams(
            collective_id=0, has_side_effects=True, vmem_limit_bytes=60 * 2**20
        ),
        name="forward_step",
    )(
        tokens,
        cot,
        qkv_weight,
        router_weight,
        attn_gain,
        ffn_gain,
        routes,
        cosine,
        sine,
        seg,
        out_weight.reshape(pieces, rows, width),
        gate_weight.reshape(experts, pieces, rows, hidden),
        up_weight.reshape(experts, pieces, rows, hidden),
        down_weight.reshape(-1, down_rows, width),
    )


def scatter_group(links, blocks, pass2, pass3, near2, near3, far, out2, out3):
    n2, n3 = links.group(2), links.group(3)
    start, direct = [], []

    def send_own_rows():
        start.append(links.go(blocks(1, 0), near2, n2))
        start.append(links.go(blocks(1, 1), near3, n3))

    def send_other_rows():
        direct.append(links.go(blocks(3, 1), far(3, 1), n3))
        direct.append(links.go(blocks(2, 0), far(2, 0), n2))

    relay = [links.copy(out3, far(3, 0), n3), links.copy(out2, far(2, 1), n2)]

    def forward():
        start[0].wait_recv()
        out3[...] = (pass3[...].astype(f32) + near2[...].astype(f32)).astype(bf16)
        relay[0].start()
        start[1].wait_recv()
        out2[...] = (pass2[...].astype(f32) + near3[...].astype(f32)).astype(bf16)
        relay[1].start()

    def finish():
        for copy in direct + relay:
            copy.wait_recv()

    def sent():
        for copy in start + direct + relay:
            copy.wait_send()

    return send_own_rows, send_other_rows, forward, finish, sent


def group_scratch(width):
    quarter = HALF // 2
    return [
        VMEM((quarter, width), bf16),
        VMEM((quarter, width), bf16),
        VMEM((HALF, width), bf16),
        VMEM((HALF, width), bf16),
        VMEM((quarter, width), bf16),
        VMEM((quarter, width), bf16),
    ]


def norm_back_rows(grad, gain, values, scale, inner, width):
    return scale * (grad * gain - values * (scale * inner * (1.0 / width)))


def column(row_vector):
    return jnp.broadcast_to(row_vector, (128, row_vector.shape[1])).T


def half_swap(v):
    return jnp.concatenate([v[:, HALF:], v[:, :HALF]], axis=1)


def reduce_kernel(
    partial,
    vectors,
    hidden_h,
    cot_h,
    scale_h,
    gain,
    normed_h,
    grads_h,
    weighted_h,
    cot_all_h,
    far_2,
    far_3,
    hidden_grad_h,
    hidden_low,
    vector_sums,
    gain_part,
    shard,
    hidden_grad,
    hidden,
    cot,
    scale,
    normed,
    grads,
    weighted,
    cot_all,
    normed_t,
    mine_p,
    pass2,
    pass3,
    near2,
    near3,
    far2,
    far3,
    out2,
    out3,
    vec_in,
    low,
    up_part,
    down_part,
    up_near,
    down_near,
    *rest,
):
    up_scratch, down_scratch = rest[0:5], rest[5:10]
    send, recv, sems, local = rest[10:]
    links = Links(send, recv)
    width = hidden_grad.shape[1]
    step = HALF // 4
    quarter = HALF // 2
    count, _, both = grads.shape
    side = both // 2
    fetch = Fetch(sems)
    fetch.start("normed", (normed_h, normed))
    fetch.start("grads", *[(grads_h.at[e], grads.at[e]) for e in range(count)])
    fetch.start("down", (weighted_h, weighted), (cot_all_h, cot_all))
    fetch.start(
        "pass",
        (partial.at[HALF + quarter :, 0:width], pass2),
        (partial.at[HALF : HALF + quarter, width:], pass3),
    )
    fetch.start(
        "own",
        (partial.at[0:HALF, 0:width], mine_p),
        (hidden_h, hidden),
        (cot_h, cot),
        (scale_h, scale),
        (far_2, far2.at[0:quarter]),
        (far_3, far3.at[quarter:]),
    )
    links.greet([links.group(k) for k in (1, 2, 3)] + links.plane())

    vec_copies = [links.go(vectors, vec_in.at[k - 1], links.group(k)) for k in (1, 2, 3)]

    def chunk(c):
        def blocks(k, h):
            first = (HALF if k & 2 else 0) + h * quarter + c * step
            cols = slice((k & 1) * width, (k & 1) * width + width)
            return partial.at[first : first + step, cols]

        def far(k, h):
            first = h * quarter + c * step
            return (far2 if k == 2 else far3).at[first : first + step]

        here = slice(c * step, (c + 1) * step)
        return scatter_group(
            links,
            blocks,
            pass2.at[here],
            pass3.at[here],
            near2.at[here],
            near3.at[here],
            far,
            out2.at[here],
            out3.at[here],
        )

    chunks = [chunk(c) for c in range(2)]
    own_rows, _, forward, finish, sent = [
        [functions[i] for functions in chunks] for i in range(5)
    ]
    own_rows[0]()
    own_rows[1]()

    kept = up_scratch[4].shape[0]
    up = PlaneSum(
        links,
        lambda ab, core: [(slice(None), up_part.at[core, ab])],
        *up_scratch,
        shard.at[:, 0:kept],
        count,
        near=up_near,
    )
    down = PlaneSum(
        links,
        lambda ab, core: [(slice(None), down_part.at[core, ab])],
        *down_scratch,
        shard.at[:, kept:],
        count,
        near=down_near,
    )
    up.start()
    down.start()
    fetch.wait("normed")
    for i in range(4):
        rows = slice(i * 256, (i + 1) * 256)
        normed_t[:, rows] = normed[rows].T
    state = {}

    def prepare():
        for copy in vec_copies:
            copy.wait()
        vec = vectors[...] + vec_in[0] + half_swap(vec_in[1] + vec_in[2])
        vector_sums[...] = vec
        fetch.wait("own")
        state["inner"] = column(vec[6:7, 0:HALF])[:, 0:1]
        state["part"] = jnp.zeros((8, width), f32)
        state["gain"] = gain[...].reshape(1, width)

    def norm_back(c):
        for h in range(2):
            first = h * quarter + c * step
            rows = slice(first, first + step)
            grad = mine_p[rows].astype(f32) + far2[rows].astype(f32) + far3[rows].astype(f32)
            values = hidden[rows]
            scale_rows = scale[rows, 0:1]
            back = norm_back_rows(
                grad, state["gain"], values, scale_rows, state["inner"][rows], 2 * width
            )
            back = back + cot[rows].astype(f32)
            hidden_grad[rows] = back
            low[rows] = back.astype(bf16)
            state["part"] = state["part"] + jnp.sum(
                (grad * values * scale_rows).reshape(step // 8, 8, width), axis=0
            )

    def gather(c):
        def own(h):
            first = h * quarter + c * step
            return low.at[first : first + step]

        def dst(k, h):
            first = (HALF if k & 2 else 0) + h * quarter + c * step
            cols = slice((k & 1) * width, (k & 1) * width + width)
            return hidden_low.at[first : first + step, cols]

        return gather_group(links, own, dst)

    gathers = []

    def finish_chunk(c):
        finish[c]()
        norm_back(c)
        gathers.append(gather(c))

    fetch.wait("grads", "down", "pass")
    pending = []
    for e in range(count):
        for ab in range(2):
            rows = slice(e * width, (e + 1) * width)
            part = nn(normed_t[ab * width : (ab + 1) * width], grads[e])
            for which in range(2):
                up_part[which, ab, rows] = part[:, which * side : (which + 1) * side].astype(
                    bf16
                )
            up.core_send(ab, e)
            rows = slice(e * side, (e + 1) * side)
            part = tn(weighted[:, rows], cot_all[:, ab * width : (ab + 1) * width])
            for which in range(2):
                down_part[which, ab, rows] = part[:, which * side : (which + 1) * side].astype(
                    bf16
                )
            down.core_send(ab, e)
            if (e, ab) == (0, 1):
                forward[0]()
            if (e, ab) == (1, 0):
                forward[1]()
            pending.append((ab, e))
            if len(pending) > 1:
                up.first_send(*pending[-2])
                down.first_send(*pending[-2])
            if (e, ab) == (2, 0):
                prepare()
                finish_chunk(0)
    up.first_send(*pending[-1])
    down.first_send(*pending[-1])
    finish_chunk(1)
    keep = pltpu.make_async_copy(hidden_grad, hidden_grad_h, local.at[1])
    keep.start()
    gain_part[...] = jnp.broadcast_to(jnp.sum(state["part"], axis=0, keepdims=True), (8, width))
    mine = pltpu.make_async_copy(low, hidden_low.at[0:HALF, 0:width], local.at[0])
    mine.start()
    for step_of in pending:
        up.relay(*step_of)
        down.relay(*step_of)
    gathers[0][0]()
    for ab in range(2):
        up.second_send(ab)
        down.second_send(ab)
    gathers[1][0]()
    for ab in (1, 0):
        up.last_sum(ab)
        down.last_sum(ab)
    up.wait_peer()
    down.wait_peer()
    mine.wait()
    keep.wait()
    for c in range(2):
        for wait in gathers[c][1:]:
            wait()
        sent[c]()
    up.done()
    down.done()


def reduce_step(
    partial, vectors, hidden, cot, scale, gain, normed, grads, weighted, cot_all, far_2, far_3
):
    xs, zs, _ = dp_sizes()
    width = hidden.shape[1]
    count, total, both = grads.shape
    side = both // 2
    up_rows, down_rows = count * width, count * side
    quarter = HALF // 2
    return pl.pallas_call(
        reduce_kernel,
        out_shape=(
            jax.ShapeDtypeStruct((HALF, width), f32),
            jax.ShapeDtypeStruct((2 * HALF, 2 * width), bf16),
            jax.ShapeDtypeStruct(vectors.shape, f32),
            jax.ShapeDtypeStruct((8, width), f32),
            jax.ShapeDtypeStruct(
                (2, pad16(up_rows // (xs * zs)) + pad16(down_rows // (xs * zs)), side), bf16
            ),
        ),
        in_specs=[ANY, WHOLE, ANY, ANY, ANY, WHOLE] + [ANY] * 6,
        out_specs=(ANY, ANY, WHOLE, WHOLE, WHOLE),
        scratch_shapes=[
            VMEM((HALF, width), f32),
            VMEM((HALF, width), f32),
            VMEM((HALF, width), bf16),
            VMEM((HALF, 128), f32),
            VMEM(normed.shape, bf16),
            VMEM(grads.shape, bf16),
            VMEM(weighted.shape, bf16),
            VMEM(cot_all.shape, bf16),
            VMEM((2 * width, total), bf16),
            VMEM((HALF, width), bf16),
            VMEM((quarter, width), bf16),
            VMEM((quarter, width), bf16),
        ]
        + group_scratch(width)
        + [
            VMEM((3,) + vectors.shape, f32),
            VMEM((HALF, width), bf16),
            VMEM((2, 2, up_rows, side), bf16),
            VMEM((2, 2, down_rows, side), bf16),
            VMEM((2, 2, up_rows // xs // 2, side), bf16),
            VMEM((2, 2, down_rows // xs // 2, side), bf16),
        ]
        + plane_scratch(up_rows, side)
        + plane_scratch(down_rows, side)
        + [
            pltpu.SemaphoreType.DMA((160,)),
            pltpu.SemaphoreType.DMA((160,)),
            pltpu.SemaphoreType.DMA((16,)),
            pltpu.SemaphoreType.DMA((2,)),
        ],
        compiler_params=pltpu.CompilerParams(
            collective_id=2, has_side_effects=True, vmem_limit_bytes=60 * 2**20
        ),
        name="reduce_step",
    )(partial, vectors, hidden, cot, scale, gain, normed, grads, weighted, cot_all, far_2, far_3)


def attn_back_kernel(
    heads,
    q_h,
    k_h,
    v_h,
    lse,
    seg,
    cos_h,
    sin_h,
    context_h,
    hidden_low_h,
    out_weight,
    qkv_h,
    normed_h,
    small_all,
    gates,
    vec_sums,
    ffn_part,
    tokens_h,
    scale_h,
    gain,
    hidden_grad_h,
    layer_h,
    hidden_h,
    expert_shard,
    input_grad,
    layer_out,
    small_out,
    attn_sums,
    expert_sums,
    q,
    k,
    v,
    cos_ref,
    sin_ref,
    context,
    hidden_low,
    qkv,
    normed,
    tokens,
    scale,
    hidden_grad,
    kt,
    do,
    dk,
    dv,
    grads,
    partial,
    qkv_part,
    out_part,
    near2,
    near3,
    far2,
    far3,
    out2,
    out3,
    layer_mine,
    layer_pass2,
    layer_pass3,
    hidden,
    lnear2,
    lnear3,
    lfar2,
    lfar3,
    lout2,
    lout3,
    vec_own,
    vec_in,
    small_own,
    small_in,
    attn_shard,
    segk,
    segq,
    *rest,
):
    attn_scratch = rest[0:5]
    send, recv, sems, local = rest[5:]
    links = Links(send, recv)
    xs, zs, cs = links.xs, links.zs, links.cs
    row = links.row
    total, full = normed.shape
    width = full // 2
    quarter = HALF // 2
    head_scale = HEAD**-0.5
    fetch = Fetch(sems)
    fetch.start("out", (context_h, context), (hidden_low_h, hidden_low))
    fetch.start("attention", (q_h, q), (k_h, k), (v_h, v))
    fetch.start("turn", (cos_h, cos_ref), (sin_h, sin_ref))
    fetch.start("normed", (normed_h, normed))
    fetch.start("qkv", (qkv_h, qkv))
    fetch.start(
        "own",
        (tokens_h, tokens),
        (scale_h, scale),
        (hidden_grad_h, hidden_grad),
    )
    fetch.start(
        "layer",
        (layer_h.at[0:HALF, 0:width], layer_mine),
        (layer_h.at[HALF + quarter :, 0:width], layer_pass2),
        (layer_h.at[HALF : HALF + quarter, width:], layer_pass3),
        (hidden_h, hidden),
    )
    links.greet([links.group(k) for k in (1, 2, 3)] + links.plane())

    def layer_blocks(k, h):
        first = (HALF if k & 2 else 0) + h * quarter
        cols = slice((k & 1) * width, (k & 1) * width + width)
        return layer_h.at[first : first + quarter, cols]

    def halves_of(a, b):
        return lambda k, h: (a if k == 2 else b).at[h * quarter : (h + 1) * quarter]

    layer_own, layer_other, layer_forward, layer_finish, layer_sent = scatter_group(
        links,
        layer_blocks,
        layer_pass2,
        layer_pass3,
        lnear2,
        lnear3,
        halves_of(lfar2, lfar3),
        lout2,
        lout3,
    )
    layer_own()
    layer_other()
    segq[...] = seg[...].astype(f32)
    segk[...] = column(segq[...])

    cols_all = qkv.shape[1]

    def parts(ab, core):
        first = ab * width + core * SIDE
        return [
            (slice(0, cols_all), qkv_part.at[at(first, SIDE)]),
            (slice(cols_all, cols_all + SIDE), out_part.at[:, at(first, SIDE, 128)]),
        ]

    attn_sum = PlaneSum(links, parts, *attn_scratch, attn_shard, 1, True)
    attn_sum.start()
    attn_gather = PlaneGather(links, attn_shard, attn_sums, local.at[0])
    expert_gather = PlaneGather(links, expert_shard, expert_sums, local.at[1])
    expert_gather.near(0)
    expert_gather.near(1)
    piece_rows = expert_shard.shape[1]
    cuts = [0, pad16(piece_rows * 5 // 14), pad16(piece_rows * 5 // 7), piece_rows]

    def spread(i):
        for ab in range(2):
            expert_gather.far(ab, slice(cuts[i], cuts[i + 1]), True)

    fetch.wait("out")
    out_part[...] = tn(context[...], hidden_low[...]).astype(bf16)
    for ab in range(2):
        attn_sum.core_send(ab, 0, 1)

    for h in range(2):
        rows = at(HALF * jnp.bitwise_xor(row, h), HALF)
        do[h * HALF : (h + 1) * HALF] = nt(hidden_low[rows], out_weight[...]).astype(bf16)
    fetch.wait("attention", "turn")
    for ab in range(2):
        attn_sum.first_send(ab, 0, 1)
    for i in range(3):
        spread(i)
    kt[...] = k[...].astype(f32).T.astype(bf16)
    dk[...] = jnp.zeros_like(dk)
    dv[...] = jnp.zeros_like(dv)

    def back(grad, here):
        return grad * cos_ref[here] - swap_halves(grad) * sin_ref[here]

    def rows_of(i):
        place = i * BLOCK // HALF
        return at(HALF * jnp.bitwise_xor(row, place) + (i * BLOCK - place * HALF), BLOCK, BLOCK)

    inners = []
    for i in range(total // BLOCK):
        first, last = window(i, BLOCK)
        here = slice(i * BLOCK, (i + 1) * BLOCK)
        allowed = allowed_keys(segk, segq, i, first, last)
        rows = rows_of(i)
        inner_q = jnp.zeros((BLOCK, 1), f32)
        for h in range(heads):
            cols = slice(h * HEAD, (h + 1) * HEAD)
            s = nt(k[first:last], q[here, cols]) * head_scale
            s = jnp.where(allowed, s, MASKED)
            p = jnp.exp(s - lse[h : h + 1, here])
            dp = nt(v[first:last], do[here, cols])
            inner = jnp.sum(dp * p, axis=0, keepdims=True)
            ds = (p * (dp - inner)).astype(bf16)
            dq = (nn(kt[:, first:last], ds) * head_scale).T
            inner_q = inner_q + jnp.sum(dq * q[here, cols].astype(f32), axis=1, keepdims=True)
            grads[rows, cols] = back(dq, here).astype(bf16)
            dk[first:last] += nn(ds, q[here, cols]) * head_scale
            dv[first:last] += nn(p.astype(bf16), do[here, cols])
        inners.append(inner_q)
        if i == 2:
            fetch.wait("layer")
            layer_forward()
    expert_gather.relay()

    gate_rows = gates[...].T[0:8, :]
    sums = vec_sums[...]
    mask = lax.broadcasted_iota(jnp.int32, sums.shape, 0) < 6
    sums = jnp.where(mask, sums, 0.0)
    logits_grad = gate_rows * (sums - jnp.sum(gate_rows * sums, axis=0, keepdims=True))
    logits_low = jnp.where(mask, logits_grad, 0.0).astype(bf16)
    router = jnp.where(
        lax.broadcasted_iota(jnp.int32, (8, full), 0) < 6, small_all[...], 0.0
    )
    router_low = router.astype(bf16)
    once = jnp.where((row == 0) & (links.col == 0), 1.0, 0.0)
    fetch.wait("normed")
    router_grad = nn(logits_low, normed[...])
    router_inner = once * jnp.sum(
        logits_low.astype(f32) * nt(router_low, normed[...]), axis=0, keepdims=True
    )
    for i in range(total // BLOCK):
        here = slice(i * BLOCK, (i + 1) * BLOCK)
        rows = rows_of(i)
        key_grad, value_grad = dk[here], dv[here]
        inner = inners[i] + jnp.sum(
            key_grad * k[here].astype(f32) + value_grad * v[here].astype(f32),
            axis=1,
            keepdims=True,
        )
        grads[rows, heads * HEAD : (heads + 1) * HEAD] = back(key_grad, here).astype(bf16)
        grads[rows, (heads + 1) * HEAD :] = value_grad.astype(bf16)
        vec_own[:, rows] = jnp.broadcast_to(inner, (BLOCK, 128)).T[0:8, :]
    vec_own[...] += router_inner
    vec_copies = [links.go(vec_own, vec_in.at[k - 1], links.group(k)) for k in (1, 2, 3)]

    def blocks(k, h):
        first = (HALF if k & 2 else 0) + h * quarter
        cols = slice((k & 1) * width, (k & 1) * width + width)
        return partial.at[first : first + quarter, cols]

    own_rows, other_rows, forward, finish, sent = scatter_group(
        links,
        blocks,
        partial.at[HALF + quarter :, 0:width],
        partial.at[HALF : HALF + quarter, width:],
        near2,
        near3,
        halves_of(far2, far3),
        out2,
        out3,
    )
    fetch.wait("qkv")
    partial[0:HALF] = nt(grads[0:HALF], qkv[...]).astype(bf16)
    own_rows()
    expert_gather.relay()
    partial[HALF:] = nt(grads[HALF:], qkv[...]).astype(bf16)
    other_rows()

    gain_sums = {}
    for mine in (False, True):
        which = links.core if mine else 1 - links.core
        for ab in range(2):
            first = ab * width + which * SIDE
            part = tn(normed[:, at(first, SIDE, 128)], grads[...])
            rows = at(first, SIDE)
            qkv_part[rows] = part.astype(bf16)
            gain_sum = jnp.sum(part * qkv[rows].astype(f32), axis=1, keepdims=True)
            gain_sums[mine, ab] = jnp.broadcast_to(gain_sum, (SIDE, 128)).T[0:8, :]
            if not mine:
                attn_sum.core_send(ab, 0, 0)
    for ab in range(2):
        attn_sum.first_send(ab, 0, 0)
    expert_gather.relay()

    halves = []
    for ab in range(2):
        a, b = gain_sums[True, ab], gain_sums[False, ab]
        first = links.core == 0
        halves.append(jnp.concatenate([jnp.where(first, a, b), jnp.where(first, b, a)], axis=1))
    gain_row = jnp.concatenate(halves, axis=1)
    gain_row = gain_row + once * jnp.sum(router_grad * router, axis=0, keepdims=True)
    gain_row = gain_row / small_all[6:7, :]
    ffn = jnp.concatenate([ffn_part[...], jnp.zeros((8, width), f32)], axis=1)
    index = lax.broadcasted_iota(jnp.int32, (8, full), 0)
    small_own[0] = jnp.where(index < 6, router_grad, jnp.where(index == 6, gain_row, ffn))

    def small_stage(stage):
        if stage < 3:
            base = (0, 1, xs)[stage]
            devices = [
                links.other_core() if stage == 0 else links.place(stage - 1, k)
                for k in range(1, (cs, xs, zs)[stage])
            ]
        else:
            base = xs + zs - 1
            devices = [links.group(k) for k in (1, 2, 3)]
        copies = [
            (links.go(small_own.at[stage], small_in.at[base + i], device), base + i)
            for i, device in enumerate(devices)
        ]

        def done():
            value = small_own[stage]
            came = []
            for copy, i in copies:
                copy.wait()
                came.append(small_in[i])
            if stage < 3:
                for v in came:
                    value = value + v
                small_own[stage + 1] = value
            else:
                swap = came[0] + came[2]
                total_rows = (
                    value + came[1] + jnp.concatenate([swap[:, width:], swap[:, :width]], axis=1)
                )
                eight = lax.broadcasted_iota(jnp.int32, (8, width), 0)
                small_out[...] = jnp.where(
                    eight < 6, value[:, 0:width], total_rows[:, 0:width]
                )

        return done

    done = small_stage(0)
    layer_finish()
    for h in range(4):
        rows = slice(h * 128, (h + 1) * 128)
        layer_out[rows] = (
            hidden[rows]
            + layer_mine[rows].astype(f32)
            + lfar2[rows].astype(f32)
            + lfar3[rows].astype(f32)
        ).astype(bf16)
    done()
    done = small_stage(1)
    expert_gather.swap(slice(0, cuts[2]), 4)
    for ab in range(2):
        attn_sum.second_send(ab)
    expert_gather.swap(slice(cuts[2], piece_rows), 2)
    for ab in (1, 0):
        attn_sum.last_sum(ab)
    attn_gather.near(0)
    forward()
    for copy in vec_copies:
        copy.wait()
    vec = vec_own[...] + vec_in[0] + half_swap(vec_in[1] + vec_in[2])
    inner = column(vec[6:7, 0:HALF])[:, 0:1]
    fetch.wait("own")
    gain_in = gain[...].reshape(1, width)
    done()
    done = small_stage(2)
    attn_sum.wait_peer()
    attn_gather.near(1)
    attn_gather.far(0)
    attn_gather.far(1)
    done()
    done = small_stage(3)
    finish()
    for h in range(4):
        rows = slice(h * 128, (h + 1) * 128)
        grad = (
            partial[rows, 0:width].astype(f32)
            + far2[rows].astype(f32)
            + far3[rows].astype(f32)
            + tn(logits_low[:, rows], router_low[:, 0:width])
        )
        input_grad[rows] = hidden_grad[rows] + norm_back_rows(
            grad,
            gain_in,
            tokens[rows].astype(f32),
            scale[rows, 0:1],
            inner[rows],
            full,
        )
    done()
    attn_gather.swap()
    sent()
    layer_sent()
    attn_sum.done()
    expert_gather.done()
    attn_gather.done()


def attn_back(
    q,
    k,
    v,
    lse,
    seg,
    cosine,
    sine,
    context,
    hidden_low,
    out_weight,
    qkv_weight,
    normed,
    small_all,
    gates,
    vec_sums,
    ffn_part,
    tokens,
    scale,
    gain,
    hidden_grad,
    layer_part,
    hidden,
    expert_shard,
):
    xs, zs, cs = dp_sizes()
    total, full = normed.shape
    width = full // 2
    quarter = HALF // 2
    heads = q.shape[1] // HEAD
    cols = qkv_weight.shape[1]
    piece = (2 * SIDE // (xs * zs), (cols + SIDE) // 2)
    return pl.pallas_call(
        functools.partial(attn_back_kernel, heads),
        out_shape=(
            jax.ShapeDtypeStruct((HALF, width), f32),
            jax.ShapeDtypeStruct((HALF, width), bf16),
            jax.ShapeDtypeStruct((8, width), f32),
            jax.ShapeDtypeStruct((cs, 2, xs * zs) + piece, bf16),
            jax.ShapeDtypeStruct((cs, 2, xs * zs) + expert_shard.shape[1:], bf16),
        ),
        in_specs=[ANY] * 3
        + [WHOLE] * 2
        + [ANY] * 4
        + [WHOLE]
        + [ANY] * 2
        + [WHOLE] * 4
        + [ANY] * 2
        + [WHOLE] + [ANY] * 3 + [WHOLE],
        out_specs=(WHOLE, WHOLE, WHOLE, ANY, ANY),
        scratch_shapes=[
            VMEM(q.shape, bf16),
            VMEM(k.shape, bf16),
            VMEM(v.shape, bf16),
            VMEM(cosine.shape, f32),
            VMEM(sine.shape, f32),
            VMEM(context.shape, bf16),
            VMEM(hidden_low.shape, bf16),
            VMEM(qkv_weight.shape, bf16),
            VMEM(normed.shape, bf16),
            VMEM(tokens.shape, bf16),
            VMEM((HALF, 128), f32),
            VMEM(hidden_grad.shape, f32),
            VMEM((HEAD, total), bf16),
            VMEM(q.shape, bf16),
            VMEM(k.shape, f32),
            VMEM(v.shape, f32),
            VMEM((total, cols), bf16),
            VMEM((total, full), bf16),
            VMEM((full, cols), bf16),
            VMEM((SIDE, full), bf16),
        ]
        + group_scratch(width)
        + [
            VMEM((HALF, width), bf16),
            VMEM((quarter, width), bf16),
            VMEM((quarter, width), bf16),
            VMEM((HALF, width), f32),
        ]
        + group_scratch(width)
        + [
            VMEM((8, total), f32),
            VMEM((3, 8, total), f32),
            VMEM((4, 8, full), f32),
            VMEM((xs + zs + 2, 8, full), f32),
            VMEM((2,) + piece, bf16),
            VMEM((total, 128), f32),
            VMEM((1, total), f32),
        ]
        + plane_scratch(SIDE, cols + SIDE, True)
        + [
            pltpu.SemaphoreType.DMA((112,)),
            pltpu.SemaphoreType.DMA((112,)),
            pltpu.SemaphoreType.DMA((24,)),
            pltpu.SemaphoreType.DMA((2, 2)),
        ],
        compiler_params=pltpu.CompilerParams(
            collective_id=3, has_side_effects=True, vmem_limit_bytes=60 * 2**20
        ),
        name="attn_back",
    )(
        q,
        k,
        v,
        lse,
        seg,
        cosine,
        sine,
        context,
        hidden_low,
        out_weight,
        qkv_weight,
        normed,
        small_all,
        gates,
        vec_sums,
        ffn_part,
        tokens,
        scale,
        gain,
        hidden_grad,
        layer_part,
        hidden,
        expert_shard,
    )


def swap_halves(v):
    half = v.shape[-1] // 2
    return jnp.concatenate([v[..., half:], v[..., :half]], axis=-1)


def experts_kernel(
    normed_h,
    cot_own,
    cot_2,
    cot_3,
    gates,
    gate_weight,
    up_weight,
    down_weight,
    units,
    weighted_h,
    grads_h,
    back_h,
    out_h,
    cot_all_h,
    far_2,
    far_3,
    vec_ref,
    normed,
    cot,
    gate_up,
    down,
    weighted,
    grads,
    back,
    out,
    send,
    recv,
    sems,
):
    links = Links(send, recv)
    col = links.col
    count, _, pieces, unit, both = gate_up.shape
    blocks, down_unit, full = down.shape
    width = full // 2
    hidden = both // 2
    quarter = HALF // 2
    other, own = slice(HALF, 2 * HALF), slice(0, HALF)
    fetch = Fetch(sems)
    fetch.start("normed", (normed_h.at[other], normed.at[other]))
    for e in range(count):
        for which, weight in enumerate((gate_weight, up_weight)):
            cols = slice(which * hidden, (which + 1) * hidden)
            fetch.start(
                ("gate_up", e),
                (weight.at[col * count + e], gate_up.at[e, 0, :, :, cols]),
                (
                    units.at[which, :, (3 + e) * unit : (4 + e) * unit],
                    gate_up.at[e, 1, :, :, cols],
                ),
            )
    fetch.start(
        "cot",
        (cot_2, cot.at[HALF + quarter :, 0:width]),
        (cot_3, cot.at[HALF : HALF + quarter, width:]),
        (cot_own, cot.at[own, 0:width]),
    )
    fetch.start("down", (down_weight.at[pl.ds(col * blocks, blocks)], down.at[:, :, 0:width]))
    for j in range(-(-blocks // pieces)):
        n = min(pieces, blocks - j * pieces)
        start = (3 + count) * unit + j * down_unit
        for core in range(2):
            first = width + core * SIDE
            fetch.start(
                "down",
                (
                    units.at[core, 0:n, start : start + down_unit],
                    down.at[j * pieces : j * pieces + n, :, first : first + SIDE],
                ),
            )
    fetch.start("normed_own", (normed_h.at[own], normed.at[own]))
    links.greet([links.group(2), links.group(3)])
    direct = [
        links.go(cot_own.at[0:quarter], cot.at[HALF : HALF + quarter, 0:width], links.group(2)),
        links.go(cot_own.at[quarter:], cot.at[HALF + quarter :, width:], links.group(3)),
    ]
    relays = [
        links.go(cot_3, cot.at[0:quarter, width:], links.group(2)),
        links.go(cot_2, cot.at[quarter:HALF, width:], links.group(3)),
    ]
    fetch.wait("normed")
    all_pres = [[], []]
    for e in range(count):
        fetch.wait(("gate_up", e))
        all_pres[0].append(nn(normed[other], gate_up[e].reshape(full, both)))
    fetch.wait("normed_own")
    for e in range(count):
        all_pres[1].append(nn(normed[own], gate_up[e].reshape(full, both)))
    for step, rows in enumerate((other, own)):
        lanes = lax.broadcasted_iota(jnp.int32, (HALF, 128), 1)
        vec = jnp.zeros((HALF, 128), f32)
        inner = jnp.zeros((HALF, 1), f32)
        pres = all_pres[step]
        if step == 0:
            fetch.wait("cot", "down")
            for copy in direct:
                copy.wait_recv()
        else:
            for copy in relays:
                copy.wait_recv()
        y = cot[rows]
        for e in range(count):
            down_e = down[...].reshape(count, hidden, full)[e]
            here = lanes == col * count + e
            gate = jnp.sum(jnp.where(here, gates[rows], 0.0), axis=1, keepdims=True)
            gate_pre, up_pre = pres[e][:, :hidden], pres[e][:, hidden:]
            sigmoid = 1.0 / (1.0 + jnp.exp(-gate_pre))
            silu = gate_pre * sigmoid
            activated = silu * up_pre
            weighted[rows, e * hidden : (e + 1) * hidden] = (gate * activated).astype(bf16)
            weighted_grad = nt(y, down_e)
            both_terms = activated * weighted_grad
            part = jnp.sum(both_terms, axis=1, keepdims=True)
            vec = vec + jnp.where(here, part, 0.0)
            slope = 1.0 + gate_pre * (1.0 - sigmoid)
            g = gate * weighted_grad
            gate_grad = g * up_pre * (sigmoid * slope)
            up_grad = g * silu
            inner = inner + gate * (
                part + jnp.sum(both_terms * slope, axis=1, keepdims=True)
            )
            grads[e, rows] = jnp.concatenate([gate_grad, up_grad], axis=1).astype(bf16)
        fetch.start("out", *[(grads.at[e, rows], grads_h.at[e, rows]) for e in range(count)])
        fetch.start("out", (weighted.at[rows], weighted_h.at[rows]))
        fetch.start("out", (cot.at[rows], cot_all_h.at[rows]))
        total = None
        for e in range(count):
            term = nt(grads[e, rows], gate_up[e].reshape(full, both))
            total = term if total is None else total + term
        back[rows] = total.astype(bf16)
        if step == 0:
            sums = [
                links.go(back.at[HALF + quarter :, width:], far_3, links.group(3)),
                links.go(back.at[HALF : HALF + quarter, 0:width], far_2, links.group(2)),
            ]
        fetch.start("out", (back.at[rows], back_h.at[rows]))
        out[rows] = nn(weighted[rows], down[...].reshape(count * hidden, full)).astype(bf16)
        fetch.start("out", (out.at[rows], out_h.at[rows]))
        vec = jnp.where(lanes == 6, inner, vec)
        vec_ref[:, rows] = vec.T[0:8, :]
    for copy in direct + relays:
        copy.wait_send()
    for copy in sums:
        copy.wait()
    fetch.wait("out")


def experts_step(
    normed, cot_own, cot_2, cot_3, gates, gate_weight, up_weight, down_weight, units
):
    total, width = normed.shape
    experts, own_width, hidden = gate_weight.shape
    count = experts // 2
    both = 2 * hidden
    hid = count * hidden
    pieces = units.shape[1]
    unit, down_unit = unit_rows()
    return pl.pallas_call(
        experts_kernel,
        out_shape=(
            jax.ShapeDtypeStruct((total, hid), bf16),
            jax.ShapeDtypeStruct((count, total, both), bf16),
            jax.ShapeDtypeStruct((total, width), bf16),
            jax.ShapeDtypeStruct((total, width), bf16),
            jax.ShapeDtypeStruct((total, width), bf16),
            jax.ShapeDtypeStruct((HALF // 2, own_width), bf16),
            jax.ShapeDtypeStruct((HALF // 2, own_width), bf16),
            jax.ShapeDtypeStruct((8, total), f32),
        ),
        in_specs=[ANY] * 4 + [WHOLE] + [ANY] * 4,
        out_specs=(ANY,) * 7 + (WHOLE,),
        scratch_shapes=[
            VMEM((total, width), bf16),
            VMEM((total, width), bf16),
            VMEM((count, 2, pieces, unit, both), bf16),
            VMEM((hid // down_unit, down_unit, width), bf16),
            VMEM((total, hid), bf16),
            VMEM((count, total, both), bf16),
            VMEM((total, width), bf16),
            VMEM((total, width), bf16),
            pltpu.SemaphoreType.DMA((6,)),
            pltpu.SemaphoreType.DMA((6,)),
            pltpu.SemaphoreType.DMA((48,)),
        ],
        compiler_params=pltpu.CompilerParams(
            collective_id=1, has_side_effects=True, vmem_limit_bytes=60 * 2**20
        ),
        name="experts",
    )(
        normed,
        cot_own,
        cot_2,
        cot_3,
        gates,
        gate_weight.reshape(experts, pieces, unit, hidden),
        up_weight.reshape(experts, pieces, unit, hidden),
        down_weight.reshape(-1, down_unit, own_width),
        units,
    )


def window(i, block):
    first = max(0, (i + 1) * block - 512 - block)
    return first, (i + 1) * block


def allowed_keys(segk, segq, i, first, last):
    width = last - first
    keys = lax.broadcasted_iota(jnp.int32, (width, BLOCK), 0) + first
    queries = lax.broadcasted_iota(jnp.int32, (width, BLOCK), 1) + i * BLOCK
    same = segk[first:last, 0:1] == segq[:, i * BLOCK : (i + 1) * BLOCK]
    return (keys <= queries) & same


def finish_kernel(
    col_ref,
    sums,
    input_ref,
    layer_ref,
    small,
    attn_h,
    gate_ref,
    up_ref,
    down_ref,
    input_out,
    layer_out,
    router_ref,
    attn_gain,
    ffn_gain,
    qkv_out,
    out_out,
    attn_sums,
    qkv_grad,
    out_grad,
    sems,
):
    ab, j = pl.program_id(0), pl.program_id(1)
    steps = pl.num_programs(1)
    count, rows = gate_ref.shape[1:3]
    down_rows = down_ref.shape[2]
    fetch = pltpu.make_async_copy(attn_h, attn_sums, sems.at[0])
    store = [
        pltpu.make_async_copy(qkv_grad, qkv_out, sems.at[1]),
        pltpu.make_async_copy(out_grad, out_out, sems.at[2]),
    ]

    @pl.when((ab == 0) & (j == 0))
    def _():
        fetch.start()

    cores, _, pieces = sums.shape[:3]
    step, down_step = count * rows // pieces, count * down_rows // pieces
    first = pad16(step)
    for which, ref in enumerate((gate_ref, up_ref)):
        block = sums[which, 0, :, 0:step].astype(f32)
        ref[0] = block.reshape(count, rows, SIDE)
    for core in range(cores):
        block = sums[core, 0, :, first : first + down_step].astype(f32)
        down_ref[0, :, :, core * SIDE : (core + 1) * SIDE] = block.reshape(
            count, down_rows, SIDE
        )
    input_out[...] = input_ref[...]
    layer_out[...] = layer_ref[...]

    @pl.when((ab == 1) & (j == 0))
    def _():
        fetch.wait()
        col = col_ref[0]
        cores, _, pieces = attn_sums.shape[:3]
        kept_rows = SIDE // pieces
        middle = attn_sums.shape[4]
        pair = middle - SIDE
        for core in range(cores):
            kept = None
            here = slice(core * SIDE, (core + 1) * SIDE)
            for part in range(2):
                half = col if part == 0 else 1 - col
                block = attn_sums[core, part].astype(f32)
                left = block[:, 0:kept_rows].reshape(SIDE, middle)
                right = block[:, kept_rows:].reshape(SIDE, middle)
                qkv_grad[here, at(half * SIDE, SIDE, 128)] = left[:, 0:SIDE]
                out_grad[at(half * SIDE, SIDE), here] = right[:, pair:]
                both = jnp.concatenate([left[:, SIDE:], right[:, 0:pair]], axis=1)
                kept = both if kept is None else kept + both
            qkv_grad[here, 2 * SIDE :] = kept
        for copy in store:
            copy.start()
        value = small[...]
        attn_gain[...] = value[6:7].reshape(attn_gain.shape)
        ffn_gain[...] = value[7:8].reshape(ffn_gain.shape)
        router_ref[...] = value[0 : router_ref.shape[0]]

    @pl.when((ab == 1) & (j == steps - 1))
    def _():
        for copy in store:
            copy.wait()


def finish_step(sums, input_grad, layer_out, small, attn_sums, col, experts):
    xs, zs, cs = dp_sizes()
    piece = sums.shape[-2]
    own_rows, width = input_grad.shape
    part = own_rows // (2 * xs)
    cols = SIDE + 2 * HEAD
    count = experts // 2

    def out_spec(rows, width):
        return pl.BlockSpec(
            (1, count, rows, width),
            lambda ab, j, col_ref: (jnp.where(ab == 0, col_ref[0], 1 - col_ref[0]), 0, j, 0),
        )

    rows_spec = pl.BlockSpec((part, width), lambda ab, j, col_ref: (ab * xs + j, 0))

    def whole(shape):
        return pl.BlockSpec(shape, lambda ab, j, col_ref: (0,) * len(shape))

    return pl.pallas_call(
        finish_kernel,
        grid_spec=pltpu.PrefetchScalarGridSpec(
            num_scalar_prefetch=1,
            grid=(2, xs),
            in_specs=[
                pl.BlockSpec(
                    (cs, 1, zs, piece, SIDE), lambda ab, j, col_ref: (0, ab, j, 0, 0)
                ),
                rows_spec,
                rows_spec,
                whole(small.shape),
                ANY,
            ],
            out_specs=(
                out_spec(width // xs, SIDE),
                out_spec(width // xs, SIDE),
                out_spec(SIDE // xs, width),
                rows_spec,
                rows_spec,
                whole((experts, width)),
                whole((width,)),
                whole((width,)),
                ANY,
                ANY,
            ),
            scratch_shapes=[
                VMEM(attn_sums.shape, bf16),
                VMEM((2 * SIDE, SIDE + cols), f32),
                VMEM((2 * SIDE, 2 * SIDE), f32),
                pltpu.SemaphoreType.DMA((3,)),
            ],
        ),
        out_shape=(
            jax.ShapeDtypeStruct((2, count, width, SIDE), f32),
            jax.ShapeDtypeStruct((2, count, width, SIDE), f32),
            jax.ShapeDtypeStruct((2, count, SIDE, width), f32),
            jax.ShapeDtypeStruct(input_grad.shape, f32),
            jax.ShapeDtypeStruct(layer_out.shape, bf16),
            jax.ShapeDtypeStruct((experts, width), f32),
            jax.ShapeDtypeStruct((width,), f32),
            jax.ShapeDtypeStruct((width,), f32),
            jax.ShapeDtypeStruct((2 * SIDE, SIDE + cols), f32),
            jax.ShapeDtypeStruct((2 * SIDE, 2 * SIDE), f32),
        ),
        compiler_params=pltpu.CompilerParams(vmem_limit_bytes=56 * 2**20),
        name="finish",
    )(col.reshape(1), sums, input_grad, layer_out, small, attn_sums)


def turn_tables(total):
    steps_up = np.arange(HEAD // 2, dtype=np.float32) * np.float32(2.0 / HEAD)
    inverse = np.exp(np.float32(-math.log(ROPE_BASE)) * steps_up)
    angles = (np.arange(total, dtype=np.float32)[:, None] * inverse[None, :]).astype(np.float64)
    cosine, sine = np.cos(angles), np.sin(angles)
    return (
        np.concatenate([cosine, cosine], axis=1).astype(np.float32),
        np.concatenate([-sine, sine], axis=1).astype(np.float32),
    )


def local(
    tokens,
    cotangent,
    attn_gain,
    ffn_gain,
    qkv_weight,
    out_weight,
    router_weight,
    gate_weight,
    up_weight,
    down_weight,
    routes,
    segments,
):
    col = lax.axis_index("col")
    xs, zs, cs = dp_sizes()
    own_rows, own_width = tokens.shape
    experts, _, hidden = gate_weight.shape
    pieces = xs * zs
    cosine, sine = turn_tables(2 * own_rows)
    seg = segments[None]
    (
        normed_one,
        queries,
        keys,
        values,
        context,
        qkv_local,
        normed_two,
        out_quarter,
        cot_2,
        cot_3,
        units,
        lse,
        gates,
        scale_one,
        small_all,
        hidden_own,
        scale_two,
    ) = forward_step(
        tokens,
        cotangent,
        qkv_weight,
        router_weight.T,
        attn_gain,
        ffn_gain,
        routes.T,
        cosine,
        sine,
        seg,
        out_weight,
        gate_weight,
        up_weight,
        down_weight,
    )
    (
        weighted,
        pre_grads,
        normed_two_part,
        layer_part,
        cot_all,
        far_2,
        far_3,
        expert_vec,
    ) = experts_step(
        normed_two,
        cotangent,
        cot_2,
        cot_3,
        gates,
        gate_weight,
        up_weight,
        down_weight,
        units.reshape((cs, pieces) + units.shape[3:]),
    )
    hidden_grad, hidden_low, vec_sums, ffn_part, shard = reduce_step(
        normed_two_part,
        expert_vec,
        hidden_own,
        cotangent,
        scale_two,
        ffn_gain,
        normed_two,
        pre_grads,
        weighted,
        cot_all,
        far_2,
        far_3,
    )
    input_grad, layer_out, small_sums, attn_sums, expert_sums = attn_back(
        queries,
        keys,
        values,
        lse,
        seg,
        cosine,
        sine,
        context,
        hidden_low,
        out_quarter.reshape(SIDE, 2 * own_width),
        qkv_local,
        normed_one,
        small_all,
        gates,
        vec_sums,
        ffn_part,
        tokens,
        scale_one,
        attn_gain,
        hidden_grad,
        layer_part,
        hidden_own,
        shard,
    )
    (
        gate_grad,
        up_grad,
        down_grad,
        input_grad,
        layer_out,
        router_grad,
        attn_gain_grad,
        ffn_gain_grad,
        qkv_grad,
        out_grad,
    ) = finish_step(
        expert_sums,
        input_grad,
        layer_out,
        small_sums,
        attn_sums,
        col,
        experts,
    )
    router_grad = router_grad.T
    gate_grad = gate_grad.reshape(experts, own_width, hidden)
    up_grad = up_grad.reshape(experts, own_width, hidden)
    down_grad = down_grad.reshape(experts, hidden, own_width)
    return (
        layer_out,
        input_grad,
        attn_gain_grad,
        ffn_gain_grad,
        qkv_grad,
        out_grad,
        router_grad,
        gate_grad,
        up_grad,
        down_grad,
    )


def solution(mesh):
    in_specs = (
        P(("dp", "row"), "col"),
        P(("dp", "row"), "col"),
        P("col"),
        P("col"),
        P("col", "row"),
        P("row", "col"),
        P("col", None),
        P(None, "col", "row"),
        P(None, "col", "row"),
        P(None, "row", "col"),
        P("dp", None),
        P("dp"),
    )
    out_specs = (
        P(("dp", "row"), "col"),
        P(("dp", "row"), "col"),
        P("col"),
        P("col"),
        P("col", "row"),
        P("row", "col"),
        P("col", None),
        P(None, "col", "row"),
        P(None, "col", "row"),
        P(None, "row", "col"),
    )
    return jax.shard_map(local, mesh=mesh, in_specs=in_specs, out_specs=out_specs, check_vma=False)
```

```python
import functools
import math

import jax
import jax.numpy as jnp
import numpy as np
from jax import lax
from jax.experimental import pallas as pl
from jax.experimental.pallas import tpu as pltpu
from jax.sharding import PartitionSpec as P

f32 = jnp.float32
bf16 = jnp.bfloat16

HEAD = 128
GROUP_HEADS = 6
EPS = 1e-06
ROPE_BASE = 10000.0
MASKED = -1e30
BLOCK = 256


MESH = pl.DeviceIdType.MESH
VMEM = pltpu.VMEM
ANY = pl.BlockSpec(memory_space=pl.ANY)
WHOLE = pl.BlockSpec(memory_space=pltpu.VMEM)
HALF = 512
SIDE = 384


def dp_sizes():
    total = lax.axis_size("dp")
    cores = 2 if total % 2 == 0 else 1
    side = math.isqrt(total // cores)
    return side, side, cores


def dp_place():
    xs, zs, cs = dp_sizes()
    d = lax.axis_index("dp")
    return d // (zs * cs), (d // cs) % zs, d % cs


def nt(a, b):
    return lax.dot_general(a, b, (((1,), (1,)), ((), ())), preferred_element_type=f32)


def nn(a, b):
    return lax.dot_general(a, b, (((1,), (0,)), ((), ())), preferred_element_type=f32)


def tn(a, b):
    return lax.dot_general(a, b, (((0,), (0,)), ((), ())), preferred_element_type=f32)


class Links:
    def __init__(self, send, recv):
        self.send, self.recv = send, recv
        self.used = 0
        self.dp = lax.axis_index("dp")
        self.row = lax.axis_index("row")
        self.col = lax.axis_index("col")
        self.xs, self.zs, self.cs = dp_sizes()
        self.x, self.z, self.core = dp_place()

    def group(self, k):
        row = 1 - self.row if k & 2 else self.row
        col = 1 - self.col if k & 1 else self.col
        return (self.dp, row, col)

    def other_core(self):
        return (self.dp + 1 - 2 * self.core, self.row, self.col)

    def place(self, axis, k):
        x, z = self.x, self.z
        if axis == 0:
            x = (x + k) % self.xs
        else:
            z = (z + k) % self.zs
        return ((x * self.zs + z) * self.cs + self.core, self.row, self.col)

    def greet(self, devices):
        barrier = pltpu.get_barrier_semaphore()
        for device in devices:
            pl.semaphore_signal(barrier, inc=1, device_id=device, device_id_type=MESH)
        pl.semaphore_wait(barrier, len(devices))

    def plane(self):
        return (
            ([self.other_core()] if self.cs == 2 else [])
            + [self.place(0, k) for k in range(1, self.xs)]
            + [self.place(1, k) for k in range(1, self.zs)]
        )

    def copy(self, src, dst, device):
        i = self.used
        self.used += 1
        return pltpu.make_async_remote_copy(
            src_ref=src,
            dst_ref=dst,
            send_sem=self.send.at[i],
            recv_sem=self.recv.at[i],
            device_id=device,
            device_id_type=MESH,
        )

    def go(self, src, dst, device):
        copy = self.copy(src, dst, device)
        copy.start()
        return copy


def at(start, size, step=16):
    return pl.ds(pl.multiple_of(start, step), size)


class Fetch:
    def __init__(self, sems):
        self.sems = sems
        self.used = 0
        self.named = {}

    def start(self, name, *pairs):
        copies = self.named.setdefault(name, [])
        for src, dst in pairs:
            copy = pltpu.make_async_copy(src, dst, self.sems.at[self.used])
            self.used += 1
            copy.start()
            copies.append(copy)

    def wait(self, *names):
        for name in names:
            for copy in self.named.pop(name):
                copy.wait()


def pad16(n):
    return -(-n // 16) * 16


class PlaneSum:
    def __init__(
        self, links, parts, came, in1, piece, in2, peer, shard, groups=1, fold=False, near=None
    ):
        self.links, self.parts, self.came, self.in1 = links, parts, came, in1
        self.fold, self.near = fold, near
        self.ring = {}
        self.piece, self.in2, self.peer, self.shard = piece, in2, peer, shard
        self.sizes = (links.xs, links.zs)
        self.places = (links.x, links.z)
        self.sent = []
        self.first, self.second, self.core = {}, {}, {}
        self.groups = groups
        self.group_rows = came.shape[1] // groups
        self.chunk = self.group_rows // links.xs
        self.rows2 = groups * self.chunk // links.zs

    def start(self):
        kept, rows = self.rows2 * (2 if self.fold else 1), self.piece.shape[2]
        if kept < rows:
            shape = self.piece.shape
            self.piece[:, :, kept:] = jnp.zeros(shape[:2] + (rows - kept, shape[3]), bf16)

    def core_send(self, ab, g=0, which=0):
        if self.links.cs == 1:
            return
        rows = slice(g * self.group_rows, (g + 1) * self.group_rows)
        cols, part = self.parts(ab, 1 - self.links.core)[which]
        copy = self.links.go(
            part.at[rows], self.came.at[ab, rows, cols], self.links.other_core()
        )
        self.core.setdefault((ab, g), []).append(copy)
        self.sent.append(copy)

    def first_send(self, ab, g=0, which=None):
        copies = self.core.get((ab, g), [])
        for copy in copies:
            copy.wait_recv()
        del copies[:]
        total = self.came.at[ab]
        step = 96
        parts = self.parts(ab, self.links.core)
        chosen = parts if which is None else [parts[which]]
        for cols, mine in chosen:

            @pl.loop(0, self.group_rows // step)
            def _(i):
                here = at(g * self.group_rows + i * step, step)
                total[here, cols] = (
                    total[here, cols].astype(f32) + mine[here].astype(f32)
                ).astype(bf16)

        n, place = self.sizes[ab], self.places[ab]
        if self.near is not None and n == 4:
            half = self.chunk // 2
            first = g * self.chunk
            right, left = self.links.place(ab, 1), self.links.place(ab, 3)

            def rows_of(j, h):
                start = g * self.group_rows + ((place + j) % n) * self.chunk + h * half
                return self.came.at[ab, at(start, half)]

            here = slice(g * half, (g + 1) * half)
            passed = [
                self.links.go(rows_of(2, 0), self.near.at[ab, 0, here], right),
                self.links.go(rows_of(2, 1), self.near.at[ab, 1, here], left),
            ]
            from_left, from_right = self.in1.at[ab, 0], self.in1.at[ab, 1]
            top, end = slice(first, first + half), slice(first + half, first + self.chunk)
            direct = [
                self.links.go(rows_of(1, 1), from_left.at[end], right),
                self.links.go(rows_of(3, 0), from_right.at[top], left),
            ]
            self.ring[ab, g] = (
                passed,
                rows_of,
                here,
                self.links.copy(rows_of(1, 0), from_left.at[top], right),
                self.links.copy(rows_of(3, 1), from_right.at[end], left),
            )
            self.sent += passed + direct
            self.first[ab, g, 1] = direct
            return
        cols = slice(None) if which is None else parts[which][0]
        for k in range(1, n):
            j = (place + k) % n
            copy = self.links.go(
                self.came.at[ab, at(g * self.group_rows + j * self.chunk, self.chunk), cols],
                self.in1.at[ab, k - 1, g * self.chunk : (g + 1) * self.chunk, cols],
                self.links.place(ab, k),
            )
            self.first.setdefault((ab, g, k), []).append(copy)
            self.sent.append(copy)

    def relay(self, ab, g=0):
        if (ab, g) not in self.ring:
            return
        passed, rows_of, here, to_right, to_left = self.ring[ab, g]
        for i, (j, h, copy) in enumerate(((1, 0, to_right), (3, 1, to_left))):
            passed[i].wait_recv()
            mine = rows_of(j, h)
            mine[...] = (mine[...].astype(f32) + self.near[ab, i, here].astype(f32)).astype(bf16)
            copy.start()
            self.sent.append(copy)
            self.first[ab, g, 2 + i] = [copy]

    def second_send(self, ab):
        n, place = self.sizes[ab], self.places[ab]
        owns = []
        for g in range(self.groups):
            own = self.came[ab, at(g * self.group_rows + place * self.chunk, self.chunk)].astype(
                f32
            )
            for k in range(1, n):
                for copy in self.first[ab, g, k]:
                    copy.wait_recv()
            for k in range(1, 3 if (ab, g) in self.ring else n):
                own = own + self.in1[ab, k - 1, g * self.chunk : (g + 1) * self.chunk].astype(
                    f32
                )
            owns.append(own)
        own = owns[0] if self.groups == 1 else jnp.concatenate(owns, axis=0)
        kept = self.rows2
        n, place = self.sizes[1 - ab], self.places[1 - ab]
        for j in range(n):
            block = own[j * kept : (j + 1) * kept]
            if self.fold:
                middle = block.shape[1] // 2
                block = jnp.concatenate([block[:, :middle], block[:, middle:]], axis=0)
            self.piece[ab, j, 0 : block.shape[0]] = block.astype(bf16)
        for k in range(1, n):
            j = (place + k) % n
            copy = self.links.go(
                self.piece.at[ab, j], self.in2.at[ab, k - 1], self.links.place(1 - ab, k)
            )
            self.second[ab, k] = copy
            self.sent.append(copy)

    def last_sum(self, ab):
        n, place = self.sizes[1 - ab], self.places[1 - ab]
        value = self.piece[ab, place].astype(f32)
        for k in range(1, n):
            self.second[ab, k].wait_recv()
            value = value + self.in2[ab, k - 1].astype(f32)
        if ab == 0:
            self.shard[0] = value.astype(bf16)
        else:
            self.peer[...] = value.astype(bf16)
            self.swap = self.links.go(self.peer, self.shard.at[1], self.links.group(1))

    def wait_peer(self):
        self.swap.wait()

    def done(self):
        for copy in self.sent:
            copy.wait_send()


class PlaneGather:
    def __init__(self, links, shard, sums, local):
        self.links, self.shard, self.sums, self.local = links, shard, sums, local
        self.relayed = []
        self.sizes = (links.xs, links.zs)
        self.home, self.first, self.second, self.last = {}, {}, [], []
        self.relays = []

    def near(self, ab):
        links = self.links
        x, z = links.x, links.z
        index = (x * links.zs + z) if ab == 0 else (z * links.xs + x)
        here = self.sums.at[links.core, ab, index]
        copy = pltpu.make_async_copy(self.shard.at[ab], here, self.local.at[ab])
        copy.start()
        self.home[ab] = copy
        self.first[ab] = [
            links.go(self.shard.at[ab], here, links.place(1 - ab, k))
            for k in range(1, self.sizes[1 - ab])
        ]

    def far(self, ab, rows=slice(None), ring=False):
        links = self.links
        if ab in self.home:
            for copy in self.first[ab]:
                copy.wait()
            self.home.pop(ab).wait()
        n = self.sizes[1 - ab]
        place = links.x if ab == 0 else links.z
        block = self.sums.at[links.core, ab, pl.ds(place * n, n), rows]
        ring = ring and self.sizes[ab] == 4
        copies = [
            links.go(block, block, links.place(ab, k))
            for k in ((1, 3) if ring else range(1, self.sizes[ab]))
        ]
        self.second.append(copies)
        if ring:
            self.relays.append((ab, rows, copies))

    def relay(self):
        links = self.links
        for ab, rows, copies in self.relays[:2]:
            n = self.sizes[1 - ab]
            place = links.x if ab == 0 else links.z
            half = n // 2
            passed = []
            for i, (k, to) in enumerate(((3, 1), (1, 3))):
                copies[i].wait_recv()
                first = ((place + k) % 4) * n + i * half
                block = self.sums.at[links.core, ab, pl.ds(first, half), rows]
                passed.append(links.go(block, block, links.place(ab, to)))
            self.relayed.append((copies, passed))
        del self.relays[:2]

    def swap(self, rows=slice(None), count=2, ab=None):
        links = self.links
        for copies in self.second[:count]:
            passed = [p for c, p in self.relayed if c is copies]
            for copy in copies:
                copy.wait_send()
                if not passed:
                    copy.wait_recv()
            for copy in passed[0] if passed else ():
                copy.wait()
        del self.second[:count]
        if links.cs == 2:
            if ab is None:
                block = self.sums.at[links.core, :, :, rows]
            else:
                block = self.sums.at[links.core, ab]
            self.last.append(links.go(block, block, links.other_core()))

    def done(self):
        for copy in self.last:
            copy.wait()


def plane_scratch(rows, width, fold=False):
    xs, zs, _ = dp_sizes()
    n1, n2 = max(xs - 1, 1), max(zs - 1, 1)
    kept = rows // (xs * zs)
    shape = (2 * kept, width // 2) if fold else (pad16(kept), width)
    return [
        VMEM((2, rows, width), bf16),
        VMEM((2, n1, rows // xs, width), bf16),
        VMEM((2, zs) + shape, bf16),
        VMEM((2, n2) + shape, bf16),
        VMEM(shape, bf16),
    ]


def gather_group(links, own, dst):
    first = {}
    for k, order in ((2, (1, 0)), (3, (0, 1))):
        for h in order:
            first[k, h] = links.copy(own(h), dst(k, h), links.group(k))
    for key in ((2, 1), (3, 0), (2, 0), (3, 1)):
        first[key].start()
    relay = [
        links.copy(dst(3, 0), dst(1, 0), links.group(2)),
        links.copy(dst(2, 1), dst(1, 1), links.group(3)),
    ]

    def forward():
        first[3, 0].wait_recv()
        relay[0].start()
        first[2, 1].wait_recv()
        relay[1].start()

    def near():
        first[2, 0].wait_recv()
        first[3, 1].wait_recv()

    def far():
        for copy in relay:
            copy.wait_recv()

    def sent():
        for copy in list(first.values()) + relay:
            copy.wait_send()

    return forward, near, far, sent


def unit_rows():
    xs, zs, _ = dp_sizes()
    return 768 // (xs * zs), min(SIDE, 768 // (xs * zs))


def down_units(hid):
    xs, zs, _ = dp_sizes()
    return -(-(hid // unit_rows()[1]) // (xs * zs))


class Units:
    def __init__(self, links, units, out_weight, gate_weight, up_weight, down_weight):
        self.links, self.units = links, units
        rows, down_rows = unit_rows()
        xs, zs = links.xs, links.zs
        pieces = xs * zs
        place = links.x * zs + links.z
        lanes = at(links.core * SIDE, SIDE, 128)
        home = units.at[links.core, links.x, links.z]
        self.out_rows = 3 * rows
        self.cut = 4 * rows
        self.total = units.shape[3]
        self.fetch = []
        for k in (1, 2, 3):
            col = 1 - links.col if k & 1 else links.col
            index = (place + col * (pieces // 2)) % pieces
            self.fetch.append(
                links.go(
                    out_weight.at[index, :, lanes],
                    home.at[(k - 1) * rows : k * rows],
                    links.group(k),
                )
            )
        count = gate_weight.shape[0] // 2
        first = (1 - links.col) * count
        for e in range(count):
            i = links.used
            links.used += 1
            to = home.at[(3 + e) * rows : (4 + e) * rows]
            either = [
                pltpu.make_async_remote_copy(
                    src_ref=weight.at[first + e, place],
                    dst_ref=to,
                    send_sem=links.send.at[i],
                    recv_sem=links.recv.at[i],
                    device_id=links.group(1),
                    device_id_type=MESH,
                )
                for weight in (gate_weight, up_weight)
            ]
            for which in range(2):

                @pl.when(links.core == which)
                def _(copy=either[which]):
                    copy.start()

            self.fetch.append(either[0])
        blocks = down_weight.shape[0] // 2
        for j in range(down_units(blocks * down_rows)):
            index = jnp.minimum(j * pieces + place, blocks - 1)
            start = (3 + count) * rows + j * down_rows
            self.fetch.append(
                links.go(
                    down_weight.at[(1 - links.col) * blocks + index, :, lanes],
                    home.at[start : start + down_rows],
                    links.group(1),
                )
            )

    def near(self):
        for copy in self.fetch:
            copy.wait()
        links = self.links
        home = self.units.at[links.core, links.x, links.z]
        self.first = []
        for rows, axis, n in (
            (slice(0, self.cut), 1, links.zs),
            (slice(self.cut, self.total), 0, links.xs),
        ):
            for k in range(1, n):
                self.first.append(links.go(home.at[rows], home.at[rows], links.place(axis, k)))

    def far(self):
        for copy in self.first:
            copy.wait()
        links, units = self.links, self.units
        self.second = []
        line = units.at[links.core, links.x, :, 0 : self.cut]
        for k in range(1, links.xs):
            self.second.append(links.go(line, line, links.place(0, k)))
        line = units.at[links.core, :, links.z, self.cut : self.total]
        for k in range(1, links.zs):
            self.second.append(links.go(line, line, links.place(1, k)))

    def swap(self):
        for copy in self.second:
            copy.wait()
        links = self.links
        self.last = []
        for rows in (slice(0, self.out_rows), slice(self.out_rows, self.total)):
            block = self.units.at[links.core, :, :, rows]
            self.last.append(links.go(block, block, links.other_core()))

    def wait_out(self):
        self.last[0].wait()

    def done(self):
        self.last[1].wait()


def forward_kernel(
    heads,
    tokens,
    cot_h,
    qkv_weight,
    router_weight,
    attn_gain,
    ffn_gain,
    routes,
    cosine,
    sine,
    seg,
    out_weight,
    gate_weight,
    up_weight,
    down_weight,
    normed_h,
    q_h,
    k_h,
    v_h,
    context_h,
    qkv_h,
    normed_two_h,
    quarter_h,
    cot_2,
    cot_3,
    units,
    lse,
    gates_ref,
    scale_one,
    small_all,
    hidden_own,
    scale_two,
    tokens_all,
    qkv_all,
    normed,
    q,
    k,
    v,
    vt,
    contexts,
    weight,
    hidden,
    normed_two,
    small,
    segk,
    segq,
    route_cols,
    send,
    recv,
    sems,
):
    links = Links(send, recv)
    row, col = links.row, links.col
    zs, cs = links.zs, links.cs
    total, full = normed.shape
    width = full // 2
    quarter = HALF // 2
    small[0:6, :] = router_weight[...].astype(f32)
    small[6:7, :] = attn_gain[...].reshape(1, width)
    small[7:8, :] = ffn_gain[...].reshape(1, width)
    links.greet([links.group(k) for k in (1, 2, 3)] + links.plane())

    def own(h):
        return tokens.at[h * quarter : (h + 1) * quarter]

    def dst(k, h):
        rows = (HALF if k & 2 else 0) + h * quarter
        return tokens_all.at[rows : rows + quarter, (k & 1) * width : (k & 1) * width + width]

    share = width // (cs * zs)
    start = links.core * (width // cs) + links.z * share
    there = at(width + start, share)
    fetch_qkv = [
        links.go(
            qkv_weight.at[at(start, share), at((1 - col) * SIDE, SIDE, 128)],
            qkv_all.at[there, 0:SIDE],
            links.group(1),
        ),
        links.go(
            qkv_weight.at[at(start, share), 2 * SIDE :], qkv_all.at[there, SIDE:], links.group(1)
        ),
        links.go(small, small_all.at[:, width:], links.group(1)),
    ]
    shares = Units(links, units, out_weight, gate_weight, up_weight, down_weight)
    forward, near, far, tokens_sent = gather_group(links, own, dst)
    fetch = Fetch(sems)
    pieces = weight.shape[1]
    half = pieces // 2
    fetch.start(
        "weight",
        *[
            (
                out_weight.at[pl.ds((col if h == 0 else 1 - col) * half, half)],
                weight.at[0, h * half : (h + 1) * half, :, 0:width],
            )
            for h in range(2)
        ],
    )
    tokens_all[0:HALF, 0:width] = tokens[...]
    qkv_all[0:width, 0:SIDE] = qkv_weight[:, at(col * SIDE, SIDE, 128)]
    qkv_all[0:width, SIDE:] = qkv_weight[:, 2 * SIDE :]
    small_all[:, 0:width] = small[...]
    segq[...] = seg[...].astype(f32)
    segk[...] = column(segq[...])
    count = routes.shape[0]
    route_cols[...] = jnp.concatenate(
        [routes[...].astype(f32), jnp.zeros((128 - count, total), f32)], axis=0
    ).T
    for copy in fetch_qkv:
        copy.wait()
    spread = [
        links.go(qkv_all.at[there], qkv_all.at[there], links.place(1, k)) for k in range(1, zs)
    ]
    shares.near()
    forward()
    for copy in spread:
        copy.wait()
    if cs == 2:
        block = qkv_all.at[at(width + links.core * (width // 2), width // 2)]
        swap_qkv = links.go(block, block, links.other_core())
    shares.far()
    if cs == 2:
        swap_qkv.wait()
    near()

    def project(i):
        rows = slice(i * BLOCK, (i + 1) * BLOCK)
        place = i * BLOCK // HALF
        here = at(
            HALF * jnp.bitwise_xor(row, place) + (i * BLOCK - place * HALF), BLOCK, BLOCK
        )
        x = tokens_all[rows].astype(f32)
        scale = lax.rsqrt(jnp.sum(x * x, axis=1, keepdims=True) * (1.0 / full) + EPS)
        low = (x * scale * small_all[6:7, :]).astype(bf16)
        normed[rows] = low
        if i * BLOCK < HALF:
            scale_one[rows] = jnp.broadcast_to(scale, (BLOCK, 128))
        router = jnp.concatenate([small_all[...], jnp.zeros((120, full), f32)], axis=0)
        logits = nt(low, router.astype(bf16))
        lanes = lax.broadcasted_iota(jnp.int32, (BLOCK, 128), 1).astype(f32)
        chosen = lanes == route_cols[here, 0:1]
        for j in range(1, count):
            chosen = chosen | (lanes == route_cols[here, j : j + 1])
        masked = jnp.where(chosen, logits, MASKED)
        raised = jnp.exp(masked - jnp.max(masked, axis=1, keepdims=True))
        raised = jnp.where(chosen, raised, 0.0)
        gates_ref[rows] = raised / jnp.sum(raised, axis=1, keepdims=True)
        projected = nn(low, qkv_all[...])
        for h in range(heads + 1):
            part = projected[:, h * HEAD : (h + 1) * HEAD]
            turned = (part * cosine[here] + swap_halves(part) * sine[here]).astype(bf16)
            if h < heads:
                q[here, h * HEAD : (h + 1) * HEAD] = turned
            else:
                k[here] = turned
        v[here] = projected[:, (heads + 1) * HEAD :].astype(bf16)

    project(2)
    project(3)
    far()
    cot_copies = [
        links.go(cot_h.at[h * quarter : (h + 1) * quarter], out, links.group(k))
        for k, out, h in ((2, cot_2, 1), (3, cot_3, 0))
    ]
    project(0)
    project(1)
    fetch.start("out", (normed, normed_h), (q, q_h), (k, k_h), (v, v_h), (qkv_all, qkv_h))

    vt[...] = v[...].astype(f32).T.astype(bf16)

    def block(j, h, head):
        first = j * SIDE + head * HEAD
        return contexts.at[h * HALF : (h + 1) * HALF, first : first + HEAD]

    sends, relays = {}, []
    for head in range(heads):
        cols = slice(head * HEAD, (head + 1) * HEAD)
        for i in range(total // BLOCK):
            first, last = window(i, BLOCK)
            here = slice(i * BLOCK, (i + 1) * BLOCK)
            allowed = allowed_keys(segk, segq, i, first, last)
            place = i * BLOCK // HALF
            rows = at(
                HALF * jnp.bitwise_xor(row, place) + (i * BLOCK - place * HALF), BLOCK, BLOCK
            )
            s = nt(k[first:last], q[here, cols]) * (HEAD**-0.5)
            s = jnp.where(allowed, s, MASKED)
            top = jnp.max(s, axis=0, keepdims=True)
            p = jnp.exp(s - top)
            total_p = jnp.sum(p, axis=0, keepdims=True)
            p = (p * (1.0 / total_p)).astype(bf16)
            ot = nn(vt[:, first:last], p)
            contexts[rows, cols] = ot.T.astype(bf16)
            lse[head : head + 1, here] = top + jnp.log(total_p)
        for j, h in ((2, 0), (3, 1), (2, 1), (3, 0)):
            sends[j, 1 - h, head] = links.go(
                block(0, h, head), block(j, 1 - h, head), links.group(j)
            )
    lse[heads:, :] = jnp.zeros((8 - heads, total), f32)
    fetch.start("context", (contexts.at[:, 0:SIDE], context_h))
    shares.swap()
    for head in range(heads):
        sends[3, 0, head].wait_recv()
        relays.append(links.go(block(3, 0, head), block(1, 1, head), links.group(2)))
        sends[2, 1, head].wait_recv()
        relays.append(links.go(block(2, 1, head), block(1, 0, head), links.group(3)))

    shares.wait_out()
    rows = weight.shape[2]
    for j in (1, 2, 3):
        for core in range(2):
            first = (j & 1) * width + core * SIDE
            fetch.start(
                "weight",
                *[
                    (
                        units.at[core, x, :, (j - 1) * rows : j * rows],
                        weight.at[j // 2, x * zs : (x + 1) * zs, :, first : first + SIDE],
                    )
                    for x in range(links.xs)
                ],
            )
    for head in range(heads):
        sends[2, 0, head].wait_recv()
        sends[3, 1, head].wait_recv()
    fetch.wait("weight")
    w_own = weight[0, 0:half].reshape(SIDE, full)
    w_far = weight[1].reshape(width, full)
    fetch.start("quarter", (weight.at[0, 0:half], quarter_h))
    for i in range(2):
        rows = slice(i * HALF, (i + 1) * HALF)
        hidden[rows] = (
            tokens_all[rows].astype(f32)
            + nn(contexts[rows, 0:SIDE], w_own)
            + nn(contexts[rows, 2 * SIDE :], w_far)
        )
    for copy in relays:
        copy.wait_recv()
    w_peer = weight[0, half:].reshape(SIDE, full)
    for i in range(2):
        rows = slice(i * HALF, (i + 1) * HALF)
        value = hidden[rows] + nn(contexts[rows, SIDE : 2 * SIDE], w_peer)
        scale = lax.rsqrt(jnp.sum(value * value, axis=1, keepdims=True) * (1.0 / full) + EPS)
        normed_two[rows] = (value * scale * small_all[7:8, :]).astype(bf16)
        if i == 0:
            scale_two[...] = jnp.broadcast_to(scale, (HALF, 128))
            hidden_own[...] = value[:, 0:width]
        fetch.start("out", (normed_two.at[rows], normed_two_h.at[rows]))
    tokens_sent()
    for copy in relays + list(sends.values()):
        copy.wait_send()
    for copy in cot_copies:
        copy.wait()
    shares.done()
    fetch.wait("out", "context", "quarter")


def forward_step(
    tokens,
    cot,
    qkv_weight,
    router_weight,
    attn_gain,
    ffn_gain,
    routes,
    cosine,
    sine,
    seg,
    out_weight,
    gate_weight,
    up_weight,
    down_weight,
):
    xs, zs, cs = dp_sizes()
    pieces = xs * zs
    rows, down_rows = unit_rows()
    width = tokens.shape[1]
    full, total = 2 * width, 2 * HALF
    heads = SIDE // HEAD
    experts, _, hidden = gate_weight.shape
    hid = experts // 2 * hidden
    unit_total = (3 + experts // 2) * rows + down_units(hid) * down_rows
    out = [
        jax.ShapeDtypeStruct((total, full), bf16),
        jax.ShapeDtypeStruct((total, SIDE), bf16),
        jax.ShapeDtypeStruct((total, HEAD), bf16),
        jax.ShapeDtypeStruct((total, HEAD), bf16),
        jax.ShapeDtypeStruct((total, SIDE), bf16),
        jax.ShapeDtypeStruct((full, SIDE + 2 * HEAD), bf16),
        jax.ShapeDtypeStruct((total, full), bf16),
        jax.ShapeDtypeStruct((pieces // 2, rows, full), bf16),
        jax.ShapeDtypeStruct((HALF // 2, width), bf16),
        jax.ShapeDtypeStruct((HALF // 2, width), bf16),
        jax.ShapeDtypeStruct((cs, xs, zs, unit_total, SIDE), bf16),
        jax.ShapeDtypeStruct((8, total), f32),
        jax.ShapeDtypeStruct((total, 128), f32),
        jax.ShapeDtypeStruct((HALF, 128), f32),
        jax.ShapeDtypeStruct((8, full), f32),
        jax.ShapeDtypeStruct((HALF, width), f32),
        jax.ShapeDtypeStruct((HALF, 128), f32),
    ]
    return pl.pallas_call(
        functools.partial(forward_kernel, heads),
        out_shape=tuple(out),
        in_specs=[WHOLE, ANY] + [WHOLE] * 8 + [ANY] * 4,
        out_specs=(ANY,) * 11 + (WHOLE,) * 6,
        scratch_shapes=[
            VMEM((total, full), bf16),
            VMEM((full, SIDE + 2 * HEAD), bf16),
            VMEM((total, full), bf16),
            VMEM((total, SIDE), bf16),
            VMEM((total, HEAD), bf16),
            VMEM((total, HEAD), bf16),
            VMEM((HEAD, total), bf16),
            VMEM((total, full), bf16),
            VMEM((2, pieces, rows, full), bf16),
            VMEM((total, full), f32),
            VMEM((total, full), bf16),
            VMEM((8, width), f32),
            VMEM((total, 128), f32),
            VMEM((1, total), f32),
            VMEM((total, 128), f32),
            pltpu.SemaphoreType.DMA((80,)),
            pltpu.SemaphoreType.DMA((80,)),
            pltpu.SemaphoreType.DMA((48,)),
        ],
        compiler_params=pltpu.CompilerParams(
            collective_id=0, has_side_effects=True, vmem_limit_bytes=60 * 2**20
        ),
        name="forward_step",
    )(
        tokens,
        cot,
        qkv_weight,
        router_weight,
        attn_gain,
        ffn_gain,
        routes,
        cosine,
        sine,
        seg,
        out_weight.reshape(pieces, rows, width),
        gate_weight.reshape(experts, pieces, rows, hidden),
        up_weight.reshape(experts, pieces, rows, hidden),
        down_weight.reshape(-1, down_rows, width),
    )


def scatter_group(links, blocks, pass2, pass3, near2, near3, far, out2, out3):
    n2, n3 = links.group(2), links.group(3)
    start, direct = [], []

    def send_own_rows():
        start.append(links.go(blocks(1, 0), near2, n2))
        start.append(links.go(blocks(1, 1), near3, n3))

    def send_other_rows():
        direct.append(links.go(blocks(3, 1), far(3, 1), n3))
        direct.append(links.go(blocks(2, 0), far(2, 0), n2))

    relay = [links.copy(out3, far(3, 0), n3), links.copy(out2, far(2, 1), n2)]

    def forward():
        start[0].wait_recv()
        out3[...] = (pass3[...].astype(f32) + near2[...].astype(f32)).astype(bf16)
        relay[0].start()
        start[1].wait_recv()
        out2[...] = (pass2[...].astype(f32) + near3[...].astype(f32)).astype(bf16)
        relay[1].start()

    def finish():
        for copy in direct + relay:
            copy.wait_recv()

    def sent():
        for copy in start + direct + relay:
            copy.wait_send()

    return send_own_rows, send_other_rows, forward, finish, sent


def group_scratch(width):
    quarter = HALF // 2
    return [
        VMEM((quarter, width), bf16),
        VMEM((quarter, width), bf16),
        VMEM((HALF, width), bf16),
        VMEM((HALF, width), bf16),
        VMEM((quarter, width), bf16),
        VMEM((quarter, width), bf16),
    ]


def norm_back_rows(grad, gain, values, scale, inner, width):
    return scale * (grad * gain - values * (scale * inner * (1.0 / width)))


def column(row_vector):
    return jnp.broadcast_to(row_vector, (128, row_vector.shape[1])).T


def half_swap(v):
    return jnp.concatenate([v[:, HALF:], v[:, :HALF]], axis=1)


def reduce_kernel(
    partial,
    vectors,
    hidden_h,
    cot_h,
    scale_h,
    gain,
    normed_h,
    grads_h,
    weighted_h,
    cot_all_h,
    far_2,
    far_3,
    hidden_grad_h,
    hidden_low,
    vector_sums,
    gain_part,
    shard,
    hidden_grad,
    hidden,
    cot,
    scale,
    normed,
    grads,
    weighted,
    cot_all,
    normed_t,
    mine_p,
    pass2,
    pass3,
    near2,
    near3,
    far2,
    far3,
    out2,
    out3,
    vec_in,
    low,
    up_part,
    down_part,
    up_near,
    down_near,
    *rest,
):
    up_scratch, down_scratch = rest[0:5], rest[5:10]
    send, recv, sems, local = rest[10:]
    links = Links(send, recv)
    width = hidden_grad.shape[1]
    step = HALF // 4
    quarter = HALF // 2
    count, _, both = grads.shape
    side = both // 2
    fetch = Fetch(sems)
    fetch.start("normed", (normed_h, normed))
    fetch.start("grads", *[(grads_h.at[e], grads.at[e]) for e in range(count)])
    fetch.start("down", (weighted_h, weighted), (cot_all_h, cot_all))
    fetch.start(
        "pass",
        (partial.at[HALF + quarter :, 0:width], pass2),
        (partial.at[HALF : HALF + quarter, width:], pass3),
    )
    fetch.start(
        "own",
        (partial.at[0:HALF, 0:width], mine_p),
        (hidden_h, hidden),
        (cot_h, cot),
        (scale_h, scale),
        (far_2, far2.at[0:quarter]),
        (far_3, far3.at[quarter:]),
    )
    links.greet([links.group(k) for k in (1, 2, 3)] + links.plane())

    vec_copies = [links.go(vectors, vec_in.at[k - 1], links.group(k)) for k in (1, 2, 3)]

    def chunk(c):
        def blocks(k, h):
            first = (HALF if k & 2 else 0) + h * quarter + c * step
            cols = slice((k & 1) * width, (k & 1) * width + width)
            return partial.at[first : first + step, cols]

        def far(k, h):
            first = h * quarter + c * step
            return (far2 if k == 2 else far3).at[first : first + step]

        here = slice(c * step, (c + 1) * step)
        return scatter_group(
            links,
            blocks,
            pass2.at[here],
            pass3.at[here],
            near2.at[here],
            near3.at[here],
            far,
            out2.at[here],
            out3.at[here],
        )

    chunks = [chunk(c) for c in range(2)]
    own_rows, _, forward, finish, sent = [
        [functions[i] for functions in chunks] for i in range(5)
    ]
    own_rows[0]()
    own_rows[1]()

    kept = up_scratch[4].shape[0]
    up = PlaneSum(
        links,
        lambda ab, core: [(slice(None), up_part.at[core, ab])],
        *up_scratch,
        shard.at[:, 0:kept],
        count,
        near=up_near,
    )
    down = PlaneSum(
        links,
        lambda ab, core: [(slice(None), down_part.at[core, ab])],
        *down_scratch,
        shard.at[:, kept:],
        count,
        near=down_near,
    )
    up.start()
    down.start()
    fetch.wait("normed")
    for i in range(4):
        rows = slice(i * 256, (i + 1) * 256)
        normed_t[:, rows] = normed[rows].T
    state = {}

    def prepare():
        for copy in vec_copies:
            copy.wait()
        vec = vectors[...] + vec_in[0] + half_swap(vec_in[1] + vec_in[2])
        vector_sums[...] = vec
        fetch.wait("own")
        state["inner"] = column(vec[6:7, 0:HALF])[:, 0:1]
        state["part"] = jnp.zeros((8, width), f32)
        state["gain"] = gain[...].reshape(1, width)

    def norm_back(c):
        for h in range(2):
            first = h * quarter + c * step
            rows = slice(first, first + step)
            grad = mine_p[rows].astype(f32) + far2[rows].astype(f32) + far3[rows].astype(f32)
            values = hidden[rows]
            scale_rows = scale[rows, 0:1]
            back = norm_back_rows(
                grad, state["gain"], values, scale_rows, state["inner"][rows], 2 * width
            )
            back = back + cot[rows].astype(f32)
            hidden_grad[rows] = back
            low[rows] = back.astype(bf16)
            state["part"] = state["part"] + jnp.sum(
                (grad * values * scale_rows).reshape(step // 8, 8, width), axis=0
            )

    def gather(c):
        def own(h):
            first = h * quarter + c * step
            return low.at[first : first + step]

        def dst(k, h):
            first = (HALF if k & 2 else 0) + h * quarter + c * step
            cols = slice((k & 1) * width, (k & 1) * width + width)
            return hidden_low.at[first : first + step, cols]

        return gather_group(links, own, dst)

    gathers = []

    def finish_chunk(c):
        finish[c]()
        norm_back(c)
        gathers.append(gather(c))

    fetch.wait("grads", "down", "pass")
    pending = []
    for e in range(count):
        for ab in range(2):
            rows = slice(e * width, (e + 1) * width)
            part = nn(normed_t[ab * width : (ab + 1) * width], grads[e])
            for which in range(2):
                up_part[which, ab, rows] = part[:, which * side : (which + 1) * side].astype(
                    bf16
                )
            up.core_send(ab, e)
            rows = slice(e * side, (e + 1) * side)
            part = tn(weighted[:, rows], cot_all[:, ab * width : (ab + 1) * width])
            for which in range(2):
                down_part[which, ab, rows] = part[:, which * side : (which + 1) * side].astype(
                    bf16
                )
            down.core_send(ab, e)
            if (e, ab) == (0, 1):
                forward[0]()
            if (e, ab) == (1, 0):
                forward[1]()
            pending.append((ab, e))
            if len(pending) > 1:
                up.first_send(*pending[-2])
                down.first_send(*pending[-2])
            if (e, ab) == (2, 0):
                prepare()
                finish_chunk(0)
    up.first_send(*pending[-1])
    down.first_send(*pending[-1])
    finish_chunk(1)
    keep = pltpu.make_async_copy(hidden_grad, hidden_grad_h, local.at[1])
    keep.start()
    gain_part[...] = jnp.broadcast_to(jnp.sum(state["part"], axis=0, keepdims=True), (8, width))
    mine = pltpu.make_async_copy(low, hidden_low.at[0:HALF, 0:width], local.at[0])
    mine.start()
    for step_of in pending:
        up.relay(*step_of)
        down.relay(*step_of)
    gathers[0][0]()
    for ab in range(2):
        up.second_send(ab)
        down.second_send(ab)
    gathers[1][0]()
    for ab in (1, 0):
        up.last_sum(ab)
        down.last_sum(ab)
    up.wait_peer()
    down.wait_peer()
    mine.wait()
    keep.wait()
    for c in range(2):
        for wait in gathers[c][1:]:
            wait()
        sent[c]()
    up.done()
    down.done()


def reduce_step(
    partial, vectors, hidden, cot, scale, gain, normed, grads, weighted, cot_all, far_2, far_3
):
    xs, zs, _ = dp_sizes()
    width = hidden.shape[1]
    count, total, both = grads.shape
    side = both // 2
    up_rows, down_rows = count * width, count * side
    quarter = HALF // 2
    return pl.pallas_call(
        reduce_kernel,
        out_shape=(
            jax.ShapeDtypeStruct((HALF, width), f32),
            jax.ShapeDtypeStruct((2 * HALF, 2 * width), bf16),
            jax.ShapeDtypeStruct(vectors.shape, f32),
            jax.ShapeDtypeStruct((8, width), f32),
            jax.ShapeDtypeStruct(
                (2, pad16(up_rows // (xs * zs)) + pad16(down_rows // (xs * zs)), side), bf16
            ),
        ),
        in_specs=[ANY, WHOLE, ANY, ANY, ANY, WHOLE] + [ANY] * 6,
        out_specs=(ANY, ANY, WHOLE, WHOLE, WHOLE),
        scratch_shapes=[
            VMEM((HALF, width), f32),
            VMEM((HALF, width), f32),
            VMEM((HALF, width), bf16),
            VMEM((HALF, 128), f32),
            VMEM(normed.shape, bf16),
            VMEM(grads.shape, bf16),
            VMEM(weighted.shape, bf16),
            VMEM(cot_all.shape, bf16),
            VMEM((2 * width, total), bf16),
            VMEM((HALF, width), bf16),
            VMEM((quarter, width), bf16),
            VMEM((quarter, width), bf16),
        ]
        + group_scratch(width)
        + [
            VMEM((3,) + vectors.shape, f32),
            VMEM((HALF, width), bf16),
            VMEM((2, 2, up_rows, side), bf16),
            VMEM((2, 2, down_rows, side), bf16),
            VMEM((2, 2, up_rows // xs // 2, side), bf16),
            VMEM((2, 2, down_rows // xs // 2, side), bf16),
        ]
        + plane_scratch(up_rows, side)
        + plane_scratch(down_rows, side)
        + [
            pltpu.SemaphoreType.DMA((160,)),
            pltpu.SemaphoreType.DMA((160,)),
            pltpu.SemaphoreType.DMA((16,)),
            pltpu.SemaphoreType.DMA((2,)),
        ],
        compiler_params=pltpu.CompilerParams(
            collective_id=2, has_side_effects=True, vmem_limit_bytes=60 * 2**20
        ),
        name="reduce_step",
    )(partial, vectors, hidden, cot, scale, gain, normed, grads, weighted, cot_all, far_2, far_3)


def attn_back_kernel(
    heads,
    q_h,
    k_h,
    v_h,
    lse,
    seg,
    cos_h,
    sin_h,
    context_h,
    hidden_low_h,
    out_weight,
    qkv_h,
    normed_h,
    small_all,
    gates,
    vec_sums,
    ffn_part,
    tokens_h,
    scale_h,
    gain,
    hidden_grad_h,
    layer_h,
    hidden_h,
    expert_shard,
    input_grad,
    layer_out,
    small_out,
    attn_sums,
    expert_sums,
    q,
    k,
    v,
    cos_ref,
    sin_ref,
    context,
    hidden_low,
    qkv,
    normed,
    tokens,
    scale,
    hidden_grad,
    kt,
    do,
    dk,
    dv,
    grads,
    partial,
    qkv_part,
    out_part,
    near2,
    near3,
    far2,
    far3,
    out2,
    out3,
    layer_mine,
    layer_pass2,
    layer_pass3,
    hidden,
    lnear2,
    lnear3,
    lfar2,
    lfar3,
    lout2,
    lout3,
    vec_own,
    vec_in,
    small_own,
    small_in,
    attn_shard,
    segk,
    segq,
    *rest,
):
    attn_scratch = rest[0:5]
    send, recv, sems, local = rest[5:]
    links = Links(send, recv)
    xs, zs, cs = links.xs, links.zs, links.cs
    row = links.row
    total, full = normed.shape
    width = full // 2
    quarter = HALF // 2
    head_scale = HEAD**-0.5
    fetch = Fetch(sems)
    fetch.start("out", (context_h, context), (hidden_low_h, hidden_low))
    fetch.start("attention", (q_h, q), (k_h, k), (v_h, v))
    fetch.start("turn", (cos_h, cos_ref), (sin_h, sin_ref))
    fetch.start("normed", (normed_h, normed))
    fetch.start("qkv", (qkv_h, qkv))
    fetch.start(
        "own",
        (tokens_h, tokens),
        (scale_h, scale),
        (hidden_grad_h, hidden_grad),
    )
    fetch.start(
        "layer",
        (layer_h.at[0:HALF, 0:width], layer_mine),
        (layer_h.at[HALF + quarter :, 0:width], layer_pass2),
        (layer_h.at[HALF : HALF + quarter, width:], layer_pass3),
        (hidden_h, hidden),
    )
    links.greet([links.group(k) for k in (1, 2, 3)] + links.plane())

    def layer_blocks(k, h):
        first = (HALF if k & 2 else 0) + h * quarter
        cols = slice((k & 1) * width, (k & 1) * width + width)
        return layer_h.at[first : first + quarter, cols]

    def halves_of(a, b):
        return lambda k, h: (a if k == 2 else b).at[h * quarter : (h + 1) * quarter]

    layer_own, layer_other, layer_forward, layer_finish, layer_sent = scatter_group(
        links,
        layer_blocks,
        layer_pass2,
        layer_pass3,
        lnear2,
        lnear3,
        halves_of(lfar2, lfar3),
        lout2,
        lout3,
    )
    layer_own()
    layer_other()
    segq[...] = seg[...].astype(f32)
    segk[...] = column(segq[...])

    cols_all = qkv.shape[1]

    def parts(ab, core):
        first = ab * width + core * SIDE
        return [
            (slice(0, cols_all), qkv_part.at[at(first, SIDE)]),
            (slice(cols_all, cols_all + SIDE), out_part.at[:, at(first, SIDE, 128)]),
        ]

    attn_sum = PlaneSum(links, parts, *attn_scratch, attn_shard, 1, True)
    attn_sum.start()
    attn_gather = PlaneGather(links, attn_shard, attn_sums, local.at[0])
    expert_gather = PlaneGather(links, expert_shard, expert_sums, local.at[1])
    expert_gather.near(0)
    expert_gather.near(1)
    piece_rows = expert_shard.shape[1]
    cuts = [0, pad16(piece_rows * 5 // 14), pad16(piece_rows * 5 // 7), piece_rows]

    def spread(i):
        for ab in range(2):
            expert_gather.far(ab, slice(cuts[i], cuts[i + 1]), True)

    fetch.wait("out")
    out_part[...] = tn(context[...], hidden_low[...]).astype(bf16)
    for ab in range(2):
        attn_sum.core_send(ab, 0, 1)

    for h in range(2):
        rows = at(HALF * jnp.bitwise_xor(row, h), HALF)
        do[h * HALF : (h + 1) * HALF] = nt(hidden_low[rows], out_weight[...]).astype(bf16)
    fetch.wait("attention", "turn")
    for ab in range(2):
        attn_sum.first_send(ab, 0, 1)
    for i in range(3):
        spread(i)
    kt[...] = k[...].astype(f32).T.astype(bf16)
    dk[...] = jnp.zeros_like(dk)
    dv[...] = jnp.zeros_like(dv)

    def back(grad, here):
        return grad * cos_ref[here] - swap_halves(grad) * sin_ref[here]

    def rows_of(i):
        place = i * BLOCK // HALF
        return at(HALF * jnp.bitwise_xor(row, place) + (i * BLOCK - place * HALF), BLOCK, BLOCK)

    inners = []
    for i in range(total // BLOCK):
        first, last = window(i, BLOCK)
        here = slice(i * BLOCK, (i + 1) * BLOCK)
        allowed = allowed_keys(segk, segq, i, first, last)
        rows = rows_of(i)
        inner_q = jnp.zeros((BLOCK, 1), f32)
        for h in range(heads):
            cols = slice(h * HEAD, (h + 1) * HEAD)
            s = nt(k[first:last], q[here, cols]) * head_scale
            s = jnp.where(allowed, s, MASKED)
            p = jnp.exp(s - lse[h : h + 1, here])
            dp = nt(v[first:last], do[here, cols])
            inner = jnp.sum(dp * p, axis=0, keepdims=True)
            ds = (p * (dp - inner)).astype(bf16)
            dq = (nn(kt[:, first:last], ds) * head_scale).T
            inner_q = inner_q + jnp.sum(dq * q[here, cols].astype(f32), axis=1, keepdims=True)
            grads[rows, cols] = back(dq, here).astype(bf16)
            dk[first:last] += nn(ds, q[here, cols]) * head_scale
            dv[first:last] += nn(p.astype(bf16), do[here, cols])
        inners.append(inner_q)
        if i == 2:
            fetch.wait("layer")
            layer_forward()
    expert_gather.relay()

    gate_rows = gates[...].T[0:8, :]
    sums = vec_sums[...]
    mask = lax.broadcasted_iota(jnp.int32, sums.shape, 0) < 6
    sums = jnp.where(mask, sums, 0.0)
    logits_grad = gate_rows * (sums - jnp.sum(gate_rows * sums, axis=0, keepdims=True))
    logits_low = jnp.where(mask, logits_grad, 0.0).astype(bf16)
    router = jnp.where(
        lax.broadcasted_iota(jnp.int32, (8, full), 0) < 6, small_all[...], 0.0
    )
    router_low = router.astype(bf16)
    once = jnp.where((row == 0) & (links.col == 0), 1.0, 0.0)
    fetch.wait("normed")
    router_grad = nn(logits_low, normed[...])
    router_inner = once * jnp.sum(
        logits_low.astype(f32) * nt(router_low, normed[...]), axis=0, keepdims=True
    )
    for i in range(total // BLOCK):
        here = slice(i * BLOCK, (i + 1) * BLOCK)
        rows = rows_of(i)
        key_grad, value_grad = dk[here], dv[here]
        inner = inners[i] + jnp.sum(
            key_grad * k[here].astype(f32) + value_grad * v[here].astype(f32),
            axis=1,
            keepdims=True,
        )
        grads[rows, heads * HEAD : (heads + 1) * HEAD] = back(key_grad, here).astype(bf16)
        grads[rows, (heads + 1) * HEAD :] = value_grad.astype(bf16)
        vec_own[:, rows] = jnp.broadcast_to(inner, (BLOCK, 128)).T[0:8, :]
    vec_own[...] += router_inner
    vec_copies = [links.go(vec_own, vec_in.at[k - 1], links.group(k)) for k in (1, 2, 3)]

    def blocks(k, h):
        first = (HALF if k & 2 else 0) + h * quarter
        cols = slice((k & 1) * width, (k & 1) * width + width)
        return partial.at[first : first + quarter, cols]

    own_rows, other_rows, forward, finish, sent = scatter_group(
        links,
        blocks,
        partial.at[HALF + quarter :, 0:width],
        partial.at[HALF : HALF + quarter, width:],
        near2,
        near3,
        halves_of(far2, far3),
        out2,
        out3,
    )
    fetch.wait("qkv")
    partial[0:HALF] = nt(grads[0:HALF], qkv[...]).astype(bf16)
    own_rows()
    expert_gather.relay()
    partial[HALF:] = nt(grads[HALF:], qkv[...]).astype(bf16)
    other_rows()

    gain_sums = {}
    for mine in (False, True):
        which = links.core if mine else 1 - links.core
        for ab in range(2):
            first = ab * width + which * SIDE
            part = tn(normed[:, at(first, SIDE, 128)], grads[...])
            rows = at(first, SIDE)
            qkv_part[rows] = part.astype(bf16)
            gain_sum = jnp.sum(part * qkv[rows].astype(f32), axis=1, keepdims=True)
            gain_sums[mine, ab] = jnp.broadcast_to(gain_sum, (SIDE, 128)).T[0:8, :]
            if not mine:
                attn_sum.core_send(ab, 0, 0)
    for ab in range(2):
        attn_sum.first_send(ab, 0, 0)
    expert_gather.relay()

    halves = []
    for ab in range(2):
        a, b = gain_sums[True, ab], gain_sums[False, ab]
        first = links.core == 0
        halves.append(jnp.concatenate([jnp.where(first, a, b), jnp.where(first, b, a)], axis=1))
    gain_row = jnp.concatenate(halves, axis=1)
    gain_row = gain_row + once * jnp.sum(router_grad * router, axis=0, keepdims=True)
    gain_row = gain_row / small_all[6:7, :]
    ffn = jnp.concatenate([ffn_part[...], jnp.zeros((8, width), f32)], axis=1)
    index = lax.broadcasted_iota(jnp.int32, (8, full), 0)
    small_own[0] = jnp.where(index < 6, router_grad, jnp.where(index == 6, gain_row, ffn))

    def small_stage(stage):
        if stage < 3:
            base = (0, 1, xs)[stage]
            devices = [
                links.other_core() if stage == 0 else links.place(stage - 1, k)
                for k in range(1, (cs, xs, zs)[stage])
            ]
        else:
            base = xs + zs - 1
            devices = [links.group(k) for k in (1, 2, 3)]
        copies = [
            (links.go(small_own.at[stage], small_in.at[base + i], device), base + i)
            for i, device in enumerate(devices)
        ]

        def done():
            value = small_own[stage]
            came = []
            for copy, i in copies:
                copy.wait()
                came.append(small_in[i])
            if stage < 3:
                for v in came:
                    value = value + v
                small_own[stage + 1] = value
            else:
                swap = came[0] + came[2]
                total_rows = (
                    value + came[1] + jnp.concatenate([swap[:, width:], swap[:, :width]], axis=1)
                )
                eight = lax.broadcasted_iota(jnp.int32, (8, width), 0)
                small_out[...] = jnp.where(
                    eight < 6, value[:, 0:width], total_rows[:, 0:width]
                )

        return done

    done = small_stage(0)
    layer_finish()
    for h in range(4):
        rows = slice(h * 128, (h + 1) * 128)
        layer_out[rows] = (
            hidden[rows]
            + layer_mine[rows].astype(f32)
            + lfar2[rows].astype(f32)
            + lfar3[rows].astype(f32)
        ).astype(bf16)
    done()
    done = small_stage(1)
    expert_gather.swap(slice(0, cuts[2]), 4)
    for ab in range(2):
        attn_sum.second_send(ab)
    expert_gather.swap(slice(cuts[2], piece_rows), 2)
    for ab in (1, 0):
        attn_sum.last_sum(ab)
    attn_gather.near(0)
    forward()
    for copy in vec_copies:
        copy.wait()
    vec = vec_own[...] + vec_in[0] + half_swap(vec_in[1] + vec_in[2])
    inner = column(vec[6:7, 0:HALF])[:, 0:1]
    fetch.wait("own")
    gain_in = gain[...].reshape(1, width)
    done()
    done = small_stage(2)
    attn_sum.wait_peer()
    attn_gather.near(1)
    attn_gather.far(0)
    attn_gather.far(1)
    done()
    done = small_stage(3)
    finish()
    attn_gather.swap(count=1, ab=0)
    for h in range(4):
        rows = slice(h * 128, (h + 1) * 128)
        grad = (
            partial[rows, 0:width].astype(f32)
            + far2[rows].astype(f32)
            + far3[rows].astype(f32)
            + tn(logits_low[:, rows], router_low[:, 0:width])
        )
        input_grad[rows] = hidden_grad[rows] + norm_back_rows(
            grad,
            gain_in,
            tokens[rows].astype(f32),
            scale[rows, 0:1],
            inner[rows],
            full,
        )
    done()
    attn_gather.swap(count=1, ab=1)
    sent()
    layer_sent()
    attn_sum.done()
    expert_gather.done()
    attn_gather.done()


def attn_back(
    q,
    k,
    v,
    lse,
    seg,
    cosine,
    sine,
    context,
    hidden_low,
    out_weight,
    qkv_weight,
    normed,
    small_all,
    gates,
    vec_sums,
    ffn_part,
    tokens,
    scale,
    gain,
    hidden_grad,
    layer_part,
    hidden,
    expert_shard,
):
    xs, zs, cs = dp_sizes()
    total, full = normed.shape
    width = full // 2
    quarter = HALF // 2
    heads = q.shape[1] // HEAD
    cols = qkv_weight.shape[1]
    piece = (2 * SIDE // (xs * zs), (cols + SIDE) // 2)
    return pl.pallas_call(
        functools.partial(attn_back_kernel, heads),
        out_shape=(
            jax.ShapeDtypeStruct((HALF, width), f32),
            jax.ShapeDtypeStruct((HALF, width), bf16),
            jax.ShapeDtypeStruct((8, width), f32),
            jax.ShapeDtypeStruct((cs, 2, xs * zs) + piece, bf16),
            jax.ShapeDtypeStruct((cs, 2, xs * zs) + expert_shard.shape[1:], bf16),
        ),
        in_specs=[ANY] * 3
        + [WHOLE] * 2
        + [ANY] * 4
        + [WHOLE]
        + [ANY] * 2
        + [WHOLE] * 4
        + [ANY] * 2
        + [WHOLE] + [ANY] * 3 + [WHOLE],
        out_specs=(WHOLE, WHOLE, WHOLE, ANY, ANY),
        scratch_shapes=[
            VMEM(q.shape, bf16),
            VMEM(k.shape, bf16),
            VMEM(v.shape, bf16),
            VMEM(cosine.shape, f32),
            VMEM(sine.shape, f32),
            VMEM(context.shape, bf16),
            VMEM(hidden_low.shape, bf16),
            VMEM(qkv_weight.shape, bf16),
            VMEM(normed.shape, bf16),
            VMEM(tokens.shape, bf16),
            VMEM((HALF, 128), f32),
            VMEM(hidden_grad.shape, f32),
            VMEM((HEAD, total), bf16),
            VMEM(q.shape, bf16),
            VMEM(k.shape, f32),
            VMEM(v.shape, f32),
            VMEM((total, cols), bf16),
            VMEM((total, full), bf16),
            VMEM((full, cols), bf16),
            VMEM((SIDE, full), bf16),
        ]
        + group_scratch(width)
        + [
            VMEM((HALF, width), bf16),
            VMEM((quarter, width), bf16),
            VMEM((quarter, width), bf16),
            VMEM((HALF, width), f32),
        ]
        + group_scratch(width)
        + [
            VMEM((8, total), f32),
            VMEM((3, 8, total), f32),
            VMEM((4, 8, full), f32),
            VMEM((xs + zs + 2, 8, full), f32),
            VMEM((2,) + piece, bf16),
            VMEM((total, 128), f32),
            VMEM((1, total), f32),
        ]
        + plane_scratch(SIDE, cols + SIDE, True)
        + [
            pltpu.SemaphoreType.DMA((128,)),
            pltpu.SemaphoreType.DMA((128,)),
            pltpu.SemaphoreType.DMA((24,)),
            pltpu.SemaphoreType.DMA((2, 2)),
        ],
        compiler_params=pltpu.CompilerParams(
            collective_id=3, has_side_effects=True, vmem_limit_bytes=60 * 2**20
        ),
        name="attn_back",
    )(
        q,
        k,
        v,
        lse,
        seg,
        cosine,
        sine,
        context,
        hidden_low,
        out_weight,
        qkv_weight,
        normed,
        small_all,
        gates,
        vec_sums,
        ffn_part,
        tokens,
        scale,
        gain,
        hidden_grad,
        layer_part,
        hidden,
        expert_shard,
    )


def swap_halves(v):
    half = v.shape[-1] // 2
    return jnp.concatenate([v[..., half:], v[..., :half]], axis=-1)


def experts_kernel(
    normed_h,
    cot_own,
    cot_2,
    cot_3,
    gates,
    gate_weight,
    up_weight,
    down_weight,
    units,
    weighted_h,
    grads_h,
    back_h,
    out_h,
    cot_all_h,
    far_2,
    far_3,
    vec_ref,
    normed,
    cot,
    gate_up,
    down,
    weighted,
    grads,
    back,
    out,
    send,
    recv,
    sems,
):
    links = Links(send, recv)
    col = links.col
    count, _, pieces, unit, both = gate_up.shape
    blocks, down_unit, full = down.shape
    width = full // 2
    hidden = both // 2
    quarter = HALF // 2
    other, own = slice(HALF, 2 * HALF), slice(0, HALF)
    fetch = Fetch(sems)
    fetch.start("normed", (normed_h.at[other], normed.at[other]))
    for e in range(count):
        for which, weight in enumerate((gate_weight, up_weight)):
            cols = slice(which * hidden, (which + 1) * hidden)
            fetch.start(
                ("gate_up", e),
                (weight.at[col * count + e], gate_up.at[e, 0, :, :, cols]),
                (
                    units.at[which, :, (3 + e) * unit : (4 + e) * unit],
                    gate_up.at[e, 1, :, :, cols],
                ),
            )
    fetch.start(
        "cot",
        (cot_2, cot.at[HALF + quarter :, 0:width]),
        (cot_3, cot.at[HALF : HALF + quarter, width:]),
        (cot_own, cot.at[own, 0:width]),
    )
    fetch.start("down", (down_weight.at[pl.ds(col * blocks, blocks)], down.at[:, :, 0:width]))
    for j in range(-(-blocks // pieces)):
        n = min(pieces, blocks - j * pieces)
        start = (3 + count) * unit + j * down_unit
        for core in range(2):
            first = width + core * SIDE
            fetch.start(
                "down",
                (
                    units.at[core, 0:n, start : start + down_unit],
                    down.at[j * pieces : j * pieces + n, :, first : first + SIDE],
                ),
            )
    fetch.start("normed_own", (normed_h.at[own], normed.at[own]))
    links.greet([links.group(2), links.group(3)])
    direct = [
        links.go(cot_own.at[0:quarter], cot.at[HALF : HALF + quarter, 0:width], links.group(2)),
        links.go(cot_own.at[quarter:], cot.at[HALF + quarter :, width:], links.group(3)),
    ]
    relays = [
        links.go(cot_3, cot.at[0:quarter, width:], links.group(2)),
        links.go(cot_2, cot.at[quarter:HALF, width:], links.group(3)),
    ]
    fetch.wait("normed")
    all_pres = [[], []]
    for e in range(count):
        fetch.wait(("gate_up", e))
        all_pres[0].append(nn(normed[other], gate_up[e].reshape(full, both)))
    fetch.wait("normed_own")
    for e in range(count):
        all_pres[1].append(nn(normed[own], gate_up[e].reshape(full, both)))
    for step, rows in enumerate((other, own)):
        lanes = lax.broadcasted_iota(jnp.int32, (HALF, 128), 1)
        vec = jnp.zeros((HALF, 128), f32)
        inner = jnp.zeros((HALF, 1), f32)
        pres = all_pres[step]
        if step == 0:
            fetch.wait("cot", "down")
            for copy in direct:
                copy.wait_recv()
        else:
            for copy in relays:
                copy.wait_recv()
        y = cot[rows]
        for e in range(count):
            down_e = down[...].reshape(count, hidden, full)[e]
            here = lanes == col * count + e
            gate = jnp.sum(jnp.where(here, gates[rows], 0.0), axis=1, keepdims=True)
            gate_pre, up_pre = pres[e][:, :hidden], pres[e][:, hidden:]
            sigmoid = 1.0 / (1.0 + jnp.exp(-gate_pre))
            silu = gate_pre * sigmoid
            activated = silu * up_pre
            weighted[rows, e * hidden : (e + 1) * hidden] = (gate * activated).astype(bf16)
            weighted_grad = nt(y, down_e)
            both_terms = activated * weighted_grad
            part = jnp.sum(both_terms, axis=1, keepdims=True)
            vec = vec + jnp.where(here, part, 0.0)
            slope = 1.0 + gate_pre * (1.0 - sigmoid)
            g = gate * weighted_grad
            gate_grad = g * up_pre * (sigmoid * slope)
            up_grad = g * silu
            inner = inner + gate * (
                part + jnp.sum(both_terms * slope, axis=1, keepdims=True)
            )
            grads[e, rows] = jnp.concatenate([gate_grad, up_grad], axis=1).astype(bf16)
        fetch.start("out", *[(grads.at[e, rows], grads_h.at[e, rows]) for e in range(count)])
        fetch.start("out", (weighted.at[rows], weighted_h.at[rows]))
        fetch.start("out", (cot.at[rows], cot_all_h.at[rows]))
        total = None
        for e in range(count):
            term = nt(grads[e, rows], gate_up[e].reshape(full, both))
            total = term if total is None else total + term
        back[rows] = total.astype(bf16)
        if step == 0:
            sums = [
                links.go(back.at[HALF + quarter :, width:], far_3, links.group(3)),
                links.go(back.at[HALF : HALF + quarter, 0:width], far_2, links.group(2)),
            ]
        fetch.start("out", (back.at[rows], back_h.at[rows]))
        out[rows] = nn(weighted[rows], down[...].reshape(count * hidden, full)).astype(bf16)
        fetch.start("out", (out.at[rows], out_h.at[rows]))
        vec = jnp.where(lanes == 6, inner, vec)
        vec_ref[:, rows] = vec.T[0:8, :]
    for copy in direct + relays:
        copy.wait_send()
    for copy in sums:
        copy.wait()
    fetch.wait("out")


def experts_step(
    normed, cot_own, cot_2, cot_3, gates, gate_weight, up_weight, down_weight, units
):
    total, width = normed.shape
    experts, own_width, hidden = gate_weight.shape
    count = experts // 2
    both = 2 * hidden
    hid = count * hidden
    pieces = units.shape[1]
    unit, down_unit = unit_rows()
    return pl.pallas_call(
        experts_kernel,
        out_shape=(
            jax.ShapeDtypeStruct((total, hid), bf16),
            jax.ShapeDtypeStruct((count, total, both), bf16),
            jax.ShapeDtypeStruct((total, width), bf16),
            jax.ShapeDtypeStruct((total, width), bf16),
            jax.ShapeDtypeStruct((total, width), bf16),
            jax.ShapeDtypeStruct((HALF // 2, own_width), bf16),
            jax.ShapeDtypeStruct((HALF // 2, own_width), bf16),
            jax.ShapeDtypeStruct((8, total), f32),
        ),
        in_specs=[ANY] * 4 + [WHOLE] + [ANY] * 4,
        out_specs=(ANY,) * 7 + (WHOLE,),
        scratch_shapes=[
            VMEM((total, width), bf16),
            VMEM((total, width), bf16),
            VMEM((count, 2, pieces, unit, both), bf16),
            VMEM((hid // down_unit, down_unit, width), bf16),
            VMEM((total, hid), bf16),
            VMEM((count, total, both), bf16),
            VMEM((total, width), bf16),
            VMEM((total, width), bf16),
            pltpu.SemaphoreType.DMA((6,)),
            pltpu.SemaphoreType.DMA((6,)),
            pltpu.SemaphoreType.DMA((48,)),
        ],
        compiler_params=pltpu.CompilerParams(
            collective_id=1, has_side_effects=True, vmem_limit_bytes=60 * 2**20
        ),
        name="experts",
    )(
        normed,
        cot_own,
        cot_2,
        cot_3,
        gates,
        gate_weight.reshape(experts, pieces, unit, hidden),
        up_weight.reshape(experts, pieces, unit, hidden),
        down_weight.reshape(-1, down_unit, own_width),
        units,
    )


def window(i, block):
    first = max(0, (i + 1) * block - 512 - block)
    return first, (i + 1) * block


def allowed_keys(segk, segq, i, first, last):
    width = last - first
    keys = lax.broadcasted_iota(jnp.int32, (width, BLOCK), 0) + first
    queries = lax.broadcasted_iota(jnp.int32, (width, BLOCK), 1) + i * BLOCK
    same = segk[first:last, 0:1] == segq[:, i * BLOCK : (i + 1) * BLOCK]
    return (keys <= queries) & same


def finish_kernel(
    col_ref,
    sums,
    input_ref,
    layer_ref,
    small,
    attn_h,
    gate_ref,
    up_ref,
    down_ref,
    input_out,
    layer_out,
    router_ref,
    attn_gain,
    ffn_gain,
    qkv_out,
    out_out,
    attn_sums,
    qkv_grad,
    out_grad,
    sems,
):
    ab, j = pl.program_id(0), pl.program_id(1)
    steps = pl.num_programs(1)
    count, rows = gate_ref.shape[1:3]
    down_rows = down_ref.shape[2]
    fetch = pltpu.make_async_copy(attn_h, attn_sums, sems.at[0])
    store = [
        pltpu.make_async_copy(qkv_grad, qkv_out, sems.at[1]),
        pltpu.make_async_copy(out_grad, out_out, sems.at[2]),
    ]

    @pl.when((ab == 0) & (j == 0))
    def _():
        fetch.start()

    cores, _, pieces = sums.shape[:3]
    step, down_step = count * rows // pieces, count * down_rows // pieces
    first = pad16(step)
    for which, ref in enumerate((gate_ref, up_ref)):
        block = sums[which, 0, :, 0:step].astype(f32)
        ref[0] = block.reshape(count, rows, SIDE)
    for core in range(cores):
        block = sums[core, 0, :, first : first + down_step].astype(f32)
        down_ref[0, :, :, core * SIDE : (core + 1) * SIDE] = block.reshape(
            count, down_rows, SIDE
        )
    input_out[...] = input_ref[...]
    layer_out[...] = layer_ref[...]

    @pl.when((ab == 1) & (j == 0))
    def _():
        fetch.wait()
        col = col_ref[0]
        cores, _, pieces = attn_sums.shape[:3]
        kept_rows = SIDE // pieces
        middle = attn_sums.shape[4]
        pair = middle - SIDE
        for core in range(cores):
            kept = None
            here = slice(core * SIDE, (core + 1) * SIDE)
            for part in range(2):
                half = col if part == 0 else 1 - col
                block = attn_sums[core, part].astype(f32)
                left = block[:, 0:kept_rows].reshape(SIDE, middle)
                right = block[:, kept_rows:].reshape(SIDE, middle)
                qkv_grad[here, at(half * SIDE, SIDE, 128)] = left[:, 0:SIDE]
                out_grad[at(half * SIDE, SIDE), here] = right[:, pair:]
                both = jnp.concatenate([left[:, SIDE:], right[:, 0:pair]], axis=1)
                kept = both if kept is None else kept + both
            qkv_grad[here, 2 * SIDE :] = kept
        for copy in store:
            copy.start()
        value = small[...]
        attn_gain[...] = value[6:7].reshape(attn_gain.shape)
        ffn_gain[...] = value[7:8].reshape(ffn_gain.shape)
        router_ref[...] = value[0 : router_ref.shape[0]]

    @pl.when((ab == 1) & (j == steps - 1))
    def _():
        for copy in store:
            copy.wait()


def finish_step(sums, input_grad, layer_out, small, attn_sums, col, experts):
    xs, zs, cs = dp_sizes()
    piece = sums.shape[-2]
    own_rows, width = input_grad.shape
    part = own_rows // (2 * xs)
    cols = SIDE + 2 * HEAD
    count = experts // 2

    def out_spec(rows, width):
        return pl.BlockSpec(
            (1, count, rows, width),
            lambda ab, j, col_ref: (jnp.where(ab == 0, col_ref[0], 1 - col_ref[0]), 0, j, 0),
        )

    rows_spec = pl.BlockSpec((part, width), lambda ab, j, col_ref: (ab * xs + j, 0))

    def whole(shape):
        return pl.BlockSpec(shape, lambda ab, j, col_ref: (0,) * len(shape))

    return pl.pallas_call(
        finish_kernel,
        grid_spec=pltpu.PrefetchScalarGridSpec(
            num_scalar_prefetch=1,
            grid=(2, xs),
            in_specs=[
                pl.BlockSpec(
                    (cs, 1, zs, piece, SIDE), lambda ab, j, col_ref: (0, ab, j, 0, 0)
                ),
                rows_spec,
                rows_spec,
                whole(small.shape),
                ANY,
            ],
            out_specs=(
                out_spec(width // xs, SIDE),
                out_spec(width // xs, SIDE),
                out_spec(SIDE // xs, width),
                rows_spec,
                rows_spec,
                whole((experts, width)),
                whole((width,)),
                whole((width,)),
                ANY,
                ANY,
            ),
            scratch_shapes=[
                VMEM(attn_sums.shape, bf16),
                VMEM((2 * SIDE, SIDE + cols), f32),
                VMEM((2 * SIDE, 2 * SIDE), f32),
                pltpu.SemaphoreType.DMA((3,)),
            ],
        ),
        out_shape=(
            jax.ShapeDtypeStruct((2, count, width, SIDE), f32),
            jax.ShapeDtypeStruct((2, count, width, SIDE), f32),
            jax.ShapeDtypeStruct((2, count, SIDE, width), f32),
            jax.ShapeDtypeStruct(input_grad.shape, f32),
            jax.ShapeDtypeStruct(layer_out.shape, bf16),
            jax.ShapeDtypeStruct((experts, width), f32),
            jax.ShapeDtypeStruct((width,), f32),
            jax.ShapeDtypeStruct((width,), f32),
            jax.ShapeDtypeStruct((2 * SIDE, SIDE + cols), f32),
            jax.ShapeDtypeStruct((2 * SIDE, 2 * SIDE), f32),
        ),
        compiler_params=pltpu.CompilerParams(vmem_limit_bytes=56 * 2**20),
        name="finish",
    )(col.reshape(1), sums, input_grad, layer_out, small, attn_sums)


def turn_tables(total):
    steps_up = np.arange(HEAD // 2, dtype=np.float32) * np.float32(2.0 / HEAD)
    inverse = np.exp(np.float32(-math.log(ROPE_BASE)) * steps_up)
    angles = (np.arange(total, dtype=np.float32)[:, None] * inverse[None, :]).astype(np.float64)
    cosine, sine = np.cos(angles), np.sin(angles)
    return (
        np.concatenate([cosine, cosine], axis=1).astype(np.float32),
        np.concatenate([-sine, sine], axis=1).astype(np.float32),
    )


def local(
    tokens,
    cotangent,
    attn_gain,
    ffn_gain,
    qkv_weight,
    out_weight,
    router_weight,
    gate_weight,
    up_weight,
    down_weight,
    routes,
    segments,
):
    col = lax.axis_index("col")
    xs, zs, cs = dp_sizes()
    own_rows, own_width = tokens.shape
    experts, _, hidden = gate_weight.shape
    pieces = xs * zs
    cosine, sine = turn_tables(2 * own_rows)
    seg = segments[None]
    (
        normed_one,
        queries,
        keys,
        values,
        context,
        qkv_local,
        normed_two,
        out_quarter,
        cot_2,
        cot_3,
        units,
        lse,
        gates,
        scale_one,
        small_all,
        hidden_own,
        scale_two,
    ) = forward_step(
        tokens,
        cotangent,
        qkv_weight,
        router_weight.T,
        attn_gain,
        ffn_gain,
        routes.T,
        cosine,
        sine,
        seg,
        out_weight,
        gate_weight,
        up_weight,
        down_weight,
    )
    (
        weighted,
        pre_grads,
        normed_two_part,
        layer_part,
        cot_all,
        far_2,
        far_3,
        expert_vec,
    ) = experts_step(
        normed_two,
        cotangent,
        cot_2,
        cot_3,
        gates,
        gate_weight,
        up_weight,
        down_weight,
        units.reshape((cs, pieces) + units.shape[3:]),
    )
    hidden_grad, hidden_low, vec_sums, ffn_part, shard = reduce_step(
        normed_two_part,
        expert_vec,
        hidden_own,
        cotangent,
        scale_two,
        ffn_gain,
        normed_two,
        pre_grads,
        weighted,
        cot_all,
        far_2,
        far_3,
    )
    input_grad, layer_out, small_sums, attn_sums, expert_sums = attn_back(
        queries,
        keys,
        values,
        lse,
        seg,
        cosine,
        sine,
        context,
        hidden_low,
        out_quarter.reshape(SIDE, 2 * own_width),
        qkv_local,
        normed_one,
        small_all,
        gates,
        vec_sums,
        ffn_part,
        tokens,
        scale_one,
        attn_gain,
        hidden_grad,
        layer_part,
        hidden_own,
        shard,
    )
    (
        gate_grad,
        up_grad,
        down_grad,
        input_grad,
        layer_out,
        router_grad,
        attn_gain_grad,
        ffn_gain_grad,
        qkv_grad,
        out_grad,
    ) = finish_step(
        expert_sums,
        input_grad,
        layer_out,
        small_sums,
        attn_sums,
        col,
        experts,
    )
    router_grad = router_grad.T
    gate_grad = gate_grad.reshape(experts, own_width, hidden)
    up_grad = up_grad.reshape(experts, own_width, hidden)
    down_grad = down_grad.reshape(experts, hidden, own_width)
    return (
        layer_out,
        input_grad,
        attn_gain_grad,
        ffn_gain_grad,
        qkv_grad,
        out_grad,
        router_grad,
        gate_grad,
        up_grad,
        down_grad,
    )


def solution(mesh):
    in_specs = (
        P(("dp", "row"), "col"),
        P(("dp", "row"), "col"),
        P("col"),
        P("col"),
        P("col", "row"),
        P("row", "col"),
        P("col", None),
        P(None, "col", "row"),
        P(None, "col", "row"),
        P(None, "row", "col"),
        P("dp", None),
        P("dp"),
    )
    out_specs = (
        P(("dp", "row"), "col"),
        P(("dp", "row"), "col"),
        P("col"),
        P("col"),
        P("col", "row"),
        P("row", "col"),
        P("col", None),
        P(None, "col", "row"),
        P(None, "col", "row"),
        P(None, "row", "col"),
    )
    return jax.shard_map(local, mesh=mesh, in_specs=in_specs, out_specs=out_specs, check_vma=False)
```
